32 devices in a mesh: role: 2 (over core), group: 4 (over z), tp: 4 (over y, x).
Axes of the slice: x: 2, y: 2, z: 4, core: 2. Of those that a mesh axis runs over, the one named last changes fastest.
Arguments:
- kv_pages: bfloat16 [2, 4, 4, 64, 128, 512], P('role', 'group', 'tp'), may hold values from -24 to 24, as said below
- send_list: int32 [4, 12, 3], replicated, may hold values from 0 to 63, as said below
- wanted: int32 [4, 6], replicated, may hold values from 0 to 31, as said below
- lengths: int32 [4, 8], P('group'), may hold values from 1 to 1024, as said below
- tables: int32 [4, 8, 8], P('group'), may hold values from 0 to 69, as said below
- queries: bfloat16 [4, 8, 8192], P('group', None, 'tp'), may hold values from -160 to 160
- new_kv: bfloat16 [4, 8, 2048], P('group', None, 'tp'), may hold values from -24 to 24, as said below
- out_weight: bfloat16 [8192, 8192], P('tp', 'role'), may hold values from -3 to 3
Outputs:
- mixed: bfloat16 [4, 8, 8192], P('group', None, ('role', 'tp'))
The draws below stay inside these ranges and needn't reach their ends.
Inputs may be any that keep to these rules, and one draw needn't show every extreme that they name: `send_list`: column 0 holds 12 distinct store pages of a prefill group, from 8 on; column 1 the destination decode group; column 2 the destination slot. The pairs (destination group, slot) are distinct over all groups. At most 4 pages go from one prefill group to one decode group, and one decode group receives exactly 4 from every prefill group. `wanted`: row g lists 6 distinct pages; page o * 8 + p is store slot p of prefill group o. Each row names pages of exactly 3 owner groups, 2 of each. `lengths`: in every group some row has exactly 1024 tokens. `tables`: entry j of a row serves its tokens j * 128 to (j + 1) * 128 - 1 below its length. An entry below 64 names a slot of the decode device's cache; an entry s from 64 on names the (s - 64)-th wanted page of the group. The entries a row reads are distinct, no cache slot is read by two rows of a group, and entries past a row's last page are 0. `new_kv`: indices of tp that hold the same key-value head hold equal new keys and values. `kv_pages`: indices of tp that hold the same key-value head hold equal pages.
All inputs are finite; a program needn't handle non-finite values.
Results may differ from the reference program's by a relative error of at most 0.006.
Values may be sent and summed in bfloat16 or wider, within the bound.
No kernel may reach another device: no remote copies, remote signals or barrier semaphores. Data moves between devices by JAX's collectives and lax.ppermute only.
A program may use at most 128 MiB of HBM per device.

```python
import math
import jax
import jax.numpy as jnp
from jax import lax

D = 8192
QHEADS = 64
KVH = 8
HD = 128
PAGE = 128
CTX = 1024
ROWS = 8
CAP = 4
PRE_DEV = 8
CAPP = 2
OWNERS = 3
KV_DEV = 2
SENDS = 12
MAXP = 8
SLOTS = 64
WANT = 6
PREFIX = 32
N_GROUP = 4
N_TP = 4


def length_draw(key):
    key = jax.random.fold_in(key, 902)
    first, second = jax.random.split(key)
    drawn = jax.random.randint(first, (N_GROUP, ROWS), 1, CTX + 1)
    longest = jax.random.randint(second, (N_GROUP, 1), 0, ROWS)
    return jnp.where(jnp.arange(ROWS)[None, :] == longest, CTX, drawn).astype(jnp.int32)


def held_heads():
    return jnp.arange(N_TP)[:, None] * KVH // N_TP + jnp.arange(KV_DEV)[None, :]


def draw_kv_pages(key, part):
    key = jax.random.fold_in(key, 11)
    values = jnp.clip(jax.random.normal(key, (2, N_GROUP, KVH, SLOTS, PAGE, 2, HD), jnp.float32), -6.0, 6.0)
    values = values.astype(jnp.bfloat16)[:, :, held_heads()]
    values = jnp.transpose(values, (0, 1, 2, 4, 5, 3, 6, 7))
    return values.reshape(2, N_GROUP, N_TP, SLOTS, PAGE, 2 * KV_DEV * HD)


def draw_new_kv(key, part):
    key = jax.random.fold_in(key, 13)
    values = jnp.clip(jax.random.normal(key, (N_GROUP, ROWS, KVH, 2, HD), jnp.float32), -6.0, 6.0)
    values = values.astype(jnp.bfloat16)[:, :, held_heads()]
    return values.reshape(N_GROUP, ROWS, N_TP * KV_DEV * 2 * HD)


def draw_queries(key, part):
    key = jax.random.fold_in(key, 12)
    first = jax.random.fold_in(key, 0)
    values = jnp.clip(jax.random.normal(first, (N_GROUP, ROWS, QHEADS, HD), jnp.float32), -6.0, 6.0)
    return values.reshape(N_GROUP, ROWS, QHEADS * HD).astype(jnp.bfloat16)


def draw_send_list(key, part):
    key = jax.random.fold_in(key, 14)
    streams = jax.random.split(key, 5)
    target = jax.random.randint(streams[0], (), 0, N_GROUP)
    offsets = jax.random.randint(streams[1], (N_GROUP,), 0, N_GROUP - 1)
    others = jax.vmap(lambda k: jax.random.permutation(k, N_GROUP - 1))(jax.random.split(streams[2], N_GROUP))
    step = jnp.arange(SENDS)
    index = (step[None, :] - CAP + offsets[:, None]) % (N_GROUP - 1)
    picked = jnp.take_along_axis(others, index, 1)
    picked = picked + (picked >= target).astype(jnp.int32)
    target_group = jnp.where(step[None, :] < CAP, target, picked)
    store_pages = jax.vmap(lambda k: PRE_DEV + jax.random.permutation(k, SLOTS - PRE_DEV)[:SENDS])(jax.random.split(streams[3], N_GROUP))
    flat = target_group.reshape(-1)
    matches = (flat[:, None] == jnp.arange(N_GROUP)[None, :]).astype(jnp.int32)
    order_rank = jnp.sum((jnp.cumsum(matches, 0) - matches) * matches, 1)
    slot_order = jax.vmap(lambda k: jax.random.permutation(k, SLOTS))(jax.random.split(streams[4], N_GROUP))
    target_slot = slot_order[flat, order_rank].reshape(N_GROUP, SENDS)
    return jnp.stack([store_pages, target_group, target_slot], -1).astype(jnp.int32)


def draw_wanted(key, part):
    key = jax.random.fold_in(key, 15)
    streams = jax.random.split(key, 3)
    owners = jax.vmap(lambda k: jax.random.permutation(k, N_GROUP)[:OWNERS])(jax.random.split(streams[0], N_GROUP))
    chosen = jax.vmap(lambda k: jax.random.permutation(k, PRE_DEV)[:CAPP])(jax.random.split(streams[1], N_GROUP * OWNERS))
    page_ids = (owners[:, :, None] * PRE_DEV + chosen.reshape(N_GROUP, OWNERS, CAPP)).reshape(N_GROUP, WANT)
    shuffle = jax.vmap(lambda k: jax.random.permutation(k, WANT))(jax.random.split(streams[2], N_GROUP))
    return jnp.take_along_axis(page_ids, shuffle, 1).astype(jnp.int32)


def draw_lengths(key, part):
    return length_draw(key)


def draw_tables(key, part):
    drawn_lengths = length_draw(key)
    key = jax.random.fold_in(key, 16)
    streams = jax.random.split(key, 3)
    page_count = (drawn_lengths + PAGE - 1) // PAGE
    prefix_count = jnp.minimum(jax.random.randint(streams[0], (N_GROUP, ROWS), 0, min(5, WANT + 1)), page_count - 1)
    start = jax.random.randint(streams[1], (N_GROUP, ROWS), 0, WANT)
    own_count = page_count - prefix_count
    offset = jnp.cumsum(own_count, 1) - own_count
    slot_order = jax.vmap(lambda k: jax.random.permutation(k, SLOTS))(jax.random.split(streams[2], N_GROUP))
    step = jnp.arange(MAXP)[None, None, :]
    local_index = jnp.clip(offset[:, :, None] + step - prefix_count[:, :, None], 0, SLOTS - 1)
    local = jax.vmap(lambda order, index: order[index])(slot_order, local_index)
    shared = SLOTS + (start[:, :, None] + step) % WANT
    table = jnp.where(step < prefix_count[:, :, None], shared, jnp.where(step < page_count[:, :, None], local, 0))
    return table.astype(jnp.int32)


def strengthened(values, own_key, source, target, parts, factor):
    def block_of(axis_at):
        return (jnp.arange(values.shape[axis_at]) // (values.shape[axis_at] // parts)).reshape((-1,) + (1,) * (values.ndim - 1 - axis_at))

    one_side = jax.random.permutation(own_key, parts)[block_of(target)]
    second = (block_of(target) + parts // 2) % parts
    return jnp.where((block_of(source) == one_side) | (block_of(source) == second), factor * values, values)


def shard_levels(key, extent, cuts, smallest, top_value):
    loudness = 1.0
    for axis_at, parts in cuts:
        steps = jax.random.uniform(jax.random.fold_in(jax.random.fold_in(key, 6), axis_at), (parts,), jnp.float32, smallest / len(cuts), top_value / len(cuts))
        loudness = loudness * jnp.repeat(jnp.exp(steps), extent[axis_at] // parts).reshape((-1,) + (1,) * (len(extent) - 1 - axis_at))
    return loudness


def noise_with(stream_key, extent, scale, bound, shards, heavy, kind=jnp.bfloat16):
    values = scale * jax.random.normal(stream_key, extent, jnp.float32)
    if shards:
        values = values * shard_levels(stream_key, extent, shards, -0.22, 0.18)
    return jnp.clip(strengthened(values, jax.random.fold_in(stream_key, 3), *heavy), -bound, bound).astype(kind)


def setup_inputs(seed: int = 0) -> dict:
    key_list = jax.random.split(jax.random.key(seed), 9)
    return {
        "kv_pages": draw_kv_pages(jax.random.fold_in(key_list[8], 71), 0),
        "send_list": draw_send_list(jax.random.fold_in(key_list[8], 71), 0),
        "wanted": draw_wanted(jax.random.fold_in(key_list[8], 71), 0),
        "lengths": draw_lengths(jax.random.fold_in(key_list[8], 71), 0),
        "tables": draw_tables(jax.random.fold_in(key_list[8], 71), 0),
        "queries": draw_queries(jax.random.fold_in(key_list[8], 71), 0),
        "new_kv": draw_new_kv(jax.random.fold_in(key_list[8], 71), 0),
        "out_weight": noise_with(key_list[7], (QHEADS * HD, D), 8 ** -0.5, 3.0, ((0, 4), (1, 2)), (0, 1, 4, 2.0)),
    }


def reference(kv_pages, send_list, wanted, lengths, tables, queries, new_kv, out_weight):
    prefill_store = kv_pages[0]
    decode_cache = kv_pages[1]
    sources = jnp.repeat(jnp.arange(N_GROUP, dtype=jnp.int32), SENDS)
    page_ids = send_list[:, :, 0].reshape(-1)
    targets = send_list[:, :, 1].reshape(-1)
    target_slots = send_list[:, :, 2].reshape(-1)
    moved = prefill_store[sources, :, page_ids]
    decode_cache = decode_cache.at[targets, :, target_slots].set(moved)
    prefix = jnp.transpose(prefill_store[:, :, :PRE_DEV], (1, 0, 2, 3, 4)).reshape(N_TP, PREFIX, PAGE, 2 * KV_DEV * HD)
    per_held = QHEADS // N_TP // KV_DEV

    def one_group(group_item):
        group_cache, wanted_row, token_counts, table, query, fresh = group_item
        page_pool = jnp.concatenate([group_cache, prefix[:, wanted_row]], 1)
        pages = page_pool[:, table].reshape(N_TP, ROWS, CTX, KV_DEV, 2 * HD).astype(jnp.float32)
        cache_keys = pages[..., :HD]
        cache_values = pages[..., HD:]
        query_heads = query.reshape(ROWS, N_TP, KV_DEV, per_held, HD).astype(jnp.float32)
        fresh_kv = fresh.reshape(ROWS, N_TP, KV_DEV, 2, HD).astype(jnp.float32)
        scores = jnp.einsum('rtjhd,trkjd->rtjhk', query_heads, cache_keys) / math.sqrt(HD)
        own_score = jnp.einsum('rtjhd,rtjd->rtjh', query_heads, fresh_kv[:, :, :, 0]) / math.sqrt(HD)
        is_valid = (jnp.arange(CTX)[None, :] < token_counts[:, None])[:, None, None, None, :]
        row_top = jnp.maximum(lax.optimization_barrier(jnp.max(jnp.where(is_valid, scores, -jnp.inf), -1)), own_score)
        lifted = jnp.where(is_valid, jnp.exp(scores - row_top[..., None]), 0.0)
        own_lift = jnp.exp(own_score - row_top)
        row_total = lax.optimization_barrier(jnp.sum(lifted, -1)) + own_lift
        weights = (lifted / row_total[..., None]).astype(jnp.bfloat16)
        own_weight = (own_lift / row_total).astype(jnp.bfloat16)
        attended = jnp.einsum('rtjhk,trkjd->rtjhd', weights.astype(jnp.float32), cache_values)
        attended = attended + own_weight.astype(jnp.float32)[..., None] * fresh_kv[:, :, :, None, 1]
        attended = attended.astype(jnp.bfloat16).reshape(ROWS, QHEADS * HD)
        return jnp.dot(attended, out_weight, preferred_element_type=jnp.float32).astype(jnp.bfloat16)
    return lax.map(one_group, (decode_cache, wanted, lengths, tables, queries, new_kv))
```

```python
import functools
import math

import jax
import jax.numpy as jnp
from jax import lax
from jax.experimental import pallas as pl
from jax.experimental.pallas import tpu as pltpu
from jax.sharding import PartitionSpec as P

KVH = 8
HD = 128
CAP = 4
CAPP = 2
PRE_DEV = 8
LANES = 128
NEG = -1e30
SCALE = 1.0 / math.sqrt(HD)
PARTS = CAP + CAPP


def head_rows(q, first, count):
    return jnp.concatenate([q[:, (first + i) * HD : (first + i + 1) * HD] for i in range(count)], 0)


def stats_block(columns):
    rows = columns[0].shape[0]
    lane = lax.broadcasted_iota(jnp.int32, (rows, LANES), 1)
    out = jnp.zeros((rows, LANES), jnp.float32)
    for h, column in enumerate(columns):
        out = jnp.where(lane == h, column, out)
    return out


def list_pages(send, wanted, owner, target, slots, page_list, slot_list, base):
    for c in range(PARTS):
        page_list[base + c] = 0
        slot_list[base + c] = -1
    sends = send.shape[1] // 3

    def sent(j, count):
        hit = send[owner, 3 * j + 1] == target

        @pl.when(hit)
        def _():
            page_list[base + count] = send[owner, 3 * j]
            slot_list[base + count] = send[owner, 3 * j + 2]

        return count + hit.astype(jnp.int32)

    lax.fori_loop(0, sends, sent, 0, unroll=True)

    def prefix(j, count):
        page = wanted[target, j]
        hit = page // PRE_DEV == owner

        @pl.when(hit)
        def _():
            page_list[base + CAP + count] = page % PRE_DEV
            slot_list[base + CAP + count] = slots + j

        return count + hit.astype(jnp.int32)

    lax.fori_loop(0, wanted.shape[1], prefix, 0, unroll=True)


def owner_part(qa, pages, slot_list, base, out, held, per_held, maxp):
    rows = qa.shape[0]
    wide = held * per_held * HD
    q = qa[:, :wide].astype(jnp.float32)
    tab = qa[:, wide : wide + LANES].astype(jnp.float32)
    cnt = qa[:, wide + LANES : wide + 2 * LANES].astype(jnp.float32)
    lane = lax.broadcasted_iota(jnp.int32, (rows, LANES), 1)
    masks = []
    for c in range(PARTS):
        entry = slot_list[base + c].astype(jnp.float32)
        valid = jnp.sum(jnp.where(tab == entry, cnt, 0.0), 1, keepdims=True)
        masks.append(lane.astype(jnp.float32) < valid)
    mask = jnp.concatenate(masks, 1)[None]
    tops, sums = [], []
    for j in range(held):
        qj = head_rows(q, j * per_held, per_held).astype(jnp.bfloat16)
        keys = jnp.concatenate([pages[c, :, 2 * j * HD : (2 * j + 1) * HD] for c in range(PARTS)], 0)
        values = jnp.concatenate([pages[c, :, (2 * j + 1) * HD : (2 * j + 2) * HD] for c in range(PARTS)], 0)
        s = lax.dot_general(qj, keys, (((1,), (1,)), ((), ())), preferred_element_type=jnp.float32)
        s = s.reshape(per_held, rows, s.shape[1]) * SCALE
        s = jnp.where(mask, s, NEG)
        top = jnp.max(s, 2, keepdims=True)
        p = jnp.where(mask, jnp.exp(s - top), 0.0)
        total = jnp.sum(p, 2, keepdims=True)
        p = p.reshape(per_held * rows, p.shape[2]).astype(jnp.bfloat16)
        acc = jnp.dot(p, values, preferred_element_type=jnp.float32)
        out[j * per_held * rows : (j + 1) * per_held * rows, :] = acc
        tops += [top[i] for i in range(per_held)]
        sums += [total[i] for i in range(per_held)]
    end = held * per_held * rows
    out[end : end + rows, :] = stats_block(tops)
    out[end + rows : end + 2 * rows, :] = stats_block(sums)


def resident_part(qa, new_kv, send, tables, lengths, group, kv, pages, flags, sems, out, held, per_held):
    rows = qa.shape[0]
    maxp = tables.shape[1]
    slots = flags.shape[0]
    copies = []
    for r in range(rows):
        for e in range(maxp):
            slot = tables[r, e]
            slot = jnp.where(slot < slots, slot, 0)
            copy = pltpu.make_async_copy(kv.at[slot], pages.at[r, e], sems.at[r, e])
            copy.start()
            copies.append(copy)

    def clear(i, _):
        flags[i] = 0
        return 0

    lax.fori_loop(0, slots, clear, 0, unroll=8)
    sends = send.shape[1] // 3

    def mark(o, _):
        for j in range(sends):

            @pl.when(send[o, 3 * j + 1] == group)
            def _():
                flags[send[o, 3 * j + 2]] = 1

        return 0

    lax.fori_loop(0, send.shape[0], mark, 0)
    wide = held * per_held * HD
    q = qa[:, :wide].astype(jnp.float32)
    fresh = new_kv[...].astype(jnp.float32)
    lane = lax.broadcasted_iota(jnp.int32, (rows, LANES), 1)
    row = lax.broadcasted_iota(jnp.int32, (rows, LANES), 0)
    qs, owns, accs, tops, sums = [], [], [], [], []
    for j in range(held):
        qf = head_rows(q, j * per_held, per_held)
        qs.append(qf.astype(jnp.bfloat16))
        key = fresh[:, 2 * j * HD : (2 * j + 1) * HD]
        own = jnp.sum(qf.reshape(per_held, rows, HD) * key[None], 2, keepdims=True) * SCALE
        owns.append(own)
        tops.append(own)
        sums.append(jnp.zeros_like(own))
        accs.append(jnp.zeros((per_held * rows, HD), jnp.float32))
    for r in range(rows):
        masks = []
        for e in range(maxp):
            slot = tables[r, e]
            here = jnp.logical_and(slot < slots, flags[jnp.minimum(slot, slots - 1)] == 0)
            valid = jnp.where(here, lengths[0, r] - e * LANES, 0)
            masks.append(jnp.logical_and(lane < valid, row == r))
        mask = jnp.concatenate(masks, 1)[None]
        for e in range(maxp):
            copies[r * maxp + e].wait()
        for j in range(held):
            keys = jnp.concatenate([pages[r, e, :, 2 * j * HD : (2 * j + 1) * HD] for e in range(maxp)], 0)
            values = jnp.concatenate([pages[r, e, :, (2 * j + 1) * HD : (2 * j + 2) * HD] for e in range(maxp)], 0)
            s = lax.dot_general(qs[j], keys, (((1,), (1,)), ((), ())), preferred_element_type=jnp.float32)
            s = s.reshape(per_held, rows, s.shape[1]) * SCALE
            s = jnp.where(mask, s, NEG)
            top = jnp.maximum(jnp.max(s, 2, keepdims=True), owns[j])
            p = jnp.where(mask, jnp.exp(s - top), 0.0)
            sums[j] += jnp.sum(p, 2, keepdims=True)
            tops[j] = jnp.maximum(tops[j], top)
            p = p.reshape(per_held * rows, p.shape[2]).astype(jnp.bfloat16)
            accs[j] += jnp.dot(p, values, preferred_element_type=jnp.float32)
    all_tops, all_sums = [], []
    for j in range(held):
        value = fresh[:, (2 * j + 1) * HD : (2 * j + 2) * HD]
        lift = jnp.exp(owns[j] - tops[j])
        weight = lift.astype(jnp.bfloat16).astype(jnp.float32)
        acc = accs[j].reshape(per_held, rows, HD) + weight * value[None]
        out[j * per_held * rows : (j + 1) * per_held * rows, :] = acc.reshape(per_held * rows, HD)
        total = sums[j] + lift
        all_tops += [tops[j][i] for i in range(per_held)]
        all_sums += [total[i] for i in range(per_held)]
    end = held * per_held * rows
    out[end : end + rows, :] = stats_block(all_tops)
    out[end + rows : end + 2 * rows, :] = stats_block(all_sums)


def first_kernel(held, per_held, send, wanted, tables, lengths, qa, new_kv, kv, out, pages, flags, page_list, slot_list, sems):
    group = lax.axis_index("group")
    prefill = lax.axis_index("role") == 0

    @pl.when(prefill)
    def _():
        list_pages(send, wanted, group, group, kv.shape[0], page_list, slot_list, 0)
        copies = [pltpu.make_async_copy(kv.at[page_list[c]], pages.at[0, c], sems.at[0, c]) for c in range(PARTS)]
        for copy in copies:
            copy.start()
        for copy in copies:
            copy.wait()
        owner_part(qa, pages.at[0], slot_list, 0, out, held, per_held, tables.shape[1])

    @pl.when(jnp.logical_not(prefill))
    def _():
        resident_part(qa, new_kv, send, tables, lengths, group, kv, pages, flags, sems, out, held, per_held)


def second_kernel(held, per_held, maxp, count, send, wanted, *refs):
    qas, kv, outs = refs[:count], refs[count], refs[count + 1 : 2 * count + 1]
    pages, page_list, slot_list, sems = refs[2 * count + 1 :]
    group = lax.axis_index("group")
    groups = count + 1

    @pl.when(lax.axis_index("role") == 0)
    def _():
        copies = []
        for k in range(count):
            target = lax.rem(group - (k + 1) + groups, groups)
            list_pages(send, wanted, group, target, kv.shape[0], page_list, slot_list, k * PARTS)
            for c in range(PARTS):
                copy = pltpu.make_async_copy(kv.at[page_list[k * PARTS + c]], pages.at[k, c], sems.at[k, c])
                copy.start()
                copies.append(copy)
        for k in range(count):
            for c in range(PARTS):
                copies[k * PARTS + c].wait()
            owner_part(qas[k], pages.at[k], slot_list, k * PARTS, outs[k], held, per_held, maxp)


def merge_kernel(heads, rows, *refs):
    parts, out = refs[:-1], refs[-1]
    end = heads * rows
    tops = [part[end : end + rows, :] for part in parts]
    top = functools.reduce(jnp.maximum, tops)
    factors = [jnp.exp(t - top) for t in tops]
    total = functools.reduce(jnp.add, [f * part[end + rows : end + 2 * rows, :] for f, part in zip(factors, parts)])
    lane = lax.broadcasted_iota(jnp.int32, total.shape, 1)
    total = jnp.where(lane < heads, total, 1.0)
    factors = [f / total for f in factors]
    columns = []
    for h in range(heads):
        terms = [f[:, h : h + 1] * part[h * rows : (h + 1) * rows, :] for f, part in zip(factors, parts)]
        columns.append(functools.reduce(jnp.add, terms))
    out[...] = jnp.concatenate(columns, 1).astype(out.dtype)


def per_device(kv_pages, send_list, wanted, lengths, tables, queries, new_kv, out_weight):
    stored = kv_pages[0, 0, 0]
    slots, page = stored.shape[0], stored.shape[1]
    groups, tps = lax.axis_size("group"), lax.axis_size("tp")
    held = max(1, KVH // tps)
    rows, wide = queries.shape[1], queries.shape[2]
    heads = wide // HD
    per_held = heads // held
    maxp = tables.shape[2]
    send = send_list.reshape(groups, -1)
    counts = jnp.clip(lengths[0][:, None] - jnp.arange(maxp, dtype=jnp.int32)[None, :] * page, 0, page)
    pad = jnp.zeros((rows, LANES - maxp), jnp.bfloat16)
    qa = jnp.concatenate(
        [queries[0], tables[0].astype(jnp.bfloat16), pad, counts.astype(jnp.bfloat16), pad], 1
    )
    asked = [
        lax.ppermute(qa, ("role", "group"), [(i, (i + k) % groups) for i in range(groups)]) for k in range(1, groups)
    ]
    part_shape = jax.ShapeDtypeStruct(((heads + 2) * rows, HD), jnp.float32)
    smem = pl.BlockSpec(memory_space=pltpu.SMEM)
    vmem = pl.BlockSpec(memory_space=pltpu.VMEM)
    hbm = pl.BlockSpec(memory_space=pl.ANY)
    page_shape = stored.shape[1:]
    mine = pl.pallas_call(
        functools.partial(first_kernel, held, per_held),
        out_shape=part_shape,
        in_specs=[smem] * 4 + [vmem, vmem, hbm],
        out_specs=vmem,
        scratch_shapes=[
            pltpu.VMEM((rows, maxp) + page_shape, jnp.bfloat16),
            pltpu.SMEM((slots,), jnp.int32),
            pltpu.SMEM((PARTS,), jnp.int32),
            pltpu.SMEM((PARTS,), jnp.int32),
            pltpu.SemaphoreType.DMA((rows, maxp)),
        ],
        compiler_params=pltpu.CompilerParams(vmem_limit_bytes=20 * 2**20),
        name="resident",
    )(send, wanted, tables[0], lengths, qa, new_kv[0], stored)
    count = groups - 1
    theirs = pl.pallas_call(
        functools.partial(second_kernel, held, per_held, maxp, count),
        out_shape=[part_shape] * count,
        in_specs=[smem] * 2 + [vmem] * count + [hbm],
        out_specs=[vmem] * count,
        scratch_shapes=[
            pltpu.VMEM((count, PARTS) + page_shape, jnp.bfloat16),
            pltpu.SMEM((count * PARTS,), jnp.int32),
            pltpu.SMEM((count * PARTS,), jnp.int32),
            pltpu.SemaphoreType.DMA((count, PARTS)),
        ],
        compiler_params=pltpu.CompilerParams(vmem_limit_bytes=20 * 2**20),
        name="owned",
    )(send, wanted, *asked, stored)
    parts = [mine, lax.ppermute(mine, "role", [(0, 1)])]
    for k in range(1, groups):
        parts.append(
            lax.ppermute(theirs[k - 1], ("role", "group"), [(i, groups + (i - k) % groups) for i in range(groups)])
        )
    attended = pl.pallas_call(
        functools.partial(merge_kernel, heads, rows),
        out_shape=jax.ShapeDtypeStruct((rows, wide), jnp.bfloat16),
        in_specs=[vmem] * len(parts),
        out_specs=vmem,
        name="merge",
    )(*parts)
    partner = lax.ppermute(attended, "role", [(1, 0)])
    heads_here = jnp.where(lax.axis_index("role") == 0, partner, attended)
    partial_value = jnp.dot(heads_here, out_weight, preferred_element_type=jnp.float32)
    me = lax.axis_index("tp")
    share = partial_value.shape[1] // tps

    def chunk(index):
        return lax.dynamic_slice_in_dim(partial_value, lax.rem(index, tps) * share, share, 1)

    total = chunk(me)
    for d in range(1, tps):
        total = total + lax.ppermute(chunk(me + d), "tp", [(i, (i + d) % tps) for i in range(tps)])
    return total.astype(jnp.bfloat16)[None]


def solution(mesh):
    return jax.shard_map(
        per_device,
        mesh=mesh,
        in_specs=(
            P("role", "group", "tp", None, None, None),
            P(),
            P(),
            P("group", None),
            P("group", None, None),
            P("group", None, "tp"),
            P("group", None, "tp"),
            P("tp", "role"),
        ),
        out_specs=P("group", None, ("role", "tp")),
        check_vma=False,
    )
```

```python
import functools
import math

import jax
import jax.numpy as jnp
from jax import lax
from jax.experimental import pallas as pl
from jax.experimental.pallas import tpu as pltpu
from jax.sharding import PartitionSpec as P

KVH = 8
HD = 128
CAP = 4
CAPP = 2
PRE_DEV = 8
LANES = 128
NEG = -1e30
SCALE = 1.0 / math.sqrt(HD)
PARTS = CAP + CAPP
MIB = 2**20


def dot(a, b, ca, cb):
    return lax.dot_general(a, b, (((ca,), (cb,)), ((), ())), preferred_element_type=jnp.float32)


def query_block(qa, held, per_held):
    q = qa[:, : held * per_held * HD].astype(jnp.float32)
    rows = q.shape[0]
    bands = []
    for j in range(held):
        heads = [q[:, (j * per_held + i) * HD : (j * per_held + i + 1) * HD] for i in range(per_held)]
        band = jnp.concatenate(heads, 0)
        blank = jnp.zeros_like(band)
        bands.append(jnp.concatenate([band if i == j else blank for i in range(held)], 1))
    return jnp.concatenate(bands, 0).astype(jnp.bfloat16)


def entry_rows(qa, held, per_held, maxp):
    wide = held * per_held * HD
    aux = qa[:, wide : wide + LANES].astype(jnp.float32)
    turned = jnp.concatenate([aux] * (held * per_held), 0).T
    return turned[:maxp], turned[maxp : 2 * maxp]


def lanes_of(page, first, held):
    return jnp.concatenate([page[:, (2 * j + first) * HD : (2 * j + first + 1) * HD] for j in range(held)], 1)


def write_part(out, acc, top, total, held, per_held):
    count = acc.shape[0]
    band = count // held
    for j in range(held):
        out[j * band : (j + 1) * band, :] = acc[j * band : (j + 1) * band, j * HD : (j + 1) * HD]
    out[count : count + 1, :count] = top
    out[count + 1 : count + 2, :count] = total


def owner_part(qa, pages, entries, out, held, per_held, maxp):
    q = query_block(qa, held, per_held)
    tab, cnt = entry_rows(qa, held, per_held, maxp)
    count = q.shape[0]
    token = lax.broadcasted_iota(jnp.int32, (LANES, count), 0).astype(jnp.float32)
    masks = []
    for c in range(PARTS):
        valid = jnp.sum(jnp.where(tab == entries[c : c + 1, :count], cnt, 0.0), 0, keepdims=True)
        masks.append(token < valid)
    mask = jnp.concatenate(masks, 0)
    keys = jnp.concatenate([lanes_of(pages.at[c], 0, held) for c in range(PARTS)], 0)
    values = jnp.concatenate([lanes_of(pages.at[c], 1, held) for c in range(PARTS)], 0)
    s = jnp.where(mask, dot(keys, q, 1, 1) * SCALE, NEG)
    top = jnp.max(s, 0, keepdims=True)
    p = jnp.where(mask, jnp.exp(s - top), 0.0)
    total = jnp.sum(p, 0, keepdims=True)
    acc = dot(p.astype(jnp.bfloat16), values, 0, 0)
    write_part(out, acc, top, total, held, per_held)


def resident_part(qa, new_kv, send, tables, group, kv, pages, sems, out, held, per_held):
    rows = qa.shape[0]
    maxp = tables.shape[1]
    slots = kv.shape[0]
    copies = []
    for r in range(rows):
        for e in range(maxp):
            slot = tables[r, e]
            slot = jnp.where(slot < slots, slot, 0)
            copy = pltpu.make_async_copy(kv.at[slot], pages.at[r, e], sems.at[r, e])
            copy.start()
            copies.append(copy)
    q = query_block(qa, held, per_held)
    tab, cnt = entry_rows(qa, held, per_held, maxp)
    count = q.shape[0]
    gone = tab >= slots
    for o in range(send.shape[1]):
        for i in range(send.shape[2]):
            slot = jnp.where(send[1, o, i] == group, send[2, o, i], -1)
            gone = jnp.logical_or(gone, tab == slot.astype(jnp.float32))
    cnt = jnp.where(gone, 0.0, cnt)
    lane_row = lax.rem(lax.broadcasted_iota(jnp.int32, (1, count), 1), rows)
    token = lax.broadcasted_iota(jnp.int32, (LANES, count), 0).astype(jnp.float32)
    fresh = new_kv[...].astype(jnp.float32)
    fresh = jnp.concatenate([fresh, jnp.zeros_like(fresh)], 0).astype(jnp.bfloat16)
    own_mask = lax.broadcasted_iota(jnp.int32, (2 * rows, count), 0) == lane_row
    own = dot(lanes_of(fresh, 0, held), q, 1, 1) * SCALE
    own_top = jnp.max(jnp.where(own_mask, own, NEG), 0, keepdims=True)
    tops, total, acc = own_top, 0.0, 0.0
    for r in range(rows):
        for e in range(maxp):
            copies[r * maxp + e].wait()
        valid = jnp.where(lane_row == r, cnt, 0.0)
        mask = jnp.concatenate([token < valid[e : e + 1] for e in range(maxp)], 0)
        keys = jnp.concatenate([lanes_of(pages.at[r, e], 0, held) for e in range(maxp)], 0)
        values = jnp.concatenate([lanes_of(pages.at[r, e], 1, held) for e in range(maxp)], 0)
        s = jnp.where(mask, dot(keys, q, 1, 1) * SCALE, NEG)
        top = jnp.maximum(jnp.max(s, 0, keepdims=True), own_top)
        p = jnp.where(mask, jnp.exp(s - top), 0.0)
        total = total + jnp.sum(p, 0, keepdims=True)
        tops = jnp.maximum(tops, top)
        acc = acc + dot(p.astype(jnp.bfloat16), values, 0, 0)
    lift = jnp.where(own_mask, jnp.exp(own - tops), 0.0)
    total = total + jnp.sum(lift, 0, keepdims=True)
    acc = acc + dot(lift.astype(jnp.bfloat16), lanes_of(fresh, 1, held), 0, 0)
    write_part(out, acc, tops, total, held, per_held)


def list_pages(send, wanted, owner, target, slots, page_list, slot_list, base):
    for c in range(PARTS):
        page_list[base + c] = 0
        slot_list[base + c] = -1
    at = jnp.int32(base)
    for i in range(send.shape[2]):
        hit = send[1, owner, i] == target

        @pl.when(hit)
        def _(at=at, i=i):
            page_list[at] = send[0, owner, i]
            slot_list[at] = send[2, owner, i]

        at = at + hit.astype(jnp.int32)
    at = jnp.int32(base + CAP)
    for i in range(wanted.shape[1]):
        page = wanted[target, i]
        first = owner * PRE_DEV
        hit = jnp.logical_and(page >= first, page < first + PRE_DEV)

        @pl.when(hit)
        def _(at=at, i=i, page=page):
            page_list[at] = page - owner * PRE_DEV
            slot_list[at] = slots + i

        at = at + hit.astype(jnp.int32)


def first_kernel(held, per_held, groups, qa, new_kv, send_hbm, wanted_hbm, tables_hbm, kv, *refs):
    out, chosen, entries, pages, send, wanted, tables, page_list, slot_list, int_sems, chosen_sems, sems = refs
    group = lax.axis_index("group")
    prefill = lax.axis_index("role") == 0
    maxp = tables.shape[1]
    ints = [
        pltpu.make_async_copy(a, b, int_sems.at[i])
        for i, (a, b) in enumerate(((send_hbm, send), (wanted_hbm, wanted), (tables_hbm, tables)))
    ]
    for copy in ints:
        copy.start()
    for copy in ints:
        copy.wait()

    @pl.when(prefill)
    def _():
        copies = []
        for k in range(groups):
            target = lax.rem(group - k + groups, groups)
            list_pages(send, wanted, group, target, kv.shape[0], page_list, slot_list, k * PARTS)
            for c in range(PARTS):
                at = k * PARTS + c
                copy = pltpu.make_async_copy(kv.at[page_list[at]], chosen.at[at], chosen_sems.at[at])
                copy.start()
                copies.append(copy)
                entry = slot_list[at].astype(jnp.float32)
                entries[at : at + 1, :] = jnp.full((1, LANES), entry, jnp.float32)
        for copy in copies[:PARTS]:
            copy.wait()
        owner_part(qa, chosen.at[pl.ds(0, PARTS)], entries[:PARTS, :], out, held, per_held, maxp)
        for copy in copies[PARTS:]:
            copy.wait()

    @pl.when(jnp.logical_not(prefill))
    def _():
        resident_part(qa, new_kv, send, tables, group, kv, pages, sems, out, held, per_held)


def second_kernel(held, per_held, maxp, count, chosen, entries, *refs):
    qas, outs = refs[:count], refs[count:]

    @pl.when(lax.axis_index("role") == 0)
    def _():
        for k in range(count):
            at = (k + 1) * PARTS
            owner_part(
                qas[k], chosen.at[pl.ds(at, PARTS)], entries[at : at + PARTS, :], outs[k], held, per_held, maxp
            )


def merge_kernel(heads, rows, *refs):
    parts, out = refs[:-1], refs[-1]
    count = heads * rows
    pad = -len(parts) % 8
    tops = jnp.concatenate([part[count : count + 1, :count] for part in parts], 0)
    totals = jnp.concatenate([part[count + 1 : count + 2, :count] for part in parts], 0)
    factors = jnp.exp(tops - jnp.max(tops, 0, keepdims=True))
    factors = factors / jnp.sum(factors * totals, 0, keepdims=True)
    factors = jnp.concatenate([factors, jnp.zeros((pad, count), jnp.float32)], 0).T
    terms = [factors[:, i : i + 1] * part[:count, :] for i, part in enumerate(parts)]
    merged = functools.reduce(jnp.add, terms)
    out[...] = jnp.concatenate([merged[h * rows : (h + 1) * rows] for h in range(heads)], 1).astype(out.dtype)


def project_kernel(steps, attended, partner, weight, *outs):
    tps = lax.axis_size("tp")
    share = outs[0].shape[1]
    here = jnp.where(lax.axis_index("role") == 0, partner[...].astype(jnp.float32), attended[...].astype(jnp.float32))
    here = here.astype(jnp.bfloat16)
    for d, out in zip(steps, outs):
        first = lax.rem(lax.axis_index("tp") + d, tps) * share
        columns = pl.ds(pl.multiple_of(first, LANES), share)
        out[...] = jnp.dot(here, weight[:, columns], preferred_element_type=jnp.float32)


def per_device(kv_pages, send_list, wanted, lengths, tables, queries, new_kv, out_weight):
    stored = kv_pages[0, 0, 0]
    slots, page = stored.shape[0], stored.shape[1]
    groups, tps = lax.axis_size("group"), lax.axis_size("tp")
    held = max(1, KVH // tps)
    rows, wide = queries.shape[1], queries.shape[2]
    heads = wide // HD
    per_held = heads // held
    maxp = tables.shape[2]
    send = jnp.transpose(send_list, (2, 0, 1))
    counts = jnp.clip(lengths[0][:, None] - jnp.arange(maxp, dtype=jnp.int32)[None, :] * page, 0, page)
    qa = (
        jnp.pad(queries[0], ((0, 0), (0, LANES)))
        + jnp.pad(tables[0].astype(jnp.bfloat16), ((0, 0), (wide, LANES - maxp)))
        + jnp.pad(counts.astype(jnp.bfloat16), ((0, 0), (wide + maxp, LANES - 2 * maxp)))
    )
    asked = [
        lax.ppermute(qa, ("role", "group"), [(groups + i, (i + k) % groups) for i in range(groups)])
        for k in range(1, groups)
    ]
    part_shape = jax.ShapeDtypeStruct((heads * rows + 8, HD), jnp.float32)
    vmem = pl.BlockSpec(memory_space=pltpu.VMEM)
    hbm = pl.BlockSpec(memory_space=pltpu.HBM)
    page_shape = stored.shape[1:]
    chosen_count = groups * PARTS
    mine, chosen, entries = pl.pallas_call(
        functools.partial(first_kernel, held, per_held, groups),
        out_shape=[
            part_shape,
            jax.ShapeDtypeStruct((chosen_count,) + page_shape, jnp.bfloat16),
            jax.ShapeDtypeStruct((chosen_count, LANES), jnp.float32),
        ],
        in_specs=[vmem, vmem, hbm, hbm, hbm, hbm],
        out_specs=[vmem] * 3,
        scratch_shapes=[
            pltpu.VMEM((rows, maxp) + page_shape, jnp.bfloat16),
            pltpu.SMEM(send.shape, jnp.int32),
            pltpu.SMEM(wanted.shape, jnp.int32),
            pltpu.SMEM(tables.shape[1:], jnp.int32),
            pltpu.SMEM((chosen_count,), jnp.int32),
            pltpu.SMEM((chosen_count,), jnp.int32),
            pltpu.SemaphoreType.DMA((3,)),
            pltpu.SemaphoreType.DMA((chosen_count,)),
            pltpu.SemaphoreType.DMA((rows, maxp)),
        ],
        compiler_params=pltpu.CompilerParams(vmem_limit_bytes=24 * MIB),
        cost_estimate=pl.CostEstimate(flops=4 * 10**9, bytes_accessed=12 * MIB, transcendentals=10**6),
        name="resident",
    )(qa, new_kv[0], send, wanted, tables[0], stored)
    count = groups - 1
    theirs = pl.pallas_call(
        functools.partial(second_kernel, held, per_held, maxp, count),
        out_shape=[part_shape] * count,
        in_specs=[vmem] * (2 + count),
        out_specs=[vmem] * count,
        compiler_params=pltpu.CompilerParams(vmem_limit_bytes=16 * MIB),
        cost_estimate=pl.CostEstimate(flops=4 * 10**9, bytes_accessed=8 * MIB, transcendentals=10**6),
        name="owned",
    )(chosen, entries, *asked)
    parts = [mine, lax.ppermute(mine, "role", [(0, 1)])]
    for k in range(1, groups):
        parts.append(
            lax.ppermute(theirs[k - 1], ("role", "group"), [(i, groups + (i - k) % groups) for i in range(groups)])
        )
    attended = pl.pallas_call(
        functools.partial(merge_kernel, heads, rows),
        out_shape=jax.ShapeDtypeStruct((rows, wide), jnp.bfloat16),
        in_specs=[vmem] * len(parts),
        out_specs=vmem,
        compiler_params=pltpu.CompilerParams(vmem_limit_bytes=8 * MIB),
        name="merge",
    )(*parts)
    partner = lax.ppermute(attended, "role", [(1, 0)])
    share = out_weight.shape[1] // tps

    def project(steps, name):
        return pl.pallas_call(
            functools.partial(project_kernel, steps),
            out_shape=[jax.ShapeDtypeStruct((rows, share), jnp.float32)] * len(steps),
            in_specs=[vmem] * 3,
            out_specs=[vmem] * len(steps),
            compiler_params=pltpu.CompilerParams(vmem_limit_bytes=24 * MIB),
            cost_estimate=pl.CostEstimate(
                flops=len(steps) * 32 * wide * share, bytes_accessed=len(steps) * 2 * wide * share, transcendentals=0
            ),
            name=name,
        )(attended, partner, out_weight)

    steps = list(range(1, tps))
    sent = project(steps, "project")
    arrived = [lax.ppermute(part, "tp", [(i, (i + d) % tps) for i in range(tps)]) for d, part in zip(steps, sent)]
    total = functools.reduce(jnp.add, arrived, project([0], "project_own")[0])
    return total.astype(jnp.bfloat16)[None]


def solution(mesh):
    return jax.shard_map(
        per_device,
        mesh=mesh,
        in_specs=(
            P("role", "group", "tp", None, None, None),
            P(),
            P(),
            P("group", None),
            P("group", None, None),
            P("group", None, "tp"),
            P("group", None, "tp"),
            P("tp", "role"),
        ),
        out_specs=P("group", None, ("role", "tp")),
        check_vma=False,
    )
```

```python
import functools
import math

import jax
import jax.numpy as jnp
from jax import lax
from jax.experimental import pallas as pl
from jax.experimental.pallas import tpu as pltpu
from jax.sharding import PartitionSpec as P

KVH = 8
HD = 128
CAP = 4
CAPP = 2
PRE_DEV = 8
LANES = 128
PAGE = 128
NEG = -1e30
SCALE = 1.0 / math.sqrt(HD)
PARTS = CAP + CAPP
MIB = 2**20


def dot(a, b, ca, cb):
    return lax.dot_general(a, b, (((ca,), (cb,)), ((), ())), preferred_element_type=jnp.float32)


def query_block(qa, held, per_held):
    q = qa[:, : held * per_held * HD].astype(jnp.float32)
    rows = q.shape[0]
    bands = []
    for j in range(held):
        heads = [q[:, (j * per_held + i) * HD : (j * per_held + i + 1) * HD] for i in range(per_held)]
        band = jnp.concatenate(heads, 0)
        blank = jnp.zeros_like(band)
        bands.append(jnp.concatenate([band if i == j else blank for i in range(held)], 1))
    return jnp.concatenate(bands, 0).astype(jnp.bfloat16)


def entry_rows(qa, held, per_held, maxp):
    rows = qa.shape[0]
    wide = held * per_held * HD
    aux = qa[:, wide : wide + LANES].astype(jnp.float32)
    lane = lax.broadcasted_iota(jnp.int32, (rows, LANES), 1) - maxp
    row = lax.broadcasted_iota(jnp.int32, (rows, LANES), 0)
    parts = jnp.where(lane == row, 8.0 * aux[:1], jnp.where(lane == row + rows, aux[:1], 0.0))
    length = jnp.sum(parts, 1, keepdims=True)
    turned = jnp.concatenate([jnp.where(lane == 0, length, aux)] * (held * per_held), 0).T
    first = lax.broadcasted_iota(jnp.int32, (maxp, 1), 0).astype(jnp.float32) * PAGE
    return turned[:maxp], jnp.clip(turned[maxp : maxp + 1] - first, 0.0, PAGE)


def lanes_of(page, first, held):
    return jnp.concatenate([page[:, (2 * j + first) * HD : (2 * j + first + 1) * HD] for j in range(held)], 1)


def write_part(out, acc, top, total, held, per_held):
    count = acc.shape[0]
    band = count // held
    for j in range(held):
        out[j * band : (j + 1) * band, :] = acc[j * band : (j + 1) * band, j * HD : (j + 1) * HD]
    out[count : count + 1, :count] = top
    out[count + 1 : count + 2, :count] = total


def owner_part(qa, pages, entries, out, held, per_held, maxp):
    q = query_block(qa, held, per_held)
    tab, cnt = entry_rows(qa, held, per_held, maxp)
    count = q.shape[0]
    token = lax.broadcasted_iota(jnp.int32, (PAGE, count), 0).astype(jnp.float32)
    masks = []
    for c in range(PARTS):
        valid = jnp.sum(jnp.where(tab == entries[c : c + 1, :count], cnt, 0.0), 0, keepdims=True)
        masks.append(token < valid)
    mask = jnp.concatenate(masks, 0)
    keys = jnp.concatenate([lanes_of(pages.at[c], 0, held) for c in range(PARTS)], 0)
    values = jnp.concatenate([lanes_of(pages.at[c], 1, held) for c in range(PARTS)], 0)
    s = jnp.where(mask, dot(keys, q, 1, 1) * SCALE, NEG)
    top = jnp.max(s, 0, keepdims=True)
    p = jnp.where(mask, jnp.exp(s - top), 0.0)
    total = jnp.sum(p, 0, keepdims=True)
    acc = dot(p.astype(jnp.bfloat16), values, 0, 0)
    write_part(out, acc, top, total, held, per_held)


def resident_part(qa, fresh_at, send, tables, maxp, group, kv, pages, sems, out, held, per_held):
    rows = qa.shape[0]
    slots = kv.shape[0]
    copies = []
    for r in range(rows):
        for e in range(maxp):
            slot = tables[r, e]
            slot = jnp.where(slot < slots, slot, 0)
            copy = pltpu.make_async_copy(kv.at[slot], pages.at[r, e], sems.at[r, e])
            copy.start()
            copies.append(copy)
    q = query_block(qa, held, per_held)
    tab, cnt = entry_rows(qa, held, per_held, maxp)
    count = q.shape[0]
    gone = tab >= slots
    for o in range(send.shape[1]):
        for i in range(send.shape[2]):
            slot = jnp.where(send[1, o, i] == group, send[2, o, i], -1)
            gone = jnp.logical_or(gone, tab == slot.astype(jnp.float32))
    cnt = jnp.where(gone, 0.0, cnt)
    lane_row = lax.rem(lax.broadcasted_iota(jnp.int32, (1, count), 1), rows)
    token = lax.broadcasted_iota(jnp.int32, (PAGE, count), 0).astype(jnp.float32)
    fresh = qa[:, fresh_at : fresh_at + 2 * held * HD].astype(jnp.float32)
    fresh = jnp.concatenate([fresh, jnp.zeros_like(fresh)], 0).astype(jnp.bfloat16)
    own_mask = lax.broadcasted_iota(jnp.int32, (2 * rows, count), 0) == lane_row
    own = dot(lanes_of(fresh, 0, held), q, 1, 1) * SCALE
    own_top = jnp.max(jnp.where(own_mask, own, NEG), 0, keepdims=True)
    tops, total, acc = own_top, 0.0, 0.0
    for r in range(rows):
        for e in range(maxp):
            copies[r * maxp + e].wait()
        valid = jnp.where(lane_row == r, cnt, 0.0)
        mask = jnp.concatenate([token < valid[e : e + 1] for e in range(maxp)], 0)
        keys = jnp.concatenate([lanes_of(pages.at[r, e], 0, held) for e in range(maxp)], 0)
        values = jnp.concatenate([lanes_of(pages.at[r, e], 1, held) for e in range(maxp)], 0)
        s = jnp.where(mask, dot(keys, q, 1, 1) * SCALE, NEG)
        top = jnp.maximum(jnp.max(s, 0, keepdims=True), own_top)
        p = jnp.where(mask, jnp.exp(s - top), 0.0)
        total = total + jnp.sum(p, 0, keepdims=True)
        tops = jnp.maximum(tops, top)
        acc = acc + dot(p.astype(jnp.bfloat16), values, 0, 0)
    lift = jnp.where(own_mask, jnp.exp(own - tops), 0.0)
    total = total + jnp.sum(lift, 0, keepdims=True)
    acc = acc + dot(lift.astype(jnp.bfloat16), lanes_of(fresh, 1, held), 0, 0)
    write_part(out, acc, tops, total, held, per_held)


def list_pages(send, wanted, owner, target, slots, page_list, slot_list, base):
    for c in range(PARTS):
        page_list[base + c] = 0
        slot_list[base + c] = -1
    at = jnp.int32(base)
    for i in range(send.shape[2]):
        hit = send[1, owner, i] == target

        @pl.when(hit)
        def _(at=at, i=i):
            page_list[at] = send[0, owner, i]
            slot_list[at] = send[2, owner, i]

        at = at + hit.astype(jnp.int32)
    at = jnp.int32(base + CAP)
    for i in range(wanted.shape[1]):
        page = wanted[target, i]
        first = owner * PRE_DEV
        hit = jnp.logical_and(page >= first, page < first + PRE_DEV)

        @pl.when(hit)
        def _(at=at, i=i, page=page):
            page_list[at] = page - owner * PRE_DEV
            slot_list[at] = slots + i

        at = at + hit.astype(jnp.int32)


def first_kernel(held, per_held, groups, maxp, qa, send_hbm, wanted_hbm, tables_hbm, kv, *refs):
    out, chosen, entries, pages, send, wanted, tables, page_list, slot_list, list_sems, chosen_sems, sems = refs
    group = lax.axis_index("group")
    prefill = lax.axis_index("role") == 0
    fresh_at = held * per_held * HD + LANES
    lists = ((send_hbm, send), (wanted_hbm, wanted), (tables_hbm, tables))
    copies = [pltpu.make_async_copy(a, b, list_sems.at[i]) for i, (a, b) in enumerate(lists)]
    for copy in copies:
        copy.start()
    for copy in copies:
        copy.wait()

    @pl.when(prefill)
    def _():
        copies = []
        for k in range(groups):
            target = lax.rem(group - k + groups, groups)
            list_pages(send, wanted, group, target, kv.shape[0], page_list, slot_list, k * PARTS)
            for c in range(PARTS):
                at = k * PARTS + c
                copy = pltpu.make_async_copy(kv.at[page_list[at]], chosen.at[at], chosen_sems.at[at])
                copy.start()
                copies.append(copy)
                entry = slot_list[at].astype(jnp.float32)
                entries[at : at + 1, :] = jnp.full((1, LANES), entry, jnp.float32)
        for copy in copies[:PARTS]:
            copy.wait()
        owner_part(qa, chosen.at[pl.ds(0, PARTS)], entries[:PARTS, :], out, held, per_held, maxp)
        for copy in copies[PARTS:]:
            copy.wait()

    @pl.when(jnp.logical_not(prefill))
    def _():
        resident_part(qa, fresh_at, send, tables, maxp, group, kv, pages, sems, out, held, per_held)


def second_kernel(held, per_held, maxp, count, chosen, entries, *refs):
    qas, outs = refs[:count], refs[count:]

    @pl.when(lax.axis_index("role") == 0)
    def _():
        for k in range(count):
            at = (k + 1) * PARTS
            owner_part(
                qas[k], chosen.at[pl.ds(at, PARTS)], entries[at : at + PARTS, :], outs[k], held, per_held, maxp
            )


def merge_kernel(heads, rows, *refs):
    parts, out = refs[:-1], refs[-1]
    count = heads * rows
    pad = -len(parts) % 8
    tops = jnp.concatenate([part[count : count + 1, :count] for part in parts], 0)
    totals = jnp.concatenate([part[count + 1 : count + 2, :count] for part in parts], 0)
    factors = jnp.exp(tops - jnp.max(tops, 0, keepdims=True))
    factors = factors / jnp.sum(factors * totals, 0, keepdims=True)
    factors = jnp.concatenate([factors, jnp.zeros((pad, count), jnp.float32)], 0).T
    terms = [factors[:, i : i + 1] * part[:count, :] for i, part in enumerate(parts)]
    merged = functools.reduce(jnp.add, terms)
    out[...] = jnp.concatenate([merged[h * rows : (h + 1) * rows] for h in range(heads)], 1).astype(out.dtype)


def project_kernel(steps, attended, partner, weight, *outs):
    tps = lax.axis_size("tp")
    share = outs[0].shape[1]
    here = jnp.where(lax.axis_index("role") == 0, partner[...].astype(jnp.float32), attended[...].astype(jnp.float32))
    here = here.astype(jnp.bfloat16)
    for d, out in zip(steps, outs):
        first = lax.rem(lax.axis_index("tp") + d, tps) * share
        columns = pl.ds(pl.multiple_of(first, LANES), share)
        out[...] = jnp.dot(here, weight[:, columns], preferred_element_type=jnp.float32)


def per_device(kv_pages, send_list, wanted, lengths, tables, queries, new_kv, out_weight):
    stored = kv_pages[0, 0, 0]
    slots = stored.shape[0]
    groups, tps = lax.axis_size("group"), lax.axis_size("tp")
    held = max(1, KVH // tps)
    rows, wide = queries.shape[1], queries.shape[2]
    heads = wide // HD
    per_held = heads // held
    maxp = tables.shape[2]
    send = jnp.transpose(send_list, (2, 0, 1))
    fresh_at = wide + LANES
    width = fresh_at + new_kv.shape[2]

    def place(block, at):
        return jnp.pad(block, ((0, rows - block.shape[0]), (at, width - at - block.shape[1])))

    high = lax.shift_right_logical(place(lengths, wide + maxp), 3)
    low = jnp.bitwise_and(place(lengths, wide + maxp + rows), 7)
    integers = place(tables[0], wide) + high + low
    qa = place(queries[0], 0) + place(new_kv[0], fresh_at) + integers.astype(jnp.bfloat16)
    asked = [
        lax.ppermute(qa, ("role", "group"), [(groups + i, (i + k) % groups) for i in range(groups)])
        for k in range(1, groups)
    ]
    part_shape = jax.ShapeDtypeStruct((heads * rows + 8, HD), jnp.float32)
    vmem = pl.BlockSpec(memory_space=pltpu.VMEM)
    hbm = pl.BlockSpec(memory_space=pltpu.HBM)
    page_shape = stored.shape[1:]
    chosen_count = groups * PARTS
    mine, chosen, entries = pl.pallas_call(
        functools.partial(first_kernel, held, per_held, groups, maxp),
        out_shape=[
            part_shape,
            jax.ShapeDtypeStruct((chosen_count,) + page_shape, jnp.bfloat16),
            jax.ShapeDtypeStruct((chosen_count, LANES), jnp.float32),
        ],
        in_specs=[vmem, hbm, hbm, hbm, hbm],
        out_specs=[vmem] * 3,
        scratch_shapes=[
            pltpu.VMEM((rows, maxp) + page_shape, jnp.bfloat16),
            pltpu.SMEM(send.shape, jnp.int32),
            pltpu.SMEM(wanted.shape, jnp.int32),
            pltpu.SMEM(tables.shape[1:], jnp.int32),
            pltpu.SMEM((chosen_count,), jnp.int32),
            pltpu.SMEM((chosen_count,), jnp.int32),
            pltpu.SemaphoreType.DMA((3,)),
            pltpu.SemaphoreType.DMA((chosen_count,)),
            pltpu.SemaphoreType.DMA((rows, maxp)),
        ],
        compiler_params=pltpu.CompilerParams(vmem_limit_bytes=24 * MIB),
        cost_estimate=pl.CostEstimate(flops=4 * 10**9, bytes_accessed=12 * MIB, transcendentals=10**6),
        name="resident",
    )(qa, *[pltpu.with_memory_space_constraint(x, pltpu.HBM) for x in (send, wanted, tables[0], stored)])
    count = groups - 1
    theirs = pl.pallas_call(
        functools.partial(second_kernel, held, per_held, maxp, count),
        out_shape=[part_shape] * count,
        in_specs=[vmem] * (2 + count),
        out_specs=[vmem] * count,
        compiler_params=pltpu.CompilerParams(vmem_limit_bytes=16 * MIB),
        cost_estimate=pl.CostEstimate(flops=4 * 10**9, bytes_accessed=8 * MIB, transcendentals=10**6),
        name="owned",
    )(chosen, entries, *asked)
    mine, theirs = lax.optimization_barrier((mine, theirs))
    parts = [mine, lax.ppermute(mine, "role", [(0, 1)])]
    for k in range(1, groups):
        parts.append(
            lax.ppermute(theirs[k - 1], ("role", "group"), [(i, groups + (i - k) % groups) for i in range(groups)])
        )
    attended = pl.pallas_call(
        functools.partial(merge_kernel, heads, rows),
        out_shape=jax.ShapeDtypeStruct((rows, wide), jnp.bfloat16),
        in_specs=[vmem] * len(parts),
        out_specs=vmem,
        compiler_params=pltpu.CompilerParams(vmem_limit_bytes=8 * MIB),
        name="merge",
    )(*parts)
    partner = lax.ppermute(attended, "role", [(1, 0)])
    share = out_weight.shape[1] // tps

    def project(steps, name):
        return pl.pallas_call(
            functools.partial(project_kernel, steps),
            out_shape=[jax.ShapeDtypeStruct((rows, share), jnp.float32)] * len(steps),
            in_specs=[vmem] * 3,
            out_specs=[vmem] * len(steps),
            compiler_params=pltpu.CompilerParams(vmem_limit_bytes=24 * MIB),
            cost_estimate=pl.CostEstimate(
                flops=len(steps) * 32 * wide * share, bytes_accessed=len(steps) * 2 * wide * share, transcendentals=0
            ),
            name=name,
        )(attended, partner, out_weight)

    steps = list(range(1, tps))
    sent = project(steps, "project")
    arrived = [lax.ppermute(part, "tp", [(i, (i + d) % tps) for i in range(tps)]) for d, part in zip(steps, sent)]
    total = functools.reduce(jnp.add, arrived, project([0], "project_own")[0])
    return total.astype(jnp.bfloat16)[None]


def solution(mesh):
    return jax.shard_map(
        per_device,
        mesh=mesh,
        in_specs=(
            P("role", "group", "tp", None, None, None),
            P(),
            P(),
            P("group", None),
            P("group", None, None),
            P("group", None, "tp"),
            P("group", None, "tp"),
            P("tp", "role"),
        ),
        out_specs=P("group", None, ("role", "tp")),
        check_vma=False,
    )
```

```python
import functools
import math

import jax
import jax.numpy as jnp
from jax import lax
from jax.experimental import pallas as pl
from jax.experimental.pallas import tpu as pltpu
from jax.sharding import PartitionSpec as P

KVH = 8
HD = 128
CAP = 4
CAPP = 2
PRE_DEV = 8
LANES = 128
PAGE = 128
NEG = -1e30
SCALE = 1.0 / math.sqrt(HD)
PARTS = CAP + CAPP
MIB = 2**20


def dot(a, b, ca, cb):
    return lax.dot_general(a, b, (((ca,), (cb,)), ((), ())), preferred_element_type=jnp.float32)


def query_block(qa, held, per_held):
    q = qa[:, : held * per_held * HD].astype(jnp.float32)
    rows = q.shape[0]
    bands = []
    for j in range(held):
        heads = [q[:, (j * per_held + i) * HD : (j * per_held + i + 1) * HD] for i in range(per_held)]
        band = jnp.concatenate(heads, 0)
        blank = jnp.zeros_like(band)
        bands.append(jnp.concatenate([band if i == j else blank for i in range(held)], 1))
    return jnp.concatenate(bands, 0).astype(jnp.bfloat16)


def entry_rows(qa, held, per_held, maxp):
    rows = qa.shape[0]
    wide = held * per_held * HD
    aux = qa[:, wide : wide + LANES].astype(jnp.float32)
    lane = lax.broadcasted_iota(jnp.int32, (rows, LANES), 1) - maxp
    row = lax.broadcasted_iota(jnp.int32, (rows, LANES), 0)
    parts = jnp.where(lane == row, 8.0 * aux[:1], jnp.where(lane == row + rows, aux[:1], 0.0))
    length = jnp.sum(parts, 1, keepdims=True)
    turned = jnp.concatenate([jnp.where(lane == 0, length, aux)] * (held * per_held), 0).T
    first = lax.broadcasted_iota(jnp.int32, (maxp, 1), 0).astype(jnp.float32) * PAGE
    return turned[:maxp], jnp.clip(turned[maxp : maxp + 1] - first, 0.0, PAGE)


def lanes_of(page, first, held):
    return jnp.concatenate([page[:, (2 * j + first) * HD : (2 * j + first + 1) * HD] for j in range(held)], 1)


def write_part(out, acc, top, total, held, per_held):
    count = acc.shape[0]
    band = count // held
    for j in range(held):
        out[j * band : (j + 1) * band, :] = acc[j * band : (j + 1) * band, j * HD : (j + 1) * HD]
    out[count : count + 1, :count] = top
    out[count + 1 : count + 2, :count] = total


def owner_part(qa, pages, entries, out, held, per_held, maxp):
    q = query_block(qa, held, per_held)
    tab, cnt = entry_rows(qa, held, per_held, maxp)
    count = q.shape[0]
    token = lax.broadcasted_iota(jnp.int32, (PAGE, count), 0).astype(jnp.float32)
    masks = []
    for c in range(PARTS):
        valid = jnp.sum(jnp.where(tab == entries[c : c + 1, :count], cnt, 0.0), 0, keepdims=True)
        masks.append(token < valid)
    mask = jnp.concatenate(masks, 0)
    keys = jnp.concatenate([lanes_of(pages.at[c], 0, held) for c in range(PARTS)], 0)
    values = jnp.concatenate([lanes_of(pages.at[c], 1, held) for c in range(PARTS)], 0)
    s = jnp.where(mask, dot(keys, q, 1, 1) * SCALE, NEG)
    top = jnp.max(s, 0, keepdims=True)
    p = jnp.where(mask, jnp.exp(s - top), 0.0)
    total = jnp.sum(p, 0, keepdims=True)
    acc = dot(p.astype(jnp.bfloat16), values, 0, 0)
    write_part(out, acc, top, total, held, per_held)


def resident_part(qa, fresh_at, send, tables, maxp, group, kv, pages, sems, out, held, per_held):
    rows = qa.shape[0]
    slots = kv.shape[0]
    copies = []
    for r in range(rows):
        for e in range(maxp):
            slot = tables[r, e]
            slot = jnp.where(slot < slots, slot, 0)
            copy = pltpu.make_async_copy(kv.at[slot], pages.at[r, e], sems.at[r, e])
            copy.start()
            copies.append(copy)
    q = query_block(qa, held, per_held)
    tab, cnt = entry_rows(qa, held, per_held, maxp)
    count = q.shape[0]
    gone = tab >= slots
    for o in range(send.shape[1]):
        for i in range(send.shape[2]):
            slot = jnp.where(send[1, o, i] == group, send[2, o, i], -1)
            gone = jnp.logical_or(gone, tab == slot.astype(jnp.float32))
    cnt = jnp.where(gone, 0.0, cnt)
    lane_row = lax.rem(lax.broadcasted_iota(jnp.int32, (1, count), 1), rows)
    token = lax.broadcasted_iota(jnp.int32, (PAGE, count), 0).astype(jnp.float32)
    fresh = qa[:, fresh_at : fresh_at + 2 * held * HD].astype(jnp.float32)
    fresh = jnp.concatenate([fresh, jnp.zeros_like(fresh)], 0).astype(jnp.bfloat16)
    own_mask = lax.broadcasted_iota(jnp.int32, (2 * rows, count), 0) == lane_row
    own = dot(lanes_of(fresh, 0, held), q, 1, 1) * SCALE
    own_top = jnp.max(jnp.where(own_mask, own, NEG), 0, keepdims=True)
    tops, total, acc = own_top, 0.0, 0.0
    for r in range(rows):
        for e in range(maxp):
            copies[r * maxp + e].wait()
        valid = jnp.where(lane_row == r, cnt, 0.0)
        mask = jnp.concatenate([token < valid[e : e + 1] for e in range(maxp)], 0)
        keys = jnp.concatenate([lanes_of(pages.at[r, e], 0, held) for e in range(maxp)], 0)
        values = jnp.concatenate([lanes_of(pages.at[r, e], 1, held) for e in range(maxp)], 0)
        s = jnp.where(mask, dot(keys, q, 1, 1) * SCALE, NEG)
        top = jnp.maximum(jnp.max(s, 0, keepdims=True), own_top)
        p = jnp.where(mask, jnp.exp(s - top), 0.0)
        total = total + jnp.sum(p, 0, keepdims=True)
        tops = jnp.maximum(tops, top)
        acc = acc + dot(p.astype(jnp.bfloat16), values, 0, 0)
    lift = jnp.where(own_mask, jnp.exp(own - tops), 0.0)
    total = total + jnp.sum(lift, 0, keepdims=True)
    acc = acc + dot(lift.astype(jnp.bfloat16), lanes_of(fresh, 1, held), 0, 0)
    write_part(out, acc, tops, total, held, per_held)


def list_pages(send, wanted, owner, target, slots, page_list, slot_list, base):
    for c in range(PARTS):
        page_list[base + c] = 0
        slot_list[base + c] = -1
    at = jnp.int32(base)
    for i in range(send.shape[2]):
        hit = send[1, owner, i] == target

        @pl.when(hit)
        def _(at=at, i=i):
            page_list[at] = send[0, owner, i]
            slot_list[at] = send[2, owner, i]

        at = at + hit.astype(jnp.int32)
    at = jnp.int32(base + CAP)
    for i in range(wanted.shape[1]):
        page = wanted[target, i]
        first = owner * PRE_DEV
        hit = jnp.logical_and(page >= first, page < first + PRE_DEV)

        @pl.when(hit)
        def _(at=at, i=i, page=page):
            page_list[at] = page - owner * PRE_DEV
            slot_list[at] = slots + i

        at = at + hit.astype(jnp.int32)


def first_kernel(held, per_held, groups, maxp, qa, send_hbm, wanted_hbm, tables_hbm, kv, *refs):
    out, chosen, entries, pages, send, wanted, tables, page_list, slot_list, list_sems, chosen_sems, sems = refs
    group = lax.axis_index("group")
    prefill = lax.axis_index("role") == 0
    fresh_at = held * per_held * HD + LANES
    lists = ((send_hbm, send), (wanted_hbm, wanted), (tables_hbm, tables))
    copies = [pltpu.make_async_copy(a, b, list_sems.at[i]) for i, (a, b) in enumerate(lists)]
    for copy in copies:
        copy.start()
    for copy in copies:
        copy.wait()

    @pl.when(prefill)
    def _():
        copies = []
        for k in range(groups):
            target = lax.rem(group - k + groups, groups)
            list_pages(send, wanted, group, target, kv.shape[0], page_list, slot_list, k * PARTS)
            for c in range(PARTS):
                at = k * PARTS + c
                copy = pltpu.make_async_copy(kv.at[page_list[at]], chosen.at[at], chosen_sems.at[at])
                copy.start()
                copies.append(copy)
                entry = slot_list[at].astype(jnp.float32)
                entries[at : at + 1, :] = jnp.full((1, LANES), entry, jnp.float32)
        for copy in copies[:PARTS]:
            copy.wait()
        owner_part(qa, chosen.at[pl.ds(0, PARTS)], entries[:PARTS, :], out, held, per_held, maxp)
        for copy in copies[PARTS:]:
            copy.wait()

    @pl.when(jnp.logical_not(prefill))
    def _():
        resident_part(qa, fresh_at, send, tables, maxp, group, kv, pages, sems, out, held, per_held)


def second_kernel(held, per_held, maxp, count, chosen, entries, *refs):
    qas, outs = refs[:count], refs[count:]

    @pl.when(lax.axis_index("role") == 0)
    def _():
        for k in range(count):
            at = (k + 1) * PARTS
            owner_part(
                qas[k], chosen.at[pl.ds(at, PARTS)], entries[at : at + PARTS, :], outs[k], held, per_held, maxp
            )


def merge_kernel(heads, rows, *refs):
    parts, out = refs[:-1], refs[-1]
    count = heads * rows
    pad = -len(parts) % 8
    tops = jnp.concatenate([part[count : count + 1, :count] for part in parts], 0)
    totals = jnp.concatenate([part[count + 1 : count + 2, :count] for part in parts], 0)
    factors = jnp.exp(tops - jnp.max(tops, 0, keepdims=True))
    factors = factors / jnp.sum(factors * totals, 0, keepdims=True)
    factors = jnp.concatenate([factors, jnp.zeros((pad, count), jnp.float32)], 0).T
    terms = [factors[:, i : i + 1] * part[:count, :] for i, part in enumerate(parts)]
    merged = functools.reduce(jnp.add, terms)
    out[...] = jnp.concatenate([merged[h * rows : (h + 1) * rows] for h in range(heads)], 1).astype(out.dtype)


def project_kernel(steps, attended, partner, weight, *outs):
    tps = lax.axis_size("tp")
    share = outs[0].shape[1]
    here = jnp.where(lax.axis_index("role") == 0, partner[...].astype(jnp.float32), attended[...].astype(jnp.float32))
    here = here.astype(jnp.bfloat16)
    for d, out in zip(steps, outs):
        first = lax.rem(lax.axis_index("tp") + d, tps) * share
        columns = pl.ds(pl.multiple_of(first, LANES), share)
        out[...] = jnp.dot(here, weight[:, columns], preferred_element_type=jnp.float32)


def per_device(kv_pages, send_list, wanted, lengths, tables, queries, new_kv, out_weight):
    stored = kv_pages[0, 0, 0]
    slots = stored.shape[0]
    groups, tps = lax.axis_size("group"), lax.axis_size("tp")
    held = max(1, KVH // tps)
    rows, wide = queries.shape[1], queries.shape[2]
    heads = wide // HD
    per_held = heads // held
    maxp = tables.shape[2]
    send = jnp.transpose(send_list, (2, 0, 1))
    fresh_at = wide + LANES
    width = fresh_at + new_kv.shape[2]

    def place(block, at):
        return jnp.pad(block, ((0, rows - block.shape[0]), (at, width - at - block.shape[1])))

    high = lax.shift_right_logical(place(lengths, wide + maxp), 3)
    low = jnp.bitwise_and(place(lengths, wide + maxp + rows), 7)
    integers = place(tables[0], wide) + high + low
    qa = place(queries[0], 0) + place(new_kv[0], fresh_at) + integers.astype(jnp.bfloat16)
    asked = [
        lax.ppermute(
            qa, ("role", "group"), [pair for i in range(groups) for pair in ((groups + i, (i + k) % groups), (i, groups + i))]
        )
        for k in range(1, groups)
    ]
    part_shape = jax.ShapeDtypeStruct((heads * rows + 8, HD), jnp.float32)
    vmem = pl.BlockSpec(memory_space=pltpu.VMEM)
    hbm = pl.BlockSpec(memory_space=pltpu.HBM)
    page_shape = stored.shape[1:]
    chosen_count = groups * PARTS
    mine, chosen, entries = pl.pallas_call(
        functools.partial(first_kernel, held, per_held, groups, maxp),
        out_shape=[
            part_shape,
            jax.ShapeDtypeStruct((chosen_count,) + page_shape, jnp.bfloat16),
            jax.ShapeDtypeStruct((chosen_count, LANES), jnp.float32),
        ],
        in_specs=[vmem, hbm, hbm, hbm, hbm],
        out_specs=[vmem] * 3,
        scratch_shapes=[
            pltpu.VMEM((rows, maxp) + page_shape, jnp.bfloat16),
            pltpu.SMEM(send.shape, jnp.int32),
            pltpu.SMEM(wanted.shape, jnp.int32),
            pltpu.SMEM(tables.shape[1:], jnp.int32),
            pltpu.SMEM((chosen_count,), jnp.int32),
            pltpu.SMEM((chosen_count,), jnp.int32),
            pltpu.SemaphoreType.DMA((3,)),
            pltpu.SemaphoreType.DMA((chosen_count,)),
            pltpu.SemaphoreType.DMA((rows, maxp)),
        ],
        compiler_params=pltpu.CompilerParams(vmem_limit_bytes=24 * MIB),
        cost_estimate=pl.CostEstimate(flops=4 * 10**9, bytes_accessed=12 * MIB, transcendentals=10**6),
        name="resident",
    )(qa, *[pltpu.with_memory_space_constraint(x, pltpu.HBM) for x in (send, wanted, tables[0], stored)])
    count = groups - 1
    theirs = pl.pallas_call(
        functools.partial(second_kernel, held, per_held, maxp, count),
        out_shape=[part_shape] * count,
        in_specs=[vmem] * (2 + count),
        out_specs=[vmem] * count,
        compiler_params=pltpu.CompilerParams(vmem_limit_bytes=16 * MIB),
        cost_estimate=pl.CostEstimate(flops=4 * 10**9, bytes_accessed=8 * MIB, transcendentals=10**6),
        name="owned",
    )(chosen, entries, *asked)
    mine, theirs = lax.optimization_barrier((mine, theirs))
    parts = [mine, lax.ppermute(mine, "role", [(0, 1), (1, 0)])]
    for k in range(1, groups):
        pairs = [pair for i in range(groups) for pair in ((i, groups + (i - k) % groups), (groups + i, i))]
        parts.append(lax.ppermute(theirs[k - 1], ("role", "group"), pairs))
    attended = pl.pallas_call(
        functools.partial(merge_kernel, heads, rows),
        out_shape=jax.ShapeDtypeStruct((rows, wide), jnp.bfloat16),
        in_specs=[vmem] * len(parts),
        out_specs=vmem,
        compiler_params=pltpu.CompilerParams(vmem_limit_bytes=8 * MIB),
        name="merge",
    )(*parts)
    partner = lax.ppermute(attended, "role", [(0, 1), (1, 0)])
    share = out_weight.shape[1] // tps

    def project(steps, name):
        return pl.pallas_call(
            functools.partial(project_kernel, steps),
            out_shape=[jax.ShapeDtypeStruct((rows, share), jnp.float32)] * len(steps),
            in_specs=[vmem] * 3,
            out_specs=[vmem] * len(steps),
            compiler_params=pltpu.CompilerParams(vmem_limit_bytes=24 * MIB),
            cost_estimate=pl.CostEstimate(
                flops=len(steps) * 32 * wide * share, bytes_accessed=len(steps) * 2 * wide * share, transcendentals=0
            ),
            name=name,
        )(attended, partner, out_weight)

    steps = list(range(1, tps))
    sent = project(steps, "project")
    arrived = [lax.ppermute(part, "tp", [(i, (i + d) % tps) for i in range(tps)]) for d, part in zip(steps, sent)]
    total = functools.reduce(jnp.add, arrived, project([0], "project_own")[0])
    return total.astype(jnp.bfloat16)[None]


def solution(mesh):
    return jax.shard_map(
        per_device,
        mesh=mesh,
        in_specs=(
            P("role", "group", "tp", None, None, None),
            P(),
            P(),
            P("group", None),
            P("group", None, None),
            P("group", None, "tp"),
            P("group", None, "tp"),
            P("tp", "role"),
        ),
        out_specs=P("group", None, ("role", "tp")),
        check_vma=False,
    )
```

```python
import functools
import math

import jax
import jax.numpy as jnp
from jax import lax
from jax.experimental import pallas as pl
from jax.experimental.pallas import tpu as pltpu
from jax.sharding import PartitionSpec as P

KVH = 8
HD = 128
CAP = 4
CAPP = 2
PRE_DEV = 8
LANES = 128
PAGE = 128
NEG = -1e30
SCALE = 1.0 / math.sqrt(HD)
PARTS = CAP + CAPP
CHUNK = 8
MIB = 2**20


def dot(a, b, ca, cb):
    return lax.dot_general(a, b, (((ca,), (cb,)), ((), ())), preferred_element_type=jnp.float32)


def query_block(qa, held, per_held):
    q = qa[:, : held * per_held * HD].astype(jnp.float32)
    rows = q.shape[0]
    bands = []
    for j in range(held):
        heads = [q[:, (j * per_held + i) * HD : (j * per_held + i + 1) * HD] for i in range(per_held)]
        band = jnp.concatenate(heads, 0)
        blank = jnp.zeros_like(band)
        bands.append(jnp.concatenate([band if i == j else blank for i in range(held)], 1))
    return jnp.concatenate(bands, 0).astype(jnp.bfloat16)


def entry_rows(qa, held, per_held, maxp):
    rows = qa.shape[0]
    wide = held * per_held * HD
    aux = qa[:, wide : wide + LANES].astype(jnp.float32)
    lane = lax.broadcasted_iota(jnp.int32, (rows, LANES), 1) - maxp
    row = lax.broadcasted_iota(jnp.int32, (rows, LANES), 0)
    parts = jnp.where(lane == row, 8.0 * aux[:1], jnp.where(lane == row + rows, aux[:1], 0.0))
    length = jnp.sum(parts, 1, keepdims=True)
    turned = jnp.concatenate([jnp.where(lane == 0, length, aux)] * (held * per_held), 0).T
    first = lax.broadcasted_iota(jnp.int32, (maxp, 1), 0).astype(jnp.float32) * PAGE
    return turned[:maxp], jnp.clip(turned[maxp : maxp + 1] - first, 0.0, PAGE)


def lanes_of(page, first, held):
    return jnp.concatenate([page[:, (2 * j + first) * HD : (2 * j + first + 1) * HD] for j in range(held)], 1)


def write_part(out, acc, top, total, held, per_held):
    count = acc.shape[0]
    band = count // held
    for j in range(held):
        out[j * band : (j + 1) * band, :] = acc[j * band : (j + 1) * band, j * HD : (j + 1) * HD]
    out[count : count + 1, :count] = top
    out[count + 1 : count + 2, :count] = total


def owner_part(qa, pages, entries, out, held, per_held, maxp):
    q = query_block(qa, held, per_held)
    tab, cnt = entry_rows(qa, held, per_held, maxp)
    count = q.shape[0]
    token = lax.broadcasted_iota(jnp.int32, (PAGE, count), 0).astype(jnp.float32)
    masks = []
    for c in range(PARTS):
        valid = jnp.sum(jnp.where(tab == entries[c : c + 1, :count], cnt, 0.0), 0, keepdims=True)
        masks.append(token < valid)
    mask = jnp.concatenate(masks, 0)
    keys = jnp.concatenate([lanes_of(pages.at[c], 0, held) for c in range(PARTS)], 0)
    values = jnp.concatenate([lanes_of(pages.at[c], 1, held) for c in range(PARTS)], 0)
    s = jnp.where(mask, dot(keys, q, 1, 1) * SCALE, NEG)
    top = jnp.max(s, 0, keepdims=True)
    p = jnp.where(mask, jnp.exp(s - top), 0.0)
    total = jnp.sum(p, 0, keepdims=True)
    acc = dot(p.astype(jnp.bfloat16), values, 0, 0)
    write_part(out, acc, top, total, held, per_held)


def resident_part(qa, fresh_at, send, tables, lengths, maxp, group, kv, pages, flags, listed, scores, sems, out, held, per_held):
    rows = qa.shape[0]
    slots = kv.shape[0]
    for i in range(slots):
        flags[i] = 0
    for o in range(send.shape[1]):
        for i in range(send.shape[2]):
            flags[jnp.where(send[1, o, i] == group, send[2, o, i], slots)] = 1
    listed_count = jnp.int32(0)
    for r in range(rows):
        for e in range(maxp):
            slot = tables[r, e]
            tokens = jnp.minimum(lengths[0, r] - e * PAGE, PAGE)
            here = jnp.logical_and(slot < slots, flags[jnp.minimum(slot, slots - 1)] == 0)
            needed = jnp.logical_and(tokens > 0, here)
            listed[0, listed_count] = slot
            listed[1, listed_count] = r
            listed[2, listed_count] = tokens
            listed_count = listed_count + needed.astype(jnp.int32)
    for i in range(CHUNK):
        listed[0, listed_count + i] = 0
        listed[1, listed_count + i] = 0
        listed[2, listed_count + i] = 0
    chunks = (listed_count + CHUNK - 1) // CHUNK

    def page_copy(i):
        return pltpu.make_async_copy(kv.at[listed[0, i]], pages.at[i], sems.at[i])

    def start(c, _):
        for i in range(CHUNK):
            page_copy(c * CHUNK + i).start()
        return 0

    lax.fori_loop(0, chunks, start, 0)
    q = query_block(qa, held, per_held)
    count = q.shape[0]
    lane_row = lax.rem(lax.broadcasted_iota(jnp.int32, (1, count), 1), rows)
    token = lax.broadcasted_iota(jnp.int32, (PAGE, count), 0)
    fresh = qa[:, fresh_at : fresh_at + 2 * held * HD].astype(jnp.float32)
    fresh = jnp.concatenate([fresh, jnp.zeros_like(fresh)], 0).astype(jnp.bfloat16)
    own_mask = lax.broadcasted_iota(jnp.int32, (2 * rows, count), 0) == lane_row
    own = jnp.where(own_mask, dot(lanes_of(fresh, 0, held), q, 1, 1) * SCALE, NEG)

    def score(c, top):
        first = c * CHUNK
        masks = []
        for i in range(CHUNK):
            page_copy(first + i).wait()
            masks.append(token < jnp.where(lane_row == listed[1, first + i], listed[2, first + i], 0))
        mask = jnp.concatenate(masks, 0)
        keys = jnp.concatenate([lanes_of(pages.at[first + i], 0, held) for i in range(CHUNK)], 0)
        s = jnp.where(mask, dot(keys, q, 1, 1) * SCALE, NEG)
        scores[c] = s
        return jnp.maximum(top, jnp.max(s, 0, keepdims=True))

    top = lax.fori_loop(0, chunks, score, jnp.max(own, 0, keepdims=True))

    def weigh(c, carry):
        total, acc = carry
        first = c * CHUNK
        p = jnp.exp(scores[c] - top)
        values = jnp.concatenate([lanes_of(pages.at[first + i], 1, held) for i in range(CHUNK)], 0)
        return total + jnp.sum(p, 0, keepdims=True), acc + dot(p.astype(jnp.bfloat16), values, 0, 0)

    lift = jnp.exp(own - top)
    total = jnp.sum(lift, 0, keepdims=True)
    acc = dot(lift.astype(jnp.bfloat16), lanes_of(fresh, 1, held), 0, 0)
    total, acc = lax.fori_loop(0, chunks, weigh, (total, acc))
    write_part(out, acc, top, total, held, per_held)


def list_pages(send, wanted, owner, target, slots, page_list, slot_list, base):
    for c in range(PARTS):
        page_list[base + c] = 0
        slot_list[base + c] = -1
    at = jnp.int32(base)
    for i in range(send.shape[2]):
        hit = send[1, owner, i] == target
        page_list[at] = send[0, owner, i]
        slot_list[at] = jnp.where(hit, send[2, owner, i], -1)
        at = at + hit.astype(jnp.int32)
    at = jnp.int32(base + CAP)
    page_list[at] = 0
    slot_list[at] = -1
    for i in range(wanted.shape[1]):
        page = wanted[target, i] - owner * PRE_DEV
        hit = jnp.logical_and(page >= 0, page < PRE_DEV)
        page_list[at] = jnp.where(hit, page, 0)
        slot_list[at] = jnp.where(hit, slots + i, -1)
        at = at + hit.astype(jnp.int32)


def first_kernel(held, per_held, groups, maxp, qa, send_hbm, wanted_hbm, tables_hbm, lengths_hbm, kv, *refs):
    out, chosen, entries, pages, scores, send, wanted, tables, lengths = refs[:9]
    flags, listed, page_list, slot_list, list_sems, chosen_sems, sems = refs[9:]
    group = lax.axis_index("group")
    prefill = lax.axis_index("role") == 0
    fresh_at = held * per_held * HD + LANES
    lists = ((send_hbm, send), (wanted_hbm, wanted), (tables_hbm, tables), (lengths_hbm, lengths))
    copies = [pltpu.make_async_copy(a, b, list_sems.at[i]) for i, (a, b) in enumerate(lists)]
    for copy in copies:
        copy.start()
    for copy in copies:
        copy.wait()

    @pl.when(prefill)
    def _():
        copies = []
        for k in range(groups):
            target = lax.rem(group - k + groups, groups)
            list_pages(send, wanted, group, target, kv.shape[0], page_list, slot_list, k * PARTS)
            for c in range(PARTS):
                at = k * PARTS + c
                copy = pltpu.make_async_copy(kv.at[page_list[at]], chosen.at[at], chosen_sems.at[at])
                copy.start()
                copies.append(copy)
                entry = slot_list[at].astype(jnp.float32)
                entries[at : at + 1, :] = jnp.full((1, LANES), entry, jnp.float32)
        for copy in copies[:PARTS]:
            copy.wait()
        owner_part(qa, chosen.at[pl.ds(0, PARTS)], entries[:PARTS, :], out, held, per_held, maxp)
        for copy in copies[PARTS:]:
            copy.wait()

    @pl.when(jnp.logical_not(prefill))
    def _():
        resident_part(
            qa, fresh_at, send, tables, lengths, maxp, group, kv, pages, flags, listed, scores, sems, out, held, per_held
        )


def second_kernel(held, per_held, maxp, count, chosen, entries, *refs):
    qas, outs = refs[:count], refs[count:]

    @pl.when(lax.axis_index("role") == 0)
    def _():
        for k in range(count):
            at = (k + 1) * PARTS
            owner_part(
                qas[k], chosen.at[pl.ds(at, PARTS)], entries[at : at + PARTS, :], outs[k], held, per_held, maxp
            )


def merge_kernel(heads, rows, *refs):
    parts, out = refs[:-1], refs[-1]
    count = heads * rows
    pad = -len(parts) % 8
    tops = jnp.concatenate([part[count : count + 1, :count] for part in parts], 0)
    totals = jnp.concatenate([part[count + 1 : count + 2, :count] for part in parts], 0)
    factors = jnp.exp(tops - jnp.max(tops, 0, keepdims=True))
    factors = factors / jnp.sum(factors * totals, 0, keepdims=True)
    factors = jnp.concatenate([factors, jnp.zeros((pad, count), jnp.float32)], 0).T
    terms = [factors[:, i : i + 1] * part[:count, :] for i, part in enumerate(parts)]
    merged = functools.reduce(jnp.add, terms)
    out[...] = jnp.concatenate([merged[h * rows : (h + 1) * rows] for h in range(heads)], 1).astype(out.dtype)


def project_kernel(steps, attended, partner, weight, *outs):
    tps = lax.axis_size("tp")
    share = outs[0].shape[1]
    here = jnp.where(lax.axis_index("role") == 0, partner[...].astype(jnp.float32), attended[...].astype(jnp.float32))
    here = here.astype(jnp.bfloat16)
    for d, out in zip(steps, outs):
        first = lax.rem(lax.axis_index("tp") + d, tps) * share
        columns = pl.ds(pl.multiple_of(first, LANES), share)
        out[...] = jnp.dot(here, weight[:, columns], preferred_element_type=jnp.float32)


def per_device(kv_pages, send_list, wanted, lengths, tables, queries, new_kv, out_weight):
    stored = kv_pages[0, 0, 0]
    slots = stored.shape[0]
    groups, tps = lax.axis_size("group"), lax.axis_size("tp")
    held = max(1, KVH // tps)
    rows, wide = queries.shape[1], queries.shape[2]
    heads = wide // HD
    per_held = heads // held
    maxp = tables.shape[2]
    send = jnp.transpose(send_list, (2, 0, 1))
    fresh_at = wide + LANES
    width = fresh_at + new_kv.shape[2]

    def place(block, at):
        return jnp.pad(block, ((0, rows - block.shape[0]), (at, width - at - block.shape[1])))

    high = lax.shift_right_logical(place(lengths, wide + maxp), 3)
    low = jnp.bitwise_and(place(lengths, wide + maxp + rows), 7)
    integers = place(tables[0], wide) + high + low
    qa = place(queries[0], 0) + place(new_kv[0], fresh_at) + integers.astype(jnp.bfloat16)
    asked = [
        lax.ppermute(
            qa, ("role", "group"), [pair for i in range(groups) for pair in ((groups + i, (i + k) % groups), (i, groups + i))]
        )
        for k in range(1, groups)
    ]
    part_shape = jax.ShapeDtypeStruct((heads * rows + 8, HD), jnp.float32)
    vmem = pl.BlockSpec(memory_space=pltpu.VMEM)
    hbm = pl.BlockSpec(memory_space=pltpu.HBM)
    page_shape = stored.shape[1:]
    chosen_count = groups * PARTS
    read_count = -(-rows * maxp // CHUNK) * CHUNK
    lists = [send, wanted, tables[0], lengths]
    mine, chosen, entries = pl.pallas_call(
        functools.partial(first_kernel, held, per_held, groups, maxp),
        out_shape=[
            part_shape,
            jax.ShapeDtypeStruct((chosen_count,) + page_shape, jnp.bfloat16),
            jax.ShapeDtypeStruct((chosen_count, LANES), jnp.float32),
        ],
        in_specs=[vmem] + [hbm] * 5,
        out_specs=[vmem] * 3,
        scratch_shapes=[
            pltpu.VMEM((read_count,) + page_shape, jnp.bfloat16),
            pltpu.VMEM((read_count // CHUNK, CHUNK * PAGE, heads * rows), jnp.float32),
            pltpu.SMEM(send.shape, jnp.int32),
            pltpu.SMEM(wanted.shape, jnp.int32),
            pltpu.SMEM(tables.shape[1:], jnp.int32),
            pltpu.SMEM(lengths.shape, jnp.int32),
            pltpu.SMEM((slots + 1,), jnp.int32),
            pltpu.SMEM((3, read_count + CHUNK), jnp.int32),
            pltpu.SMEM((chosen_count + 1,), jnp.int32),
            pltpu.SMEM((chosen_count + 1,), jnp.int32),
            pltpu.SemaphoreType.DMA((len(lists),)),
            pltpu.SemaphoreType.DMA((chosen_count,)),
            pltpu.SemaphoreType.DMA((read_count,)),
        ],
        compiler_params=pltpu.CompilerParams(vmem_limit_bytes=24 * MIB),
        cost_estimate=pl.CostEstimate(flops=4 * 10**9, bytes_accessed=12 * MIB, transcendentals=10**6),
        name="resident",
    )(qa, *[pltpu.with_memory_space_constraint(x, pltpu.HBM) for x in lists + [stored]])
    count = groups - 1
    theirs = pl.pallas_call(
        functools.partial(second_kernel, held, per_held, maxp, count),
        out_shape=[part_shape] * count,
        in_specs=[vmem] * (2 + count),
        out_specs=[vmem] * count,
        compiler_params=pltpu.CompilerParams(vmem_limit_bytes=16 * MIB),
        cost_estimate=pl.CostEstimate(flops=4 * 10**9, bytes_accessed=8 * MIB, transcendentals=10**6),
        name="owned",
    )(chosen, entries, *asked)
    mine, theirs = lax.optimization_barrier((mine, theirs))
    parts = [mine, lax.ppermute(mine, "role", [(0, 1), (1, 0)])]
    for k in range(1, groups):
        pairs = [pair for i in range(groups) for pair in ((i, groups + (i - k) % groups), (groups + i, i))]
        parts.append(lax.ppermute(theirs[k - 1], ("role", "group"), pairs))
    attended = pl.pallas_call(
        functools.partial(merge_kernel, heads, rows),
        out_shape=jax.ShapeDtypeStruct((rows, wide), jnp.bfloat16),
        in_specs=[vmem] * len(parts),
        out_specs=vmem,
        compiler_params=pltpu.CompilerParams(vmem_limit_bytes=8 * MIB),
        name="merge",
    )(*parts)
    partner = lax.ppermute(attended, "role", [(0, 1), (1, 0)])
    share = out_weight.shape[1] // tps

    def project(steps, name):
        return pl.pallas_call(
            functools.partial(project_kernel, steps),
            out_shape=[jax.ShapeDtypeStruct((rows, share), jnp.float32)] * len(steps),
            in_specs=[vmem] * 3,
            out_specs=[vmem] * len(steps),
            compiler_params=pltpu.CompilerParams(vmem_limit_bytes=24 * MIB),
            cost_estimate=pl.CostEstimate(
                flops=len(steps) * 32 * wide * share, bytes_accessed=len(steps) * 2 * wide * share, transcendentals=0
            ),
            name=name,
        )(attended, partner, out_weight)

    steps = list(range(1, tps))
    sent = project(steps, "project")
    arrived = [lax.ppermute(part, "tp", [(i, (i + d) % tps) for i in range(tps)]) for d, part in zip(steps, sent)]
    total = functools.reduce(jnp.add, arrived, project([0], "project_own")[0])
    return total.astype(jnp.bfloat16)[None]


def solution(mesh):
    return jax.shard_map(
        per_device,
        mesh=mesh,
        in_specs=(
            P("role", "group", "tp", None, None, None),
            P(),
            P(),
            P("group", None),
            P("group", None, None),
            P("group", None, "tp"),
            P("group", None, "tp"),
            P("tp", "role"),
        ),
        out_specs=P("group", None, ("role", "tp")),
        check_vma=False,
    )
```

```python
import functools
import math

import jax
import jax.numpy as jnp
from jax import lax
from jax.experimental import pallas as pl
from jax.experimental.pallas import tpu as pltpu
from jax.sharding import PartitionSpec as P

KVH = 8
HD = 128
CAP = 4
CAPP = 2
PRE_DEV = 8
LANES = 128
PAGE = 128
NEG = -1e30
SCALE = 1.0 / math.sqrt(HD)
PARTS = CAP + CAPP
CHUNK = 8
BLOCK = 8
MIB = 2**20


def dot(a, b, ca, cb):
    return lax.dot_general(a, b, (((ca,), (cb,)), ((), ())), preferred_element_type=jnp.float32)


def query_block(qa, held, per_held):
    q = qa[:, : held * per_held * HD].astype(jnp.float32)
    rows = q.shape[0]
    bands = []
    for j in range(held):
        heads = [q[:, (j * per_held + i) * HD : (j * per_held + i + 1) * HD] for i in range(per_held)]
        band = jnp.concatenate(heads, 0)
        blank = jnp.zeros_like(band)
        bands.append(jnp.concatenate([band if i == j else blank for i in range(held)], 1))
    return jnp.concatenate(bands, 0).astype(jnp.bfloat16)


def entry_rows(qa, held, per_held, maxp):
    rows = qa.shape[0]
    wide = held * per_held * HD
    aux = qa[:, wide : wide + LANES].astype(jnp.float32)
    lane = lax.broadcasted_iota(jnp.int32, (rows, LANES), 1) - maxp
    row = lax.broadcasted_iota(jnp.int32, (rows, LANES), 0)
    parts = jnp.where(lane == row, 8.0 * aux[:1], jnp.where(lane == row + rows, aux[:1], 0.0))
    length = jnp.sum(parts, 1, keepdims=True)
    turned = jnp.concatenate([jnp.where(lane == 0, length, aux)] * (held * per_held), 0).T
    first = lax.broadcasted_iota(jnp.int32, (maxp, 1), 0).astype(jnp.float32) * PAGE
    return turned[:maxp], jnp.clip(turned[maxp : maxp + 1] - first, 0.0, PAGE)


def lanes_of(page, first, held):
    return jnp.concatenate([page[:, (2 * j + first) * HD : (2 * j + first + 1) * HD] for j in range(held)], 1)


def write_part(out, acc, top, total, held, per_held):
    count = acc.shape[0]
    band = count // held
    for j in range(held):
        out[j * band : (j + 1) * band, :] = acc[j * band : (j + 1) * band, j * HD : (j + 1) * HD]
    out[count : count + 1, :count] = top
    out[count + 1 : count + 2, :count] = total


def owner_part(qa, pages, entries, out, held, per_held, maxp):
    q = query_block(qa, held, per_held)
    tab, cnt = entry_rows(qa, held, per_held, maxp)
    count = q.shape[0]
    token = lax.broadcasted_iota(jnp.int32, (PAGE, count), 0).astype(jnp.float32)
    masks = []
    for c in range(PARTS):
        valid = jnp.sum(jnp.where(tab == entries[c : c + 1, :count], cnt, 0.0), 0, keepdims=True)
        masks.append(token < valid)
    mask = jnp.concatenate(masks, 0)
    keys = jnp.concatenate([lanes_of(pages.at[c], 0, held) for c in range(PARTS)], 0)
    values = jnp.concatenate([lanes_of(pages.at[c], 1, held) for c in range(PARTS)], 0)
    s = jnp.where(mask, dot(keys, q, 1, 1) * SCALE, NEG)
    top = jnp.max(s, 0, keepdims=True)
    p = jnp.where(mask, jnp.exp(s - top), 0.0)
    total = jnp.sum(p, 0, keepdims=True)
    acc = dot(p.astype(jnp.bfloat16), values, 0, 0)
    write_part(out, acc, top, total, held, per_held)


def resident_part(qa, fresh_at, lists_ready, send, tables, lengths, maxp, group, kv, pages, flags, listed, sems, out, held, per_held):
    rows = qa.shape[0]
    slots = kv.shape[0]
    q = query_block(qa, held, per_held)
    count = q.shape[0]
    lane_row = lax.rem(lax.broadcasted_iota(jnp.int32, (1, count), 1), rows)
    token = lax.broadcasted_iota(jnp.int32, (PAGE, count), 0)
    fresh = qa[:, fresh_at : fresh_at + 2 * held * HD].astype(jnp.float32)
    fresh = jnp.concatenate([fresh, jnp.zeros_like(fresh)], 0).astype(jnp.bfloat16)
    own_mask = lax.broadcasted_iota(jnp.int32, (2 * rows, count), 0) == lane_row
    own = jnp.where(own_mask, dot(lanes_of(fresh, 0, held), q, 1, 1) * SCALE, NEG)
    own_top = jnp.max(own, 0, keepdims=True)
    lift = jnp.exp(own - own_top)
    own_total = jnp.sum(lift, 0, keepdims=True)
    own_acc = dot(lift.astype(jnp.bfloat16), lanes_of(fresh, 1, held), 0, 0)
    for i in range(slots):
        flags[i] = 0

    lists_ready()
    for o in range(send.shape[1]):
        for i in range(send.shape[2]):
            flags[jnp.where(send[1, o, i] == group, send[2, o, i], slots)] = 1

    def page_copy(slot, i):
        return pltpu.make_async_copy(kv.at[slot], pages.at[i], sems.at[i])

    listed_count = jnp.int32(0)
    for r in range(rows):
        length = lengths[0, r]
        for e in range(maxp):
            slot = tables[r, e]
            tokens = jnp.minimum(length - e * PAGE, PAGE)
            here = jnp.logical_and(slot < slots, flags[jnp.minimum(slot, slots - 1)] == 0)
            needed = jnp.logical_and(tokens > 0, here)
            listed[0, listed_count] = r
            listed[1, listed_count] = tokens

            @pl.when(needed)
            def _(slot=slot, at=listed_count):
                page_copy(slot, at).start()

            listed_count = listed_count + needed.astype(jnp.int32)
    chunks = (listed_count + CHUNK - 1) // CHUNK

    def fill(i, _):
        listed[0, i] = 0
        listed[1, i] = 0
        page_copy(0, i).start()
        return 0

    lax.fori_loop(listed_count, chunks * CHUNK, fill, 0)

    def step(c, carry):
        old_top, total, acc = carry
        blocks = [c * CHUNK + b for b in range(0, CHUNK, BLOCK)]
        scores, top = [], old_top
        for first in blocks:
            masks = []
            for i in range(BLOCK):
                masks.append(token < jnp.where(lane_row == listed[0, first + i], listed[1, first + i], 0))
            for i in range(BLOCK):
                page_copy(0, first + i).wait()
            keys = jnp.concatenate([lanes_of(pages.at[first + i], 0, held) for i in range(BLOCK)], 0)
            scores.append(jnp.where(jnp.concatenate(masks, 0), dot(keys, q, 1, 1) * SCALE, NEG))
            top = jnp.maximum(top, jnp.max(scores[-1], 0, keepdims=True))
        fade = jnp.exp(old_top - top)
        total = total * fade
        acc = acc * jnp.broadcast_to(fade, (8, count)).T[:, :1]
        for first, s in zip(blocks, scores):
            p = jnp.exp(s - top)
            total = total + jnp.sum(p, 0, keepdims=True)
            values = jnp.concatenate([lanes_of(pages.at[first + i], 1, held) for i in range(BLOCK)], 0)
            acc = acc + dot(p.astype(jnp.bfloat16), values, 0, 0)
        return top, total, acc

    top, total, acc = lax.fori_loop(0, chunks, step, (own_top, own_total, own_acc))
    write_part(out, acc, top, total, held, per_held)


def list_pages(send, wanted, owner, target, slots, page_list, slot_list, base):
    for c in range(PARTS):
        page_list[base + c] = 0
        slot_list[base + c] = -1
    at = jnp.int32(base)
    for i in range(send.shape[2]):
        hit = send[1, owner, i] == target
        page_list[at] = send[0, owner, i]
        slot_list[at] = jnp.where(hit, send[2, owner, i], -1)
        at = at + hit.astype(jnp.int32)
    at = jnp.int32(base + CAP)
    page_list[at] = 0
    slot_list[at] = -1
    for i in range(wanted.shape[1]):
        page = wanted[target, i] - owner * PRE_DEV
        hit = jnp.logical_and(page >= 0, page < PRE_DEV)
        page_list[at] = jnp.where(hit, page, 0)
        slot_list[at] = jnp.where(hit, slots + i, -1)
        at = at + hit.astype(jnp.int32)


def first_kernel(held, per_held, groups, maxp, qa, send_hbm, wanted_hbm, tables_hbm, lengths_hbm, kv, *refs):
    out, chosen, entries, pages, send, wanted, tables, lengths = refs[:8]
    flags, listed, page_list, slot_list, list_sems, chosen_sems, sems = refs[8:]
    group = lax.axis_index("group")
    prefill = lax.axis_index("role") == 0
    fresh_at = held * per_held * HD + LANES
    lists = ((send_hbm, send), (wanted_hbm, wanted), (tables_hbm, tables), (lengths_hbm, lengths))
    copies = [pltpu.make_async_copy(a, b, list_sems.at[i]) for i, (a, b) in enumerate(lists)]
    for copy in copies:
        copy.start()

    def lists_ready():
        for copy in copies:
            copy.wait()

    @pl.when(prefill)
    def _():
        lists_ready()
        copies = []
        for k in range(groups):
            target = lax.rem(group - k + groups, groups)
            list_pages(send, wanted, group, target, kv.shape[0], page_list, slot_list, k * PARTS)
            for c in range(PARTS):
                at = k * PARTS + c
                copy = pltpu.make_async_copy(kv.at[page_list[at]], chosen.at[at], chosen_sems.at[at])
                copy.start()
                copies.append(copy)
                entry = slot_list[at].astype(jnp.float32)
                entries[at : at + 1, :] = jnp.full((1, LANES), entry, jnp.float32)
        for copy in copies[:PARTS]:
            copy.wait()
        owner_part(qa, chosen.at[pl.ds(0, PARTS)], entries[:PARTS, :], out, held, per_held, maxp)
        for copy in copies[PARTS:]:
            copy.wait()

    @pl.when(jnp.logical_not(prefill))
    def _():
        resident_part(
            qa, fresh_at, lists_ready, send, tables, lengths, maxp, group, kv, pages, flags, listed, sems, out, held, per_held
        )


def second_kernel(held, per_held, maxp, count, chosen, entries, *refs):
    qas, outs = refs[:count][::-1], refs[count:]

    @pl.when(lax.axis_index("role") == 0)
    def _():
        for k in range(count):
            at = (k + 1) * PARTS
            owner_part(
                qas[k], chosen.at[pl.ds(at, PARTS)], entries[at : at + PARTS, :], outs[k], held, per_held, maxp
            )


def merge_kernel(heads, rows, *refs):
    parts, out = refs[:-1], refs[-1]
    count = heads * rows
    pad = -len(parts) % 8
    tops = jnp.concatenate([part[count : count + 1, :count] for part in parts], 0)
    totals = jnp.concatenate([part[count + 1 : count + 2, :count] for part in parts], 0)
    factors = jnp.exp(tops - jnp.max(tops, 0, keepdims=True))
    factors = factors / jnp.sum(factors * totals, 0, keepdims=True)
    factors = jnp.concatenate([factors, jnp.zeros((pad, count), jnp.float32)], 0).T
    terms = [factors[:, i : i + 1] * part[:count, :] for i, part in enumerate(parts)]
    merged = functools.reduce(jnp.add, terms)
    out[...] = jnp.concatenate([merged[h * rows : (h + 1) * rows] for h in range(heads)], 1).astype(out.dtype)


def project_kernel(steps, attended, partner, weight, *outs):
    share = outs[0].shape[1]
    here = jnp.where(lax.axis_index("role") == 0, partner[...].astype(jnp.float32), attended[...].astype(jnp.float32))
    here = here.astype(jnp.bfloat16)
    for d, out in zip(steps, outs):
        first = lax.bitwise_xor(lax.axis_index("tp"), d) * share
        columns = pl.ds(pl.multiple_of(first, LANES), share)
        out[...] = jnp.dot(here, weight[:, columns], preferred_element_type=jnp.float32)


def per_device(kv_pages, send_list, wanted, lengths, tables, queries, new_kv, out_weight):
    stored = kv_pages[0, 0, 0]
    slots = stored.shape[0]
    groups, tps = lax.axis_size("group"), lax.axis_size("tp")
    held = max(1, KVH // tps)
    rows, wide = queries.shape[1], queries.shape[2]
    heads = wide // HD
    per_held = heads // held
    maxp = tables.shape[2]
    send = jnp.transpose(send_list, (2, 0, 1))
    fresh_at = wide + LANES
    width = fresh_at + new_kv.shape[2]

    def place(block, at):
        return jnp.pad(block, ((0, rows - block.shape[0]), (at, width - at - block.shape[1])))

    high = lax.shift_right_logical(place(lengths, wide + maxp), 3)
    low = jnp.bitwise_and(place(lengths, wide + maxp + rows), 7)
    integers = place(tables[0], wide) + high + low
    qa = place(queries[0], 0) + place(new_kv[0], fresh_at) + integers.astype(jnp.bfloat16)
    asked = []
    for k in range(1, groups):
        pairs = [pair for i in range(groups) for pair in ((groups + i, (i + k) % groups), (i, groups + i))]
        asked.append(lax.ppermute(qa, ("role", "group"), pairs))
    part_shape = jax.ShapeDtypeStruct((heads * rows + 8, HD), jnp.float32)
    vmem = pl.BlockSpec(memory_space=pltpu.VMEM)
    hbm = pl.BlockSpec(memory_space=pltpu.HBM)
    page_shape = stored.shape[1:]
    chosen_count = groups * PARTS
    read_count = -(-rows * maxp // CHUNK) * CHUNK
    lists = [send, wanted, tables[0], lengths]
    mine, chosen, entries = pl.pallas_call(
        functools.partial(first_kernel, held, per_held, groups, maxp),
        out_shape=[
            part_shape,
            jax.ShapeDtypeStruct((chosen_count,) + page_shape, jnp.bfloat16),
            jax.ShapeDtypeStruct((chosen_count, LANES), jnp.float32),
        ],
        in_specs=[vmem] + [hbm] * 5,
        out_specs=[vmem] * 3,
        scratch_shapes=[
            pltpu.VMEM((read_count,) + page_shape, jnp.bfloat16),
            pltpu.SMEM(send.shape, jnp.int32),
            pltpu.SMEM(wanted.shape, jnp.int32),
            pltpu.SMEM(tables.shape[1:], jnp.int32),
            pltpu.SMEM(lengths.shape, jnp.int32),
            pltpu.SMEM((slots + 1,), jnp.int32),
            pltpu.SMEM((2, read_count), jnp.int32),
            pltpu.SMEM((chosen_count + 1,), jnp.int32),
            pltpu.SMEM((chosen_count + 1,), jnp.int32),
            pltpu.SemaphoreType.DMA((len(lists),)),
            pltpu.SemaphoreType.DMA((chosen_count,)),
            pltpu.SemaphoreType.DMA((read_count,)),
        ],
        compiler_params=pltpu.CompilerParams(vmem_limit_bytes=24 * MIB),
        name="resident",
    )(qa, *[pltpu.with_memory_space_constraint(x, pltpu.HBM) for x in lists + [stored]])
    out_weight, chosen, entries, mine = lax.optimization_barrier((out_weight, chosen, entries, mine))
    count = groups - 1
    theirs = pl.pallas_call(
        functools.partial(second_kernel, held, per_held, maxp, count),
        out_shape=[part_shape] * count,
        in_specs=[vmem] * (2 + count),
        out_specs=[vmem] * count,
        compiler_params=pltpu.CompilerParams(vmem_limit_bytes=16 * MIB),
        cost_estimate=pl.CostEstimate(flops=4 * 10**9, bytes_accessed=8 * MIB, transcendentals=10**6),
        name="owned",
    )(chosen, entries, *reversed(asked))
    mine, theirs = lax.optimization_barrier((mine, theirs))
    parts = [mine, lax.ppermute(mine, "role", [(0, 1), (1, 0)])]
    for k in range(1, groups):
        pairs = [pair for i in range(groups) for pair in ((i, groups + (i - k) % groups), (groups + i, i))]
        parts.append(lax.ppermute(theirs[k - 1], ("role", "group"), pairs))
    attended = pl.pallas_call(
        functools.partial(merge_kernel, heads, rows),
        out_shape=jax.ShapeDtypeStruct((rows, wide), jnp.bfloat16),
        in_specs=[vmem] * len(parts),
        out_specs=vmem,
        compiler_params=pltpu.CompilerParams(vmem_limit_bytes=8 * MIB),
        name="merge",
    )(*parts)
    partner = lax.ppermute(attended, "role", [(0, 1), (1, 0)])
    share = out_weight.shape[1] // tps

    def project(steps, name):
        return pl.pallas_call(
            functools.partial(project_kernel, steps),
            out_shape=[jax.ShapeDtypeStruct((rows, share), jnp.float32)] * len(steps),
            in_specs=[vmem] * 3,
            out_specs=[vmem] * len(steps),
            compiler_params=pltpu.CompilerParams(vmem_limit_bytes=24 * MIB),
            cost_estimate=pl.CostEstimate(
                flops=len(steps) * 32 * wide * share, bytes_accessed=len(steps) * 2 * wide * share, transcendentals=0
            ),
            name=name,
        )(attended, partner, out_weight)

    steps = list(range(1, tps))
    sent = project(steps, "project")
    arrived = [lax.ppermute(part, "tp", [(i, i ^ d) for i in range(tps)]) for d, part in zip(steps, sent)]
    total = functools.reduce(jnp.add, arrived, project([0], "project_own")[0])
    return total.astype(jnp.bfloat16)[None]


def solution(mesh):
    return jax.shard_map(
        per_device,
        mesh=mesh,
        in_specs=(
            P("role", "group", "tp", None, None, None),
            P(),
            P(),
            P("group", None),
            P("group", None, None),
            P("group", None, "tp"),
            P("group", None, "tp"),
            P("tp", "role"),
        ),
        out_specs=P("group", None, ("role", "tp")),
        check_vma=False,
    )
```

```python
import functools
import math

import jax
import jax.numpy as jnp
from jax import lax
from jax.experimental import pallas as pl
from jax.experimental.pallas import tpu as pltpu
from jax.sharding import PartitionSpec as P

KVH = 8
HD = 128
CAP = 4
CAPP = 2
PRE_DEV = 8
LANES = 128
PAGE = 128
NEG = -1e30
SCALE = 1.0 / math.sqrt(HD)
PARTS = CAP + CAPP
CHUNK = 8
BLOCK = 8
MIB = 2**20


def dot(a, b, ca, cb):
    return lax.dot_general(a, b, (((ca,), (cb,)), ((), ())), preferred_element_type=jnp.float32)


def query_block(qa, held, per_held):
    q = qa[:, : held * per_held * HD].astype(jnp.float32)
    rows = q.shape[0]
    bands = []
    for j in range(held):
        heads = [q[:, (j * per_held + i) * HD : (j * per_held + i + 1) * HD] for i in range(per_held)]
        band = jnp.concatenate(heads, 0)
        blank = jnp.zeros_like(band)
        bands.append(jnp.concatenate([band if i == j else blank for i in range(held)], 1))
    return jnp.concatenate(bands, 0).astype(jnp.bfloat16)


def entry_rows(qa, held, per_held, maxp):
    rows = qa.shape[0]
    wide = held * per_held * HD
    aux = qa[:, wide : wide + LANES].astype(jnp.float32)
    lane = lax.broadcasted_iota(jnp.int32, (rows, LANES), 1) - maxp
    row = lax.broadcasted_iota(jnp.int32, (rows, LANES), 0)
    parts = jnp.where(lane == row, 8.0 * aux[:1], jnp.where(lane == row + rows, aux[:1], 0.0))
    length = jnp.sum(parts, 1, keepdims=True)
    turned = jnp.concatenate([jnp.where(lane == 0, length, aux)] * (held * per_held), 0).T
    first = lax.broadcasted_iota(jnp.int32, (maxp, 1), 0).astype(jnp.float32) * PAGE
    return turned[:maxp], jnp.clip(turned[maxp : maxp + 1] - first, 0.0, PAGE)


def lanes_of(page, first, held):
    return jnp.concatenate([page[:, (2 * j + first) * HD : (2 * j + first + 1) * HD] for j in range(held)], 1)


def write_part(out, acc, top, total, held, per_held):
    count = acc.shape[0]
    band = count // held
    for j in range(held):
        out[j * band : (j + 1) * band, :] = acc[j * band : (j + 1) * band, j * HD : (j + 1) * HD]
    out[count : count + 1, :count] = top
    out[count + 1 : count + 2, :count] = total


def owner_part(qa, pages, entries, out, held, per_held, maxp):
    q = query_block(qa, held, per_held)
    tab, cnt = entry_rows(qa, held, per_held, maxp)
    count = q.shape[0]
    token = lax.broadcasted_iota(jnp.int32, (PAGE, count), 0).astype(jnp.float32)
    masks = []
    for c in range(PARTS):
        valid = jnp.sum(jnp.where(tab == entries[c : c + 1, :count], cnt, 0.0), 0, keepdims=True)
        masks.append(token < valid)
    mask = jnp.concatenate(masks, 0)
    keys = jnp.concatenate([lanes_of(pages.at[c], 0, held) for c in range(PARTS)], 0)
    values = jnp.concatenate([lanes_of(pages.at[c], 1, held) for c in range(PARTS)], 0)
    s = jnp.where(mask, dot(keys, q, 1, 1) * SCALE, NEG)
    top = jnp.max(s, 0, keepdims=True)
    p = jnp.where(mask, jnp.exp(s - top), 0.0)
    total = jnp.sum(p, 0, keepdims=True)
    acc = dot(p.astype(jnp.bfloat16), values, 0, 0)
    write_part(out, acc, top, total, held, per_held)


def resident_part(qa, fresh_at, lists_ready, send, tables, lengths, maxp, group, kv, pages, flags, listed, sems, out, held, per_held):
    rows = qa.shape[0]
    slots = kv.shape[0]
    q = query_block(qa, held, per_held)
    count = q.shape[0]
    lane_row = lax.rem(lax.broadcasted_iota(jnp.int32, (1, count), 1), rows)
    token = lax.broadcasted_iota(jnp.int32, (PAGE, count), 0)
    fresh = qa[:, fresh_at : fresh_at + 2 * held * HD].astype(jnp.float32)
    fresh = jnp.concatenate([fresh, jnp.zeros_like(fresh)], 0).astype(jnp.bfloat16)
    own_mask = lax.broadcasted_iota(jnp.int32, (2 * rows, count), 0) == lane_row
    own = jnp.where(own_mask, dot(lanes_of(fresh, 0, held), q, 1, 1) * SCALE, NEG)
    own_top = jnp.max(own, 0, keepdims=True)
    lift = jnp.exp(own - own_top)
    own_total = jnp.sum(lift, 0, keepdims=True)
    own_acc = dot(lift.astype(jnp.bfloat16), lanes_of(fresh, 1, held), 0, 0)
    for i in range(slots):
        flags[i] = 0

    lists_ready()
    for o in range(send.shape[1]):
        for i in range(send.shape[2]):
            flags[jnp.where(send[1, o, i] == group, send[2, o, i], slots)] = 1

    def page_copy(slot, i):
        return pltpu.make_async_copy(kv.at[slot], pages.at[i], sems.at[i])

    listed_count = jnp.int32(0)
    for r in range(rows):
        length = lengths[0, r]
        for e in range(maxp):
            slot = tables[r, e]
            tokens = jnp.minimum(length - e * PAGE, PAGE)
            here = jnp.logical_and(slot < slots, flags[jnp.minimum(slot, slots - 1)] == 0)
            needed = jnp.logical_and(tokens > 0, here)
            listed[0, listed_count] = r
            listed[1, listed_count] = tokens

            @pl.when(needed)
            def _(slot=slot, at=listed_count):
                page_copy(slot, at).start()

            listed_count = listed_count + needed.astype(jnp.int32)
    chunks = (listed_count + CHUNK - 1) // CHUNK

    def fill(i, _):
        listed[0, i] = 0
        listed[1, i] = 0
        page_copy(0, i).start()
        return 0

    lax.fori_loop(listed_count, chunks * CHUNK, fill, 0)

    def step(c, carry):
        old_top, total, acc = carry
        blocks = [c * CHUNK + b for b in range(0, CHUNK, BLOCK)]
        scores, top = [], old_top
        for first in blocks:
            masks = []
            for i in range(BLOCK):
                masks.append(token < jnp.where(lane_row == listed[0, first + i], listed[1, first + i], 0))
            for i in range(BLOCK):
                page_copy(0, first + i).wait()
            keys = jnp.concatenate([lanes_of(pages.at[first + i], 0, held) for i in range(BLOCK)], 0)
            scores.append(jnp.where(jnp.concatenate(masks, 0), dot(keys, q, 1, 1) * SCALE, NEG))
            top = jnp.maximum(top, jnp.max(scores[-1], 0, keepdims=True))
        fade = jnp.exp(old_top - top)
        total = total * fade
        acc = acc * jnp.broadcast_to(fade, (8, count)).T[:, :1]
        for first, s in zip(blocks, scores):
            p = jnp.exp(s - top)
            total = total + jnp.sum(p, 0, keepdims=True)
            values = jnp.concatenate([lanes_of(pages.at[first + i], 1, held) for i in range(BLOCK)], 0)
            acc = acc + dot(p.astype(jnp.bfloat16), values, 0, 0)
        return top, total, acc

    top, total, acc = lax.fori_loop(0, chunks, step, (own_top, own_total, own_acc))
    write_part(out, acc, top, total, held, per_held)


def list_pages(send, wanted, owner, target, slots, page_list, slot_list, base):
    for c in range(PARTS):
        page_list[base + c] = 0
        slot_list[base + c] = -1
    at = jnp.int32(base)
    for i in range(send.shape[2]):
        hit = send[1, owner, i] == target
        page_list[at] = send[0, owner, i]
        slot_list[at] = jnp.where(hit, send[2, owner, i], -1)
        at = at + hit.astype(jnp.int32)
    at = jnp.int32(base + CAP)
    page_list[at] = 0
    slot_list[at] = -1
    for i in range(wanted.shape[1]):
        page = wanted[target, i] - owner * PRE_DEV
        hit = jnp.logical_and(page >= 0, page < PRE_DEV)
        page_list[at] = jnp.where(hit, page, 0)
        slot_list[at] = jnp.where(hit, slots + i, -1)
        at = at + hit.astype(jnp.int32)


def first_kernel(held, per_held, groups, maxp, qa, send_hbm, wanted_hbm, tables_hbm, lengths_hbm, kv, *refs):
    out, chosen, entries, pages, send, wanted, tables, lengths = refs[:8]
    flags, listed, page_list, slot_list, list_sems, chosen_sems, sems = refs[8:]
    group = lax.axis_index("group")
    prefill = lax.axis_index("role") == 0
    fresh_at = held * per_held * HD + LANES
    lists = ((send_hbm, send), (wanted_hbm, wanted), (tables_hbm, tables), (lengths_hbm, lengths))
    copies = [pltpu.make_async_copy(a, b, list_sems.at[i]) for i, (a, b) in enumerate(lists)]
    for copy in copies:
        copy.start()

    def lists_ready():
        for copy in copies:
            copy.wait()

    @pl.when(prefill)
    def _():
        lists_ready()
        copies = []
        for k in range(groups):
            target = lax.rem(group - k + groups, groups)
            list_pages(send, wanted, group, target, kv.shape[0], page_list, slot_list, k * PARTS)
            for c in range(PARTS):
                at = k * PARTS + c
                copy = pltpu.make_async_copy(kv.at[page_list[at]], chosen.at[at], chosen_sems.at[at])
                copy.start()
                copies.append(copy)
                entry = slot_list[at].astype(jnp.float32)
                entries[at : at + 1, :] = jnp.full((1, LANES), entry, jnp.float32)
        for copy in copies[:PARTS]:
            copy.wait()
        owner_part(qa, chosen.at[pl.ds(0, PARTS)], entries[:PARTS, :], out, held, per_held, maxp)
        for copy in copies[PARTS:]:
            copy.wait()

    @pl.when(jnp.logical_not(prefill))
    def _():
        resident_part(
            qa, fresh_at, lists_ready, send, tables, lengths, maxp, group, kv, pages, flags, listed, sems, out, held, per_held
        )


def second_kernel(held, per_held, maxp, count, chosen, entries, *refs):
    qas, outs = refs[:count][::-1], refs[count:]

    @pl.when(lax.axis_index("role") == 0)
    def _():
        for k in range(count):
            at = (k + 1) * PARTS
            owner_part(
                qas[k], chosen.at[pl.ds(at, PARTS)], entries[at : at + PARTS, :], outs[k], held, per_held, maxp
            )


def merge_kernel(heads, rows, *refs):
    parts, out = refs[:-1], refs[-1]
    count = heads * rows
    pad = -len(parts) % 8
    tops = jnp.concatenate([part[count : count + 1, :count] for part in parts], 0)
    totals = jnp.concatenate([part[count + 1 : count + 2, :count] for part in parts], 0)
    factors = jnp.exp(tops - jnp.max(tops, 0, keepdims=True))
    factors = factors / jnp.sum(factors * totals, 0, keepdims=True)
    factors = jnp.concatenate([factors, jnp.zeros((pad, count), jnp.float32)], 0).T
    terms = [factors[:, i : i + 1] * part[:count, :] for i, part in enumerate(parts)]
    merged = functools.reduce(jnp.add, terms)
    out[...] = jnp.concatenate([merged[h * rows : (h + 1) * rows] for h in range(heads)], 1).astype(out.dtype)


def project_kernel(steps, attended, partner, weight, *outs):
    tps = lax.axis_size("tp")
    share = outs[0].shape[1]
    here = jnp.where(lax.axis_index("role") == 0, partner[...].astype(jnp.float32), attended[...].astype(jnp.float32))
    here = here.astype(jnp.bfloat16)
    for d, out in zip(steps, outs):
        first = lax.rem(lax.axis_index("tp") + d, tps) * share
        columns = pl.ds(pl.multiple_of(first, LANES), share)
        out[...] = jnp.dot(here, weight[:, columns], preferred_element_type=jnp.float32)


def per_device(kv_pages, send_list, wanted, lengths, tables, queries, new_kv, out_weight):
    stored = kv_pages[0, 0, 0]
    slots = stored.shape[0]
    groups, tps = lax.axis_size("group"), lax.axis_size("tp")
    held = max(1, KVH // tps)
    rows, wide = queries.shape[1], queries.shape[2]
    heads = wide // HD
    per_held = heads // held
    maxp = tables.shape[2]
    send = jnp.transpose(send_list, (2, 0, 1))
    fresh_at = wide + LANES
    width = fresh_at + new_kv.shape[2]

    def place(block, at):
        return jnp.pad(block, ((0, rows - block.shape[0]), (at, width - at - block.shape[1])))

    high = lax.shift_right_logical(place(lengths, wide + maxp), 3)
    low = jnp.bitwise_and(place(lengths, wide + maxp + rows), 7)
    integers = place(tables[0], wide) + high + low
    qa = place(queries[0], 0) + place(new_kv[0], fresh_at) + integers.astype(jnp.bfloat16)
    asked = []
    for k in range(1, groups):
        pairs = [pair for i in range(groups) for pair in ((groups + i, (i + k) % groups), (i, groups + i))]
        asked.append(lax.ppermute(qa, ("role", "group"), pairs))
    part_shape = jax.ShapeDtypeStruct((heads * rows + 8, HD), jnp.float32)
    vmem = pl.BlockSpec(memory_space=pltpu.VMEM)
    hbm = pl.BlockSpec(memory_space=pltpu.HBM)
    page_shape = stored.shape[1:]
    chosen_count = groups * PARTS
    read_count = -(-rows * maxp // CHUNK) * CHUNK
    lists = [send, wanted, tables[0], lengths]
    mine, chosen, entries = pl.pallas_call(
        functools.partial(first_kernel, held, per_held, groups, maxp),
        out_shape=[
            part_shape,
            jax.ShapeDtypeStruct((chosen_count,) + page_shape, jnp.bfloat16),
            jax.ShapeDtypeStruct((chosen_count, LANES), jnp.float32),
        ],
        in_specs=[vmem] + [hbm] * 5,
        out_specs=[vmem] * 3,
        scratch_shapes=[
            pltpu.VMEM((read_count,) + page_shape, jnp.bfloat16),
            pltpu.SMEM(send.shape, jnp.int32),
            pltpu.SMEM(wanted.shape, jnp.int32),
            pltpu.SMEM(tables.shape[1:], jnp.int32),
            pltpu.SMEM(lengths.shape, jnp.int32),
            pltpu.SMEM((slots + 1,), jnp.int32),
            pltpu.SMEM((2, read_count), jnp.int32),
            pltpu.SMEM((chosen_count + 1,), jnp.int32),
            pltpu.SMEM((chosen_count + 1,), jnp.int32),
            pltpu.SemaphoreType.DMA((len(lists),)),
            pltpu.SemaphoreType.DMA((chosen_count,)),
            pltpu.SemaphoreType.DMA((read_count,)),
        ],
        compiler_params=pltpu.CompilerParams(vmem_limit_bytes=24 * MIB),
        name="resident",
    )(qa, *[pltpu.with_memory_space_constraint(x, pltpu.HBM) for x in lists + [stored]])
    out_weight, chosen, entries, mine = lax.optimization_barrier((out_weight, chosen, entries, mine))
    count = groups - 1
    theirs = pl.pallas_call(
        functools.partial(second_kernel, held, per_held, maxp, count),
        out_shape=[part_shape] * count,
        in_specs=[vmem] * (2 + count),
        out_specs=[vmem] * count,
        compiler_params=pltpu.CompilerParams(vmem_limit_bytes=16 * MIB),
        cost_estimate=pl.CostEstimate(flops=4 * 10**10, bytes_accessed=8 * MIB, transcendentals=10**6),
        name="owned",
    )(chosen, entries, *reversed(asked))
    mine, theirs = lax.optimization_barrier((mine, theirs))
    parts = [mine, lax.ppermute(mine, "role", [(0, 1), (1, 0)])]
    for k in range(1, groups):
        pairs = [pair for i in range(groups) for pair in ((i, groups + (i - k) % groups), (groups + i, i))]
        parts.append(lax.ppermute(theirs[k - 1], ("role", "group"), pairs))
    attended = pl.pallas_call(
        functools.partial(merge_kernel, heads, rows),
        out_shape=jax.ShapeDtypeStruct((rows, wide), jnp.bfloat16),
        in_specs=[vmem] * len(parts),
        out_specs=vmem,
        compiler_params=pltpu.CompilerParams(vmem_limit_bytes=8 * MIB),
        name="merge",
    )(*parts)
    partner = lax.ppermute(attended, "role", [(0, 1), (1, 0)])
    share = out_weight.shape[1] // tps

    def project(steps, name):
        return pl.pallas_call(
            functools.partial(project_kernel, steps),
            out_shape=[jax.ShapeDtypeStruct((rows, share), jnp.float32)] * len(steps),
            in_specs=[vmem] * 3,
            out_specs=[vmem] * len(steps),
            compiler_params=pltpu.CompilerParams(vmem_limit_bytes=24 * MIB),
            cost_estimate=pl.CostEstimate(
                flops=len(steps) * 32 * wide * share, bytes_accessed=len(steps) * 2 * wide * share, transcendentals=0
            ),
            name=name,
        )(attended, partner, out_weight)

    steps = list(range(1, tps))
    sent = project(steps, "project")
    arrived = [lax.ppermute(part, "tp", [(i, (i + d) % tps) for i in range(tps)]) for d, part in zip(steps, sent)]
    total = functools.reduce(jnp.add, arrived, project([0], "project_own")[0])
    return total.astype(jnp.bfloat16)[None]


def solution(mesh):
    return jax.shard_map(
        per_device,
        mesh=mesh,
        in_specs=(
            P("role", "group", "tp", None, None, None),
            P(),
            P(),
            P("group", None),
            P("group", None, None),
            P("group", None, "tp"),
            P("group", None, "tp"),
            P("tp", "role"),
        ),
        out_specs=P("group", None, ("role", "tp")),
        check_vma=False,
    )
```

```python
import functools
import math

import jax
import jax.numpy as jnp
from jax import lax
from jax.experimental import pallas as pl
from jax.experimental.pallas import tpu as pltpu
from jax.sharding import PartitionSpec as P

KVH = 8
HD = 128
CAP = 4
CAPP = 2
PRE_DEV = 8
LANES = 128
PAGE = 128
NEG = -1e30
SCALE = 1.0 / math.sqrt(HD)
PARTS = CAP + CAPP
CHUNK = 8
STATS = 16
MIB = 2**20


def dot(a, b, ca, cb):
    return lax.dot_general(a, b, (((ca,), (cb,)), ((), ())), preferred_element_type=jnp.float32)


def query_block(qa, held, per_held):
    q = qa[:, : held * per_held * HD].astype(jnp.float32)
    rows = q.shape[0]
    bands = []
    for j in range(held):
        heads = [q[:, (j * per_held + i) * HD : (j * per_held + i + 1) * HD] for i in range(per_held)]
        band = jnp.concatenate(heads, 0)
        blank = jnp.zeros_like(band)
        bands.append(jnp.concatenate([band if i == j else blank for i in range(held)], 1))
    return jnp.concatenate(bands, 0).astype(jnp.bfloat16)


def entry_rows(qa, held, per_held, maxp):
    rows = qa.shape[0]
    wide = held * per_held * HD
    aux = qa[:, wide : wide + LANES].astype(jnp.float32)
    lane = lax.broadcasted_iota(jnp.int32, (rows, LANES), 1) - maxp
    row = lax.broadcasted_iota(jnp.int32, (rows, LANES), 0)
    parts = jnp.where(lane == row, 8.0 * aux[:1], jnp.where(lane == row + rows, aux[:1], 0.0))
    length = jnp.sum(parts, 1, keepdims=True)
    turned = jnp.concatenate([jnp.where(lane == 0, length, aux)] * (held * per_held), 0).T
    first = lax.broadcasted_iota(jnp.int32, (maxp, 1), 0).astype(jnp.float32) * PAGE
    return turned[:maxp], jnp.clip(turned[maxp : maxp + 1] - first, 0.0, PAGE)


def lanes_of(page, first, held):
    return jnp.concatenate([page[:, (2 * j + first) * HD : (2 * j + first + 1) * HD] for j in range(held)], 1)


def pieces(x):
    high = x.astype(jnp.bfloat16).astype(jnp.float32)
    middle = (x - high).astype(jnp.bfloat16).astype(jnp.float32)
    return [high, middle, x - high - middle]


def write_part(out, acc, top, total, held, per_held):
    count = acc.shape[0]
    band = count // held
    out[:count, :] = jnp.concatenate(
        [acc[j * band : (j + 1) * band, j * HD : (j + 1) * HD] for j in range(held)], 0
    ).astype(out.dtype)
    rows = pieces(top) + pieces(total)
    block = jnp.concatenate(rows + [jnp.zeros((STATS - len(rows), count), jnp.float32)], 0)
    if count < LANES:
        block = jnp.concatenate([block, jnp.zeros((STATS, LANES - count), jnp.float32)], 1)
    out[count:, :] = block.astype(out.dtype)


def owner_part(qa, pages, entries, out, held, per_held, maxp):
    q = query_block(qa, held, per_held)
    tab, cnt = entry_rows(qa, held, per_held, maxp)
    count = q.shape[0]
    token = lax.broadcasted_iota(jnp.int32, (PAGE, count), 0).astype(jnp.float32)
    masks = []
    for c in range(PARTS):
        valid = jnp.sum(jnp.where(tab == entries[c : c + 1, :count], cnt, 0.0), 0, keepdims=True)
        masks.append(token < valid)
    mask = jnp.concatenate(masks, 0)
    keys = jnp.concatenate([lanes_of(pages.at[c], 0, held) for c in range(PARTS)], 0)
    values = jnp.concatenate([lanes_of(pages.at[c], 1, held) for c in range(PARTS)], 0)
    s = jnp.where(mask, dot(keys, q, 1, 1) * SCALE, NEG)
    top = jnp.max(s, 0, keepdims=True)
    p = jnp.where(mask, jnp.exp(s - top), 0.0)
    total = jnp.sum(p, 0, keepdims=True)
    acc = dot(p.astype(jnp.bfloat16), values, 0, 0)
    write_part(out, acc, top, total, held, per_held)


def resident_part(
    span, qa, fresh_at, lists_ready, send, tables, lengths, maxp, group, kv, pages, flags, listed, sems, out, held, per_held
):
    rows = qa.shape[0]
    slots = kv.shape[0]
    q = query_block(qa, held, per_held)
    count = q.shape[0]
    lane_row = lax.rem(lax.broadcasted_iota(jnp.int32, (1, count), 1), rows)
    token = lax.broadcasted_iota(jnp.int32, (PAGE, count), 0)
    fresh = qa[:, fresh_at : fresh_at + 2 * held * HD].astype(jnp.float32)
    fresh = jnp.concatenate([fresh, jnp.zeros_like(fresh)], 0).astype(jnp.bfloat16)
    own_mask = lax.broadcasted_iota(jnp.int32, (2 * rows, count), 0) == lane_row
    own = jnp.where(own_mask, dot(lanes_of(fresh, 0, held), q, 1, 1) * SCALE, NEG)
    own_top = jnp.max(own, 0, keepdims=True)
    here = jnp.logical_and(lane_row >= span[0], lane_row < span[1])
    lift = jnp.where(here, jnp.exp(own - own_top), 0.0)
    own_total = jnp.sum(lift, 0, keepdims=True)
    own_acc = dot(lift.astype(jnp.bfloat16), lanes_of(fresh, 1, held), 0, 0)
    for i in range(slots):
        flags[i] = 0

    lists_ready()
    for o in range(send.shape[1]):
        for i in range(send.shape[2]):
            flags[jnp.where(send[1, o, i] == group, send[2, o, i], slots)] = 1

    def page_copy(slot, i):
        return pltpu.make_async_copy(kv.at[slot], pages.at[i], sems.at[i])

    listed_count = jnp.int32(0)
    for r in range(*span):
        length = lengths[0, r]
        for e in range(maxp):
            slot = tables[r, e]
            tokens = jnp.minimum(length - e * PAGE, PAGE)
            here = jnp.logical_and(slot < slots, flags[jnp.minimum(slot, slots - 1)] == 0)
            needed = jnp.logical_and(tokens > 0, here)
            listed[0, listed_count] = r
            listed[1, listed_count] = tokens

            @pl.when(needed)
            def _(slot=slot, at=listed_count):
                page_copy(slot, at).start()

            listed_count = listed_count + needed.astype(jnp.int32)
    chunks = (listed_count + CHUNK - 1) // CHUNK

    def fill(i, _):
        listed[0, i] = 0
        listed[1, i] = 0
        page_copy(0, i).start()
        return 0

    lax.fori_loop(listed_count, chunks * CHUNK, fill, 0)

    def step(c, carry):
        top, total, acc = carry
        first = c * CHUNK
        masks = []
        for i in range(CHUNK):
            masks.append(token < jnp.where(lane_row == listed[0, first + i], listed[1, first + i], 0))
        for i in range(CHUNK):
            page_copy(0, first + i).wait()
        keys = jnp.concatenate([lanes_of(pages.at[first + i], 0, held) for i in range(CHUNK)], 0)
        values = jnp.concatenate([lanes_of(pages.at[first + i], 1, held) for i in range(CHUNK)], 0)
        s = jnp.where(jnp.concatenate(masks, 0), dot(keys, q, 1, 1) * SCALE, NEG)
        new_top = jnp.maximum(top, jnp.max(s, 0, keepdims=True))
        p = jnp.exp(s - new_top)
        fade = jnp.exp(top - new_top)
        total = total * fade + jnp.sum(p, 0, keepdims=True)
        acc = acc * jnp.broadcast_to(fade, (8, count)).T[:, :1] + dot(p.astype(jnp.bfloat16), values, 0, 0)
        return new_top, total, acc

    top, total, acc = lax.fori_loop(0, chunks, step, (own_top, own_total, own_acc))
    write_part(out, acc, top, total, held, per_held)


def list_pages(send, wanted, owner, target, slots, page_list, slot_list, base):
    for c in range(PARTS):
        page_list[base + c] = 0
        slot_list[base + c] = -1
    at = jnp.int32(base)
    for i in range(send.shape[2]):
        hit = send[1, owner, i] == target
        page_list[at] = send[0, owner, i]
        slot_list[at] = jnp.where(hit, send[2, owner, i], -1)
        at = at + hit.astype(jnp.int32)
    at = jnp.int32(base + CAP)
    page_list[at] = 0
    slot_list[at] = -1
    for i in range(wanted.shape[1]):
        page = wanted[target, i] - owner * PRE_DEV
        hit = jnp.logical_and(page >= 0, page < PRE_DEV)
        page_list[at] = jnp.where(hit, page, 0)
        slot_list[at] = jnp.where(hit, slots + i, -1)
        at = at + hit.astype(jnp.int32)


def copy_lists(pairs, sems):
    copies = [pltpu.make_async_copy(a, b, sems.at[i]) for i, (a, b) in enumerate(pairs)]
    for copy in copies:
        copy.start()

    def ready():
        for copy in copies:
            copy.wait()

    return ready


def first_kernel(span, held, per_held, groups, maxp, qa, send_hbm, wanted_hbm, tables_hbm, lengths_hbm, kv, *refs):
    out, sent, chosen, entries, pages, send, wanted, tables, lengths = refs[:9]
    flags, listed, page_list, slot_list, list_sems, chosen_sems, sems = refs[9:]
    group = lax.axis_index("group")
    prefill = lax.axis_index("role") == 0
    fresh_at = held * per_held * HD + LANES
    lists = ((send_hbm, send), (wanted_hbm, wanted), (tables_hbm, tables), (lengths_hbm, lengths))
    lists_ready = copy_lists(lists, list_sems)

    @pl.when(prefill)
    def _():
        lists_ready()
        copies = []
        for k in range(groups):
            target = lax.rem(group - k + groups, groups)
            list_pages(send, wanted, group, target, kv.shape[0], page_list, slot_list, k * PARTS)
            for c in range(PARTS):
                at = k * PARTS + c
                copy = pltpu.make_async_copy(kv.at[page_list[at]], chosen.at[at], chosen_sems.at[at])
                copy.start()
                copies.append(copy)
                entry = slot_list[at].astype(jnp.float32)
                entries[at : at + 1, :] = jnp.full((1, LANES), entry, jnp.float32)
        for copy in copies[:PARTS]:
            copy.wait()
        owner_part(qa, chosen.at[pl.ds(0, PARTS)], entries[:PARTS, :], sent, held, per_held, maxp)
        for copy in copies[PARTS:]:
            copy.wait()

    @pl.when(jnp.logical_not(prefill))
    def _():
        resident_part(
            span, qa, fresh_at, lists_ready, send, tables, lengths, maxp, group, kv, pages, flags, listed, sems, out, held, per_held
        )


def third_kernel(span, held, per_held, maxp, qa, send_hbm, tables_hbm, lengths_hbm, kv, *refs):
    out, pages, send, tables, lengths, flags, listed, list_sems, sems = refs
    group = lax.axis_index("group")
    fresh_at = held * per_held * HD + LANES

    @pl.when(lax.axis_index("role") == 1)
    def _():
        lists_ready = copy_lists(((send_hbm, send), (tables_hbm, tables), (lengths_hbm, lengths)), list_sems)
        resident_part(
            span, qa, fresh_at, lists_ready, send, tables, lengths, maxp, group, kv, pages, flags, listed, sems, out, held, per_held
        )


def second_kernel(held, per_held, maxp, count, chosen, entries, *refs):
    qas, outs = refs[:count][::-1], refs[count:]

    @pl.when(lax.axis_index("role") == 0)
    def _():
        for k in range(count):
            at = (k + 1) * PARTS
            owner_part(
                qas[k], chosen.at[pl.ds(at, PARTS)], entries[at : at + PARTS, :], outs[k], held, per_held, maxp
            )


def merge_kernel(heads, rows, *refs):
    parts, out = refs[:-1], refs[-1]
    count = heads * rows
    pad = -len(parts) % 8
    stats = [part[count:, :].astype(jnp.float32)[:, :count] for part in parts]
    tops = jnp.concatenate([s[0:1] + (s[1:2] + s[2:3]) for s in stats], 0)
    totals = jnp.concatenate([s[3:4] + (s[4:5] + s[5:6]) for s in stats], 0)
    factors = jnp.exp(tops - jnp.max(tops, 0, keepdims=True))
    factors = factors / jnp.sum(factors * totals, 0, keepdims=True)
    factors = jnp.concatenate([factors, jnp.zeros((pad, count), jnp.float32)], 0).T
    terms = [factors[:, i : i + 1] * part[:count, :].astype(jnp.float32) for i, part in enumerate(parts)]
    merged = functools.reduce(jnp.add, terms)
    out[...] = jnp.concatenate([merged[h * rows : (h + 1) * rows] for h in range(heads)], 1).astype(out.dtype)


def project_kernel(steps, attended, partner, weight, *outs):
    tps = lax.axis_size("tp")
    share = outs[0].shape[1]
    here = jnp.where(lax.axis_index("role") == 0, partner[...].astype(jnp.float32), attended[...].astype(jnp.float32))
    here = here.astype(jnp.bfloat16)
    for d, out in zip(steps, outs):
        first = lax.rem(lax.axis_index("tp") + d, tps) * share
        columns = pl.ds(pl.multiple_of(first, LANES), share)
        out[...] = jnp.dot(here, weight[:, columns], preferred_element_type=jnp.float32)


def per_device(kv_pages, send_list, wanted, lengths, tables, queries, new_kv, out_weight):
    stored = kv_pages[0, 0, 0]
    slots = stored.shape[0]
    groups, tps = lax.axis_size("group"), lax.axis_size("tp")
    held = max(1, KVH // tps)
    rows, wide = queries.shape[1], queries.shape[2]
    heads = wide // HD
    per_held = heads // held
    maxp = tables.shape[2]
    send = jnp.transpose(send_list, (2, 0, 1))
    fresh_at = wide + LANES
    width = fresh_at + new_kv.shape[2]

    def place(block, at):
        return jnp.pad(block, ((0, rows - block.shape[0]), (at, width - at - block.shape[1])))

    high = lax.shift_right_logical(place(lengths, wide + maxp), 3)
    low = jnp.bitwise_and(place(lengths, wide + maxp + rows), 7)
    integers = place(tables[0], wide) + high + low
    qa = place(queries[0], 0) + place(new_kv[0], fresh_at) + integers.astype(jnp.bfloat16)
    asked = []
    for k in range(1, groups):
        pairs = [pair for i in range(groups) for pair in ((groups + i, (i + k) % groups), (i, groups + i))]
        asked.append(lax.ppermute(qa, ("role", "group"), pairs))
    part_shape = jax.ShapeDtypeStruct((heads * rows + STATS, HD), jnp.float32)
    sent_shape = jax.ShapeDtypeStruct(part_shape.shape, jnp.bfloat16)
    vmem = pl.BlockSpec(memory_space=pltpu.VMEM)
    hbm = pl.BlockSpec(memory_space=pltpu.HBM)
    page_shape = stored.shape[1:]
    chosen_count = groups * PARTS
    half = (rows + 1) // 2
    read_count = -(-half * maxp // CHUNK) * CHUNK
    lists = [send, wanted, tables[0], lengths]
    pinned = [pltpu.with_memory_space_constraint(x, pltpu.HBM) for x in lists + [stored]]
    smem = [pltpu.SMEM(x.shape, jnp.int32) for x in lists]
    reading = [pltpu.SMEM((slots + 1,), jnp.int32), pltpu.SMEM((2, read_count), jnp.int32)]
    mine, mine_sent, chosen, entries = pl.pallas_call(
        functools.partial(first_kernel, (0, half), held, per_held, groups, maxp),
        out_shape=[
            part_shape,
            sent_shape,
            jax.ShapeDtypeStruct((chosen_count,) + page_shape, jnp.bfloat16),
            jax.ShapeDtypeStruct((chosen_count, LANES), jnp.float32),
        ],
        in_specs=[vmem] + [hbm] * 5,
        out_specs=[vmem] * 4,
        scratch_shapes=[
            pltpu.VMEM((read_count,) + page_shape, jnp.bfloat16),
            *smem,
            *reading,
            pltpu.SMEM((chosen_count + 1,), jnp.int32),
            pltpu.SMEM((chosen_count + 1,), jnp.int32),
            pltpu.SemaphoreType.DMA((len(lists),)),
            pltpu.SemaphoreType.DMA((chosen_count,)),
            pltpu.SemaphoreType.DMA((read_count,)),
        ],
        compiler_params=pltpu.CompilerParams(vmem_limit_bytes=20 * MIB),
        name="resident",
    )(qa, *pinned)
    count = groups - 1
    theirs = pl.pallas_call(
        functools.partial(second_kernel, held, per_held, maxp, count),
        out_shape=[sent_shape] * count,
        in_specs=[vmem] * (2 + count),
        out_specs=[vmem] * count,
        compiler_params=pltpu.CompilerParams(vmem_limit_bytes=16 * MIB),
        cost_estimate=pl.CostEstimate(flops=4 * 10**10, bytes_accessed=8 * MIB, transcendentals=10**6),
        name="owned",
    )(chosen, entries, *reversed(asked))
    qa, mine_sent, theirs = lax.optimization_barrier((qa, mine_sent, theirs))
    rest = pl.pallas_call(
        functools.partial(third_kernel, (half, rows), held, per_held, maxp),
        out_shape=part_shape,
        in_specs=[vmem] + [hbm] * 4,
        out_specs=vmem,
        scratch_shapes=[
            pltpu.VMEM((read_count,) + page_shape, jnp.bfloat16),
            smem[0],
            smem[2],
            smem[3],
            *reading,
            pltpu.SemaphoreType.DMA((3,)),
            pltpu.SemaphoreType.DMA((read_count,)),
        ],
        compiler_params=pltpu.CompilerParams(vmem_limit_bytes=20 * MIB),
        cost_estimate=pl.CostEstimate(flops=4 * 10**9, bytes_accessed=8 * MIB, transcendentals=10**6),
        name="resident_rest",
    )(qa, pinned[0], *pinned[2:])
    parts = [mine, rest, lax.ppermute(mine_sent, "role", [(0, 1), (1, 0)])]
    for k in range(1, groups):
        pairs = [pair for i in range(groups) for pair in ((i, groups + (i - k) % groups), (groups + i, i))]
        parts.append(lax.ppermute(theirs[k - 1], ("role", "group"), pairs))
    attended = pl.pallas_call(
        functools.partial(merge_kernel, heads, rows),
        out_shape=jax.ShapeDtypeStruct((rows, wide), jnp.bfloat16),
        in_specs=[vmem] * len(parts),
        out_specs=vmem,
        compiler_params=pltpu.CompilerParams(vmem_limit_bytes=8 * MIB),
        name="merge",
    )(*parts)
    partner = lax.ppermute(attended, "role", [(0, 1), (1, 0)])
    share = out_weight.shape[1] // tps

    def project(steps, name):
        return pl.pallas_call(
            functools.partial(project_kernel, steps),
            out_shape=[jax.ShapeDtypeStruct((rows, share), jnp.float32)] * len(steps),
            in_specs=[vmem] * 3,
            out_specs=[vmem] * len(steps),
            compiler_params=pltpu.CompilerParams(vmem_limit_bytes=24 * MIB),
            cost_estimate=pl.CostEstimate(
                flops=len(steps) * 32 * wide * share, bytes_accessed=len(steps) * 2 * wide * share, transcendentals=0
            ),
            name=name,
        )(attended, partner, out_weight)

    steps = list(range(1, tps))
    sent = project(steps, "project")
    arrived = [lax.ppermute(part, "tp", [(i, (i + d) % tps) for i in range(tps)]) for d, part in zip(steps, sent)]
    total = functools.reduce(jnp.add, arrived, project([0], "project_own")[0])
    return total.astype(jnp.bfloat16)[None]


def solution(mesh):
    return jax.shard_map(
        per_device,
        mesh=mesh,
        in_specs=(
            P("role", "group", "tp", None, None, None),
            P(),
            P(),
            P("group", None),
            P("group", None, None),
            P("group", None, "tp"),
            P("group", None, "tp"),
            P("tp", "role"),
        ),
        out_specs=P("group", None, ("role", "tp")),
        check_vma=False,
    )
```

```python
import functools
import math

import jax
import jax.numpy as jnp
from jax import lax
from jax.experimental import pallas as pl
from jax.experimental.pallas import tpu as pltpu
from jax.sharding import PartitionSpec as P

KVH = 8
HD = 128
CAP = 4
CAPP = 2
PRE_DEV = 8
LANES = 128
PAGE = 128
NEG = -1e30
SCALE = 1.0 / math.sqrt(HD)
PARTS = CAP + CAPP
CHUNK = 8
STATS = 16
MIB = 2**20


def dot(a, b, ca, cb):
    return lax.dot_general(a, b, (((ca,), (cb,)), ((), ())), preferred_element_type=jnp.float32)


def query_block(qa, held, per_held):
    q = qa[:, : held * per_held * HD].astype(jnp.float32)
    rows = q.shape[0]
    bands = []
    for j in range(held):
        heads = [q[:, (j * per_held + i) * HD : (j * per_held + i + 1) * HD] for i in range(per_held)]
        band = jnp.concatenate(heads, 0)
        blank = jnp.zeros_like(band)
        bands.append(jnp.concatenate([band if i == j else blank for i in range(held)], 1))
    return jnp.concatenate(bands, 0).astype(jnp.bfloat16)


def entry_rows(qa, held, per_held, maxp):
    rows = qa.shape[0]
    wide = held * per_held * HD
    aux = qa[:, wide : wide + LANES].astype(jnp.float32)
    lane = lax.broadcasted_iota(jnp.int32, (rows, LANES), 1) - maxp
    row = lax.broadcasted_iota(jnp.int32, (rows, LANES), 0)
    parts = jnp.where(lane == row, 8.0 * aux[:1], jnp.where(lane == row + rows, aux[:1], 0.0))
    length = jnp.sum(parts, 1, keepdims=True)
    turned = jnp.concatenate([jnp.where(lane == 0, length, aux)] * (held * per_held), 0).T
    first = lax.broadcasted_iota(jnp.int32, (maxp, 1), 0).astype(jnp.float32) * PAGE
    return turned[:maxp], jnp.clip(turned[maxp : maxp + 1] - first, 0.0, PAGE)


def lanes_of(page, first, held):
    return jnp.concatenate([page[:, (2 * j + first) * HD : (2 * j + first + 1) * HD] for j in range(held)], 1)


def pieces(x):
    high = x.astype(jnp.bfloat16).astype(jnp.float32)
    middle = (x - high).astype(jnp.bfloat16).astype(jnp.float32)
    return [high, middle, x - high - middle]


def write_part(out, acc, top, total, held, per_held):
    count = acc.shape[0]
    band = count // held
    out[:count, :] = jnp.concatenate(
        [acc[j * band : (j + 1) * band, j * HD : (j + 1) * HD] for j in range(held)], 0
    ).astype(out.dtype)
    rows = pieces(top) + pieces(total)
    block = jnp.concatenate(rows + [jnp.zeros((STATS - len(rows), count), jnp.float32)], 0)
    if count < LANES:
        block = jnp.concatenate([block, jnp.zeros((STATS, LANES - count), jnp.float32)], 1)
    out[count:, :] = block.astype(out.dtype)


def owner_part(qa, pages, entries, out, held, per_held, maxp):
    q = query_block(qa, held, per_held)
    tab, cnt = entry_rows(qa, held, per_held, maxp)
    count = q.shape[0]
    token = lax.broadcasted_iota(jnp.int32, (PAGE, count), 0).astype(jnp.float32)
    masks = []
    for c in range(PARTS):
        valid = jnp.sum(jnp.where(tab == entries[c : c + 1, :count], cnt, 0.0), 0, keepdims=True)
        masks.append(token < valid)
    mask = jnp.concatenate(masks, 0)
    keys = jnp.concatenate([lanes_of(pages.at[c], 0, held) for c in range(PARTS)], 0)
    values = jnp.concatenate([lanes_of(pages.at[c], 1, held) for c in range(PARTS)], 0)
    s = jnp.where(mask, dot(keys, q, 1, 1) * SCALE, NEG)
    top = jnp.max(s, 0, keepdims=True)
    p = jnp.where(mask, jnp.exp(s - top), 0.0)
    total = jnp.sum(p, 0, keepdims=True)
    acc = dot(p.astype(jnp.bfloat16), values, 0, 0)
    write_part(out, acc, top, total, held, per_held)


def resident_part(
    span, qa, fresh_at, lists_ready, send, tables, lengths, maxp, group, kv, pages, flags, listed, sems, out, held, per_held
):
    rows = qa.shape[0]
    slots = kv.shape[0]
    q = query_block(qa, held, per_held)
    count = q.shape[0]
    lane_row = lax.rem(lax.broadcasted_iota(jnp.int32, (1, count), 1), rows)
    token = lax.broadcasted_iota(jnp.int32, (PAGE, count), 0)
    fresh = qa[:, fresh_at : fresh_at + 2 * held * HD].astype(jnp.float32)
    fresh = jnp.concatenate([fresh, jnp.zeros_like(fresh)], 0).astype(jnp.bfloat16)
    own_mask = lax.broadcasted_iota(jnp.int32, (2 * rows, count), 0) == lane_row
    own = jnp.where(own_mask, dot(lanes_of(fresh, 0, held), q, 1, 1) * SCALE, NEG)
    own_top = jnp.max(own, 0, keepdims=True)
    here = jnp.logical_and(lane_row >= span[0], lane_row < span[1])
    lift = jnp.where(here, jnp.exp(own - own_top), 0.0)
    own_total = jnp.sum(lift, 0, keepdims=True)
    own_acc = dot(lift.astype(jnp.bfloat16), lanes_of(fresh, 1, held), 0, 0)
    for i in range(slots):
        flags[i] = 0

    lists_ready()
    for o in range(send.shape[1]):
        for i in range(send.shape[2]):
            flags[jnp.where(send[1, o, i] == group, send[2, o, i], slots)] = 1

    def page_copy(slot, i):
        return pltpu.make_async_copy(kv.at[slot], pages.at[i], sems.at[i])

    listed_count = jnp.int32(0)
    for r in range(*span):
        length = lengths[0, r]
        for e in range(maxp):
            slot = tables[r, e]
            tokens = jnp.minimum(length - e * PAGE, PAGE)
            here = jnp.logical_and(slot < slots, flags[jnp.minimum(slot, slots - 1)] == 0)
            needed = jnp.logical_and(tokens > 0, here)
            listed[0, listed_count] = r
            listed[1, listed_count] = tokens

            @pl.when(needed)
            def _(slot=slot, at=listed_count):
                page_copy(slot, at).start()

            listed_count = listed_count + needed.astype(jnp.int32)
    chunks = (listed_count + CHUNK - 1) // CHUNK

    def fill(i, _):
        listed[0, i] = 0
        listed[1, i] = 0
        page_copy(0, i).start()
        return 0

    lax.fori_loop(listed_count, chunks * CHUNK, fill, 0)

    def step(c, carry):
        top, total, acc = carry
        first = c * CHUNK
        masks = []
        for i in range(CHUNK):
            masks.append(token < jnp.where(lane_row == listed[0, first + i], listed[1, first + i], 0))
        for i in range(CHUNK):
            page_copy(0, first + i).wait()
        keys = jnp.concatenate([lanes_of(pages.at[first + i], 0, held) for i in range(CHUNK)], 0)
        values = jnp.concatenate([lanes_of(pages.at[first + i], 1, held) for i in range(CHUNK)], 0)
        s = jnp.where(jnp.concatenate(masks, 0), dot(keys, q, 1, 1) * SCALE, NEG)
        new_top = jnp.maximum(top, jnp.max(s, 0, keepdims=True))
        p = jnp.exp(s - new_top)
        fade = jnp.exp(top - new_top)
        total = total * fade + jnp.sum(p, 0, keepdims=True)
        acc = acc * jnp.broadcast_to(fade, (8, count)).T[:, :1] + dot(p.astype(jnp.bfloat16), values, 0, 0)
        return new_top, total, acc

    top, total, acc = lax.fori_loop(0, chunks, step, (own_top, own_total, own_acc))
    write_part(out, acc, top, total, held, per_held)


def list_pages(send, wanted, owner, target, slots, page_list, slot_list, base):
    for c in range(PARTS):
        page_list[base + c] = 0
        slot_list[base + c] = -1
    at = jnp.int32(base)
    for i in range(send.shape[2]):
        hit = send[1, owner, i] == target
        page_list[at] = send[0, owner, i]
        slot_list[at] = jnp.where(hit, send[2, owner, i], -1)
        at = at + hit.astype(jnp.int32)
    at = jnp.int32(base + CAP)
    page_list[at] = 0
    slot_list[at] = -1
    for i in range(wanted.shape[1]):
        page = wanted[target, i] - owner * PRE_DEV
        hit = jnp.logical_and(page >= 0, page < PRE_DEV)
        page_list[at] = jnp.where(hit, page, 0)
        slot_list[at] = jnp.where(hit, slots + i, -1)
        at = at + hit.astype(jnp.int32)


def copy_lists(pairs, sems):
    copies = [pltpu.make_async_copy(a, b, sems.at[i]) for i, (a, b) in enumerate(pairs)]
    for copy in copies:
        copy.start()

    def ready():
        for copy in copies:
            copy.wait()

    return ready


def first_kernel(span, held, per_held, groups, maxp, qa, send_hbm, wanted_hbm, tables_hbm, lengths_hbm, kv, *refs):
    out, sent, chosen, entries, pages, send, wanted, tables, lengths = refs[:9]
    flags, listed, page_list, slot_list, list_sems, chosen_sems, sems = refs[9:]
    group = lax.axis_index("group")
    prefill = lax.axis_index("role") == 0
    fresh_at = held * per_held * HD + LANES
    lists = ((send_hbm, send), (wanted_hbm, wanted), (tables_hbm, tables), (lengths_hbm, lengths))
    lists_ready = copy_lists(lists, list_sems)

    @pl.when(prefill)
    def _():
        lists_ready()
        copies = []
        for k in range(groups):
            target = lax.rem(group - k + groups, groups)
            list_pages(send, wanted, group, target, kv.shape[0], page_list, slot_list, k * PARTS)
            for c in range(PARTS):
                at = k * PARTS + c
                copy = pltpu.make_async_copy(kv.at[page_list[at]], chosen.at[at], chosen_sems.at[at])
                copy.start()
                copies.append(copy)
                entry = slot_list[at].astype(jnp.float32)
                entries[at : at + 1, :] = jnp.full((1, LANES), entry, jnp.float32)
        for copy in copies[:PARTS]:
            copy.wait()
        owner_part(qa, chosen.at[pl.ds(0, PARTS)], entries[:PARTS, :], sent, held, per_held, maxp)
        for copy in copies[PARTS:]:
            copy.wait()

    @pl.when(jnp.logical_not(prefill))
    def _():
        resident_part(
            span, qa, fresh_at, lists_ready, send, tables, lengths, maxp, group, kv, pages, flags, listed, sems, out, held, per_held
        )


def third_kernel(span, held, per_held, maxp, qa, send_hbm, tables_hbm, lengths_hbm, kv, *refs):
    out, pages, send, tables, lengths, flags, listed, list_sems, sems = refs
    group = lax.axis_index("group")
    fresh_at = held * per_held * HD + LANES

    @pl.when(lax.axis_index("role") == 1)
    def _():
        lists_ready = copy_lists(((send_hbm, send), (tables_hbm, tables), (lengths_hbm, lengths)), list_sems)
        resident_part(
            span, qa, fresh_at, lists_ready, send, tables, lengths, maxp, group, kv, pages, flags, listed, sems, out, held, per_held
        )


def second_kernel(held, per_held, maxp, count, chosen, entries, *refs):
    qas, outs = refs[:count], refs[count:]

    @pl.when(lax.axis_index("role") == 0)
    def _():
        for k in range(count):
            at = (k + 1) * PARTS
            owner_part(
                qas[k], chosen.at[pl.ds(at, PARTS)], entries[at : at + PARTS, :], outs[k], held, per_held, maxp
            )


def merge_kernel(heads, rows, *refs):
    parts, out = refs[:-1], refs[-1]
    count = heads * rows
    pad = -len(parts) % 8
    stats = [part[count:, :].astype(jnp.float32)[:, :count] for part in parts]
    tops = jnp.concatenate([s[0:1] + (s[1:2] + s[2:3]) for s in stats], 0)
    totals = jnp.concatenate([s[3:4] + (s[4:5] + s[5:6]) for s in stats], 0)
    factors = jnp.exp(tops - jnp.max(tops, 0, keepdims=True))
    factors = factors / jnp.sum(factors * totals, 0, keepdims=True)
    factors = jnp.concatenate([factors, jnp.zeros((pad, count), jnp.float32)], 0).T
    terms = [factors[:, i : i + 1] * part[:count, :].astype(jnp.float32) for i, part in enumerate(parts)]
    merged = functools.reduce(jnp.add, terms)
    out[...] = jnp.concatenate([merged[h * rows : (h + 1) * rows] for h in range(heads)], 1).astype(out.dtype)


def project_kernel(steps, attended, partner, weight, *outs):
    tps = lax.axis_size("tp")
    share = outs[0].shape[1]
    here = jnp.where(lax.axis_index("role") == 0, partner[...].astype(jnp.float32), attended[...].astype(jnp.float32))
    here = here.astype(jnp.bfloat16)
    for d, out in zip(steps, outs):
        first = lax.rem(lax.axis_index("tp") + d, tps) * share
        columns = pl.ds(pl.multiple_of(first, LANES), share)
        out[...] = jnp.dot(here, weight[:, columns], preferred_element_type=jnp.float32)


def per_device(kv_pages, send_list, wanted, lengths, tables, queries, new_kv, out_weight):
    stored = kv_pages[0, 0, 0]
    slots = stored.shape[0]
    groups, tps = lax.axis_size("group"), lax.axis_size("tp")
    held = max(1, KVH // tps)
    rows, wide = queries.shape[1], queries.shape[2]
    heads = wide // HD
    per_held = heads // held
    maxp = tables.shape[2]
    send = jnp.transpose(send_list, (2, 0, 1))
    fresh_at = wide + LANES
    width = fresh_at + new_kv.shape[2]

    def place(block, at):
        return jnp.pad(block, ((0, rows - block.shape[0]), (at, width - at - block.shape[1])))

    high = lax.shift_right_logical(place(lengths, wide + maxp), 3)
    low = jnp.bitwise_and(place(lengths, wide + maxp + rows), 7)
    integers = place(tables[0], wide) + high + low
    qa = place(queries[0], 0) + place(new_kv[0], fresh_at) + integers.astype(jnp.bfloat16)
    asked = []
    for k in range(1, groups):
        pairs = [pair for i in range(groups) for pair in ((groups + i, (i + k) % groups), (i, groups + i))]
        asked.append(lax.ppermute(qa, ("role", "group"), pairs))
    part_shape = jax.ShapeDtypeStruct((heads * rows + STATS, HD), jnp.float32)
    sent_shape = jax.ShapeDtypeStruct(part_shape.shape, jnp.bfloat16)
    vmem = pl.BlockSpec(memory_space=pltpu.VMEM)
    hbm = pl.BlockSpec(memory_space=pltpu.HBM)
    page_shape = stored.shape[1:]
    chosen_count = groups * PARTS
    cut = rows - rows // 4
    read_count = -(-cut * maxp // CHUNK) * CHUNK
    lists = [send, wanted, tables[0], lengths]
    pinned = [pltpu.with_memory_space_constraint(x, pltpu.HBM) for x in lists + [stored]]
    smem = [pltpu.SMEM(x.shape, jnp.int32) for x in lists]
    reading = [pltpu.SMEM((slots + 1,), jnp.int32), pltpu.SMEM((2, read_count), jnp.int32)]
    mine, mine_sent, chosen, entries = pl.pallas_call(
        functools.partial(first_kernel, (0, cut), held, per_held, groups, maxp),
        out_shape=[
            part_shape,
            sent_shape,
            jax.ShapeDtypeStruct((chosen_count,) + page_shape, jnp.bfloat16),
            jax.ShapeDtypeStruct((chosen_count, LANES), jnp.float32),
        ],
        in_specs=[vmem] + [hbm] * 5,
        out_specs=[vmem] * 4,
        scratch_shapes=[
            pltpu.VMEM((read_count,) + page_shape, jnp.bfloat16),
            *smem,
            *reading,
            pltpu.SMEM((chosen_count + 1,), jnp.int32),
            pltpu.SMEM((chosen_count + 1,), jnp.int32),
            pltpu.SemaphoreType.DMA((len(lists),)),
            pltpu.SemaphoreType.DMA((chosen_count,)),
            pltpu.SemaphoreType.DMA((read_count,)),
        ],
        compiler_params=pltpu.CompilerParams(vmem_limit_bytes=20 * MIB),
        name="resident",
    )(qa, *pinned)
    count = groups - 1
    theirs = pl.pallas_call(
        functools.partial(second_kernel, held, per_held, maxp, count),
        out_shape=[sent_shape] * count,
        in_specs=[vmem] * (2 + count),
        out_specs=[vmem] * count,
        compiler_params=pltpu.CompilerParams(vmem_limit_bytes=16 * MIB),
        cost_estimate=pl.CostEstimate(flops=4 * 10**10, bytes_accessed=8 * MIB, transcendentals=10**6),
        name="owned",
    )(chosen, entries, *asked)
    qa, mine_sent, theirs = lax.optimization_barrier((qa, mine_sent, theirs))
    rest = pl.pallas_call(
        functools.partial(third_kernel, (cut, rows), held, per_held, maxp),
        out_shape=part_shape,
        in_specs=[vmem] + [hbm] * 4,
        out_specs=vmem,
        scratch_shapes=[
            pltpu.VMEM((read_count,) + page_shape, jnp.bfloat16),
            smem[0],
            smem[2],
            smem[3],
            *reading,
            pltpu.SemaphoreType.DMA((3,)),
            pltpu.SemaphoreType.DMA((read_count,)),
        ],
        compiler_params=pltpu.CompilerParams(vmem_limit_bytes=20 * MIB),
        cost_estimate=pl.CostEstimate(flops=4 * 10**9, bytes_accessed=8 * MIB, transcendentals=10**6),
        name="resident_rest",
    )(qa, pinned[0], *pinned[2:])
    parts = [mine, rest, lax.ppermute(mine_sent, "role", [(0, 1), (1, 0)])]
    for k in range(1, groups):
        pairs = [pair for i in range(groups) for pair in ((i, groups + (i - k) % groups), (groups + i, i))]
        parts.append(lax.ppermute(theirs[k - 1], ("role", "group"), pairs))
    attended = pl.pallas_call(
        functools.partial(merge_kernel, heads, rows),
        out_shape=jax.ShapeDtypeStruct((rows, wide), jnp.bfloat16),
        in_specs=[vmem] * len(parts),
        out_specs=vmem,
        compiler_params=pltpu.CompilerParams(vmem_limit_bytes=8 * MIB),
        name="merge",
    )(*parts)
    partner = lax.ppermute(attended, "role", [(0, 1), (1, 0)])
    share = out_weight.shape[1] // tps

    def project(steps, name):
        return pl.pallas_call(
            functools.partial(project_kernel, steps),
            out_shape=[jax.ShapeDtypeStruct((rows, share), jnp.float32)] * len(steps),
            in_specs=[vmem] * 3,
            out_specs=[vmem] * len(steps),
            compiler_params=pltpu.CompilerParams(vmem_limit_bytes=24 * MIB),
            cost_estimate=pl.CostEstimate(
                flops=len(steps) * 32 * wide * share, bytes_accessed=len(steps) * 2 * wide * share, transcendentals=0
            ),
            name=name,
        )(attended, partner, out_weight)

    steps = list(range(1, tps))
    sent = project(steps, "project")
    arrived = [lax.ppermute(part, "tp", [(i, (i + d) % tps) for i in range(tps)]) for d, part in zip(steps, sent)]
    total = functools.reduce(jnp.add, arrived[::-1], project([0], "project_own")[0])
    return total.astype(jnp.bfloat16)[None]


def solution(mesh):
    return jax.shard_map(
        per_device,
        mesh=mesh,
        in_specs=(
            P("role", "group", "tp", None, None, None),
            P(),
            P(),
            P("group", None),
            P("group", None, None),
            P("group", None, "tp"),
            P("group", None, "tp"),
            P("tp", "role"),
        ),
        out_specs=P("group", None, ("role", "tp")),
        check_vma=False,
    )
```

```python
import functools
import math

import jax
import jax.numpy as jnp
from jax import lax
from jax.experimental import pallas as pl
from jax.experimental.pallas import tpu as pltpu
from jax.sharding import PartitionSpec as P

KVH = 8
HD = 128
CAP = 4
CAPP = 2
PRE_DEV = 8
LANES = 128
PAGE = 128
NEG = -1e30
FLOOR = -1e29
SCALE = 1.0 / math.sqrt(HD)
PARTS = CAP + CAPP
CHUNK = 8
STATS = 16
MIB = 2**20


def dot(a, b, ca, cb):
    return lax.dot_general(a, b, (((ca,), (cb,)), ((), ())), preferred_element_type=jnp.float32)


def query_block(qa, held, per_held):
    q = qa[:, : held * per_held * HD].astype(jnp.float32)
    rows = q.shape[0]
    bands = []
    for j in range(held):
        heads = [q[:, (j * per_held + i) * HD : (j * per_held + i + 1) * HD] for i in range(per_held)]
        band = jnp.concatenate(heads, 0)
        blank = jnp.zeros_like(band)
        bands.append(jnp.concatenate([band if i == j else blank for i in range(held)], 1))
    return jnp.concatenate(bands, 0).astype(jnp.bfloat16)


def entry_rows(qa, held, per_held, maxp):
    rows = qa.shape[0]
    wide = held * per_held * HD
    aux = qa[:, wide : wide + LANES].astype(jnp.float32)
    lane = lax.broadcasted_iota(jnp.int32, (rows, LANES), 1) - maxp
    row = lax.broadcasted_iota(jnp.int32, (rows, LANES), 0)
    parts = jnp.where(lane == row, 8.0 * aux[:1], jnp.where(lane == row + rows, aux[:1], 0.0))
    length = jnp.sum(parts, 1, keepdims=True)
    turned = jnp.concatenate([jnp.where(lane == 0, length, aux)] * (held * per_held), 0).T
    first = lax.broadcasted_iota(jnp.int32, (maxp, 1), 0).astype(jnp.float32) * PAGE
    return turned[:maxp], jnp.clip(turned[maxp : maxp + 1] - first, 0.0, PAGE)


def lanes_of(page, first, held):
    return jnp.concatenate([page[:, (2 * j + first) * HD : (2 * j + first + 1) * HD] for j in range(held)], 1)


def pieces(x):
    high = x.astype(jnp.bfloat16).astype(jnp.float32)
    middle = (x - high).astype(jnp.bfloat16).astype(jnp.float32)
    return [high, middle, x - high - middle]


def write_part(out, acc, top, total, held, per_held):
    count = acc.shape[0]
    band = count // held
    out[:count, :] = jnp.concatenate(
        [acc[j * band : (j + 1) * band, j * HD : (j + 1) * HD] for j in range(held)], 0
    ).astype(out.dtype)
    rows = pieces(top) + pieces(total)
    block = jnp.concatenate(rows + [jnp.zeros((STATS - len(rows), count), jnp.float32)], 0)
    if count < LANES:
        block = jnp.concatenate([block, jnp.zeros((STATS, LANES - count), jnp.float32)], 1)
    out[count:, :] = block.astype(out.dtype)


def owner_part(qa, pages, entries, out, held, per_held, maxp):
    q = query_block(qa, held, per_held)
    tab, cnt = entry_rows(qa, held, per_held, maxp)
    count = q.shape[0]
    token = lax.broadcasted_iota(jnp.int32, (PAGE, count), 0).astype(jnp.float32)
    masks = []
    for c in range(PARTS):
        valid = jnp.sum(jnp.where(tab == entries[c : c + 1, :count], cnt, 0.0), 0, keepdims=True)
        masks.append(token < valid)
    mask = jnp.concatenate(masks, 0)
    keys = jnp.concatenate([lanes_of(pages.at[c], 0, held) for c in range(PARTS)], 0)
    values = jnp.concatenate([lanes_of(pages.at[c], 1, held) for c in range(PARTS)], 0)
    s = jnp.where(mask, dot(keys, q, 1, 1) * SCALE, NEG)
    top = jnp.max(s, 0, keepdims=True)
    p = jnp.where(mask, jnp.exp(s - top), 0.0)
    total = jnp.sum(p, 0, keepdims=True)
    acc = dot(p.astype(jnp.bfloat16), values, 0, 0)
    write_part(out, acc, top, total, held, per_held)


def resident_part(qa, lists_ready, send, tables, lengths, maxp, group, kv, pages, flags, listed, sems, out, held, per_held):
    rows = qa.shape[0]
    slots = kv.shape[0]
    q = query_block(qa, held, per_held)
    count = q.shape[0]
    lane_row = lax.rem(lax.broadcasted_iota(jnp.int32, (1, count), 1), rows)
    token = lax.broadcasted_iota(jnp.int32, (PAGE, count), 0)
    for i in range(slots):
        flags[i] = 0

    lists_ready()
    for o in range(send.shape[1]):
        for i in range(send.shape[2]):
            flags[jnp.where(send[1, o, i] == group, send[2, o, i], slots)] = 1

    def page_copy(slot, i):
        return pltpu.make_async_copy(kv.at[slot], pages.at[i], sems.at[i])

    listed_count = jnp.int32(0)
    for r in range(rows):
        length = lengths[0, r]
        for e in range(maxp):
            slot = tables[r, e]
            tokens = jnp.minimum(length - e * PAGE, PAGE)
            here = jnp.logical_and(slot < slots, flags[jnp.minimum(slot, slots - 1)] == 0)
            needed = jnp.logical_and(tokens > 0, here)
            listed[0, listed_count] = r
            listed[1, listed_count] = tokens

            @pl.when(needed)
            def _(slot=slot, at=listed_count):
                page_copy(slot, at).start()

            listed_count = listed_count + needed.astype(jnp.int32)
    chunks = (listed_count + CHUNK - 1) // CHUNK

    def fill(i, _):
        listed[0, i] = 0
        listed[1, i] = 0
        page_copy(0, i).start()
        return 0

    lax.fori_loop(listed_count, chunks * CHUNK, fill, 0)

    def step(c, carry):
        top, total, acc = carry
        first = c * CHUNK
        masks = []
        for i in range(CHUNK):
            masks.append(token < jnp.where(lane_row == listed[0, first + i], listed[1, first + i], 0))
        for i in range(CHUNK):
            page_copy(0, first + i).wait()
        keys = jnp.concatenate([lanes_of(pages.at[first + i], 0, held) for i in range(CHUNK)], 0)
        values = jnp.concatenate([lanes_of(pages.at[first + i], 1, held) for i in range(CHUNK)], 0)
        s = jnp.where(jnp.concatenate(masks, 0), dot(keys, q, 1, 1) * SCALE, NEG)
        new_top = jnp.maximum(top, jnp.max(s, 0, keepdims=True))
        p = jnp.exp(s - new_top)
        fade = jnp.exp(top - new_top)
        total = total * fade + jnp.sum(p, 0, keepdims=True)
        acc = acc * jnp.broadcast_to(fade, (8, count)).T[:, :1] + dot(p.astype(jnp.bfloat16), values, 0, 0)
        return new_top, total, acc

    start = (
        jnp.full((1, count), FLOOR, jnp.float32),
        jnp.zeros((1, count), jnp.float32),
        jnp.zeros((count, held * HD), jnp.float32),
    )
    top, total, acc = lax.fori_loop(0, chunks, step, start)
    write_part(out, acc, top, total, held, per_held)


def list_pages(send, wanted, owner, target, slots, page_list, slot_list, base):
    for c in range(PARTS):
        page_list[base + c] = 0
        slot_list[base + c] = -1
    at = jnp.int32(base)
    for i in range(send.shape[2]):
        hit = send[1, owner, i] == target
        page_list[at] = send[0, owner, i]
        slot_list[at] = jnp.where(hit, send[2, owner, i], -1)
        at = at + hit.astype(jnp.int32)
    at = jnp.int32(base + CAP)
    page_list[at] = 0
    slot_list[at] = -1
    for i in range(wanted.shape[1]):
        page = wanted[target, i] - owner * PRE_DEV
        hit = jnp.logical_and(page >= 0, page < PRE_DEV)
        page_list[at] = jnp.where(hit, page, 0)
        slot_list[at] = jnp.where(hit, slots + i, -1)
        at = at + hit.astype(jnp.int32)


def copy_lists(pairs, sems):
    copies = [pltpu.make_async_copy(a, b, sems.at[i]) for i, (a, b) in enumerate(pairs)]
    for copy in copies:
        copy.start()

    def ready():
        for copy in copies:
            copy.wait()

    return ready


def first_kernel(held, per_held, groups, maxp, qa, send_hbm, wanted_hbm, tables_hbm, lengths_hbm, kv, *refs):
    out, sent, chosen, entries, pages, send, wanted, tables, lengths = refs[:9]
    flags, listed, page_list, slot_list, list_sems, chosen_sems, sems = refs[9:]
    group = lax.axis_index("group")
    prefill = lax.axis_index("role") == 0
    lists = ((send_hbm, send), (wanted_hbm, wanted), (tables_hbm, tables), (lengths_hbm, lengths))
    lists_ready = copy_lists(lists, list_sems)

    @pl.when(prefill)
    def _():
        lists_ready()
        copies = []
        for k in range(groups):
            target = lax.rem(group - k + groups, groups)
            list_pages(send, wanted, group, target, kv.shape[0], page_list, slot_list, k * PARTS)
            for c in range(PARTS):
                at = k * PARTS + c
                copy = pltpu.make_async_copy(kv.at[page_list[at]], chosen.at[at], chosen_sems.at[at])
                copy.start()
                copies.append(copy)
                entry = slot_list[at].astype(jnp.float32)
                entries[at : at + 1, :] = jnp.full((1, LANES), entry, jnp.float32)
        for copy in copies[:PARTS]:
            copy.wait()
        owner_part(qa, chosen.at[pl.ds(0, PARTS)], entries[:PARTS, :], sent, held, per_held, maxp)
        for copy in copies[PARTS:]:
            copy.wait()

    @pl.when(jnp.logical_not(prefill))
    def _():
        resident_part(
            qa, lists_ready, send, tables, lengths, maxp, group, kv, pages, flags, listed, sems, out, held, per_held
        )


def fresh_kernel(held, per_held, qa, new_kv, out):
    rows = qa.shape[0]
    q = query_block(qa, held, per_held)
    count = q.shape[0]
    lane_row = lax.rem(lax.broadcasted_iota(jnp.int32, (1, count), 1), rows)
    fresh = new_kv[...].astype(jnp.float32)
    fresh = jnp.concatenate([fresh, jnp.zeros_like(fresh)], 0).astype(jnp.bfloat16)
    mask = lax.broadcasted_iota(jnp.int32, (2 * rows, count), 0) == lane_row
    s = jnp.where(mask, dot(lanes_of(fresh, 0, held), q, 1, 1) * SCALE, NEG)
    top = jnp.max(s, 0, keepdims=True)
    p = jnp.exp(s - top)
    acc = dot(p.astype(jnp.bfloat16), lanes_of(fresh, 1, held), 0, 0)
    write_part(out, acc, top, jnp.sum(p, 0, keepdims=True), held, per_held)


def second_kernel(held, per_held, maxp, count, chosen, entries, *refs):
    qas, outs = refs[:count][::-1], refs[count:]

    @pl.when(lax.axis_index("role") == 0)
    def _():
        for k in range(count):
            at = (k + 1) * PARTS
            owner_part(
                qas[k], chosen.at[pl.ds(at, PARTS)], entries[at : at + PARTS, :], outs[k], held, per_held, maxp
            )


def merge_kernel(heads, rows, *refs):
    parts, out = refs[:-1], refs[-1]
    count = heads * rows
    pad = -len(parts) % 8
    stats = [part[count:, :].astype(jnp.float32)[:, :count] for part in parts]
    tops = jnp.concatenate([s[0:1] + (s[1:2] + s[2:3]) for s in stats], 0)
    totals = jnp.concatenate([s[3:4] + (s[4:5] + s[5:6]) for s in stats], 0)
    factors = jnp.exp(tops - jnp.max(tops, 0, keepdims=True))
    factors = factors / jnp.sum(factors * totals, 0, keepdims=True)
    factors = jnp.concatenate([factors, jnp.zeros((pad, count), jnp.float32)], 0).T
    terms = [factors[:, i : i + 1] * part[:count, :].astype(jnp.float32) for i, part in enumerate(parts)]
    merged = functools.reduce(jnp.add, terms)
    out[...] = jnp.concatenate([merged[h * rows : (h + 1) * rows] for h in range(heads)], 1).astype(out.dtype)


def project_kernel(share, first_step, attended, partner, weight, out):
    tps = lax.axis_size("tp")
    here = jnp.where(lax.axis_index("role") == 0, partner[...].astype(jnp.float32), attended[...].astype(jnp.float32))
    here = here.astype(jnp.bfloat16)
    for i in range(out.shape[1] // share):
        first = lax.bitwise_xor(lax.axis_index("tp"), tps - 1 - first_step - i) * share
        columns = pl.ds(pl.multiple_of(first, LANES), share)
        out[:, i * share : (i + 1) * share] = jnp.dot(here, weight[:, columns], preferred_element_type=jnp.float32)


def per_device(kv_pages, send_list, wanted, lengths, tables, queries, new_kv, out_weight):
    stored = kv_pages[0, 0, 0]
    slots = stored.shape[0]
    groups, tps = lax.axis_size("group"), lax.axis_size("tp")
    held = max(1, KVH // tps)
    rows, wide = queries.shape[1], queries.shape[2]
    heads = wide // HD
    per_held = heads // held
    maxp = tables.shape[2]
    send = jnp.transpose(send_list, (2, 0, 1))
    def place(block, at):
        return jnp.pad(block, ((0, rows - block.shape[0]), (at, wide + LANES - at - block.shape[1])))

    high = lax.shift_right_logical(place(lengths, wide + maxp), 3)
    low = jnp.bitwise_and(place(lengths, wide + maxp + rows), 7)
    integers = place(tables[0], wide) + high + low
    qa = place(queries[0], 0) + integers.astype(jnp.bfloat16)
    asked = []
    for k in range(1, groups):
        pairs = [pair for i in range(groups) for pair in ((groups + i, (i + k) % groups), (i, groups + i))]
        asked.append(lax.ppermute(qa, ("role", "group"), pairs))
    part_shape = jax.ShapeDtypeStruct((heads * rows + STATS, HD), jnp.float32)
    sent_shape = jax.ShapeDtypeStruct(part_shape.shape, jnp.bfloat16)
    vmem = pl.BlockSpec(memory_space=pltpu.VMEM)
    hbm = pl.BlockSpec(memory_space=pltpu.HBM)
    page_shape = stored.shape[1:]
    chosen_count = groups * PARTS
    read_count = -(-rows * maxp // CHUNK) * CHUNK
    lists = [send, wanted, tables[0], lengths]
    pinned = [pltpu.with_memory_space_constraint(x, pltpu.HBM) for x in lists + [stored]]
    smem = [pltpu.SMEM(x.shape, jnp.int32) for x in lists]
    reading = [pltpu.SMEM((slots + 1,), jnp.int32), pltpu.SMEM((2, read_count), jnp.int32)]
    mine, mine_sent, chosen, entries = pl.pallas_call(
        functools.partial(first_kernel, held, per_held, groups, maxp),
        out_shape=[
            part_shape,
            sent_shape,
            jax.ShapeDtypeStruct((chosen_count,) + page_shape, jnp.bfloat16),
            jax.ShapeDtypeStruct((chosen_count, LANES), jnp.float32),
        ],
        in_specs=[vmem] + [hbm] * 5,
        out_specs=[vmem] * 4,
        scratch_shapes=[
            pltpu.VMEM((read_count,) + page_shape, jnp.bfloat16),
            *smem,
            *reading,
            pltpu.SMEM((chosen_count + 1,), jnp.int32),
            pltpu.SMEM((chosen_count + 1,), jnp.int32),
            pltpu.SemaphoreType.DMA((len(lists),)),
            pltpu.SemaphoreType.DMA((chosen_count,)),
            pltpu.SemaphoreType.DMA((read_count,)),
        ],
        compiler_params=pltpu.CompilerParams(vmem_limit_bytes=20 * MIB),
        name="resident",
    )(qa, *pinned)
    count = groups - 1
    theirs = pl.pallas_call(
        functools.partial(second_kernel, held, per_held, maxp, count),
        out_shape=[sent_shape] * count,
        in_specs=[vmem] * (2 + count),
        out_specs=[vmem] * count,
        compiler_params=pltpu.CompilerParams(vmem_limit_bytes=16 * MIB),
        cost_estimate=pl.CostEstimate(flops=4 * 10**10, bytes_accessed=8 * MIB, transcendentals=10**6),
        name="owned",
    )(chosen, entries, *reversed(asked))
    qa, mine_sent, theirs = lax.optimization_barrier((qa, mine_sent, theirs))
    fresh = pl.pallas_call(
        functools.partial(fresh_kernel, held, per_held),
        out_shape=part_shape,
        in_specs=[vmem] * 2,
        out_specs=vmem,
        compiler_params=pltpu.CompilerParams(vmem_limit_bytes=8 * MIB),
        cost_estimate=pl.CostEstimate(flops=10**9, bytes_accessed=MIB, transcendentals=10**4),
        name="fresh",
    )(qa, new_kv[0])
    parts = [mine, fresh, lax.ppermute(mine_sent, "role", [(0, 1), (1, 0)])]
    for k in range(1, groups):
        pairs = [pair for i in range(groups) for pair in ((i, groups + (i - k) % groups), (groups + i, i))]
        parts.append(lax.ppermute(theirs[k - 1], ("role", "group"), pairs))
    attended = pl.pallas_call(
        functools.partial(merge_kernel, heads, rows),
        out_shape=jax.ShapeDtypeStruct((rows, wide), jnp.bfloat16),
        in_specs=[vmem] * len(parts),
        out_specs=vmem,
        compiler_params=pltpu.CompilerParams(vmem_limit_bytes=8 * MIB),
        name="merge",
    )(*parts)
    partner = lax.ppermute(attended, "role", [(0, 1), (1, 0)])
    share = out_weight.shape[1] // tps

    def project(first_step, steps, name):
        return pl.pallas_call(
            functools.partial(project_kernel, share, first_step),
            out_shape=jax.ShapeDtypeStruct((rows, steps * share), jnp.float32),
            in_specs=[vmem] * 3,
            out_specs=vmem,
            compiler_params=pltpu.CompilerParams(vmem_limit_bytes=24 * MIB),
            cost_estimate=pl.CostEstimate(
                flops=steps * 32 * wide * share, bytes_accessed=steps * 2 * wide * share, transcendentals=0
            ),
            name=name,
        )(attended, partner, out_weight)

    sent, kept = project(0, tps // 2, "project_sent"), project(tps // 2, tps // 2, "project_kept")
    step = tps // 2
    while True:
        arrived = lax.ppermute(sent, "tp", [(i, i ^ step) for i in range(tps)])
        if step == 1:
            return (kept + arrived).astype(jnp.bfloat16)[None]
        middle = step * share // 2
        sent = kept[:, :middle] + arrived[:, :middle]
        kept = kept[:, middle:] + arrived[:, middle:]
        step //= 2


def solution(mesh):
    return jax.shard_map(
        per_device,
        mesh=mesh,
        in_specs=(
            P("role", "group", "tp", None, None, None),
            P(),
            P(),
            P("group", None),
            P("group", None, None),
            P("group", None, "tp"),
            P("group", None, "tp"),
            P("tp", "role"),
        ),
        out_specs=P("group", None, ("role", "tp")),
        check_vma=False,
    )
```

```python
import functools
import math

import jax
import jax.numpy as jnp
from jax import lax
from jax.experimental import pallas as pl
from jax.experimental.pallas import tpu as pltpu
from jax.sharding import PartitionSpec as P

KVH = 8
HD = 128
CAP = 4
CAPP = 2
PRE_DEV = 8
LANES = 128
PAGE = 128
NEG = -1e30
FLOOR = -1e29
SCALE = 1.0 / math.sqrt(HD)
PARTS = CAP + CAPP
CHUNK = 8
STATS = 16
MIB = 2**20


def dot(a, b, ca, cb):
    return lax.dot_general(a, b, (((ca,), (cb,)), ((), ())), preferred_element_type=jnp.float32)


def query_block(qa, held, per_held):
    q = qa[:, : held * per_held * HD].astype(jnp.float32)
    rows = q.shape[0]
    bands = []
    for j in range(held):
        heads = [q[:, (j * per_held + i) * HD : (j * per_held + i + 1) * HD] for i in range(per_held)]
        band = jnp.concatenate(heads, 0)
        blank = jnp.zeros_like(band)
        bands.append(jnp.concatenate([band if i == j else blank for i in range(held)], 1))
    return jnp.concatenate(bands, 0).astype(jnp.bfloat16)


def entry_rows(qa, held, per_held, maxp):
    rows = qa.shape[0]
    wide = held * per_held * HD
    aux = qa[:, wide : wide + LANES].astype(jnp.float32)
    lane = lax.broadcasted_iota(jnp.int32, (rows, LANES), 1) - maxp
    row = lax.broadcasted_iota(jnp.int32, (rows, LANES), 0)
    parts = jnp.where(lane == row, 8.0 * aux[:1], jnp.where(lane == row + rows, aux[:1], 0.0))
    length = jnp.sum(parts, 1, keepdims=True)
    turned = jnp.concatenate([jnp.where(lane == 0, length, aux)] * (held * per_held), 0).T
    first = lax.broadcasted_iota(jnp.int32, (maxp, 1), 0).astype(jnp.float32) * PAGE
    return turned[:maxp], jnp.clip(turned[maxp : maxp + 1] - first, 0.0, PAGE)


def lanes_of(page, first, held):
    return jnp.concatenate([page[:, (2 * j + first) * HD : (2 * j + first + 1) * HD] for j in range(held)], 1)


def pieces(x):
    high = x.astype(jnp.bfloat16).astype(jnp.float32)
    middle = (x - high).astype(jnp.bfloat16).astype(jnp.float32)
    return [high, middle, x - high - middle]


def write_part(out, acc, top, total, held, per_held):
    count = acc.shape[0]
    band = count // held
    out[:count, :] = jnp.concatenate(
        [acc[j * band : (j + 1) * band, j * HD : (j + 1) * HD] for j in range(held)], 0
    ).astype(out.dtype)
    rows = pieces(top) + pieces(total)
    block = jnp.concatenate(rows + [jnp.zeros((STATS - len(rows), count), jnp.float32)], 0)
    if count < LANES:
        block = jnp.concatenate([block, jnp.zeros((STATS, LANES - count), jnp.float32)], 1)
    out[count:, :] = block.astype(out.dtype)


def owner_part(qa, pages, entries, out, held, per_held, maxp):
    q = query_block(qa, held, per_held)
    tab, cnt = entry_rows(qa, held, per_held, maxp)
    count = q.shape[0]
    token = lax.broadcasted_iota(jnp.int32, (PAGE, count), 0).astype(jnp.float32)
    masks = []
    for c in range(PARTS):
        valid = jnp.sum(jnp.where(tab == entries[c : c + 1, :count], cnt, 0.0), 0, keepdims=True)
        masks.append(token < valid)
    mask = jnp.concatenate(masks, 0)
    keys = jnp.concatenate([lanes_of(pages.at[c], 0, held) for c in range(PARTS)], 0)
    values = jnp.concatenate([lanes_of(pages.at[c], 1, held) for c in range(PARTS)], 0)
    s = jnp.where(mask, dot(keys, q, 1, 1) * SCALE, NEG)
    top = jnp.max(s, 0, keepdims=True)
    p = jnp.where(mask, jnp.exp(s - top), 0.0)
    total = jnp.sum(p, 0, keepdims=True)
    acc = dot(p.astype(jnp.bfloat16), values, 0, 0)
    write_part(out, acc, top, total, held, per_held)


def resident_part(qa, lists_ready, send, tables, lengths, maxp, group, kv, pages, flags, listed, sems, out, held, per_held):
    rows = qa.shape[0]
    slots = kv.shape[0]
    q = query_block(qa, held, per_held)
    count = q.shape[0]
    lane_row = lax.rem(lax.broadcasted_iota(jnp.int32, (1, count), 1), rows)
    token = lax.broadcasted_iota(jnp.int32, (PAGE, count), 0)
    for i in range(slots):
        flags[i] = 0

    lists_ready()
    for o in range(send.shape[1]):
        for i in range(send.shape[2]):
            flags[jnp.where(send[1, o, i] == group, send[2, o, i], slots)] = 1

    def page_copy(slot, i):
        return pltpu.make_async_copy(kv.at[slot], pages.at[i], sems.at[i])

    listed_count = jnp.int32(0)
    for r in range(rows):
        length = lengths[0, r]
        for e in range(maxp):
            slot = tables[r, e]
            tokens = jnp.minimum(length - e * PAGE, PAGE)
            here = jnp.logical_and(slot < slots, flags[jnp.minimum(slot, slots - 1)] == 0)
            needed = jnp.logical_and(tokens > 0, here)
            listed[0, listed_count] = r
            listed[1, listed_count] = tokens

            @pl.when(needed)
            def _(slot=slot, at=listed_count):
                page_copy(slot, at).start()

            listed_count = listed_count + needed.astype(jnp.int32)
    chunks = (listed_count + CHUNK - 1) // CHUNK

    def fill(i, _):
        listed[0, i] = 0
        listed[1, i] = 0
        page_copy(0, i).start()
        return 0

    lax.fori_loop(listed_count, chunks * CHUNK, fill, 0)

    def step(c, carry):
        top, total, acc = carry
        first = c * CHUNK
        masks = []
        for i in range(CHUNK):
            masks.append(token < jnp.where(lane_row == listed[0, first + i], listed[1, first + i], 0))
        for i in range(CHUNK):
            page_copy(0, first + i).wait()
        keys = jnp.concatenate([lanes_of(pages.at[first + i], 0, held) for i in range(CHUNK)], 0)
        values = jnp.concatenate([lanes_of(pages.at[first + i], 1, held) for i in range(CHUNK)], 0)
        s = jnp.where(jnp.concatenate(masks, 0), dot(keys, q, 1, 1) * SCALE, NEG)
        new_top = jnp.maximum(top, jnp.max(s, 0, keepdims=True))
        p = jnp.exp(s - new_top)
        fade = jnp.exp(top - new_top)
        total = total * fade + jnp.sum(p, 0, keepdims=True)
        acc = acc * jnp.broadcast_to(fade, (8, count)).T[:, :1] + dot(p.astype(jnp.bfloat16), values, 0, 0)
        return new_top, total, acc

    start = (
        jnp.full((1, count), FLOOR, jnp.float32),
        jnp.zeros((1, count), jnp.float32),
        jnp.zeros((count, held * HD), jnp.float32),
    )
    top, total, acc = lax.fori_loop(0, chunks, step, start)
    write_part(out, acc, top, total, held, per_held)


def list_pages(send, wanted, owner, target, slots, page_list, slot_list, base):
    for c in range(PARTS):
        page_list[base + c] = 0
        slot_list[base + c] = -1
    at = jnp.int32(base)
    for i in range(send.shape[2]):
        hit = send[1, owner, i] == target
        page_list[at] = send[0, owner, i]
        slot_list[at] = jnp.where(hit, send[2, owner, i], -1)
        at = at + hit.astype(jnp.int32)
    at = jnp.int32(base + CAP)
    page_list[at] = 0
    slot_list[at] = -1
    for i in range(wanted.shape[1]):
        page = wanted[target, i] - owner * PRE_DEV
        hit = jnp.logical_and(page >= 0, page < PRE_DEV)
        page_list[at] = jnp.where(hit, page, 0)
        slot_list[at] = jnp.where(hit, slots + i, -1)
        at = at + hit.astype(jnp.int32)


def copy_lists(pairs, sems):
    copies = [pltpu.make_async_copy(a, b, sems.at[i]) for i, (a, b) in enumerate(pairs)]
    for copy in copies:
        copy.start()

    def ready():
        for copy in copies:
            copy.wait()

    return ready


def first_kernel(held, per_held, groups, maxp, qa, send_hbm, wanted_hbm, tables_hbm, lengths_hbm, kv, *refs):
    out, sent, chosen, entries, pages, send, wanted, tables, lengths = refs[:9]
    flags, listed, page_list, slot_list, list_sems, chosen_sems, sems = refs[9:]
    group = lax.axis_index("group")
    prefill = lax.axis_index("role") == 0
    lists = ((send_hbm, send), (wanted_hbm, wanted), (tables_hbm, tables), (lengths_hbm, lengths))
    lists_ready = copy_lists(lists, list_sems)

    @pl.when(prefill)
    def _():
        lists_ready()
        copies = []
        for k in range(groups):
            target = lax.bitwise_xor(group, k)
            list_pages(send, wanted, group, target, kv.shape[0], page_list, slot_list, k * PARTS)
            for c in range(PARTS):
                at = k * PARTS + c
                copy = pltpu.make_async_copy(kv.at[page_list[at]], chosen.at[at], chosen_sems.at[at])
                copy.start()
                copies.append(copy)
                entry = slot_list[at].astype(jnp.float32)
                entries[at : at + 1, :] = jnp.full((1, LANES), entry, jnp.float32)
        for copy in copies[:PARTS]:
            copy.wait()
        owner_part(qa, chosen.at[pl.ds(0, PARTS)], entries[:PARTS, :], sent, held, per_held, maxp)
        for copy in copies[PARTS:]:
            copy.wait()

    @pl.when(jnp.logical_not(prefill))
    def _():
        resident_part(
            qa, lists_ready, send, tables, lengths, maxp, group, kv, pages, flags, listed, sems, out, held, per_held
        )


def fresh_kernel(held, per_held, qa, new_kv, out):
    rows = qa.shape[0]
    q = query_block(qa, held, per_held)
    count = q.shape[0]
    lane_row = lax.rem(lax.broadcasted_iota(jnp.int32, (1, count), 1), rows)
    fresh = new_kv[...].astype(jnp.float32)
    fresh = jnp.concatenate([fresh, jnp.zeros_like(fresh)], 0).astype(jnp.bfloat16)
    mask = lax.broadcasted_iota(jnp.int32, (2 * rows, count), 0) == lane_row
    s = jnp.where(mask, dot(lanes_of(fresh, 0, held), q, 1, 1) * SCALE, NEG)
    top = jnp.max(s, 0, keepdims=True)
    p = jnp.exp(s - top)
    acc = dot(p.astype(jnp.bfloat16), lanes_of(fresh, 1, held), 0, 0)
    write_part(out, acc, top, jnp.sum(p, 0, keepdims=True), held, per_held)


def second_kernel(held, per_held, maxp, count, chosen, entries, *refs):
    qas, outs = refs[:count][::-1], refs[count:]

    @pl.when(lax.axis_index("role") == 0)
    def _():
        for k in range(count):
            at = (k + 1) * PARTS
            owner_part(
                qas[k], chosen.at[pl.ds(at, PARTS)], entries[at : at + PARTS, :], outs[k], held, per_held, maxp
            )


def merge_kernel(heads, rows, *refs):
    parts, out = refs[:-1], refs[-1]
    count = heads * rows
    pad = -len(parts) % 8
    stats = [part[count:, :].astype(jnp.float32)[:, :count] for part in parts]
    tops = jnp.concatenate([s[0:1] + (s[1:2] + s[2:3]) for s in stats], 0)
    totals = jnp.concatenate([s[3:4] + (s[4:5] + s[5:6]) for s in stats], 0)
    factors = jnp.exp(tops - jnp.max(tops, 0, keepdims=True))
    factors = factors / jnp.sum(factors * totals, 0, keepdims=True)
    factors = jnp.concatenate([factors, jnp.zeros((pad, count), jnp.float32)], 0).T
    terms = [factors[:, i : i + 1] * part[:count, :].astype(jnp.float32) for i, part in enumerate(parts)]
    merged = functools.reduce(jnp.add, terms)
    out[...] = jnp.concatenate([merged[h * rows : (h + 1) * rows] for h in range(heads)], 1).astype(out.dtype)


def project_kernel(steps, attended, partner, weight, *outs):
    tps = lax.axis_size("tp")
    share = outs[0].shape[1]
    here = jnp.where(lax.axis_index("role") == 0, partner[...].astype(jnp.float32), attended[...].astype(jnp.float32))
    here = here.astype(jnp.bfloat16)
    for d, out in zip(steps, outs):
        first = lax.rem(lax.axis_index("tp") + d, tps) * share
        columns = pl.ds(pl.multiple_of(first, LANES), share)
        out[...] = jnp.dot(here, weight[:, columns], preferred_element_type=jnp.float32).astype(out.dtype)


def per_device(kv_pages, send_list, wanted, lengths, tables, queries, new_kv, out_weight):
    stored = kv_pages[0, 0, 0]
    slots = stored.shape[0]
    groups, tps = lax.axis_size("group"), lax.axis_size("tp")
    held = max(1, KVH // tps)
    rows, wide = queries.shape[1], queries.shape[2]
    heads = wide // HD
    per_held = heads // held
    maxp = tables.shape[2]
    send = jnp.transpose(send_list, (2, 0, 1))
    def place(block, at):
        return jnp.pad(block, ((0, rows - block.shape[0]), (at, wide + LANES - at - block.shape[1])))

    high = lax.shift_right_logical(place(lengths, wide + maxp), 3)
    low = jnp.bitwise_and(place(lengths, wide + maxp + rows), 7)
    integers = place(tables[0], wide) + high + low
    qa = place(queries[0], 0) + integers.astype(jnp.bfloat16)
    def paired(value, k, to_decode):
        first, second = (0, groups) if to_decode else (groups, 0)
        pairs = [pair for i in range(groups) for pair in ((first + i, second + (i ^ k)), (second + i, first + i))]
        return lax.ppermute(value, ("role", "group"), pairs)

    asked = [paired(qa, k, False) for k in range(1, groups)]
    part_shape = jax.ShapeDtypeStruct((heads * rows + STATS, HD), jnp.float32)
    sent_shape = jax.ShapeDtypeStruct(part_shape.shape, jnp.bfloat16)
    vmem = pl.BlockSpec(memory_space=pltpu.VMEM)
    hbm = pl.BlockSpec(memory_space=pltpu.HBM)
    page_shape = stored.shape[1:]
    chosen_count = groups * PARTS
    read_count = -(-rows * maxp // CHUNK) * CHUNK
    lists = [send, wanted, tables[0], lengths]
    pinned = [pltpu.with_memory_space_constraint(x, pltpu.HBM) for x in lists + [stored]]
    smem = [pltpu.SMEM(x.shape, jnp.int32) for x in lists]
    reading = [pltpu.SMEM((slots + 1,), jnp.int32), pltpu.SMEM((2, read_count), jnp.int32)]
    mine, mine_sent, chosen, entries = pl.pallas_call(
        functools.partial(first_kernel, held, per_held, groups, maxp),
        out_shape=[
            part_shape,
            sent_shape,
            jax.ShapeDtypeStruct((chosen_count,) + page_shape, jnp.bfloat16),
            jax.ShapeDtypeStruct((chosen_count, LANES), jnp.float32),
        ],
        in_specs=[vmem] + [hbm] * 5,
        out_specs=[vmem] * 4,
        scratch_shapes=[
            pltpu.VMEM((read_count,) + page_shape, jnp.bfloat16),
            *smem,
            *reading,
            pltpu.SMEM((chosen_count + 1,), jnp.int32),
            pltpu.SMEM((chosen_count + 1,), jnp.int32),
            pltpu.SemaphoreType.DMA((len(lists),)),
            pltpu.SemaphoreType.DMA((chosen_count,)),
            pltpu.SemaphoreType.DMA((read_count,)),
        ],
        compiler_params=pltpu.CompilerParams(vmem_limit_bytes=20 * MIB),
        name="resident",
    )(qa, *pinned)
    count = groups - 1
    theirs = pl.pallas_call(
        functools.partial(second_kernel, held, per_held, maxp, count),
        out_shape=[sent_shape] * count,
        in_specs=[vmem] * (2 + count),
        out_specs=[vmem] * count,
        compiler_params=pltpu.CompilerParams(vmem_limit_bytes=16 * MIB),
        cost_estimate=pl.CostEstimate(flops=4 * 10**10, bytes_accessed=8 * MIB, transcendentals=10**6),
        name="owned",
    )(chosen, entries, *reversed(asked))
    qa, mine_sent, theirs = lax.optimization_barrier((qa, mine_sent, theirs))
    fresh = pl.pallas_call(
        functools.partial(fresh_kernel, held, per_held),
        out_shape=part_shape,
        in_specs=[vmem] * 2,
        out_specs=vmem,
        compiler_params=pltpu.CompilerParams(vmem_limit_bytes=8 * MIB),
        cost_estimate=pl.CostEstimate(flops=10**9, bytes_accessed=MIB, transcendentals=10**4),
        name="fresh",
    )(qa, new_kv[0])
    parts = [mine, fresh] + [paired(part, k, True) for k, part in enumerate([mine_sent, *theirs])]
    attended = pl.pallas_call(
        functools.partial(merge_kernel, heads, rows),
        out_shape=jax.ShapeDtypeStruct((rows, wide), jnp.bfloat16),
        in_specs=[vmem] * len(parts),
        out_specs=vmem,
        compiler_params=pltpu.CompilerParams(vmem_limit_bytes=8 * MIB),
        name="merge",
    )(*parts)
    partner = lax.ppermute(attended, "role", [(0, 1), (1, 0)])
    share = out_weight.shape[1] // tps

    def project(steps, dtype, name):
        return pl.pallas_call(
            functools.partial(project_kernel, steps),
            out_shape=[jax.ShapeDtypeStruct((rows, share), dtype)] * len(steps),
            in_specs=[vmem] * 3,
            out_specs=[vmem] * len(steps),
            compiler_params=pltpu.CompilerParams(vmem_limit_bytes=24 * MIB),
            cost_estimate=pl.CostEstimate(
                flops=len(steps) * 32 * wide * share, bytes_accessed=len(steps) * 2 * wide * share, transcendentals=0
            ),
            name=name,
        )(attended, partner, out_weight)

    steps = list(range(1, tps))
    sent = project(steps, jnp.bfloat16, "project")
    arrived = [lax.ppermute(part, "tp", [(i, (i + d) % tps) for i in range(tps)]) for d, part in zip(steps, sent)]
    own = project([0], jnp.float32, "project_own")[0]
    total = functools.reduce(jnp.add, [part.astype(jnp.float32) for part in arrived], own)
    return total.astype(jnp.bfloat16)[None]


def solution(mesh):
    return jax.shard_map(
        per_device,
        mesh=mesh,
        in_specs=(
            P("role", "group", "tp", None, None, None),
            P(),
            P(),
            P("group", None),
            P("group", None, None),
            P("group", None, "tp"),
            P("group", None, "tp"),
            P("tp", "role"),
        ),
        out_specs=P("group", None, ("role", "tp")),
        check_vma=False,
    )
```

```python
import functools
import math

import jax
import jax.numpy as jnp
from jax import lax
from jax.experimental import pallas as pl
from jax.experimental.pallas import tpu as pltpu
from jax.sharding import PartitionSpec as P

KVH = 8
HD = 128
CAP = 4
CAPP = 2
PRE_DEV = 8
LANES = 128
PAGE = 128
NEG = -1e30
FLOOR = -1e29
SCALE = 1.0 / math.sqrt(HD)
PARTS = CAP + CAPP
CHUNK = 4
STATIC = (4, 5, 6, 7, 8)
STATS = 16
MIB = 2**20


def dot(a, b, ca, cb):
    return lax.dot_general(a, b, (((ca,), (cb,)), ((), ())), preferred_element_type=jnp.float32)


def query_block(qa, held, per_held):
    q = qa[:, : held * per_held * HD].astype(jnp.float32)
    rows = q.shape[0]
    bands = []
    for j in range(held):
        heads = [q[:, (j * per_held + i) * HD : (j * per_held + i + 1) * HD] for i in range(per_held)]
        band = jnp.concatenate(heads, 0)
        blank = jnp.zeros_like(band)
        bands.append(jnp.concatenate([band if i == j else blank for i in range(held)], 1))
    return jnp.concatenate(bands, 0).astype(jnp.bfloat16)


def entry_rows(qa, held, per_held, maxp):
    rows = qa.shape[0]
    wide = held * per_held * HD
    aux = qa[:, wide : wide + LANES].astype(jnp.float32)
    lane = lax.broadcasted_iota(jnp.int32, (rows, LANES), 1) - maxp
    row = lax.broadcasted_iota(jnp.int32, (rows, LANES), 0)
    parts = jnp.where(lane == row, 8.0 * aux[:1], jnp.where(lane == row + rows, aux[:1], 0.0))
    length = jnp.sum(parts, 1, keepdims=True)
    turned = jnp.concatenate([jnp.where(lane == 0, length, aux)] * (held * per_held), 0).T
    first = lax.broadcasted_iota(jnp.int32, (maxp, 1), 0).astype(jnp.float32) * PAGE
    return turned[:maxp], jnp.clip(turned[maxp : maxp + 1] - first, 0.0, PAGE)


def lanes_of(page, first, held):
    return jnp.concatenate([page[:, (2 * j + first) * HD : (2 * j + first + 1) * HD] for j in range(held)], 1)


def pieces(x):
    high = x.astype(jnp.bfloat16).astype(jnp.float32)
    middle = (x - high).astype(jnp.bfloat16).astype(jnp.float32)
    return [high, middle, x - high - middle]


def write_part(out, acc, top, total, held, per_held):
    count = acc.shape[0]
    band = count // held
    out[:count, :] = jnp.concatenate(
        [acc[j * band : (j + 1) * band, j * HD : (j + 1) * HD] for j in range(held)], 0
    ).astype(out.dtype)
    rows = pieces(top) + pieces(total)
    block = jnp.concatenate(rows + [jnp.zeros((STATS - len(rows), count), jnp.float32)], 0)
    if count < LANES:
        block = jnp.concatenate([block, jnp.zeros((STATS, LANES - count), jnp.float32)], 1)
    out[count:, :] = block.astype(out.dtype)


def owner_part(qa, pages, entries, out, held, per_held, maxp):
    q = query_block(qa, held, per_held)
    tab, cnt = entry_rows(qa, held, per_held, maxp)
    count = q.shape[0]
    token = lax.broadcasted_iota(jnp.int32, (PAGE, count), 0).astype(jnp.float32)
    masks = []
    for c in range(PARTS):
        valid = jnp.sum(jnp.where(tab == entries[c : c + 1, :count], cnt, 0.0), 0, keepdims=True)
        masks.append(token < valid)
    mask = jnp.concatenate(masks, 0)
    keys = jnp.concatenate([lanes_of(pages.at[c], 0, held) for c in range(PARTS)], 0)
    values = jnp.concatenate([lanes_of(pages.at[c], 1, held) for c in range(PARTS)], 0)
    s = jnp.where(mask, dot(keys, q, 1, 1) * SCALE, NEG)
    top = jnp.max(s, 0, keepdims=True)
    p = jnp.where(mask, jnp.exp(s - top), 0.0)
    total = jnp.sum(p, 0, keepdims=True)
    acc = dot(p.astype(jnp.bfloat16), values, 0, 0)
    write_part(out, acc, top, total, held, per_held)


def resident_part(qa, lists_ready, send, tables, lengths, maxp, group, kv, pages, flags, listed, sems, out, held, per_held):
    rows = qa.shape[0]
    slots = kv.shape[0]
    q = query_block(qa, held, per_held)
    count = q.shape[0]
    lane_row = lax.rem(lax.broadcasted_iota(jnp.int32, (1, count), 1), rows)
    token = lax.broadcasted_iota(jnp.int32, (PAGE, count), 0)
    for i in range(slots):
        flags[i] = 0

    lists_ready()
    for o in range(send.shape[1]):
        for i in range(send.shape[2]):
            flags[jnp.where(send[1, o, i] == group, send[2, o, i], slots)] = 1

    def page_copy(slot, i):
        return pltpu.make_async_copy(kv.at[slot], pages.at[i], sems.at[i])

    listed_count = jnp.int32(0)
    for r in range(rows):
        length = lengths[0, r]
        for e in range(maxp):
            slot = tables[r, e]
            tokens = jnp.minimum(length - e * PAGE, PAGE)
            here = jnp.logical_and(slot < slots, flags[jnp.minimum(slot, slots - 1)] == 0)
            needed = jnp.logical_and(tokens > 0, here)
            listed[0, listed_count] = r
            listed[1, listed_count] = tokens

            @pl.when(needed)
            def _(slot=slot, at=listed_count):
                page_copy(slot, at).start()

            listed_count = listed_count + needed.astype(jnp.int32)
    chunks = jnp.maximum((listed_count + CHUNK - 1) // CHUNK, STATIC[0])

    def fill(i, _):
        listed[0, i] = 0
        listed[1, i] = 0
        page_copy(0, i).start()
        return 0

    lax.fori_loop(listed_count, chunks * CHUNK, fill, 0)

    def score(c):
        first = c * CHUNK
        masks = []
        for i in range(CHUNK):
            masks.append(token < jnp.where(lane_row == listed[0, first + i], listed[1, first + i], 0))
        for i in range(CHUNK):
            page_copy(0, first + i).wait()
        keys = jnp.concatenate([lanes_of(pages.at[first + i], 0, held) for i in range(CHUNK)], 0)
        return jnp.where(jnp.concatenate(masks, 0), dot(keys, q, 1, 1) * SCALE, NEG)

    def weigh(c, s, top):
        p = jnp.exp(s - top)
        values = jnp.concatenate([lanes_of(pages.at[c * CHUNK + i], 1, held) for i in range(CHUNK)], 0)
        return jnp.sum(p, 0, keepdims=True), dot(p.astype(jnp.bfloat16), values, 0, 0)

    floor = jnp.full((1, count), FLOOR, jnp.float32)

    def straight(number):
        scores = [score(c) for c in range(number)]
        top = functools.reduce(jnp.maximum, [jnp.max(s, 0, keepdims=True) for s in scores], floor)
        terms = [weigh(c, s, top) for c, s in enumerate(scores)]
        total = functools.reduce(jnp.add, [t for t, _ in terms])
        acc = functools.reduce(jnp.add, [a for _, a in terms])
        write_part(out, acc, top, total, held, per_held)

    def step(c, carry):
        top, total, acc = carry
        s = score(c)
        new_top = jnp.maximum(top, jnp.max(s, 0, keepdims=True))
        fade = jnp.exp(top - new_top)
        more, part = weigh(c, s, new_top)
        return new_top, total * fade + more, acc * jnp.broadcast_to(fade, (8, count)).T[:, :1] + part

    for number in STATIC:

        @pl.when(chunks == number)
        def _(number=number):
            straight(number)

    @pl.when(chunks > STATIC[-1])
    def _():
        start = (floor, jnp.zeros((1, count), jnp.float32), jnp.zeros((count, held * HD), jnp.float32))
        top, total, acc = lax.fori_loop(0, chunks, step, start)
        write_part(out, acc, top, total, held, per_held)


def list_pages(send, wanted, owner, target, slots, page_list, slot_list, base):
    for c in range(PARTS):
        page_list[base + c] = 0
        slot_list[base + c] = -1
    at = jnp.int32(base)
    for i in range(send.shape[2]):
        hit = send[1, owner, i] == target
        page_list[at] = send[0, owner, i]
        slot_list[at] = jnp.where(hit, send[2, owner, i], -1)
        at = at + hit.astype(jnp.int32)
    at = jnp.int32(base + CAP)
    page_list[at] = 0
    slot_list[at] = -1
    for i in range(wanted.shape[1]):
        page = wanted[target, i] - owner * PRE_DEV
        hit = jnp.logical_and(page >= 0, page < PRE_DEV)
        page_list[at] = jnp.where(hit, page, 0)
        slot_list[at] = jnp.where(hit, slots + i, -1)
        at = at + hit.astype(jnp.int32)


def copy_lists(pairs, sems):
    copies = [pltpu.make_async_copy(a, b, sems.at[i]) for i, (a, b) in enumerate(pairs)]
    for copy in copies:
        copy.start()

    def ready():
        for copy in copies:
            copy.wait()

    return ready


def first_kernel(held, per_held, groups, maxp, qa, send_hbm, wanted_hbm, tables_hbm, lengths_hbm, kv, *refs):
    out, sent, chosen, entries, pages, send, wanted, tables, lengths = refs[:9]
    flags, listed, page_list, slot_list, list_sems, chosen_sems, sems = refs[9:]
    group = lax.axis_index("group")
    prefill = lax.axis_index("role") == 0
    lists = ((send_hbm, send), (wanted_hbm, wanted), (tables_hbm, tables), (lengths_hbm, lengths))
    lists_ready = copy_lists(lists, list_sems)

    @pl.when(prefill)
    def _():
        lists_ready()
        copies = []
        for k in range(groups):
            target = lax.bitwise_xor(group, k)
            list_pages(send, wanted, group, target, kv.shape[0], page_list, slot_list, k * PARTS)
            for c in range(PARTS):
                at = k * PARTS + c
                copy = pltpu.make_async_copy(kv.at[page_list[at]], chosen.at[at], chosen_sems.at[at])
                copy.start()
                copies.append(copy)
                entry = slot_list[at].astype(jnp.float32)
                entries[at : at + 1, :] = jnp.full((1, LANES), entry, jnp.float32)
        for copy in copies[:PARTS]:
            copy.wait()
        owner_part(qa, chosen.at[pl.ds(0, PARTS)], entries[:PARTS, :], sent, held, per_held, maxp)
        for copy in copies[PARTS:]:
            copy.wait()

    @pl.when(jnp.logical_not(prefill))
    def _():
        resident_part(
            qa, lists_ready, send, tables, lengths, maxp, group, kv, pages, flags, listed, sems, out, held, per_held
        )


def fresh_kernel(held, per_held, qa, new_kv, out):
    rows = qa.shape[0]
    q = query_block(qa, held, per_held)
    count = q.shape[0]
    lane_row = lax.rem(lax.broadcasted_iota(jnp.int32, (1, count), 1), rows)
    fresh = new_kv[...].astype(jnp.float32)
    fresh = jnp.concatenate([fresh, jnp.zeros_like(fresh)], 0).astype(jnp.bfloat16)
    mask = lax.broadcasted_iota(jnp.int32, (2 * rows, count), 0) == lane_row
    s = jnp.where(mask, dot(lanes_of(fresh, 0, held), q, 1, 1) * SCALE, NEG)
    top = jnp.max(s, 0, keepdims=True)
    p = jnp.exp(s - top)
    acc = dot(p.astype(jnp.bfloat16), lanes_of(fresh, 1, held), 0, 0)
    write_part(out, acc, top, jnp.sum(p, 0, keepdims=True), held, per_held)


def second_kernel(held, per_held, maxp, count, chosen, entries, *refs):
    qas, outs = refs[:count][::-1], refs[count:]

    @pl.when(lax.axis_index("role") == 0)
    def _():
        for k in range(count):
            at = (k + 1) * PARTS
            owner_part(
                qas[k], chosen.at[pl.ds(at, PARTS)], entries[at : at + PARTS, :], outs[k], held, per_held, maxp
            )


def merge_kernel(heads, rows, *refs):
    parts, out = refs[:-1], refs[-1]
    count = heads * rows
    pad = -len(parts) % 8
    stats = [part[count:, :].astype(jnp.float32)[:, :count] for part in parts]
    tops = jnp.concatenate([s[0:1] + (s[1:2] + s[2:3]) for s in stats], 0)
    totals = jnp.concatenate([s[3:4] + (s[4:5] + s[5:6]) for s in stats], 0)
    factors = jnp.exp(tops - jnp.max(tops, 0, keepdims=True))
    factors = factors / jnp.sum(factors * totals, 0, keepdims=True)
    factors = jnp.concatenate([factors, jnp.zeros((pad, count), jnp.float32)], 0).T
    terms = [factors[:, i : i + 1] * part[:count, :].astype(jnp.float32) for i, part in enumerate(parts)]
    merged = functools.reduce(jnp.add, terms)
    out[...] = jnp.concatenate([merged[h * rows : (h + 1) * rows] for h in range(heads)], 1).astype(out.dtype)


def project_kernel(steps, attended, partner, weight, *outs):
    tps = lax.axis_size("tp")
    share = outs[0].shape[1]
    here = jnp.where(lax.axis_index("role") == 0, partner[...].astype(jnp.float32), attended[...].astype(jnp.float32))
    here = here.astype(jnp.bfloat16)
    for d, out in zip(steps, outs):
        first = lax.rem(lax.axis_index("tp") + d, tps) * share
        columns = pl.ds(pl.multiple_of(first, LANES), share)
        out[...] = jnp.dot(here, weight[:, columns], preferred_element_type=jnp.float32).astype(out.dtype)


def per_device(kv_pages, send_list, wanted, lengths, tables, queries, new_kv, out_weight):
    stored = kv_pages[0, 0, 0]
    slots = stored.shape[0]
    groups, tps = lax.axis_size("group"), lax.axis_size("tp")
    held = max(1, KVH // tps)
    rows, wide = queries.shape[1], queries.shape[2]
    heads = wide // HD
    per_held = heads // held
    maxp = tables.shape[2]
    send = jnp.transpose(send_list, (2, 0, 1))
    def place(block, at):
        return jnp.pad(block, ((0, rows - block.shape[0]), (at, wide + LANES - at - block.shape[1])))

    high = lax.shift_right_logical(place(lengths, wide + maxp), 3)
    low = jnp.bitwise_and(place(lengths, wide + maxp + rows), 7)
    integers = place(tables[0], wide) + high + low
    qa = place(queries[0], 0) + integers.astype(jnp.bfloat16)
    def paired(value, k, to_decode):
        first, second = (0, groups) if to_decode else (groups, 0)
        pairs = [pair for i in range(groups) for pair in ((first + i, second + (i ^ k)), (second + i, first + i))]
        return lax.ppermute(value, ("role", "group"), pairs)

    asked = [paired(qa, k, False) for k in range(1, groups)]
    part_shape = jax.ShapeDtypeStruct((heads * rows + STATS, HD), jnp.float32)
    sent_shape = jax.ShapeDtypeStruct(part_shape.shape, jnp.bfloat16)
    vmem = pl.BlockSpec(memory_space=pltpu.VMEM)
    hbm = pl.BlockSpec(memory_space=pltpu.HBM)
    page_shape = stored.shape[1:]
    chosen_count = groups * PARTS
    read_count = -(-rows * maxp // CHUNK) * CHUNK
    lists = [send, wanted, tables[0], lengths]
    pinned = [pltpu.with_memory_space_constraint(x, pltpu.HBM) for x in lists + [stored]]
    smem = [pltpu.SMEM(x.shape, jnp.int32) for x in lists]
    reading = [pltpu.SMEM((slots + 1,), jnp.int32), pltpu.SMEM((2, read_count), jnp.int32)]
    mine, mine_sent, chosen, entries = pl.pallas_call(
        functools.partial(first_kernel, held, per_held, groups, maxp),
        out_shape=[
            part_shape,
            sent_shape,
            jax.ShapeDtypeStruct((chosen_count,) + page_shape, jnp.bfloat16),
            jax.ShapeDtypeStruct((chosen_count, LANES), jnp.float32),
        ],
        in_specs=[vmem] + [hbm] * 5,
        out_specs=[vmem] * 4,
        scratch_shapes=[
            pltpu.VMEM((read_count,) + page_shape, jnp.bfloat16),
            *smem,
            *reading,
            pltpu.SMEM((chosen_count + 1,), jnp.int32),
            pltpu.SMEM((chosen_count + 1,), jnp.int32),
            pltpu.SemaphoreType.DMA((len(lists),)),
            pltpu.SemaphoreType.DMA((chosen_count,)),
            pltpu.SemaphoreType.DMA((read_count,)),
        ],
        compiler_params=pltpu.CompilerParams(vmem_limit_bytes=20 * MIB),
        name="resident",
    )(qa, *pinned)
    count = groups - 1
    theirs = pl.pallas_call(
        functools.partial(second_kernel, held, per_held, maxp, count),
        out_shape=[sent_shape] * count,
        in_specs=[vmem] * (2 + count),
        out_specs=[vmem] * count,
        compiler_params=pltpu.CompilerParams(vmem_limit_bytes=16 * MIB),
        cost_estimate=pl.CostEstimate(flops=4 * 10**10, bytes_accessed=8 * MIB, transcendentals=10**6),
        name="owned",
    )(chosen, entries, *reversed(asked))
    qa, mine_sent, theirs = lax.optimization_barrier((qa, mine_sent, theirs))
    fresh = pl.pallas_call(
        functools.partial(fresh_kernel, held, per_held),
        out_shape=part_shape,
        in_specs=[vmem] * 2,
        out_specs=vmem,
        compiler_params=pltpu.CompilerParams(vmem_limit_bytes=8 * MIB),
        cost_estimate=pl.CostEstimate(flops=10**9, bytes_accessed=MIB, transcendentals=10**4),
        name="fresh",
    )(qa, new_kv[0])
    parts = [mine, fresh] + [paired(part, k, True) for k, part in enumerate([mine_sent, *theirs])]
    attended = pl.pallas_call(
        functools.partial(merge_kernel, heads, rows),
        out_shape=jax.ShapeDtypeStruct((rows, wide), jnp.bfloat16),
        in_specs=[vmem] * len(parts),
        out_specs=vmem,
        compiler_params=pltpu.CompilerParams(vmem_limit_bytes=8 * MIB),
        name="merge",
    )(*parts)
    partner = lax.ppermute(attended, "role", [(0, 1), (1, 0)])
    share = out_weight.shape[1] // tps

    def project(steps, dtype, name):
        return pl.pallas_call(
            functools.partial(project_kernel, steps),
            out_shape=[jax.ShapeDtypeStruct((rows, share), dtype)] * len(steps),
            in_specs=[vmem] * 3,
            out_specs=[vmem] * len(steps),
            compiler_params=pltpu.CompilerParams(vmem_limit_bytes=24 * MIB),
            cost_estimate=pl.CostEstimate(
                flops=len(steps) * 32 * wide * share, bytes_accessed=len(steps) * 2 * wide * share, transcendentals=0
            ),
            name=name,
        )(attended, partner, out_weight)

    steps = list(range(1, tps))
    sent = project(steps, jnp.bfloat16, "project")
    arrived = [lax.ppermute(part, "tp", [(i, (i + d) % tps) for i in range(tps)]) for d, part in zip(steps, sent)]
    own = project([0], jnp.float32, "project_own")[0]
    total = functools.reduce(jnp.add, [part.astype(jnp.float32) for part in arrived], own)
    return total.astype(jnp.bfloat16)[None]


def solution(mesh):
    return jax.shard_map(
        per_device,
        mesh=mesh,
        in_specs=(
            P("role", "group", "tp", None, None, None),
            P(),
            P(),
            P("group", None),
            P("group", None, None),
            P("group", None, "tp"),
            P("group", None, "tp"),
            P("tp", "role"),
        ),
        out_specs=P("group", None, ("role", "tp")),
        check_vma=False,
    )
```

```python
import functools
import math

import jax
import jax.numpy as jnp
from jax import lax
from jax.experimental import pallas as pl
from jax.experimental.pallas import tpu as pltpu
from jax.sharding import PartitionSpec as P

KVH = 8
HD = 128
CAP = 4
CAPP = 2
PRE_DEV = 8
LANES = 128
PAGE = 128
NEG = -1e30
FLOOR = -1e29
SCALE = 1.0 / math.sqrt(HD)
PARTS = CAP + CAPP
CHUNK = 8
STATIC = (2, 3, 4, 5)
STATS = 16
MIB = 2**20


def dot(a, b, ca, cb):
    return lax.dot_general(a, b, (((ca,), (cb,)), ((), ())), preferred_element_type=jnp.float32)


def query_block(qa, held, per_held):
    q = qa[:, : held * per_held * HD].astype(jnp.float32)
    rows = q.shape[0]
    bands = []
    for j in range(held):
        heads = [q[:, (j * per_held + i) * HD : (j * per_held + i + 1) * HD] for i in range(per_held)]
        band = jnp.concatenate(heads, 0)
        blank = jnp.zeros_like(band)
        bands.append(jnp.concatenate([band if i == j else blank for i in range(held)], 1))
    return jnp.concatenate(bands, 0).astype(jnp.bfloat16)


def entry_rows(qa, held, per_held, maxp):
    rows = qa.shape[0]
    wide = held * per_held * HD
    aux = qa[:, wide : wide + LANES].astype(jnp.float32)
    lane = lax.broadcasted_iota(jnp.int32, (rows, LANES), 1) - maxp
    row = lax.broadcasted_iota(jnp.int32, (rows, LANES), 0)
    parts = jnp.where(lane == row, 8.0 * aux[:1], jnp.where(lane == row + rows, aux[:1], 0.0))
    length = jnp.sum(parts, 1, keepdims=True)
    turned = jnp.concatenate([jnp.where(lane == 0, length, aux)] * (held * per_held), 0).T
    first = lax.broadcasted_iota(jnp.int32, (maxp, 1), 0).astype(jnp.float32) * PAGE
    return turned[:maxp], jnp.clip(turned[maxp : maxp + 1] - first, 0.0, PAGE)


def lanes_of(page, first, held):
    return jnp.concatenate([page[:, (2 * j + first) * HD : (2 * j + first + 1) * HD] for j in range(held)], 1)


def pieces(x):
    high = x.astype(jnp.bfloat16).astype(jnp.float32)
    middle = (x - high).astype(jnp.bfloat16).astype(jnp.float32)
    return [high, middle, x - high - middle]


def write_part(out, acc, top, total, held, per_held):
    count = acc.shape[0]
    band = count // held
    out[:count, :] = jnp.concatenate(
        [acc[j * band : (j + 1) * band, j * HD : (j + 1) * HD] for j in range(held)], 0
    ).astype(out.dtype)
    rows = pieces(top) + pieces(total)
    block = jnp.concatenate(rows + [jnp.zeros((STATS - len(rows), count), jnp.float32)], 0)
    if count < LANES:
        block = jnp.concatenate([block, jnp.zeros((STATS, LANES - count), jnp.float32)], 1)
    out[count:, :] = block.astype(out.dtype)


def owner_part(qa, pages, entries, out, held, per_held, maxp):
    q = query_block(qa, held, per_held)
    tab, cnt = entry_rows(qa, held, per_held, maxp)
    count = q.shape[0]
    token = lax.broadcasted_iota(jnp.int32, (PAGE, count), 0).astype(jnp.float32)
    masks = []
    for c in range(PARTS):
        valid = jnp.sum(jnp.where(tab == entries[c : c + 1, :count], cnt, 0.0), 0, keepdims=True)
        masks.append(token < valid)
    mask = jnp.concatenate(masks, 0)
    keys = jnp.concatenate([lanes_of(pages.at[c], 0, held) for c in range(PARTS)], 0)
    values = jnp.concatenate([lanes_of(pages.at[c], 1, held) for c in range(PARTS)], 0)
    s = jnp.where(mask, dot(keys, q, 1, 1) * SCALE, NEG)
    top = jnp.max(s, 0, keepdims=True)
    p = jnp.where(mask, jnp.exp(s - top), 0.0)
    total = jnp.sum(p, 0, keepdims=True)
    acc = dot(p.astype(jnp.bfloat16), values, 0, 0)
    write_part(out, acc, top, total, held, per_held)


def resident_part(qa, lists_ready, send, tables, lengths, maxp, group, kv, pages, flags, listed, sems, out, held, per_held):
    rows = qa.shape[0]
    slots = kv.shape[0]
    q = query_block(qa, held, per_held)
    count = q.shape[0]
    lane_row = lax.rem(lax.broadcasted_iota(jnp.int32, (1, count), 1), rows)
    token = lax.broadcasted_iota(jnp.int32, (PAGE, count), 0)
    for i in range(slots):
        flags[i] = 0

    lists_ready()
    for o in range(send.shape[1]):
        for i in range(send.shape[2]):
            flags[jnp.where(send[1, o, i] == group, send[2, o, i], slots)] = 1

    def page_copy(slot, i):
        return pltpu.make_async_copy(kv.at[slot], pages.at[i], sems.at[i])

    listed_count = jnp.int32(0)
    for r in range(rows):
        length = lengths[0, r]
        for e in range(maxp):
            slot = tables[r, e]
            tokens = jnp.minimum(length - e * PAGE, PAGE)
            here = jnp.logical_and(slot < slots, flags[jnp.minimum(slot, slots - 1)] == 0)
            needed = jnp.logical_and(tokens > 0, here)
            listed[0, listed_count] = r
            listed[1, listed_count] = tokens

            @pl.when(needed)
            def _(slot=slot, at=listed_count):
                page_copy(slot, at).start()

            listed_count = listed_count + needed.astype(jnp.int32)
    chunks = jnp.maximum((listed_count + CHUNK - 1) // CHUNK, STATIC[0])

    def fill(i, _):
        listed[0, i] = 0
        listed[1, i] = 0
        page_copy(0, i).start()
        return 0

    lax.fori_loop(listed_count, chunks * CHUNK, fill, 0)

    def score(c):
        first = c * CHUNK
        masks = []
        for i in range(CHUNK):
            masks.append(token < jnp.where(lane_row == listed[0, first + i], listed[1, first + i], 0))
        for i in range(CHUNK):
            page_copy(0, first + i).wait()
        keys = jnp.concatenate([lanes_of(pages.at[first + i], 0, held) for i in range(CHUNK)], 0)
        return jnp.where(jnp.concatenate(masks, 0), dot(keys, q, 1, 1) * SCALE, NEG)

    def weigh(c, s, top):
        p = jnp.exp(s - top)
        values = jnp.concatenate([lanes_of(pages.at[c * CHUNK + i], 1, held) for i in range(CHUNK)], 0)
        return jnp.sum(p, 0, keepdims=True), dot(p.astype(jnp.bfloat16), values, 0, 0)

    floor = jnp.full((1, count), FLOOR, jnp.float32)

    def straight(number):
        scores = [score(c) for c in range(number)]
        top = functools.reduce(jnp.maximum, [jnp.max(s, 0, keepdims=True) for s in scores], floor)
        terms = [weigh(c, s, top) for c, s in enumerate(scores)]
        total = functools.reduce(jnp.add, [t for t, _ in terms])
        acc = functools.reduce(jnp.add, [a for _, a in terms])
        write_part(out, acc, top, total, held, per_held)

    def step(c, carry):
        top, total, acc = carry
        s = score(c)
        new_top = jnp.maximum(top, jnp.max(s, 0, keepdims=True))
        fade = jnp.exp(top - new_top)
        more, part = weigh(c, s, new_top)
        return new_top, total * fade + more, acc * jnp.broadcast_to(fade, (8, count)).T[:, :1] + part

    for number in STATIC:

        @pl.when(chunks == number)
        def _(number=number):
            straight(number)

    @pl.when(chunks > STATIC[-1])
    def _():
        start = (floor, jnp.zeros((1, count), jnp.float32), jnp.zeros((count, held * HD), jnp.float32))
        top, total, acc = lax.fori_loop(0, chunks, step, start)
        write_part(out, acc, top, total, held, per_held)


def list_pages(send, wanted, owner, target, slots, page_list, slot_list, base):
    for c in range(PARTS):
        page_list[base + c] = 0
        slot_list[base + c] = -1
    at = jnp.int32(base)
    for i in range(send.shape[2]):
        hit = send[1, owner, i] == target
        page_list[at] = send[0, owner, i]
        slot_list[at] = jnp.where(hit, send[2, owner, i], -1)
        at = at + hit.astype(jnp.int32)
    at = jnp.int32(base + CAP)
    page_list[at] = 0
    slot_list[at] = -1
    for i in range(wanted.shape[1]):
        page = wanted[target, i] - owner * PRE_DEV
        hit = jnp.logical_and(page >= 0, page < PRE_DEV)
        page_list[at] = jnp.where(hit, page, 0)
        slot_list[at] = jnp.where(hit, slots + i, -1)
        at = at + hit.astype(jnp.int32)


def copy_lists(pairs, sems):
    copies = [pltpu.make_async_copy(a, b, sems.at[i]) for i, (a, b) in enumerate(pairs)]
    for copy in copies:
        copy.start()

    def ready():
        for copy in copies:
            copy.wait()

    return ready


def first_kernel(held, per_held, groups, maxp, qa, send_hbm, wanted_hbm, tables_hbm, lengths_hbm, kv, *refs):
    out, sent, chosen, entries, pages, send, wanted, tables, lengths = refs[:9]
    flags, listed, page_list, slot_list, list_sems, chosen_sems, sems = refs[9:]
    group = lax.axis_index("group")
    prefill = lax.axis_index("role") == 0
    lists = ((send_hbm, send), (wanted_hbm, wanted), (tables_hbm, tables), (lengths_hbm, lengths))
    lists_ready = copy_lists(lists, list_sems)

    @pl.when(prefill)
    def _():
        lists_ready()
        copies = []
        for k in range(groups):
            target = lax.bitwise_xor(group, k)
            list_pages(send, wanted, group, target, kv.shape[0], page_list, slot_list, k * PARTS)
            for c in range(PARTS):
                at = k * PARTS + c
                copy = pltpu.make_async_copy(kv.at[page_list[at]], chosen.at[at], chosen_sems.at[at])
                copy.start()
                copies.append(copy)
                entry = slot_list[at].astype(jnp.float32)
                entries[at : at + 1, :] = jnp.full((1, LANES), entry, jnp.float32)
        for copy in copies[:PARTS]:
            copy.wait()
        owner_part(qa, chosen.at[pl.ds(0, PARTS)], entries[:PARTS, :], sent, held, per_held, maxp)
        for copy in copies[PARTS:]:
            copy.wait()

    @pl.when(jnp.logical_not(prefill))
    def _():
        resident_part(
            qa, lists_ready, send, tables, lengths, maxp, group, kv, pages, flags, listed, sems, out, held, per_held
        )


def fresh_kernel(held, per_held, qa, new_kv, out):
    rows = qa.shape[0]
    q = query_block(qa, held, per_held)
    count = q.shape[0]
    lane_row = lax.rem(lax.broadcasted_iota(jnp.int32, (1, count), 1), rows)
    fresh = new_kv[...].astype(jnp.float32)
    fresh = jnp.concatenate([fresh, jnp.zeros_like(fresh)], 0).astype(jnp.bfloat16)
    mask = lax.broadcasted_iota(jnp.int32, (2 * rows, count), 0) == lane_row
    s = jnp.where(mask, dot(lanes_of(fresh, 0, held), q, 1, 1) * SCALE, NEG)
    top = jnp.max(s, 0, keepdims=True)
    p = jnp.exp(s - top)
    acc = dot(p.astype(jnp.bfloat16), lanes_of(fresh, 1, held), 0, 0)
    write_part(out, acc, top, jnp.sum(p, 0, keepdims=True), held, per_held)


def second_kernel(held, per_held, maxp, count, chosen, entries, *refs):
    qas, outs = refs[:count][::-1], refs[count:]

    @pl.when(lax.axis_index("role") == 0)
    def _():
        for k in range(count):
            at = (k + 1) * PARTS
            owner_part(
                qas[k], chosen.at[pl.ds(at, PARTS)], entries[at : at + PARTS, :], outs[k], held, per_held, maxp
            )


def merge_kernel(heads, rows, *refs):
    parts, out = refs[:-1], refs[-1]
    count = heads * rows
    pad = -len(parts) % 8
    stats = [part[count:, :].astype(jnp.float32)[:, :count] for part in parts]
    tops = jnp.concatenate([s[0:1] + (s[1:2] + s[2:3]) for s in stats], 0)
    totals = jnp.concatenate([s[3:4] + (s[4:5] + s[5:6]) for s in stats], 0)
    factors = jnp.exp(tops - jnp.max(tops, 0, keepdims=True))
    factors = factors / jnp.sum(factors * totals, 0, keepdims=True)
    factors = jnp.concatenate([factors, jnp.zeros((pad, count), jnp.float32)], 0).T
    terms = [factors[:, i : i + 1] * part[:count, :].astype(jnp.float32) for i, part in enumerate(parts)]
    merged = functools.reduce(jnp.add, terms)
    out[...] = jnp.concatenate([merged[h * rows : (h + 1) * rows] for h in range(heads)], 1).astype(out.dtype)


def project_kernel(steps, attended, partner, weight, *outs):
    tps = lax.axis_size("tp")
    share = outs[0].shape[1]
    here = jnp.where(lax.axis_index("role") == 0, partner[...].astype(jnp.float32), attended[...].astype(jnp.float32))
    here = here.astype(jnp.bfloat16)
    for d, out in zip(steps, outs):
        first = lax.rem(lax.axis_index("tp") + d, tps) * share
        columns = pl.ds(pl.multiple_of(first, LANES), share)
        out[...] = jnp.dot(here, weight[:, columns], preferred_element_type=jnp.float32).astype(out.dtype)


def per_device(kv_pages, send_list, wanted, lengths, tables, queries, new_kv, out_weight):
    stored = kv_pages[0, 0, 0]
    slots = stored.shape[0]
    groups, tps = lax.axis_size("group"), lax.axis_size("tp")
    held = max(1, KVH // tps)
    rows, wide = queries.shape[1], queries.shape[2]
    heads = wide // HD
    per_held = heads // held
    maxp = tables.shape[2]
    send = jnp.transpose(send_list, (2, 0, 1))
    def place(block, at):
        return jnp.pad(block, ((0, rows - block.shape[0]), (at, wide + LANES - at - block.shape[1])))

    high = lax.shift_right_logical(place(lengths, wide + maxp), 3)
    low = jnp.bitwise_and(place(lengths, wide + maxp + rows), 7)
    integers = place(tables[0], wide) + high + low
    qa = place(queries[0], 0) + integers.astype(jnp.bfloat16)
    def paired(value, k, to_decode):
        first, second = (0, groups) if to_decode else (groups, 0)
        pairs = [pair for i in range(groups) for pair in ((first + i, second + (i ^ k)), (second + i, first + i))]
        return lax.ppermute(value, ("role", "group"), pairs)

    asked = [paired(qa, k, False) for k in range(1, groups)]
    part_shape = jax.ShapeDtypeStruct((heads * rows + STATS, HD), jnp.float32)
    sent_shape = jax.ShapeDtypeStruct(part_shape.shape, jnp.bfloat16)
    vmem = pl.BlockSpec(memory_space=pltpu.VMEM)
    hbm = pl.BlockSpec(memory_space=pltpu.HBM)
    page_shape = stored.shape[1:]
    chosen_count = groups * PARTS
    read_count = -(-rows * maxp // CHUNK) * CHUNK
    lists = [send, wanted, tables[0], lengths]
    pinned = [pltpu.with_memory_space_constraint(x, pltpu.HBM) for x in lists + [stored]]
    smem = [pltpu.SMEM(x.shape, jnp.int32) for x in lists]
    reading = [pltpu.SMEM((slots + 1,), jnp.int32), pltpu.SMEM((2, read_count), jnp.int32)]
    mine, mine_sent, chosen, entries = pl.pallas_call(
        functools.partial(first_kernel, held, per_held, groups, maxp),
        out_shape=[
            part_shape,
            sent_shape,
            jax.ShapeDtypeStruct((chosen_count,) + page_shape, jnp.bfloat16),
            jax.ShapeDtypeStruct((chosen_count, LANES), jnp.float32),
        ],
        in_specs=[vmem] + [hbm] * 5,
        out_specs=[vmem] * 4,
        scratch_shapes=[
            pltpu.VMEM((read_count,) + page_shape, jnp.bfloat16),
            *smem,
            *reading,
            pltpu.SMEM((chosen_count + 1,), jnp.int32),
            pltpu.SMEM((chosen_count + 1,), jnp.int32),
            pltpu.SemaphoreType.DMA((len(lists),)),
            pltpu.SemaphoreType.DMA((chosen_count,)),
            pltpu.SemaphoreType.DMA((read_count,)),
        ],
        compiler_params=pltpu.CompilerParams(vmem_limit_bytes=20 * MIB),
        name="resident",
    )(qa, *pinned)
    count = groups - 1
    theirs = pl.pallas_call(
        functools.partial(second_kernel, held, per_held, maxp, count),
        out_shape=[sent_shape] * count,
        in_specs=[vmem] * (2 + count),
        out_specs=[vmem] * count,
        compiler_params=pltpu.CompilerParams(vmem_limit_bytes=16 * MIB),
        cost_estimate=pl.CostEstimate(flops=4 * 10**10, bytes_accessed=8 * MIB, transcendentals=10**6),
        name="owned",
    )(chosen, entries, *reversed(asked))
    qa, mine_sent, theirs = lax.optimization_barrier((qa, mine_sent, theirs))
    fresh = pl.pallas_call(
        functools.partial(fresh_kernel, held, per_held),
        out_shape=part_shape,
        in_specs=[vmem] * 2,
        out_specs=vmem,
        compiler_params=pltpu.CompilerParams(vmem_limit_bytes=8 * MIB),
        cost_estimate=pl.CostEstimate(flops=10**9, bytes_accessed=MIB, transcendentals=10**4),
        name="fresh",
    )(qa, new_kv[0])
    parts = [mine, fresh] + [paired(part, k, True) for k, part in enumerate([mine_sent, *theirs])][::-1]
    attended = pl.pallas_call(
        functools.partial(merge_kernel, heads, rows),
        out_shape=jax.ShapeDtypeStruct((rows, wide), jnp.bfloat16),
        in_specs=[vmem] * len(parts),
        out_specs=vmem,
        compiler_params=pltpu.CompilerParams(vmem_limit_bytes=8 * MIB),
        name="merge",
    )(*parts)
    partner = lax.ppermute(attended, "role", [(0, 1), (1, 0)])
    share = out_weight.shape[1] // tps

    def project(steps, dtype, name):
        return pl.pallas_call(
            functools.partial(project_kernel, steps),
            out_shape=[jax.ShapeDtypeStruct((rows, share), dtype)] * len(steps),
            in_specs=[vmem] * 3,
            out_specs=[vmem] * len(steps),
            compiler_params=pltpu.CompilerParams(vmem_limit_bytes=24 * MIB),
            cost_estimate=pl.CostEstimate(
                flops=len(steps) * 32 * wide * share, bytes_accessed=len(steps) * 2 * wide * share, transcendentals=0
            ),
            name=name,
        )(attended, partner, out_weight)

    steps = list(range(1, tps))
    sent = project(steps, jnp.bfloat16, "project")
    arrived = [lax.ppermute(part, "tp", [(i, (i + d) % tps) for i in range(tps)]) for d, part in zip(steps, sent)]
    own = project([0], jnp.float32, "project_own")[0]
    total = functools.reduce(jnp.add, [part.astype(jnp.float32) for part in arrived], own)
    return total.astype(jnp.bfloat16)[None]


def solution(mesh):
    return jax.shard_map(
        per_device,
        mesh=mesh,
        in_specs=(
            P("role", "group", "tp", None, None, None),
            P(),
            P(),
            P("group", None),
            P("group", None, None),
            P("group", None, "tp"),
            P("group", None, "tp"),
            P("tp", "role"),
        ),
        out_specs=P("group", None, ("role", "tp")),
        check_vma=False,
    )
```

```python
import functools
import math

import jax
import jax.numpy as jnp
from jax import lax
from jax.experimental import pallas as pl
from jax.experimental.pallas import tpu as pltpu
from jax.sharding import PartitionSpec as P

KVH = 8
HD = 128
CAP = 4
CAPP = 2
PRE_DEV = 8
LANES = 128
PAGE = 128
NEG = -1e30
FLOOR = -1e29
SCALE = 1.0 / math.sqrt(HD)
PARTS = CAP + CAPP
CHUNK = 8
STATIC = (1, 2, 3)
STATS = 16
MIB = 2**20


def dot(a, b, ca, cb):
    return lax.dot_general(a, b, (((ca,), (cb,)), ((), ())), preferred_element_type=jnp.float32)


def query_block(qa, held, per_held):
    q = qa[:, : held * per_held * HD].astype(jnp.float32)
    rows = q.shape[0]
    bands = []
    for j in range(held):
        heads = [q[:, (j * per_held + i) * HD : (j * per_held + i + 1) * HD] for i in range(per_held)]
        band = jnp.concatenate(heads, 0)
        blank = jnp.zeros_like(band)
        bands.append(jnp.concatenate([band if i == j else blank for i in range(held)], 1))
    return jnp.concatenate(bands, 0).astype(jnp.bfloat16)


def entry_rows(qa, held, per_held, maxp):
    rows = qa.shape[0]
    wide = held * per_held * HD
    aux = qa[:, wide : wide + LANES].astype(jnp.float32)
    lane = lax.broadcasted_iota(jnp.int32, (rows, LANES), 1) - maxp
    row = lax.broadcasted_iota(jnp.int32, (rows, LANES), 0)
    parts = jnp.where(lane == row, 8.0 * aux[:1], jnp.where(lane == row + rows, aux[:1], 0.0))
    length = jnp.sum(parts, 1, keepdims=True)
    turned = jnp.concatenate([jnp.where(lane == 0, length, aux)] * (held * per_held), 0).T
    first = lax.broadcasted_iota(jnp.int32, (maxp, 1), 0).astype(jnp.float32) * PAGE
    return turned[:maxp], jnp.clip(turned[maxp : maxp + 1] - first, 0.0, PAGE)


def lanes_of(page, first, held):
    return jnp.concatenate([page[:, (2 * j + first) * HD : (2 * j + first + 1) * HD] for j in range(held)], 1)


def pieces(x):
    high = x.astype(jnp.bfloat16).astype(jnp.float32)
    middle = (x - high).astype(jnp.bfloat16).astype(jnp.float32)
    return [high, middle, x - high - middle]


def write_part(out, acc, top, total, held, per_held):
    count = acc.shape[0]
    band = count // held
    out[:count, :] = jnp.concatenate(
        [acc[j * band : (j + 1) * band, j * HD : (j + 1) * HD] for j in range(held)], 0
    ).astype(out.dtype)
    rows = pieces(top) + pieces(total)
    block = jnp.concatenate(rows + [jnp.zeros((STATS - len(rows), count), jnp.float32)], 0)
    if count < LANES:
        block = jnp.concatenate([block, jnp.zeros((STATS, LANES - count), jnp.float32)], 1)
    out[count:, :] = block.astype(out.dtype)


def owner_part(qa, pages, entries, out, held, per_held, maxp):
    q = query_block(qa, held, per_held)
    tab, cnt = entry_rows(qa, held, per_held, maxp)
    count = q.shape[0]
    token = lax.broadcasted_iota(jnp.int32, (PAGE, count), 0).astype(jnp.float32)
    masks = []
    for c in range(PARTS):
        valid = jnp.sum(jnp.where(tab == entries[c : c + 1, :count], cnt, 0.0), 0, keepdims=True)
        masks.append(token < valid)
    mask = jnp.concatenate(masks, 0)
    keys = jnp.concatenate([lanes_of(pages.at[c], 0, held) for c in range(PARTS)], 0)
    values = jnp.concatenate([lanes_of(pages.at[c], 1, held) for c in range(PARTS)], 0)
    s = jnp.where(mask, dot(keys, q, 1, 1) * SCALE, NEG)
    top = jnp.max(s, 0, keepdims=True)
    p = jnp.where(mask, jnp.exp(s - top), 0.0)
    total = jnp.sum(p, 0, keepdims=True)
    acc = dot(p.astype(jnp.bfloat16), values, 0, 0)
    write_part(out, acc, top, total, held, per_held)


def resident_part(span, qa, lists_ready, send, tables, lengths, maxp, group, kv, pages, flags, listed, sems, out, held, per_held):
    rows = qa.shape[0]
    slots = kv.shape[0]
    q = query_block(qa, held, per_held)
    count = q.shape[0]
    lane_row = lax.rem(lax.broadcasted_iota(jnp.int32, (1, count), 1), rows)
    token = lax.broadcasted_iota(jnp.int32, (PAGE, count), 0)
    for i in range(slots):
        flags[i] = 0

    lists_ready()
    for o in range(send.shape[1]):
        for i in range(send.shape[2]):
            flags[jnp.where(send[1, o, i] == group, send[2, o, i], slots)] = 1

    def page_copy(slot, i):
        return pltpu.make_async_copy(kv.at[slot], pages.at[i], sems.at[i])

    listed_count = jnp.int32(0)
    for r in range(*span):
        length = lengths[0, r]
        for e in range(maxp):
            slot = tables[r, e]
            tokens = jnp.minimum(length - e * PAGE, PAGE)
            here = jnp.logical_and(slot < slots, flags[jnp.minimum(slot, slots - 1)] == 0)
            needed = jnp.logical_and(tokens > 0, here)
            listed[0, listed_count] = r
            listed[1, listed_count] = tokens

            @pl.when(needed)
            def _(slot=slot, at=listed_count):
                page_copy(slot, at).start()

            listed_count = listed_count + needed.astype(jnp.int32)
    chunks = jnp.maximum((listed_count + CHUNK - 1) // CHUNK, STATIC[0])

    def fill(i, _):
        listed[0, i] = 0
        listed[1, i] = 0
        page_copy(0, i).start()
        return 0

    lax.fori_loop(listed_count, chunks * CHUNK, fill, 0)

    def score(c):
        first = c * CHUNK
        masks = []
        for i in range(CHUNK):
            masks.append(token < jnp.where(lane_row == listed[0, first + i], listed[1, first + i], 0))
        for i in range(CHUNK):
            page_copy(0, first + i).wait()
        keys = jnp.concatenate([lanes_of(pages.at[first + i], 0, held) for i in range(CHUNK)], 0)
        return jnp.where(jnp.concatenate(masks, 0), dot(keys, q, 1, 1) * SCALE, NEG)

    def weigh(c, s, top):
        p = jnp.exp(s - top)
        values = jnp.concatenate([lanes_of(pages.at[c * CHUNK + i], 1, held) for i in range(CHUNK)], 0)
        return jnp.sum(p, 0, keepdims=True), dot(p.astype(jnp.bfloat16), values, 0, 0)

    floor = jnp.full((1, count), FLOOR, jnp.float32)

    def straight(number):
        scores = [score(c) for c in range(number)]
        top = functools.reduce(jnp.maximum, [jnp.max(s, 0, keepdims=True) for s in scores], floor)
        terms = [weigh(c, s, top) for c, s in enumerate(scores)]
        total = functools.reduce(jnp.add, [t for t, _ in terms])
        acc = functools.reduce(jnp.add, [a for _, a in terms])
        write_part(out, acc, top, total, held, per_held)

    def step(c, carry):
        top, total, acc = carry
        s = score(c)
        new_top = jnp.maximum(top, jnp.max(s, 0, keepdims=True))
        fade = jnp.exp(top - new_top)
        more, part = weigh(c, s, new_top)
        return new_top, total * fade + more, acc * jnp.broadcast_to(fade, (8, count)).T[:, :1] + part

    for number in STATIC:

        @pl.when(chunks == number)
        def _(number=number):
            straight(number)

    @pl.when(chunks > STATIC[-1])
    def _():
        start = (floor, jnp.zeros((1, count), jnp.float32), jnp.zeros((count, held * HD), jnp.float32))
        top, total, acc = lax.fori_loop(0, chunks, step, start)
        write_part(out, acc, top, total, held, per_held)


def list_pages(send, wanted, owner, target, slots, page_list, slot_list, base):
    for c in range(PARTS):
        page_list[base + c] = 0
        slot_list[base + c] = -1
    at = jnp.int32(base)
    for i in range(send.shape[2]):
        hit = send[1, owner, i] == target
        page_list[at] = send[0, owner, i]
        slot_list[at] = jnp.where(hit, send[2, owner, i], -1)
        at = at + hit.astype(jnp.int32)
    at = jnp.int32(base + CAP)
    page_list[at] = 0
    slot_list[at] = -1
    for i in range(wanted.shape[1]):
        page = wanted[target, i] - owner * PRE_DEV
        hit = jnp.logical_and(page >= 0, page < PRE_DEV)
        page_list[at] = jnp.where(hit, page, 0)
        slot_list[at] = jnp.where(hit, slots + i, -1)
        at = at + hit.astype(jnp.int32)


def copy_lists(pairs, sems):
    copies = [pltpu.make_async_copy(a, b, sems.at[i]) for i, (a, b) in enumerate(pairs)]
    for copy in copies:
        copy.start()

    def ready():
        for copy in copies:
            copy.wait()

    return ready


def first_kernel(span, held, per_held, groups, maxp, qa, send_hbm, wanted_hbm, tables_hbm, lengths_hbm, kv, *refs):
    out, sent, chosen, entries, pages, send, wanted, tables, lengths = refs[:9]
    flags, listed, page_list, slot_list, list_sems, chosen_sems, sems = refs[9:]
    group = lax.axis_index("group")
    prefill = lax.axis_index("role") == 0
    lists = ((send_hbm, send), (wanted_hbm, wanted), (tables_hbm, tables), (lengths_hbm, lengths))
    lists_ready = copy_lists(lists, list_sems)

    @pl.when(prefill)
    def _():
        lists_ready()
        copies = []
        for k in range(groups):
            target = lax.bitwise_xor(group, k)
            list_pages(send, wanted, group, target, kv.shape[0], page_list, slot_list, k * PARTS)
            for c in range(PARTS):
                at = k * PARTS + c
                copy = pltpu.make_async_copy(kv.at[page_list[at]], chosen.at[at], chosen_sems.at[at])
                copy.start()
                copies.append(copy)
                entry = slot_list[at].astype(jnp.float32)
                entries[at : at + 1, :] = jnp.full((1, LANES), entry, jnp.float32)
        for copy in copies[:PARTS]:
            copy.wait()
        owner_part(qa, chosen.at[pl.ds(0, PARTS)], entries[:PARTS, :], sent, held, per_held, maxp)
        for copy in copies[PARTS:]:
            copy.wait()

    @pl.when(jnp.logical_not(prefill))
    def _():
        resident_part(
            span, qa, lists_ready, send, tables, lengths, maxp, group, kv, pages, flags, listed, sems, out, held, per_held
        )


def fresh_part(qa, new_kv, out, held, per_held):
    rows = qa.shape[0]
    q = query_block(qa, held, per_held)
    count = q.shape[0]
    lane_row = lax.rem(lax.broadcasted_iota(jnp.int32, (1, count), 1), rows)
    fresh = new_kv[...].astype(jnp.float32)
    fresh = jnp.concatenate([fresh, jnp.zeros_like(fresh)], 0).astype(jnp.bfloat16)
    mask = lax.broadcasted_iota(jnp.int32, (2 * rows, count), 0) == lane_row
    s = jnp.where(mask, dot(lanes_of(fresh, 0, held), q, 1, 1) * SCALE, NEG)
    top = jnp.max(s, 0, keepdims=True)
    p = jnp.exp(s - top)
    acc = dot(p.astype(jnp.bfloat16), lanes_of(fresh, 1, held), 0, 0)
    write_part(out, acc, top, jnp.sum(p, 0, keepdims=True), held, per_held)


def third_kernel(span, held, per_held, maxp, qa, new_kv, send_hbm, tables_hbm, lengths_hbm, kv, *refs):
    out, fresh, pages, send, tables, lengths, flags, listed, list_sems, sems = refs
    group = lax.axis_index("group")

    @pl.when(lax.axis_index("role") == 1)
    def _():
        lists_ready = copy_lists(((send_hbm, send), (tables_hbm, tables), (lengths_hbm, lengths)), list_sems)
        fresh_part(qa, new_kv, fresh, held, per_held)
        resident_part(
            span, qa, lists_ready, send, tables, lengths, maxp, group, kv, pages, flags, listed, sems, out, held, per_held
        )


def second_kernel(held, per_held, maxp, count, chosen, entries, *refs):
    qas, outs = refs[:count][::-1], refs[count:]

    @pl.when(lax.axis_index("role") == 0)
    def _():
        for k in range(count):
            at = (k + 1) * PARTS
            owner_part(
                qas[k], chosen.at[pl.ds(at, PARTS)], entries[at : at + PARTS, :], outs[k], held, per_held, maxp
            )


def merge_kernel(heads, rows, *refs):
    parts, out = refs[:-1], refs[-1]
    count = heads * rows
    pad = -len(parts) % 8
    stats = [part[count:, :].astype(jnp.float32)[:, :count] for part in parts]
    tops = jnp.concatenate([s[0:1] + (s[1:2] + s[2:3]) for s in stats], 0)
    totals = jnp.concatenate([s[3:4] + (s[4:5] + s[5:6]) for s in stats], 0)
    factors = jnp.exp(tops - jnp.max(tops, 0, keepdims=True))
    factors = factors / jnp.sum(factors * totals, 0, keepdims=True)
    factors = jnp.concatenate([factors, jnp.zeros((pad, count), jnp.float32)], 0).T
    terms = [factors[:, i : i + 1] * part[:count, :].astype(jnp.float32) for i, part in enumerate(parts)]
    merged = functools.reduce(jnp.add, terms)
    out[...] = jnp.concatenate([merged[h * rows : (h + 1) * rows] for h in range(heads)], 1).astype(out.dtype)


def project_kernel(steps, attended, partner, weight, *outs):
    tps = lax.axis_size("tp")
    share = outs[0].shape[1]
    here = jnp.where(lax.axis_index("role") == 0, partner[...].astype(jnp.float32), attended[...].astype(jnp.float32))
    here = here.astype(jnp.bfloat16)
    for d, out in zip(steps, outs):
        first = lax.rem(lax.axis_index("tp") + d, tps) * share
        columns = pl.ds(pl.multiple_of(first, LANES), share)
        out[...] = jnp.dot(here, weight[:, columns], preferred_element_type=jnp.float32).astype(out.dtype)


def per_device(kv_pages, send_list, wanted, lengths, tables, queries, new_kv, out_weight):
    stored = kv_pages[0, 0, 0]
    slots = stored.shape[0]
    groups, tps = lax.axis_size("group"), lax.axis_size("tp")
    held = max(1, KVH // tps)
    rows, wide = queries.shape[1], queries.shape[2]
    heads = wide // HD
    per_held = heads // held
    maxp = tables.shape[2]
    send = jnp.transpose(send_list, (2, 0, 1))
    def place(block, at):
        return jnp.pad(block, ((0, rows - block.shape[0]), (at, wide + LANES - at - block.shape[1])))

    high = lax.shift_right_logical(place(lengths, wide + maxp), 3)
    low = jnp.bitwise_and(place(lengths, wide + maxp + rows), 7)
    integers = place(tables[0], wide) + high + low
    qa = place(queries[0], 0) + integers.astype(jnp.bfloat16)
    def paired(value, k, to_decode):
        first, second = (0, groups) if to_decode else (groups, 0)
        pairs = [pair for i in range(groups) for pair in ((first + i, second + (i ^ k)), (second + i, first + i))]
        return lax.ppermute(value, ("role", "group"), pairs)

    asked = [paired(qa, k, False) for k in range(1, groups)]
    part_shape = jax.ShapeDtypeStruct((heads * rows + STATS, HD), jnp.float32)
    sent_shape = jax.ShapeDtypeStruct(part_shape.shape, jnp.bfloat16)
    vmem = pl.BlockSpec(memory_space=pltpu.VMEM)
    hbm = pl.BlockSpec(memory_space=pltpu.HBM)
    page_shape = stored.shape[1:]
    chosen_count = groups * PARTS
    cut = (rows + 1) // 2
    read_count = -(-cut * maxp // CHUNK) * CHUNK
    lists = [send, wanted, tables[0], lengths]
    pinned = [pltpu.with_memory_space_constraint(x, pltpu.HBM) for x in lists + [stored]]
    smem = [pltpu.SMEM(x.shape, jnp.int32) for x in lists]
    reading = [pltpu.SMEM((slots + 1,), jnp.int32), pltpu.SMEM((2, read_count), jnp.int32)]
    mine, mine_sent, chosen, entries = pl.pallas_call(
        functools.partial(first_kernel, (0, cut), held, per_held, groups, maxp),
        out_shape=[
            part_shape,
            sent_shape,
            jax.ShapeDtypeStruct((chosen_count,) + page_shape, jnp.bfloat16),
            jax.ShapeDtypeStruct((chosen_count, LANES), jnp.float32),
        ],
        in_specs=[vmem] + [hbm] * 5,
        out_specs=[vmem] * 4,
        scratch_shapes=[
            pltpu.VMEM((read_count,) + page_shape, jnp.bfloat16),
            *smem,
            *reading,
            pltpu.SMEM((chosen_count + 1,), jnp.int32),
            pltpu.SMEM((chosen_count + 1,), jnp.int32),
            pltpu.SemaphoreType.DMA((len(lists),)),
            pltpu.SemaphoreType.DMA((chosen_count,)),
            pltpu.SemaphoreType.DMA((read_count,)),
        ],
        compiler_params=pltpu.CompilerParams(vmem_limit_bytes=20 * MIB),
        name="resident",
    )(qa, *pinned)
    count = groups - 1
    theirs = pl.pallas_call(
        functools.partial(second_kernel, held, per_held, maxp, count),
        out_shape=[sent_shape] * count,
        in_specs=[vmem] * (2 + count),
        out_specs=[vmem] * count,
        compiler_params=pltpu.CompilerParams(vmem_limit_bytes=16 * MIB),
        cost_estimate=pl.CostEstimate(flops=4 * 10**9, bytes_accessed=8 * MIB, transcendentals=10**6),
        name="owned",
    )(chosen, entries, *reversed(asked))
    qa, mine_sent, theirs = lax.optimization_barrier((qa, mine_sent, theirs))
    rest, fresh = pl.pallas_call(
        functools.partial(third_kernel, (cut, rows), held, per_held, maxp),
        out_shape=[part_shape] * 2,
        in_specs=[vmem] * 2 + [hbm] * 4,
        out_specs=[vmem] * 2,
        scratch_shapes=[
            pltpu.VMEM((read_count,) + page_shape, jnp.bfloat16),
            smem[0],
            smem[2],
            smem[3],
            *reading,
            pltpu.SemaphoreType.DMA((3,)),
            pltpu.SemaphoreType.DMA((read_count,)),
        ],
        compiler_params=pltpu.CompilerParams(vmem_limit_bytes=20 * MIB),
        name="resident_rest",
    )(qa, new_kv[0], pinned[0], *pinned[2:])
    parts = [mine, rest, fresh] + [paired(part, k, True) for k, part in enumerate([mine_sent, *theirs])][::-1]
    attended = pl.pallas_call(
        functools.partial(merge_kernel, heads, rows),
        out_shape=jax.ShapeDtypeStruct((rows, wide), jnp.bfloat16),
        in_specs=[vmem] * len(parts),
        out_specs=vmem,
        compiler_params=pltpu.CompilerParams(vmem_limit_bytes=8 * MIB),
        name="merge",
    )(*parts)
    partner = lax.ppermute(attended, "role", [(0, 1), (1, 0)])
    share = out_weight.shape[1] // tps

    def project(steps, dtype, name):
        return pl.pallas_call(
            functools.partial(project_kernel, steps),
            out_shape=[jax.ShapeDtypeStruct((rows, share), dtype)] * len(steps),
            in_specs=[vmem] * 3,
            out_specs=[vmem] * len(steps),
            compiler_params=pltpu.CompilerParams(vmem_limit_bytes=24 * MIB),
            cost_estimate=pl.CostEstimate(
                flops=len(steps) * 32 * wide * share, bytes_accessed=len(steps) * 2 * wide * share, transcendentals=0
            ),
            name=name,
        )(attended, partner, out_weight)

    steps = list(range(1, tps))
    sent = project(steps, jnp.bfloat16, "project")
    arrived = [lax.ppermute(part, "tp", [(i, (i + d) % tps) for i in range(tps)]) for d, part in zip(steps, sent)]
    own = project([0], jnp.float32, "project_own")[0]
    total = functools.reduce(jnp.add, [part.astype(jnp.float32) for part in arrived], own)
    return total.astype(jnp.bfloat16)[None]


def solution(mesh):
    return jax.shard_map(
        per_device,
        mesh=mesh,
        in_specs=(
            P("role", "group", "tp", None, None, None),
            P(),
            P(),
            P("group", None),
            P("group", None, None),
            P("group", None, "tp"),
            P("group", None, "tp"),
            P("tp", "role"),
        ),
        out_specs=P("group", None, ("role", "tp")),
        check_vma=False,
    )
```

```python
import functools
import math

import jax
import jax.numpy as jnp
from jax import lax
from jax.experimental import pallas as pl
from jax.experimental.pallas import tpu as pltpu
from jax.sharding import PartitionSpec as P

KVH = 8
HD = 128
CAP = 4
CAPP = 2
PRE_DEV = 8
LANES = 128
PAGE = 128
NEG = -1e30
FLOOR = -1e29
SCALE = 1.0 / math.sqrt(HD)
PARTS = CAP + CAPP
CHUNK = 8
STATIC = (2, 3, 4, 5)
STATS = 16
MIB = 2**20


def dot(a, b, ca, cb):
    return lax.dot_general(a, b, (((ca,), (cb,)), ((), ())), preferred_element_type=jnp.float32)


def query_block(qa, held, per_held):
    q = qa[:, : held * per_held * HD].astype(jnp.float32)
    rows = q.shape[0]
    bands = []
    for j in range(held):
        heads = [q[:, (j * per_held + i) * HD : (j * per_held + i + 1) * HD] for i in range(per_held)]
        band = jnp.concatenate(heads, 0)
        blank = jnp.zeros_like(band)
        bands.append(jnp.concatenate([band if i == j else blank for i in range(held)], 1))
    return jnp.concatenate(bands, 0).astype(jnp.bfloat16)


def entry_rows(qa, held, per_held, maxp):
    rows = qa.shape[0]
    wide = held * per_held * HD
    aux = qa[:, wide : wide + LANES].astype(jnp.float32)
    lane = lax.broadcasted_iota(jnp.int32, (rows, LANES), 1) - maxp
    row = lax.broadcasted_iota(jnp.int32, (rows, LANES), 0)
    parts = jnp.where(lane == row, 8.0 * aux[:1], jnp.where(lane == row + rows, aux[:1], 0.0))
    length = jnp.sum(parts, 1, keepdims=True)
    turned = jnp.concatenate([jnp.where(lane == 0, length, aux)] * (held * per_held), 0).T
    first = lax.broadcasted_iota(jnp.int32, (maxp, 1), 0).astype(jnp.float32) * PAGE
    return turned[:maxp], jnp.clip(turned[maxp : maxp + 1] - first, 0.0, PAGE)


def lanes_of(page, first, held):
    return jnp.concatenate([page[:, (2 * j + first) * HD : (2 * j + first + 1) * HD] for j in range(held)], 1)


def pieces(x):
    high = x.astype(jnp.bfloat16).astype(jnp.float32)
    middle = (x - high).astype(jnp.bfloat16).astype(jnp.float32)
    return [high, middle, x - high - middle]


def write_part(out, acc, top, total, held, per_held):
    count = acc.shape[0]
    band = count // held
    out[:count, :] = jnp.concatenate(
        [acc[j * band : (j + 1) * band, j * HD : (j + 1) * HD] for j in range(held)], 0
    ).astype(out.dtype)
    rows = pieces(top) + pieces(total)
    block = jnp.concatenate(rows + [jnp.zeros((STATS - len(rows), count), jnp.float32)], 0)
    if count < LANES:
        block = jnp.concatenate([block, jnp.zeros((STATS, LANES - count), jnp.float32)], 1)
    out[count:, :] = block.astype(out.dtype)


def owner_part(qa, pages, entries, out, held, per_held, maxp):
    q = query_block(qa, held, per_held)
    tab, cnt = entry_rows(qa, held, per_held, maxp)
    count = q.shape[0]
    token = lax.broadcasted_iota(jnp.int32, (PAGE, count), 0).astype(jnp.float32)
    masks = []
    for c in range(PARTS):
        valid = jnp.sum(jnp.where(tab == entries[c : c + 1, :count], cnt, 0.0), 0, keepdims=True)
        masks.append(token < valid)
    mask = jnp.concatenate(masks, 0)
    keys = jnp.concatenate([lanes_of(pages.at[c], 0, held) for c in range(PARTS)], 0)
    values = jnp.concatenate([lanes_of(pages.at[c], 1, held) for c in range(PARTS)], 0)
    s = jnp.where(mask, dot(keys, q, 1, 1) * SCALE, NEG)
    top = jnp.max(s, 0, keepdims=True)
    p = jnp.where(mask, jnp.exp(s - top), 0.0)
    total = jnp.sum(p, 0, keepdims=True)
    acc = dot(p.astype(jnp.bfloat16), values, 0, 0)
    write_part(out, acc, top, total, held, per_held)


def fetch_pages(rows, lists_ready, send, tables, lengths, maxp, group, kv, pages, valid, flags, sems):
    slots = kv.shape[0]
    lane_row = lax.rem(lax.broadcasted_iota(jnp.int32, (1, LANES), 1), rows)
    for i in range(slots):
        flags[i] = 0
    lists_ready()
    for o in range(send.shape[1]):
        for i in range(send.shape[2]):
            flags[jnp.where(send[1, o, i] == group, send[2, o, i], slots)] = 1

    def page_copy(slot, i):
        return pltpu.make_async_copy(kv.at[slot], pages.at[i], sems.at[i])

    found = jnp.int32(0)
    for r in range(rows):
        length = lengths[0, r]
        for e in range(maxp):
            slot = tables[r, e]
            tokens = jnp.minimum(length - e * PAGE, PAGE)
            here = jnp.logical_and(slot < slots, flags[jnp.minimum(slot, slots - 1)] == 0)
            needed = jnp.logical_and(tokens > 0, here)

            @pl.when(needed)
            def _(slot=slot, r=r, at=found, tokens=tokens):
                page_copy(slot, at).start()
                valid[pl.ds(at, 1), :] = jnp.where(lane_row == r, tokens.astype(jnp.float32), 0.0)

            found = found + needed.astype(jnp.int32)
    chunks = jnp.maximum((found + CHUNK - 1) // CHUNK, STATIC[0])

    def fill(i, _):
        page_copy(0, i).start()
        valid[pl.ds(i, 1), :] = jnp.zeros((1, LANES), jnp.float32)
        return 0

    lax.fori_loop(found, chunks * CHUNK, fill, 0)
    last = valid.shape[0] - 1
    valid[last : last + 1, :] = jnp.full((1, LANES), chunks.astype(jnp.float32), jnp.float32)

    def wait(c, _):
        for i in range(CHUNK):
            page_copy(0, c * CHUNK + i).wait()
        return 0

    lax.fori_loop(0, chunks, wait, 0)


def resident_part(qa, pages, valid, out, held, per_held):
    q = query_block(qa, held, per_held)
    count = q.shape[0]
    token = lax.broadcasted_iota(jnp.int32, (PAGE, count), 0).astype(jnp.float32)
    floor = jnp.full((1, count), FLOOR, jnp.float32)
    last = valid.shape[0] - 1
    chunks = jnp.max(valid[last : last + 1, :]).astype(jnp.int32)

    def score(c):
        first = c * CHUNK
        masks = [token < valid[pl.ds(first + i, 1), :][:, :count] for i in range(CHUNK)]
        keys = jnp.concatenate([lanes_of(pages.at[first + i], 0, held) for i in range(CHUNK)], 0)
        return jnp.where(jnp.concatenate(masks, 0), dot(keys, q, 1, 1) * SCALE, NEG)

    def weigh(c, s, top):
        p = jnp.exp(s - top)
        values = jnp.concatenate([lanes_of(pages.at[c * CHUNK + i], 1, held) for i in range(CHUNK)], 0)
        return jnp.sum(p, 0, keepdims=True), dot(p.astype(jnp.bfloat16), values, 0, 0)

    def straight(number):
        scores = [score(c) for c in range(number)]
        top = functools.reduce(jnp.maximum, [jnp.max(s, 0, keepdims=True) for s in scores], floor)
        terms = [weigh(c, s, top) for c, s in enumerate(scores)]
        total = functools.reduce(jnp.add, [t for t, _ in terms])
        acc = functools.reduce(jnp.add, [a for _, a in terms])
        write_part(out, acc, top, total, held, per_held)

    def step(c, carry):
        top, total, acc = carry
        s = score(c)
        new_top = jnp.maximum(top, jnp.max(s, 0, keepdims=True))
        fade = jnp.exp(top - new_top)
        more, part = weigh(c, s, new_top)
        return new_top, total * fade + more, acc * jnp.broadcast_to(fade, (8, count)).T[:, :1] + part

    for number in STATIC:

        @pl.when(chunks == number)
        def _(number=number):
            straight(number)

    @pl.when(chunks > STATIC[-1])
    def _():
        start = (floor, jnp.zeros((1, count), jnp.float32), jnp.zeros((count, held * HD), jnp.float32))
        top, total, acc = lax.fori_loop(0, chunks, step, start)
        write_part(out, acc, top, total, held, per_held)


def list_pages(send, wanted, owner, target, slots, page_list, slot_list, base):
    for c in range(PARTS):
        page_list[base + c] = 0
        slot_list[base + c] = -1
    at = jnp.int32(base)
    for i in range(send.shape[2]):
        hit = send[1, owner, i] == target
        page_list[at] = send[0, owner, i]
        slot_list[at] = jnp.where(hit, send[2, owner, i], -1)
        at = at + hit.astype(jnp.int32)
    at = jnp.int32(base + CAP)
    page_list[at] = 0
    slot_list[at] = -1
    for i in range(wanted.shape[1]):
        page = wanted[target, i] - owner * PRE_DEV
        hit = jnp.logical_and(page >= 0, page < PRE_DEV)
        page_list[at] = jnp.where(hit, page, 0)
        slot_list[at] = jnp.where(hit, slots + i, -1)
        at = at + hit.astype(jnp.int32)


def copy_lists(pairs, sems):
    copies = [pltpu.make_async_copy(a, b, sems.at[i]) for i, (a, b) in enumerate(pairs)]
    for copy in copies:
        copy.start()

    def ready():
        for copy in copies:
            copy.wait()

    return ready


def first_kernel(held, per_held, groups, maxp, qa, send_hbm, wanted_hbm, tables_hbm, lengths_hbm, kv, *refs):
    sent, chosen, entries, valid, send, wanted, tables, lengths = refs[:8]
    flags, page_list, slot_list, list_sems, sems = refs[8:]
    group = lax.axis_index("group")
    prefill = lax.axis_index("role") == 0
    lists = ((send_hbm, send), (wanted_hbm, wanted), (tables_hbm, tables), (lengths_hbm, lengths))
    lists_ready = copy_lists(lists, list_sems)

    @pl.when(prefill)
    def _():
        lists_ready()
        copies = []
        for k in range(groups):
            target = lax.bitwise_xor(group, k)
            list_pages(send, wanted, group, target, kv.shape[0], page_list, slot_list, k * PARTS)
            for c in range(PARTS):
                at = k * PARTS + c
                copy = pltpu.make_async_copy(kv.at[page_list[at]], chosen.at[at], sems.at[at])
                copy.start()
                copies.append(copy)
                entry = slot_list[at].astype(jnp.float32)
                entries[at : at + 1, :] = jnp.full((1, LANES), entry, jnp.float32)
        for copy in copies[:PARTS]:
            copy.wait()
        owner_part(qa, chosen.at[pl.ds(0, PARTS)], entries[:PARTS, :], sent, held, per_held, maxp)
        for copy in copies[PARTS:]:
            copy.wait()

    @pl.when(jnp.logical_not(prefill))
    def _():
        fetch_pages(qa.shape[0], lists_ready, send, tables, lengths, maxp, group, kv, chosen, valid, flags, sems)


def fresh_part(qa, new_kv, out, held, per_held):
    rows = qa.shape[0]
    q = query_block(qa, held, per_held)
    count = q.shape[0]
    lane_row = lax.rem(lax.broadcasted_iota(jnp.int32, (1, count), 1), rows)
    fresh = new_kv[...].astype(jnp.float32)
    fresh = jnp.concatenate([fresh, jnp.zeros_like(fresh)], 0).astype(jnp.bfloat16)
    mask = lax.broadcasted_iota(jnp.int32, (2 * rows, count), 0) == lane_row
    s = jnp.where(mask, dot(lanes_of(fresh, 0, held), q, 1, 1) * SCALE, NEG)
    top = jnp.max(s, 0, keepdims=True)
    p = jnp.exp(s - top)
    acc = dot(p.astype(jnp.bfloat16), lanes_of(fresh, 1, held), 0, 0)
    write_part(out, acc, top, jnp.sum(p, 0, keepdims=True), held, per_held)


def third_kernel(held, per_held, qa, new_kv, pages, valid, out, fresh):
    @pl.when(lax.axis_index("role") == 1)
    def _():
        fresh_part(qa, new_kv, fresh, held, per_held)
        resident_part(qa, pages, valid, out, held, per_held)


def second_kernel(held, per_held, maxp, count, chosen, entries, *refs):
    qas, outs = refs[:count][::-1], refs[count:]

    @pl.when(lax.axis_index("role") == 0)
    def _():
        for k in range(count):
            at = (k + 1) * PARTS
            owner_part(
                qas[k], chosen.at[pl.ds(at, PARTS)], entries[at : at + PARTS, :], outs[k], held, per_held, maxp
            )


def merge_kernel(heads, rows, *refs):
    parts, out = refs[:-1], refs[-1]
    count = heads * rows
    pad = -len(parts) % 8
    stats = [part[count:, :].astype(jnp.float32)[:, :count] for part in parts]
    tops = jnp.concatenate([s[0:1] + (s[1:2] + s[2:3]) for s in stats], 0)
    totals = jnp.concatenate([s[3:4] + (s[4:5] + s[5:6]) for s in stats], 0)
    factors = jnp.exp(tops - jnp.max(tops, 0, keepdims=True))
    factors = factors / jnp.sum(factors * totals, 0, keepdims=True)
    factors = jnp.concatenate([factors, jnp.zeros((pad, count), jnp.float32)], 0).T
    terms = [factors[:, i : i + 1] * part[:count, :].astype(jnp.float32) for i, part in enumerate(parts)]
    merged = functools.reduce(jnp.add, terms)
    out[...] = jnp.concatenate([merged[h * rows : (h + 1) * rows] for h in range(heads)], 1).astype(out.dtype)


def project_kernel(steps, attended, partner, weight, *outs):
    tps = lax.axis_size("tp")
    share = outs[0].shape[1]
    here = jnp.where(lax.axis_index("role") == 0, partner[...].astype(jnp.float32), attended[...].astype(jnp.float32))
    here = here.astype(jnp.bfloat16)
    for d, out in zip(steps, outs):
        first = lax.rem(lax.axis_index("tp") + d, tps) * share
        columns = pl.ds(pl.multiple_of(first, LANES), share)
        out[...] = jnp.dot(here, weight[:, columns], preferred_element_type=jnp.float32).astype(out.dtype)


def per_device(kv_pages, send_list, wanted, lengths, tables, queries, new_kv, out_weight):
    stored = kv_pages[0, 0, 0]
    slots = stored.shape[0]
    groups, tps = lax.axis_size("group"), lax.axis_size("tp")
    held = max(1, KVH // tps)
    rows, wide = queries.shape[1], queries.shape[2]
    heads = wide // HD
    per_held = heads // held
    maxp = tables.shape[2]
    send = jnp.transpose(send_list, (2, 0, 1))
    def place(block, at):
        return jnp.pad(block, ((0, rows - block.shape[0]), (at, wide + LANES - at - block.shape[1])))

    high = lax.shift_right_logical(place(lengths, wide + maxp), 3)
    low = jnp.bitwise_and(place(lengths, wide + maxp + rows), 7)
    integers = place(tables[0], wide) + high + low
    qa = place(queries[0], 0) + integers.astype(jnp.bfloat16)
    def paired(value, k, to_decode):
        first, second = (0, groups) if to_decode else (groups, 0)
        pairs = [pair for i in range(groups) for pair in ((first + i, second + (i ^ k)), (second + i, first + i))]
        return lax.ppermute(value, ("role", "group"), pairs)

    asked = [paired(qa, k, False) for k in range(1, groups)]
    part_shape = jax.ShapeDtypeStruct((heads * rows + STATS, HD), jnp.float32)
    sent_shape = jax.ShapeDtypeStruct(part_shape.shape, jnp.bfloat16)
    vmem = pl.BlockSpec(memory_space=pltpu.VMEM)
    hbm = pl.BlockSpec(memory_space=pltpu.HBM)
    page_shape = stored.shape[1:]
    chosen_count = groups * PARTS
    read_count = -(-rows * maxp // CHUNK) * CHUNK
    page_count = max(read_count, chosen_count)
    lists = [send, wanted, tables[0], lengths]
    pinned = [pltpu.with_memory_space_constraint(x, pltpu.HBM) for x in lists + [stored]]
    mine_sent, chosen, entries, valid = pl.pallas_call(
        functools.partial(first_kernel, held, per_held, groups, maxp),
        out_shape=[
            sent_shape,
            jax.ShapeDtypeStruct((page_count,) + page_shape, jnp.bfloat16),
            jax.ShapeDtypeStruct((chosen_count, LANES), jnp.float32),
            jax.ShapeDtypeStruct((read_count + 8, LANES), jnp.float32),
        ],
        in_specs=[vmem] + [hbm] * 5,
        out_specs=[vmem] * 4,
        scratch_shapes=[
            *[pltpu.SMEM(x.shape, jnp.int32) for x in lists],
            pltpu.SMEM((slots + 1,), jnp.int32),
            pltpu.SMEM((chosen_count + 1,), jnp.int32),
            pltpu.SMEM((chosen_count + 1,), jnp.int32),
            pltpu.SemaphoreType.DMA((len(lists),)),
            pltpu.SemaphoreType.DMA((page_count,)),
        ],
        compiler_params=pltpu.CompilerParams(vmem_limit_bytes=20 * MIB),
        name="resident",
    )(qa, *pinned)
    count = groups - 1
    theirs = pl.pallas_call(
        functools.partial(second_kernel, held, per_held, maxp, count),
        out_shape=[sent_shape] * count,
        in_specs=[vmem] * (2 + count),
        out_specs=[vmem] * count,
        compiler_params=pltpu.CompilerParams(vmem_limit_bytes=16 * MIB),
        cost_estimate=pl.CostEstimate(flops=4 * 10**10, bytes_accessed=8 * MIB, transcendentals=10**6),
        name="owned",
    )(chosen, entries, *reversed(asked))
    qa, mine_sent, theirs = lax.optimization_barrier((qa, mine_sent, theirs))
    mine, fresh = pl.pallas_call(
        functools.partial(third_kernel, held, per_held),
        out_shape=[part_shape] * 2,
        in_specs=[vmem] * 4,
        out_specs=[vmem] * 2,
        compiler_params=pltpu.CompilerParams(vmem_limit_bytes=16 * MIB),
        name="attend",
    )(qa, new_kv[0], chosen, valid)
    parts = [mine, fresh] + [paired(part, k, True) for k, part in enumerate([mine_sent, *theirs])][::-1]
    attended = pl.pallas_call(
        functools.partial(merge_kernel, heads, rows),
        out_shape=jax.ShapeDtypeStruct((rows, wide), jnp.bfloat16),
        in_specs=[vmem] * len(parts),
        out_specs=vmem,
        compiler_params=pltpu.CompilerParams(vmem_limit_bytes=8 * MIB),
        name="merge",
    )(*parts)
    partner = lax.ppermute(attended, "role", [(0, 1), (1, 0)])
    share = out_weight.shape[1] // tps

    def project(steps, dtype, name):
        return pl.pallas_call(
            functools.partial(project_kernel, steps),
            out_shape=[jax.ShapeDtypeStruct((rows, share), dtype)] * len(steps),
            in_specs=[vmem] * 3,
            out_specs=[vmem] * len(steps),
            compiler_params=pltpu.CompilerParams(vmem_limit_bytes=24 * MIB),
            cost_estimate=pl.CostEstimate(
                flops=len(steps) * 32 * wide * share, bytes_accessed=len(steps) * 2 * wide * share, transcendentals=0
            ),
            name=name,
        )(attended, partner, out_weight)

    steps = list(range(1, tps))
    sent = project(steps, jnp.bfloat16, "project")
    arrived = [lax.ppermute(part, "tp", [(i, (i + d) % tps) for i in range(tps)]) for d, part in zip(steps, sent)]
    own = project([0], jnp.float32, "project_own")[0]
    total = functools.reduce(jnp.add, [part.astype(jnp.float32) for part in arrived], own)
    return total.astype(jnp.bfloat16)[None]


def solution(mesh):
    return jax.shard_map(
        per_device,
        mesh=mesh,
        in_specs=(
            P("role", "group", "tp", None, None, None),
            P(),
            P(),
            P("group", None),
            P("group", None, None),
            P("group", None, "tp"),
            P("group", None, "tp"),
            P("tp", "role"),
        ),
        out_specs=P("group", None, ("role", "tp")),
        check_vma=False,
    )
```

```python
import functools
import math

import jax
import jax.numpy as jnp
from jax import lax
from jax.experimental import pallas as pl
from jax.experimental.pallas import tpu as pltpu
from jax.sharding import PartitionSpec as P

KVH = 8
HD = 128
CAP = 4
CAPP = 2
PRE_DEV = 8
LANES = 128
PAGE = 128
NEG = -1e30
FLOOR = -1e29
SCALE = 1.0 / math.sqrt(HD)
PARTS = CAP + CAPP
CHUNK = 8
STATIC = (2, 3, 4, 5)
STATS = 16
MIB = 2**20


def dot(a, b, ca, cb):
    return lax.dot_general(a, b, (((ca,), (cb,)), ((), ())), preferred_element_type=jnp.float32)


def query_block(qa, held, per_held):
    q = qa[:, : held * per_held * HD].astype(jnp.float32)
    rows = q.shape[0]
    bands = []
    for j in range(held):
        heads = [q[:, (j * per_held + i) * HD : (j * per_held + i + 1) * HD] for i in range(per_held)]
        band = jnp.concatenate(heads, 0)
        blank = jnp.zeros_like(band)
        bands.append(jnp.concatenate([band if i == j else blank for i in range(held)], 1))
    return jnp.concatenate(bands, 0).astype(jnp.bfloat16)


def entry_rows(qa, held, per_held, maxp):
    rows = qa.shape[0]
    wide = held * per_held * HD
    aux = qa[:, wide : wide + LANES].astype(jnp.float32)
    lane = lax.broadcasted_iota(jnp.int32, (rows, LANES), 1) - maxp
    row = lax.broadcasted_iota(jnp.int32, (rows, LANES), 0)
    parts = jnp.where(lane == row, 8.0 * aux[:1], jnp.where(lane == row + rows, aux[:1], 0.0))
    length = jnp.sum(parts, 1, keepdims=True)
    turned = jnp.concatenate([jnp.where(lane == 0, length, aux)] * (held * per_held), 0).T
    first = lax.broadcasted_iota(jnp.int32, (maxp, 1), 0).astype(jnp.float32) * PAGE
    return turned[:maxp], jnp.clip(turned[maxp : maxp + 1] - first, 0.0, PAGE)


def lanes_of(page, first, held):
    return jnp.concatenate([page[:, (2 * j + first) * HD : (2 * j + first + 1) * HD] for j in range(held)], 1)


def pieces(x):
    high = x.astype(jnp.bfloat16).astype(jnp.float32)
    middle = (x - high).astype(jnp.bfloat16).astype(jnp.float32)
    return [high, middle, x - high - middle]


def write_part(out, acc, top, total, held, per_held):
    count = acc.shape[0]
    band = count // held
    out[:count, :] = jnp.concatenate(
        [acc[j * band : (j + 1) * band, j * HD : (j + 1) * HD] for j in range(held)], 0
    ).astype(out.dtype)
    rows = pieces(top) + pieces(total)
    block = jnp.concatenate(rows + [jnp.zeros((STATS - len(rows), count), jnp.float32)], 0)
    if count < LANES:
        block = jnp.concatenate([block, jnp.zeros((STATS, LANES - count), jnp.float32)], 1)
    out[count:, :] = block.astype(out.dtype)


def owner_part(qa, pages, entries, out, held, per_held, maxp):
    q = query_block(qa, held, per_held)
    tab, cnt = entry_rows(qa, held, per_held, maxp)
    count = q.shape[0]
    token = lax.broadcasted_iota(jnp.int32, (PAGE, count), 0).astype(jnp.float32)
    masks = []
    for c in range(PARTS):
        valid = jnp.sum(jnp.where(tab == entries[c : c + 1, :count], cnt, 0.0), 0, keepdims=True)
        masks.append(token < valid)
    mask = jnp.concatenate(masks, 0)
    keys = jnp.concatenate([lanes_of(pages.at[c], 0, held) for c in range(PARTS)], 0)
    values = jnp.concatenate([lanes_of(pages.at[c], 1, held) for c in range(PARTS)], 0)
    s = jnp.where(mask, dot(keys, q, 1, 1) * SCALE, NEG)
    top = jnp.max(s, 0, keepdims=True)
    p = jnp.where(mask, jnp.exp(s - top), 0.0)
    total = jnp.sum(p, 0, keepdims=True)
    acc = dot(p.astype(jnp.bfloat16), values, 0, 0)
    write_part(out, acc, top, total, held, per_held)


def fetch_pages(rows, lists_ready, send, tables, lengths, maxp, group, kv, pages, valid, flags, sems):
    slots = kv.shape[0]
    lane_row = lax.rem(lax.broadcasted_iota(jnp.int32, (1, LANES), 1), rows)
    for i in range(slots):
        flags[i] = 0
    lists_ready()
    for o in range(send.shape[1]):
        for i in range(send.shape[2]):
            flags[jnp.where(send[1, o, i] == group, send[2, o, i], slots)] = 1

    def page_copy(slot, i):
        return pltpu.make_async_copy(kv.at[slot], pages.at[i], sems.at[i])

    found = jnp.int32(0)
    for r in range(rows):
        length = lengths[0, r]
        for e in range(maxp):
            slot = tables[r, e]
            tokens = jnp.minimum(length - e * PAGE, PAGE)
            here = jnp.logical_and(slot < slots, flags[jnp.minimum(slot, slots - 1)] == 0)
            needed = jnp.logical_and(tokens > 0, here)

            @pl.when(needed)
            def _(slot=slot, r=r, at=found, tokens=tokens):
                page_copy(slot, at).start()
                valid[pl.ds(at, 1), :] = jnp.where(lane_row == r, tokens.astype(jnp.float32), 0.0)

            found = found + needed.astype(jnp.int32)
    chunks = jnp.maximum((found + CHUNK - 1) // CHUNK, STATIC[0])

    def fill(i, _):
        page_copy(0, i).start()
        valid[pl.ds(i, 1), :] = jnp.zeros((1, LANES), jnp.float32)
        return 0

    lax.fori_loop(found, chunks * CHUNK, fill, 0)
    last = valid.shape[0] - 1
    valid[last : last + 1, :] = jnp.full((1, LANES), chunks.astype(jnp.float32), jnp.float32)

    def wait(c, _):
        for i in range(CHUNK):
            page_copy(0, c * CHUNK + i).wait()
        return 0

    lax.fori_loop(0, chunks, wait, 0)


def resident_part(qa, pages, valid, out, held, per_held):
    q = query_block(qa, held, per_held)
    count = q.shape[0]
    token = lax.broadcasted_iota(jnp.int32, (PAGE, count), 0).astype(jnp.float32)
    floor = jnp.full((1, count), FLOOR, jnp.float32)
    last = valid.shape[0] - 1
    chunks = jnp.max(valid[last : last + 1, :]).astype(jnp.int32)

    def score(c):
        first = c * CHUNK
        masks = [token < valid[pl.ds(first + i, 1), :][:, :count] for i in range(CHUNK)]
        keys = jnp.concatenate([lanes_of(pages.at[first + i], 0, held) for i in range(CHUNK)], 0)
        return jnp.where(jnp.concatenate(masks, 0), dot(keys, q, 1, 1) * SCALE, NEG)

    def weigh(c, s, top):
        p = jnp.exp(s - top)
        values = jnp.concatenate([lanes_of(pages.at[c * CHUNK + i], 1, held) for i in range(CHUNK)], 0)
        return jnp.sum(p, 0, keepdims=True), dot(p.astype(jnp.bfloat16), values, 0, 0)

    def straight(number):
        scores = [score(c) for c in range(number)]
        top = functools.reduce(jnp.maximum, [jnp.max(s, 0, keepdims=True) for s in scores], floor)
        terms = [weigh(c, s, top) for c, s in enumerate(scores)]
        total = functools.reduce(jnp.add, [t for t, _ in terms])
        acc = functools.reduce(jnp.add, [a for _, a in terms])
        write_part(out, acc, top, total, held, per_held)

    def step(c, carry):
        top, total, acc = carry
        s = score(c)
        new_top = jnp.maximum(top, jnp.max(s, 0, keepdims=True))
        fade = jnp.exp(top - new_top)
        more, part = weigh(c, s, new_top)
        return new_top, total * fade + more, acc * jnp.broadcast_to(fade, (8, count)).T[:, :1] + part

    for number in STATIC:

        @pl.when(chunks == number)
        def _(number=number):
            straight(number)

    @pl.when(chunks > STATIC[-1])
    def _():
        start = (floor, jnp.zeros((1, count), jnp.float32), jnp.zeros((count, held * HD), jnp.float32))
        top, total, acc = lax.fori_loop(0, chunks, step, start)
        write_part(out, acc, top, total, held, per_held)


def list_pages(send, wanted, owner, target, slots, page_list, slot_list, base):
    for c in range(PARTS):
        page_list[base + c] = 0
        slot_list[base + c] = -1
    at = jnp.int32(base)
    for i in range(send.shape[2]):
        hit = send[1, owner, i] == target
        page_list[at] = send[0, owner, i]
        slot_list[at] = jnp.where(hit, send[2, owner, i], -1)
        at = at + hit.astype(jnp.int32)
    at = jnp.int32(base + CAP)
    page_list[at] = 0
    slot_list[at] = -1
    for i in range(wanted.shape[1]):
        page = wanted[target, i] - owner * PRE_DEV
        hit = jnp.logical_and(page >= 0, page < PRE_DEV)
        page_list[at] = jnp.where(hit, page, 0)
        slot_list[at] = jnp.where(hit, slots + i, -1)
        at = at + hit.astype(jnp.int32)


def copy_lists(pairs, sems):
    copies = [pltpu.make_async_copy(a, b, sems.at[i]) for i, (a, b) in enumerate(pairs)]
    for copy in copies:
        copy.start()

    def ready():
        for copy in copies:
            copy.wait()

    return ready


def first_kernel(held, per_held, groups, maxp, qa, send_hbm, wanted_hbm, tables_hbm, lengths_hbm, kv, *refs):
    sent, chosen, entries, valid, send, wanted, tables, lengths = refs[:8]
    flags, page_list, slot_list, list_sems, sems = refs[8:]
    group = lax.axis_index("group")
    prefill = lax.axis_index("role") == 0
    lists = ((send_hbm, send), (wanted_hbm, wanted), (tables_hbm, tables), (lengths_hbm, lengths))
    lists_ready = copy_lists(lists, list_sems)

    @pl.when(prefill)
    def _():
        lists_ready()
        copies = []
        for k in range(groups):
            target = lax.bitwise_xor(group, k)
            list_pages(send, wanted, group, target, kv.shape[0], page_list, slot_list, k * PARTS)
            for c in range(PARTS):
                at = k * PARTS + c
                copy = pltpu.make_async_copy(kv.at[page_list[at]], chosen.at[at], sems.at[at])
                copy.start()
                copies.append(copy)
                entry = slot_list[at].astype(jnp.float32)
                entries[at : at + 1, :] = jnp.full((1, LANES), entry, jnp.float32)
        for copy in copies[:PARTS]:
            copy.wait()
        owner_part(qa, chosen.at[pl.ds(0, PARTS)], entries[:PARTS, :], sent, held, per_held, maxp)
        for copy in copies[PARTS:]:
            copy.wait()

    @pl.when(jnp.logical_not(prefill))
    def _():
        fetch_pages(qa.shape[0], lists_ready, send, tables, lengths, maxp, group, kv, chosen, valid, flags, sems)


def fresh_part(qa, new_kv, out, held, per_held):
    rows = qa.shape[0]
    q = query_block(qa, held, per_held)
    count = q.shape[0]
    lane_row = lax.rem(lax.broadcasted_iota(jnp.int32, (1, count), 1), rows)
    fresh = new_kv[...].astype(jnp.float32)
    fresh = jnp.concatenate([fresh, jnp.zeros_like(fresh)], 0).astype(jnp.bfloat16)
    mask = lax.broadcasted_iota(jnp.int32, (2 * rows, count), 0) == lane_row
    s = jnp.where(mask, dot(lanes_of(fresh, 0, held), q, 1, 1) * SCALE, NEG)
    top = jnp.max(s, 0, keepdims=True)
    p = jnp.exp(s - top)
    acc = dot(p.astype(jnp.bfloat16), lanes_of(fresh, 1, held), 0, 0)
    write_part(out, acc, top, jnp.sum(p, 0, keepdims=True), held, per_held)


def third_kernel(held, per_held, qa, new_kv, pages, valid, out, fresh):
    @pl.when(lax.axis_index("role") == 1)
    def _():
        fresh_part(qa, new_kv, fresh, held, per_held)
        resident_part(qa, pages, valid, out, held, per_held)


def second_kernel(held, per_held, maxp, first, count, chosen, entries, *refs):
    qas, outs = refs[:count][::-1], refs[len(refs) - count :]

    @pl.when(lax.axis_index("role") == 0)
    def _():
        for k in range(count):
            at = (first + k) * PARTS
            owner_part(
                qas[k], chosen.at[pl.ds(at, PARTS)], entries[at : at + PARTS, :], outs[k], held, per_held, maxp
            )


def merge_kernel(heads, rows, *refs):
    parts, out = refs[:-1], refs[-1]
    count = heads * rows
    pad = -len(parts) % 8
    stats = [part[count:, :].astype(jnp.float32)[:, :count] for part in parts]
    tops = jnp.concatenate([s[0:1] + (s[1:2] + s[2:3]) for s in stats], 0)
    totals = jnp.concatenate([s[3:4] + (s[4:5] + s[5:6]) for s in stats], 0)
    factors = jnp.exp(tops - jnp.max(tops, 0, keepdims=True))
    factors = factors / jnp.sum(factors * totals, 0, keepdims=True)
    factors = jnp.concatenate([factors, jnp.zeros((pad, count), jnp.float32)], 0).T
    terms = [factors[:, i : i + 1] * part[:count, :].astype(jnp.float32) for i, part in enumerate(parts)]
    merged = functools.reduce(jnp.add, terms)
    out[...] = jnp.concatenate([merged[h * rows : (h + 1) * rows] for h in range(heads)], 1).astype(out.dtype)


def project_kernel(steps, attended, partner, weight, *outs):
    tps = lax.axis_size("tp")
    share = outs[0].shape[1]
    here = jnp.where(lax.axis_index("role") == 0, partner[...].astype(jnp.float32), attended[...].astype(jnp.float32))
    here = here.astype(jnp.bfloat16)
    for d, out in zip(steps, outs):
        first = lax.rem(lax.axis_index("tp") + d, tps) * share
        columns = pl.ds(pl.multiple_of(first, LANES), share)
        out[...] = jnp.dot(here, weight[:, columns], preferred_element_type=jnp.float32).astype(out.dtype)


def per_device(kv_pages, send_list, wanted, lengths, tables, queries, new_kv, out_weight):
    stored = kv_pages[0, 0, 0]
    slots = stored.shape[0]
    groups, tps = lax.axis_size("group"), lax.axis_size("tp")
    held = max(1, KVH // tps)
    rows, wide = queries.shape[1], queries.shape[2]
    heads = wide // HD
    per_held = heads // held
    maxp = tables.shape[2]
    send = jnp.transpose(send_list, (2, 0, 1))
    def place(block, at):
        return jnp.pad(block, ((0, rows - block.shape[0]), (at, wide + LANES - at - block.shape[1])))

    high = lax.shift_right_logical(place(lengths, wide + maxp), 3)
    low = jnp.bitwise_and(place(lengths, wide + maxp + rows), 7)
    integers = place(tables[0], wide) + high + low
    qa = place(queries[0], 0) + integers.astype(jnp.bfloat16)
    def paired(value, k, to_decode):
        first, second = (0, groups) if to_decode else (groups, 0)
        pairs = [pair for i in range(groups) for pair in ((first + i, second + (i ^ k)), (second + i, first + i))]
        return lax.ppermute(value, ("role", "group"), pairs)

    asked = [paired(qa, k, False) for k in range(1, groups)]
    part_shape = jax.ShapeDtypeStruct((heads * rows + STATS, HD), jnp.float32)
    sent_shape = jax.ShapeDtypeStruct(part_shape.shape, jnp.bfloat16)
    vmem = pl.BlockSpec(memory_space=pltpu.VMEM)
    hbm = pl.BlockSpec(memory_space=pltpu.HBM)
    page_shape = stored.shape[1:]
    chosen_count = groups * PARTS
    read_count = -(-rows * maxp // CHUNK) * CHUNK
    page_count = max(read_count, chosen_count)
    lists = [send, wanted, tables[0], lengths]
    pinned = [pltpu.with_memory_space_constraint(x, pltpu.HBM) for x in lists + [stored]]
    mine_sent, chosen, entries, valid = pl.pallas_call(
        functools.partial(first_kernel, held, per_held, groups, maxp),
        out_shape=[
            sent_shape,
            jax.ShapeDtypeStruct((page_count,) + page_shape, jnp.bfloat16),
            jax.ShapeDtypeStruct((chosen_count, LANES), jnp.float32),
            jax.ShapeDtypeStruct((read_count + 8, LANES), jnp.float32),
        ],
        in_specs=[vmem] + [hbm] * 5,
        out_specs=[vmem] * 4,
        scratch_shapes=[
            *[pltpu.SMEM(x.shape, jnp.int32) for x in lists],
            pltpu.SMEM((slots + 1,), jnp.int32),
            pltpu.SMEM((chosen_count + 1,), jnp.int32),
            pltpu.SMEM((chosen_count + 1,), jnp.int32),
            pltpu.SemaphoreType.DMA((len(lists),)),
            pltpu.SemaphoreType.DMA((page_count,)),
        ],
        compiler_params=pltpu.CompilerParams(vmem_limit_bytes=20 * MIB),
        name="resident",
    )(qa, *pinned)
    theirs = []
    for first, messages in ((1, asked[:-1]), (groups - 1, asked[-1:])):
        theirs += pl.pallas_call(
            functools.partial(second_kernel, held, per_held, maxp, first, len(messages)),
            out_shape=[sent_shape] * len(messages),
            in_specs=[vmem] * (2 + len(messages) + len(theirs)),
            out_specs=[vmem] * len(messages),
            compiler_params=pltpu.CompilerParams(vmem_limit_bytes=16 * MIB),
            cost_estimate=pl.CostEstimate(flops=2 * 10**10, bytes_accessed=8 * MIB, transcendentals=10**6),
            name="owned",
        )(chosen, entries, *reversed(messages), *theirs)
    qa, mine_sent, theirs = lax.optimization_barrier((qa, mine_sent, theirs))
    mine, fresh = pl.pallas_call(
        functools.partial(third_kernel, held, per_held),
        out_shape=[part_shape] * 2,
        in_specs=[vmem] * 4,
        out_specs=[vmem] * 2,
        compiler_params=pltpu.CompilerParams(vmem_limit_bytes=16 * MIB),
        name="attend",
    )(qa, new_kv[0], chosen, valid)
    parts = [mine, fresh] + [paired(part, k, True) for k, part in enumerate([mine_sent, *theirs])][::-1]
    attended = pl.pallas_call(
        functools.partial(merge_kernel, heads, rows),
        out_shape=jax.ShapeDtypeStruct((rows, wide), jnp.bfloat16),
        in_specs=[vmem] * len(parts),
        out_specs=vmem,
        compiler_params=pltpu.CompilerParams(vmem_limit_bytes=8 * MIB),
        name="merge",
    )(*parts)
    partner = lax.ppermute(attended, "role", [(0, 1), (1, 0)])
    share = out_weight.shape[1] // tps

    def project(steps, dtype, name):
        return pl.pallas_call(
            functools.partial(project_kernel, steps),
            out_shape=[jax.ShapeDtypeStruct((rows, share), dtype)] * len(steps),
            in_specs=[vmem] * 3,
            out_specs=[vmem] * len(steps),
            compiler_params=pltpu.CompilerParams(vmem_limit_bytes=24 * MIB),
            cost_estimate=pl.CostEstimate(
                flops=len(steps) * 32 * wide * share, bytes_accessed=len(steps) * 2 * wide * share, transcendentals=0
            ),
            name=name,
        )(attended, partner, out_weight)

    steps = list(range(1, tps))
    sent = project(steps, jnp.bfloat16, "project")
    arrived = [lax.ppermute(part, "tp", [(i, (i + d) % tps) for i in range(tps)]) for d, part in zip(steps, sent)]
    own = project([0], jnp.float32, "project_own")[0]
    total = functools.reduce(jnp.add, [part.astype(jnp.float32) for part in arrived], own)
    return total.astype(jnp.bfloat16)[None]


def solution(mesh):
    return jax.shard_map(
        per_device,
        mesh=mesh,
        in_specs=(
            P("role", "group", "tp", None, None, None),
            P(),
            P(),
            P("group", None),
            P("group", None, None),
            P("group", None, "tp"),
            P("group", None, "tp"),
            P("tp", "role"),
        ),
        out_specs=P("group", None, ("role", "tp")),
        check_vma=False,
    )
```

```python
import functools
import math

import jax
import jax.numpy as jnp
from jax import lax
from jax.experimental import pallas as pl
from jax.experimental.pallas import tpu as pltpu
from jax.sharding import PartitionSpec as P

KVH = 8
HD = 128
CAP = 4
CAPP = 2
PRE_DEV = 8
LANES = 128
PAGE = 128
NEG = -1e30
FLOOR = -1e29
SCALE = 1.0 / math.sqrt(HD)
PARTS = CAP + CAPP
CHUNK = 8
STATIC = (2, 3, 4, 5)
STATS = 16
MIB = 2**20


def dot(a, b, ca, cb):
    return lax.dot_general(a, b, (((ca,), (cb,)), ((), ())), preferred_element_type=jnp.float32)


def query_block(qa, held, per_held):
    q = qa[:, : held * per_held * HD].astype(jnp.float32)
    rows = q.shape[0]
    bands = []
    for j in range(held):
        heads = [q[:, (j * per_held + i) * HD : (j * per_held + i + 1) * HD] for i in range(per_held)]
        band = jnp.concatenate(heads, 0)
        blank = jnp.zeros_like(band)
        bands.append(jnp.concatenate([band if i == j else blank for i in range(held)], 1))
    return jnp.concatenate(bands, 0).astype(jnp.bfloat16)


def entry_rows(qa, held, per_held, maxp):
    rows = qa.shape[0]
    wide = held * per_held * HD
    aux = qa[:, wide : wide + LANES].astype(jnp.float32)
    lane = lax.broadcasted_iota(jnp.int32, (rows, LANES), 1) - maxp
    row = lax.broadcasted_iota(jnp.int32, (rows, LANES), 0)
    parts = jnp.where(lane == row, 8.0 * aux[:1], jnp.where(lane == row + rows, aux[:1], 0.0))
    length = jnp.sum(parts, 1, keepdims=True)
    turned = jnp.concatenate([jnp.where(lane == 0, length, aux)] * (held * per_held), 0).T
    first = lax.broadcasted_iota(jnp.int32, (maxp, 1), 0).astype(jnp.float32) * PAGE
    return turned[:maxp], jnp.clip(turned[maxp : maxp + 1] - first, 0.0, PAGE)


def lanes_of(page, first, held):
    return jnp.concatenate([page[:, (2 * j + first) * HD : (2 * j + first + 1) * HD] for j in range(held)], 1)


def pieces(x):
    high = x.astype(jnp.bfloat16).astype(jnp.float32)
    middle = (x - high).astype(jnp.bfloat16).astype(jnp.float32)
    return [high, middle, x - high - middle]


def write_part(out, acc, top, total, held, per_held):
    count = acc.shape[0]
    band = count // held
    out[:count, :] = jnp.concatenate(
        [acc[j * band : (j + 1) * band, j * HD : (j + 1) * HD] for j in range(held)], 0
    ).astype(out.dtype)
    rows = pieces(top) + pieces(total)
    block = jnp.concatenate(rows + [jnp.zeros((STATS - len(rows), count), jnp.float32)], 0)
    if count < LANES:
        block = jnp.concatenate([block, jnp.zeros((STATS, LANES - count), jnp.float32)], 1)
    out[count:, :] = block.astype(out.dtype)


def owner_part(qa, pages, entries, out, held, per_held, maxp):
    q = query_block(qa, held, per_held)
    tab, cnt = entry_rows(qa, held, per_held, maxp)
    count = q.shape[0]
    token = lax.broadcasted_iota(jnp.int32, (PAGE, count), 0).astype(jnp.float32)
    masks = []
    for c in range(PARTS):
        valid = jnp.sum(jnp.where(tab == entries[c : c + 1, :count], cnt, 0.0), 0, keepdims=True)
        masks.append(token < valid)
    mask = jnp.concatenate(masks, 0)
    keys = jnp.concatenate([lanes_of(pages.at[c], 0, held) for c in range(PARTS)], 0)
    values = jnp.concatenate([lanes_of(pages.at[c], 1, held) for c in range(PARTS)], 0)
    s = jnp.where(mask, dot(keys, q, 1, 1) * SCALE, NEG)
    top = jnp.max(s, 0, keepdims=True)
    p = jnp.where(mask, jnp.exp(s - top), 0.0)
    total = jnp.sum(p, 0, keepdims=True)
    acc = dot(p.astype(jnp.bfloat16), values, 0, 0)
    write_part(out, acc, top, total, held, per_held)


def fetch_pages(rows, lists_ready, send, tables, lengths, maxp, group, kv, pages, valid, flags, listed, sems):
    slots = kv.shape[0]
    lane_row = lax.rem(lax.broadcasted_iota(jnp.int32, (1, LANES), 1), rows)
    for i in range(slots):
        flags[i] = 0
    lists_ready()
    for o in range(send.shape[1]):
        for i in range(send.shape[2]):
            flags[jnp.where(send[1, o, i] == group, send[2, o, i], slots)] = 1

    def page_copy(slot, i):
        return pltpu.make_async_copy(kv.at[slot], pages.at[i], sems.at[i])

    found = jnp.int32(0)
    for r in range(rows):
        length = lengths[0, r]
        for e in range(maxp):
            slot = tables[r, e]
            tokens = jnp.minimum(length - e * PAGE, PAGE)
            here = jnp.logical_and(slot < slots, flags[jnp.minimum(slot, slots - 1)] == 0)
            needed = jnp.logical_and(tokens > 0, here)

            listed[0, found] = r
            listed[1, found] = tokens

            @pl.when(needed)
            def _(slot=slot, at=found):
                page_copy(slot, at).start()

            found = found + needed.astype(jnp.int32)
    chunks = jnp.maximum((found + CHUNK - 1) // CHUNK, STATIC[0])

    def fill(i, _):
        page_copy(0, i).start()
        listed[0, i] = 0
        listed[1, i] = 0
        return 0

    lax.fori_loop(found, chunks * CHUNK, fill, 0)
    last = valid.shape[0] - 1
    valid[last : last + 1, :] = jnp.full((1, LANES), chunks.astype(jnp.float32), jnp.float32)

    def describe(c, _):
        for i in range(CHUNK):
            at = c * CHUNK + i
            tokens = listed[1, at].astype(jnp.float32)
            valid[pl.ds(at, 1), :] = jnp.where(lane_row == listed[0, at], tokens, 0.0)
        return 0

    lax.fori_loop(0, chunks, describe, 0)

    def wait(c, _):
        for i in range(CHUNK):
            page_copy(0, c * CHUNK + i).wait()
        return 0

    lax.fori_loop(0, chunks, wait, 0)


def resident_part(qa, pages, valid, out, held, per_held):
    q = query_block(qa, held, per_held)
    count = q.shape[0]
    token = lax.broadcasted_iota(jnp.int32, (PAGE, count), 0).astype(jnp.float32)
    floor = jnp.full((1, count), FLOOR, jnp.float32)
    last = valid.shape[0] - 1
    chunks = jnp.max(valid[last : last + 1, :]).astype(jnp.int32)

    def score(c):
        first = c * CHUNK
        masks = [token < valid[pl.ds(first + i, 1), :][:, :count] for i in range(CHUNK)]
        keys = jnp.concatenate([lanes_of(pages.at[first + i], 0, held) for i in range(CHUNK)], 0)
        return jnp.where(jnp.concatenate(masks, 0), dot(keys, q, 1, 1) * SCALE, NEG)

    def weigh(c, s, top):
        p = jnp.exp(s - top)
        values = jnp.concatenate([lanes_of(pages.at[c * CHUNK + i], 1, held) for i in range(CHUNK)], 0)
        return jnp.sum(p, 0, keepdims=True), dot(p.astype(jnp.bfloat16), values, 0, 0)

    def straight(number):
        scores = [score(c) for c in range(number)]
        top = functools.reduce(jnp.maximum, [jnp.max(s, 0, keepdims=True) for s in scores], floor)
        terms = [weigh(c, s, top) for c, s in enumerate(scores)]
        total = functools.reduce(jnp.add, [t for t, _ in terms])
        acc = functools.reduce(jnp.add, [a for _, a in terms])
        write_part(out, acc, top, total, held, per_held)

    def step(c, carry):
        top, total, acc = carry
        s = score(c)
        new_top = jnp.maximum(top, jnp.max(s, 0, keepdims=True))
        fade = jnp.exp(top - new_top)
        more, part = weigh(c, s, new_top)
        return new_top, total * fade + more, acc * jnp.broadcast_to(fade, (8, count)).T[:, :1] + part

    for number in STATIC:

        @pl.when(chunks == number)
        def _(number=number):
            straight(number)

    @pl.when(chunks > STATIC[-1])
    def _():
        start = (floor, jnp.zeros((1, count), jnp.float32), jnp.zeros((count, held * HD), jnp.float32))
        top, total, acc = lax.fori_loop(0, chunks, step, start)
        write_part(out, acc, top, total, held, per_held)


def list_pages(send, wanted, owner, target, slots, page_list, slot_list, base):
    for c in range(PARTS):
        page_list[base + c] = 0
        slot_list[base + c] = -1
    at = jnp.int32(base)
    for i in range(send.shape[2]):
        hit = send[1, owner, i] == target
        page_list[at] = send[0, owner, i]
        slot_list[at] = jnp.where(hit, send[2, owner, i], -1)
        at = at + hit.astype(jnp.int32)
    at = jnp.int32(base + CAP)
    page_list[at] = 0
    slot_list[at] = -1
    for i in range(wanted.shape[1]):
        page = wanted[target, i] - owner * PRE_DEV
        hit = jnp.logical_and(page >= 0, page < PRE_DEV)
        page_list[at] = jnp.where(hit, page, 0)
        slot_list[at] = jnp.where(hit, slots + i, -1)
        at = at + hit.astype(jnp.int32)


def copy_lists(pairs, sems):
    copies = [pltpu.make_async_copy(a, b, sems.at[i]) for i, (a, b) in enumerate(pairs)]
    for copy in copies:
        copy.start()

    def ready():
        for copy in copies:
            copy.wait()

    return ready


def first_kernel(held, per_held, groups, maxp, qa, send_hbm, wanted_hbm, tables_hbm, lengths_hbm, kv, *refs):
    sent, chosen, entries, valid, send, wanted, tables, lengths = refs[:8]
    flags, listed, page_list, slot_list, list_sems, sems = refs[8:]
    group = lax.axis_index("group")
    prefill = lax.axis_index("role") == 0
    lists = ((send_hbm, send), (wanted_hbm, wanted), (tables_hbm, tables), (lengths_hbm, lengths))
    lists_ready = copy_lists(lists, list_sems)

    @pl.when(prefill)
    def _():
        lists_ready()
        copies = []
        for k in range(groups):
            target = lax.bitwise_xor(group, k)
            list_pages(send, wanted, group, target, kv.shape[0], page_list, slot_list, k * PARTS)
            for c in range(PARTS):
                at = k * PARTS + c
                copy = pltpu.make_async_copy(kv.at[page_list[at]], chosen.at[at], sems.at[at])
                copy.start()
                copies.append(copy)
                entry = slot_list[at].astype(jnp.float32)
                entries[at : at + 1, :] = jnp.full((1, LANES), entry, jnp.float32)
        for copy in copies[:PARTS]:
            copy.wait()
        owner_part(qa, chosen.at[pl.ds(0, PARTS)], entries[:PARTS, :], sent, held, per_held, maxp)
        for copy in copies[PARTS:]:
            copy.wait()

    @pl.when(jnp.logical_not(prefill))
    def _():
        fetch_pages(qa.shape[0], lists_ready, send, tables, lengths, maxp, group, kv, chosen, valid, flags, listed, sems)


def fresh_part(qa, new_kv, out, held, per_held):
    rows = qa.shape[0]
    q = query_block(qa, held, per_held)
    count = q.shape[0]
    lane_row = lax.rem(lax.broadcasted_iota(jnp.int32, (1, count), 1), rows)
    fresh = new_kv[...].astype(jnp.float32)
    fresh = jnp.concatenate([fresh, jnp.zeros_like(fresh)], 0).astype(jnp.bfloat16)
    mask = lax.broadcasted_iota(jnp.int32, (2 * rows, count), 0) == lane_row
    s = jnp.where(mask, dot(lanes_of(fresh, 0, held), q, 1, 1) * SCALE, NEG)
    top = jnp.max(s, 0, keepdims=True)
    p = jnp.exp(s - top)
    acc = dot(p.astype(jnp.bfloat16), lanes_of(fresh, 1, held), 0, 0)
    write_part(out, acc, top, jnp.sum(p, 0, keepdims=True), held, per_held)


def third_kernel(held, per_held, qa, new_kv, pages, valid, out, fresh):
    @pl.when(lax.axis_index("role") == 1)
    def _():
        fresh_part(qa, new_kv, fresh, held, per_held)
        resident_part(qa, pages, valid, out, held, per_held)


def second_kernel(held, per_held, maxp, first, count, chosen, entries, *refs):
    qas, outs = refs[:count][::-1], refs[len(refs) - count :]

    @pl.when(lax.axis_index("role") == 0)
    def _():
        for k in range(count):
            at = (first + k) * PARTS
            owner_part(
                qas[k], chosen.at[pl.ds(at, PARTS)], entries[at : at + PARTS, :], outs[k], held, per_held, maxp
            )


def merge_kernel(heads, rows, *refs):
    parts, out = refs[:-1], refs[-1]
    count = heads * rows
    pad = -len(parts) % 8
    stats = [part[count:, :].astype(jnp.float32)[:, :count] for part in parts]
    tops = jnp.concatenate([s[0:1] + (s[1:2] + s[2:3]) for s in stats], 0)
    totals = jnp.concatenate([s[3:4] + (s[4:5] + s[5:6]) for s in stats], 0)
    factors = jnp.exp(tops - jnp.max(tops, 0, keepdims=True))
    factors = factors / jnp.sum(factors * totals, 0, keepdims=True)
    factors = jnp.concatenate([factors, jnp.zeros((pad, count), jnp.float32)], 0).T
    terms = [factors[:, i : i + 1] * part[:count, :].astype(jnp.float32) for i, part in enumerate(parts)]
    merged = functools.reduce(jnp.add, terms)
    out[...] = jnp.concatenate([merged[h * rows : (h + 1) * rows] for h in range(heads)], 1).astype(out.dtype)


def project_kernel(steps, attended, partner, weight, *outs):
    share = outs[0].shape[1]
    here = jnp.where(lax.axis_index("role") == 0, partner[...].astype(jnp.float32), attended[...].astype(jnp.float32))
    here = here.astype(jnp.bfloat16)
    for d, out in zip(steps, outs):
        first = lax.bitwise_xor(lax.axis_index("tp"), d) * share
        columns = pl.ds(pl.multiple_of(first, LANES), share)
        out[...] = jnp.dot(here, weight[:, columns], preferred_element_type=jnp.float32).astype(out.dtype)


def per_device(kv_pages, send_list, wanted, lengths, tables, queries, new_kv, out_weight):
    stored = kv_pages[0, 0, 0]
    slots = stored.shape[0]
    groups, tps = lax.axis_size("group"), lax.axis_size("tp")
    held = max(1, KVH // tps)
    rows, wide = queries.shape[1], queries.shape[2]
    heads = wide // HD
    per_held = heads // held
    maxp = tables.shape[2]
    send = jnp.transpose(send_list, (2, 0, 1))
    def place(block, at):
        return jnp.pad(block, ((0, rows - block.shape[0]), (at, wide + LANES - at - block.shape[1])))

    high = lax.shift_right_logical(place(lengths, wide + maxp), 3)
    low = jnp.bitwise_and(place(lengths, wide + maxp + rows), 7)
    integers = place(tables[0], wide) + high + low
    qa = place(queries[0], 0) + integers.astype(jnp.bfloat16)
    def paired(value, k, to_decode):
        first, second = (0, groups) if to_decode else (groups, 0)
        pairs = [pair for i in range(groups) for pair in ((first + i, second + (i ^ k)), (second + i, first + i))]
        return lax.ppermute(value, ("role", "group"), pairs)

    asked = [paired(qa, k, False) for k in range(1, groups)]
    part_shape = jax.ShapeDtypeStruct((heads * rows + STATS, HD), jnp.float32)
    sent_shape = jax.ShapeDtypeStruct(part_shape.shape, jnp.bfloat16)
    vmem = pl.BlockSpec(memory_space=pltpu.VMEM)
    hbm = pl.BlockSpec(memory_space=pltpu.HBM)
    page_shape = stored.shape[1:]
    chosen_count = groups * PARTS
    read_count = -(-rows * maxp // CHUNK) * CHUNK
    page_count = max(read_count, chosen_count)
    lists = [send, wanted, tables[0], lengths]
    pinned = [pltpu.with_memory_space_constraint(x, pltpu.HBM) for x in lists + [stored]]
    mine_sent, chosen, entries, valid = pl.pallas_call(
        functools.partial(first_kernel, held, per_held, groups, maxp),
        out_shape=[
            sent_shape,
            jax.ShapeDtypeStruct((page_count,) + page_shape, jnp.bfloat16),
            jax.ShapeDtypeStruct((chosen_count, LANES), jnp.float32),
            jax.ShapeDtypeStruct((read_count + 8, LANES), jnp.float32),
        ],
        in_specs=[vmem] + [hbm] * 5,
        out_specs=[vmem] * 4,
        scratch_shapes=[
            *[pltpu.SMEM(x.shape, jnp.int32) for x in lists],
            pltpu.SMEM((slots + 1,), jnp.int32),
            pltpu.SMEM((2, read_count), jnp.int32),
            pltpu.SMEM((chosen_count + 1,), jnp.int32),
            pltpu.SMEM((chosen_count + 1,), jnp.int32),
            pltpu.SemaphoreType.DMA((len(lists),)),
            pltpu.SemaphoreType.DMA((page_count,)),
        ],
        compiler_params=pltpu.CompilerParams(vmem_limit_bytes=20 * MIB),
        name="resident",
    )(qa, *pinned)
    theirs = []
    for first, messages in ((1, asked[:-1]), (groups - 1, asked[-1:])):
        theirs += pl.pallas_call(
            functools.partial(second_kernel, held, per_held, maxp, first, len(messages)),
            out_shape=[sent_shape] * len(messages),
            in_specs=[vmem] * (2 + len(messages) + len(theirs)),
            out_specs=[vmem] * len(messages),
            compiler_params=pltpu.CompilerParams(vmem_limit_bytes=16 * MIB),
            cost_estimate=pl.CostEstimate(flops=2 * 10**10, bytes_accessed=8 * MIB, transcendentals=10**6),
            name="owned",
        )(chosen, entries, *reversed(messages), *theirs)
    qa, mine_sent, theirs = lax.optimization_barrier((qa, mine_sent, theirs))
    mine, fresh = pl.pallas_call(
        functools.partial(third_kernel, held, per_held),
        out_shape=[part_shape] * 2,
        in_specs=[vmem] * 4,
        out_specs=[vmem] * 2,
        compiler_params=pltpu.CompilerParams(vmem_limit_bytes=16 * MIB),
        name="attend",
    )(qa, new_kv[0], chosen, valid)
    parts = [mine, fresh] + [paired(part, k, True) for k, part in enumerate([mine_sent, *theirs])][::-1]
    attended = pl.pallas_call(
        functools.partial(merge_kernel, heads, rows),
        out_shape=jax.ShapeDtypeStruct((rows, wide), jnp.bfloat16),
        in_specs=[vmem] * len(parts),
        out_specs=vmem,
        compiler_params=pltpu.CompilerParams(vmem_limit_bytes=8 * MIB),
        name="merge",
    )(*parts)
    partner = lax.ppermute(attended, "role", [(0, 1), (1, 0)])
    share = out_weight.shape[1] // tps

    def project(steps, dtype, name):
        return pl.pallas_call(
            functools.partial(project_kernel, steps),
            out_shape=[jax.ShapeDtypeStruct((rows, share), dtype)] * len(steps),
            in_specs=[vmem] * 3,
            out_specs=[vmem] * len(steps),
            compiler_params=pltpu.CompilerParams(vmem_limit_bytes=24 * MIB),
            cost_estimate=pl.CostEstimate(
                flops=len(steps) * 32 * wide * share, bytes_accessed=len(steps) * 2 * wide * share, transcendentals=0
            ),
            name=name,
        )(attended, partner, out_weight)

    steps = sorted(range(1, tps), key=lambda d: -d.bit_count())
    sent = project(steps, jnp.bfloat16, "project")
    arrived = [lax.ppermute(part, "tp", [(i, i ^ d) for i in range(tps)]) for d, part in zip(steps, sent)]
    own = project([0], jnp.float32, "project_own")[0]
    total = functools.reduce(jnp.add, [part.astype(jnp.float32) for part in arrived], own)
    return total.astype(jnp.bfloat16)[None]


def solution(mesh):
    return jax.shard_map(
        per_device,
        mesh=mesh,
        in_specs=(
            P("role", "group", "tp", None, None, None),
            P(),
            P(),
            P("group", None),
            P("group", None, None),
            P("group", None, "tp"),
            P("group", None, "tp"),
            P("tp", "role"),
        ),
        out_specs=P("group", None, ("role", "tp")),
        check_vma=False,
    )
```

```python
import functools
import math

import jax
import jax.numpy as jnp
from jax import lax
from jax.experimental import pallas as pl
from jax.experimental.pallas import tpu as pltpu
from jax.sharding import PartitionSpec as P

KVH = 8
HD = 128
CAP = 4
CAPP = 2
PRE_DEV = 8
LANES = 128
PAGE = 128
NEG = -1e30
FLOOR = -1e29
SCALE = 1.0 / math.sqrt(HD)
PARTS = CAP + CAPP
CHUNK = 8
STATIC = (2, 3, 4, 5)
STATS = 16
MIB = 2**20


def dot(a, b, ca, cb):
    return lax.dot_general(a, b, (((ca,), (cb,)), ((), ())), preferred_element_type=jnp.float32)


def query_block(qa, held, per_held):
    q = qa[:, : held * per_held * HD].astype(jnp.float32)
    rows = q.shape[0]
    bands = []
    for j in range(held):
        heads = [q[:, (j * per_held + i) * HD : (j * per_held + i + 1) * HD] for i in range(per_held)]
        band = jnp.concatenate(heads, 0)
        blank = jnp.zeros_like(band)
        bands.append(jnp.concatenate([band if i == j else blank for i in range(held)], 1))
    return jnp.concatenate(bands, 0).astype(jnp.bfloat16)


def entry_rows(qa, held, per_held, maxp):
    rows = qa.shape[0]
    wide = held * per_held * HD
    aux = qa[:, wide : wide + LANES].astype(jnp.float32)
    lane = lax.broadcasted_iota(jnp.int32, (rows, LANES), 1) - maxp
    row = lax.broadcasted_iota(jnp.int32, (rows, LANES), 0)
    parts = jnp.where(lane == row, 8.0 * aux[:1], jnp.where(lane == row + rows, aux[:1], 0.0))
    length = jnp.sum(parts, 1, keepdims=True)
    turned = jnp.concatenate([jnp.where(lane == 0, length, aux)] * (held * per_held), 0).T
    first = lax.broadcasted_iota(jnp.int32, (maxp, 1), 0).astype(jnp.float32) * PAGE
    return turned[:maxp], jnp.clip(turned[maxp : maxp + 1] - first, 0.0, PAGE)


def lanes_of(page, first, held):
    return jnp.concatenate([page[:, (2 * j + first) * HD : (2 * j + first + 1) * HD] for j in range(held)], 1)


def pieces(x):
    high = x.astype(jnp.bfloat16).astype(jnp.float32)
    middle = (x - high).astype(jnp.bfloat16).astype(jnp.float32)
    return [high, middle, x - high - middle]


def write_part(out, acc, top, total, held, per_held):
    count = acc.shape[0]
    band = count // held
    out[:count, :] = jnp.concatenate(
        [acc[j * band : (j + 1) * band, j * HD : (j + 1) * HD] for j in range(held)], 0
    ).astype(out.dtype)
    rows = pieces(top) + pieces(total)
    block = jnp.concatenate(rows + [jnp.zeros((STATS - len(rows), count), jnp.float32)], 0)
    if count < LANES:
        block = jnp.concatenate([block, jnp.zeros((STATS, LANES - count), jnp.float32)], 1)
    out[count:, :] = block.astype(out.dtype)


def owner_part(qa, pages, entries, out, held, per_held, maxp):
    q = query_block(qa, held, per_held)
    tab, cnt = entry_rows(qa, held, per_held, maxp)
    count = q.shape[0]
    token = lax.broadcasted_iota(jnp.int32, (PAGE, count), 0).astype(jnp.float32)
    masks = []
    for c in range(PARTS):
        valid = jnp.sum(jnp.where(tab == entries[c : c + 1, :count], cnt, 0.0), 0, keepdims=True)
        masks.append(token < valid)
    mask = jnp.concatenate(masks, 0)
    keys = jnp.concatenate([lanes_of(pages.at[c], 0, held) for c in range(PARTS)], 0)
    values = jnp.concatenate([lanes_of(pages.at[c], 1, held) for c in range(PARTS)], 0)
    s = jnp.where(mask, dot(keys, q, 1, 1) * SCALE, NEG)
    top = jnp.max(s, 0, keepdims=True)
    p = jnp.where(mask, jnp.exp(s - top), 0.0)
    total = jnp.sum(p, 0, keepdims=True)
    acc = dot(p.astype(jnp.bfloat16), values, 0, 0)
    write_part(out, acc, top, total, held, per_held)


def fetch_pages(rows, lists_ready, send, tables, lengths, maxp, group, kv, pages, valid, flags, listed, sems):
    slots = kv.shape[0]
    lane_row = lax.rem(lax.broadcasted_iota(jnp.int32, (1, LANES), 1), rows)
    for i in range(slots):
        flags[i] = 0
    lists_ready()
    for o in range(send.shape[1]):
        for i in range(send.shape[2]):
            flags[jnp.where(send[1, o, i] == group, send[2, o, i], slots)] = 1

    def page_copy(slot, i):
        return pltpu.make_async_copy(kv.at[slot], pages.at[i], sems.at[i])

    found = jnp.int32(0)
    for r in range(rows):
        length = lengths[0, r]
        for e in range(maxp):
            slot = tables[r, e]
            tokens = jnp.minimum(length - e * PAGE, PAGE)
            here = jnp.logical_and(slot < slots, flags[jnp.minimum(slot, slots - 1)] == 0)
            needed = jnp.logical_and(tokens > 0, here)

            listed[0, found] = r
            listed[1, found] = tokens

            @pl.when(needed)
            def _(slot=slot, at=found):
                page_copy(slot, at).start()

            found = found + needed.astype(jnp.int32)
    chunks = jnp.maximum((found + CHUNK - 1) // CHUNK, STATIC[0])

    def fill(i, _):
        page_copy(0, i).start()
        listed[0, i] = 0
        listed[1, i] = 0
        return 0

    lax.fori_loop(found, chunks * CHUNK, fill, 0)
    last = valid.shape[0] - 1
    valid[last : last + 1, :] = jnp.full((1, LANES), chunks.astype(jnp.float32), jnp.float32)

    def describe(c, _):
        for i in range(CHUNK):
            at = c * CHUNK + i
            tokens = listed[1, at].astype(jnp.float32)
            valid[pl.ds(at, 1), :] = jnp.where(lane_row == listed[0, at], tokens, 0.0)
        return 0

    lax.fori_loop(0, chunks, describe, 0)

    def wait(c, _):
        for i in range(CHUNK):
            page_copy(0, c * CHUNK + i).wait()
        return 0

    lax.fori_loop(0, chunks, wait, 0)


def resident_part(qa, pages, valid, out, held, per_held):
    q = query_block(qa, held, per_held)
    count = q.shape[0]
    token = lax.broadcasted_iota(jnp.int32, (PAGE, count), 0).astype(jnp.float32)
    floor = jnp.full((1, count), FLOOR, jnp.float32)
    last = valid.shape[0] - 1
    chunks = jnp.max(valid[last : last + 1, :]).astype(jnp.int32)

    def score(c):
        first = c * CHUNK
        masks = [token < valid[pl.ds(first + i, 1), :][:, :count] for i in range(CHUNK)]
        keys = jnp.concatenate([lanes_of(pages.at[first + i], 0, held) for i in range(CHUNK)], 0)
        return jnp.where(jnp.concatenate(masks, 0), dot(keys, q, 1, 1) * SCALE, NEG)

    def weigh(c, s, top):
        p = jnp.exp(s - top)
        values = jnp.concatenate([lanes_of(pages.at[c * CHUNK + i], 1, held) for i in range(CHUNK)], 0)
        return jnp.sum(p, 0, keepdims=True), dot(p.astype(jnp.bfloat16), values, 0, 0)

    def straight(number):
        scores = [score(c) for c in range(number)]
        top = functools.reduce(jnp.maximum, [jnp.max(s, 0, keepdims=True) for s in scores], floor)
        terms = [weigh(c, s, top) for c, s in enumerate(scores)]
        total = functools.reduce(jnp.add, [t for t, _ in terms])
        acc = functools.reduce(jnp.add, [a for _, a in terms])
        write_part(out, acc, top, total, held, per_held)

    def step(c, carry):
        top, total, acc = carry
        s = score(c)
        new_top = jnp.maximum(top, jnp.max(s, 0, keepdims=True))
        fade = jnp.exp(top - new_top)
        more, part = weigh(c, s, new_top)
        return new_top, total * fade + more, acc * jnp.broadcast_to(fade, (8, count)).T[:, :1] + part

    for number in STATIC:

        @pl.when(chunks == number)
        def _(number=number):
            straight(number)

    @pl.when(chunks > STATIC[-1])
    def _():
        start = (floor, jnp.zeros((1, count), jnp.float32), jnp.zeros((count, held * HD), jnp.float32))
        top, total, acc = lax.fori_loop(0, chunks, step, start)
        write_part(out, acc, top, total, held, per_held)


def list_pages(send, wanted, owner, target, slots, page_list, slot_list, base):
    for c in range(PARTS):
        page_list[base + c] = 0
        slot_list[base + c] = -1
    at = jnp.int32(base)
    for i in range(send.shape[2]):
        hit = send[1, owner, i] == target
        page_list[at] = send[0, owner, i]
        slot_list[at] = jnp.where(hit, send[2, owner, i], -1)
        at = at + hit.astype(jnp.int32)
    at = jnp.int32(base + CAP)
    page_list[at] = 0
    slot_list[at] = -1
    for i in range(wanted.shape[1]):
        page = wanted[target, i] - owner * PRE_DEV
        hit = jnp.logical_and(page >= 0, page < PRE_DEV)
        page_list[at] = jnp.where(hit, page, 0)
        slot_list[at] = jnp.where(hit, slots + i, -1)
        at = at + hit.astype(jnp.int32)


def copy_lists(pairs, sems):
    copies = [pltpu.make_async_copy(a, b, sems.at[i]) for i, (a, b) in enumerate(pairs)]
    for copy in copies:
        copy.start()

    def ready():
        for copy in copies:
            copy.wait()

    return ready


def first_kernel(held, per_held, groups, maxp, qa, send_hbm, wanted_hbm, tables_hbm, lengths_hbm, kv, *refs):
    sent, chosen, entries, valid, send, wanted, tables, lengths = refs[:8]
    flags, listed, page_list, slot_list, list_sems, sems = refs[8:]
    group = lax.axis_index("group")
    prefill = lax.axis_index("role") == 0
    lists = ((send_hbm, send), (wanted_hbm, wanted), (tables_hbm, tables), (lengths_hbm, lengths))
    lists_ready = copy_lists(lists, list_sems)

    @pl.when(prefill)
    def _():
        lists_ready()
        copies = []
        for k in range(groups):
            target = lax.bitwise_xor(group, k)
            list_pages(send, wanted, group, target, kv.shape[0], page_list, slot_list, k * PARTS)
            for c in range(PARTS):
                at = k * PARTS + c
                copy = pltpu.make_async_copy(kv.at[page_list[at]], chosen.at[at], sems.at[at])
                copy.start()
                copies.append(copy)
                entry = slot_list[at].astype(jnp.float32)
                entries[at : at + 1, :] = jnp.full((1, LANES), entry, jnp.float32)
        for copy in copies[:PARTS]:
            copy.wait()
        owner_part(qa, chosen.at[pl.ds(0, PARTS)], entries[:PARTS, :], sent, held, per_held, maxp)
        for copy in copies[PARTS:]:
            copy.wait()

    @pl.when(jnp.logical_not(prefill))
    def _():
        fetch_pages(qa.shape[0], lists_ready, send, tables, lengths, maxp, group, kv, chosen, valid, flags, listed, sems)


def fresh_part(qa, new_kv, out, held, per_held):
    rows = qa.shape[0]
    q = query_block(qa, held, per_held)
    count = q.shape[0]
    lane_row = lax.rem(lax.broadcasted_iota(jnp.int32, (1, count), 1), rows)
    fresh = new_kv[...].astype(jnp.float32)
    fresh = jnp.concatenate([fresh, jnp.zeros_like(fresh)], 0).astype(jnp.bfloat16)
    mask = lax.broadcasted_iota(jnp.int32, (2 * rows, count), 0) == lane_row
    s = jnp.where(mask, dot(lanes_of(fresh, 0, held), q, 1, 1) * SCALE, NEG)
    top = jnp.max(s, 0, keepdims=True)
    p = jnp.exp(s - top)
    acc = dot(p.astype(jnp.bfloat16), lanes_of(fresh, 1, held), 0, 0)
    write_part(out, acc, top, jnp.sum(p, 0, keepdims=True), held, per_held)


def third_kernel(held, per_held, qa, new_kv, pages, valid, out, fresh):
    @pl.when(lax.axis_index("role") == 1)
    def _():
        fresh_part(qa, new_kv, fresh, held, per_held)
        resident_part(qa, pages, valid, out, held, per_held)


def second_kernel(held, per_held, maxp, first, count, chosen, entries, *refs):
    qas, outs = refs[:count][::-1], refs[len(refs) - count :]

    @pl.when(lax.axis_index("role") == 0)
    def _():
        for k in range(count):
            at = (first + k) * PARTS
            owner_part(
                qas[k], chosen.at[pl.ds(at, PARTS)], entries[at : at + PARTS, :], outs[k], held, per_held, maxp
            )


def merge_kernel(heads, rows, *refs):
    parts, out = refs[:-1], refs[-1]
    count = heads * rows
    pad = -len(parts) % 8
    stats = [part[count:, :].astype(jnp.float32)[:, :count] for part in parts]
    tops = jnp.concatenate([s[0:1] + (s[1:2] + s[2:3]) for s in stats], 0)
    totals = jnp.concatenate([s[3:4] + (s[4:5] + s[5:6]) for s in stats], 0)
    factors = jnp.exp(tops - jnp.max(tops, 0, keepdims=True))
    factors = factors / jnp.sum(factors * totals, 0, keepdims=True)
    factors = jnp.concatenate([factors, jnp.zeros((pad, count), jnp.float32)], 0).T
    terms = [factors[:, i : i + 1] * part[:count, :].astype(jnp.float32) for i, part in enumerate(parts)]
    merged = functools.reduce(jnp.add, terms)
    out[...] = jnp.concatenate([merged[h * rows : (h + 1) * rows] for h in range(heads)], 1).astype(out.dtype)


def project_kernel(steps, attended, partner, weight, *refs):
    outs = refs[len(refs) - len(steps) :]
    share = outs[0].shape[1]
    here = jnp.where(lax.axis_index("role") == 0, partner[...].astype(jnp.float32), attended[...].astype(jnp.float32))
    here = here.astype(jnp.bfloat16)
    for d, out in zip(steps, outs):
        first = lax.bitwise_xor(lax.axis_index("tp"), d) * share
        columns = pl.ds(pl.multiple_of(first, LANES), share)
        out[...] = jnp.dot(here, weight[:, columns], preferred_element_type=jnp.float32).astype(out.dtype)


def per_device(kv_pages, send_list, wanted, lengths, tables, queries, new_kv, out_weight):
    stored = kv_pages[0, 0, 0]
    slots = stored.shape[0]
    groups, tps = lax.axis_size("group"), lax.axis_size("tp")
    held = max(1, KVH // tps)
    rows, wide = queries.shape[1], queries.shape[2]
    heads = wide // HD
    per_held = heads // held
    maxp = tables.shape[2]
    send = jnp.transpose(send_list, (2, 0, 1))
    def place(block, at):
        return jnp.pad(block, ((0, rows - block.shape[0]), (at, wide + LANES - at - block.shape[1])))

    high = lax.shift_right_logical(place(lengths, wide + maxp), 3)
    low = jnp.bitwise_and(place(lengths, wide + maxp + rows), 7)
    integers = place(tables[0], wide) + high + low
    qa = place(queries[0], 0) + integers.astype(jnp.bfloat16)
    def paired(value, k, to_decode):
        first, second = (0, groups) if to_decode else (groups, 0)
        pairs = [pair for i in range(groups) for pair in ((first + i, second + (i ^ k)), (second + i, first + i))]
        return lax.ppermute(value, ("role", "group"), pairs)

    asked = [paired(qa, k, False) for k in range(1, groups)]
    part_shape = jax.ShapeDtypeStruct((heads * rows + STATS, HD), jnp.float32)
    sent_shape = jax.ShapeDtypeStruct(part_shape.shape, jnp.bfloat16)
    vmem = pl.BlockSpec(memory_space=pltpu.VMEM)
    hbm = pl.BlockSpec(memory_space=pltpu.HBM)
    page_shape = stored.shape[1:]
    chosen_count = groups * PARTS
    read_count = -(-rows * maxp // CHUNK) * CHUNK
    page_count = max(read_count, chosen_count)
    lists = [send, wanted, tables[0], lengths]
    pinned = [pltpu.with_memory_space_constraint(x, pltpu.HBM) for x in lists + [stored]]
    mine_sent, chosen, entries, valid = pl.pallas_call(
        functools.partial(first_kernel, held, per_held, groups, maxp),
        out_shape=[
            sent_shape,
            jax.ShapeDtypeStruct((page_count,) + page_shape, jnp.bfloat16),
            jax.ShapeDtypeStruct((chosen_count, LANES), jnp.float32),
            jax.ShapeDtypeStruct((read_count + 8, LANES), jnp.float32),
        ],
        in_specs=[vmem] + [hbm] * 5,
        out_specs=[vmem] * 4,
        scratch_shapes=[
            *[pltpu.SMEM(x.shape, jnp.int32) for x in lists],
            pltpu.SMEM((slots + 1,), jnp.int32),
            pltpu.SMEM((2, read_count), jnp.int32),
            pltpu.SMEM((chosen_count + 1,), jnp.int32),
            pltpu.SMEM((chosen_count + 1,), jnp.int32),
            pltpu.SemaphoreType.DMA((len(lists),)),
            pltpu.SemaphoreType.DMA((page_count,)),
        ],
        compiler_params=pltpu.CompilerParams(vmem_limit_bytes=20 * MIB),
        name="resident",
    )(qa, *pinned)
    theirs = []
    for first, messages in ((1, asked[:-1]), (groups - 1, asked[-1:])):
        theirs += pl.pallas_call(
            functools.partial(second_kernel, held, per_held, maxp, first, len(messages)),
            out_shape=[sent_shape] * len(messages),
            in_specs=[vmem] * (2 + len(messages) + len(theirs)),
            out_specs=[vmem] * len(messages),
            compiler_params=pltpu.CompilerParams(vmem_limit_bytes=16 * MIB),
            cost_estimate=pl.CostEstimate(flops=2 * 10**10, bytes_accessed=8 * MIB, transcendentals=10**6),
            name="owned",
        )(chosen, entries, *reversed(messages), *theirs)
    qa, mine_sent, theirs = lax.optimization_barrier((qa, mine_sent, theirs))
    mine, fresh = pl.pallas_call(
        functools.partial(third_kernel, held, per_held),
        out_shape=[part_shape] * 2,
        in_specs=[vmem] * 4,
        out_specs=[vmem] * 2,
        compiler_params=pltpu.CompilerParams(vmem_limit_bytes=16 * MIB),
        name="attend",
    )(qa, new_kv[0], chosen, valid)
    parts = [mine, fresh] + [paired(part, k, True) for k, part in enumerate([mine_sent, *theirs])][::-1]
    attended = pl.pallas_call(
        functools.partial(merge_kernel, heads, rows),
        out_shape=jax.ShapeDtypeStruct((rows, wide), jnp.bfloat16),
        in_specs=[vmem] * len(parts),
        out_specs=vmem,
        compiler_params=pltpu.CompilerParams(vmem_limit_bytes=8 * MIB),
        name="merge",
    )(*parts)
    partner = lax.ppermute(attended, "role", [(0, 1), (1, 0)])
    share = out_weight.shape[1] // tps

    def project(steps, dtype, name, after=()):
        return pl.pallas_call(
            functools.partial(project_kernel, steps),
            out_shape=[jax.ShapeDtypeStruct((rows, share), dtype)] * len(steps),
            in_specs=[vmem] * (3 + len(after)),
            out_specs=[vmem] * len(steps),
            compiler_params=pltpu.CompilerParams(vmem_limit_bytes=24 * MIB),
            cost_estimate=pl.CostEstimate(
                flops=len(steps) * 32 * wide * share, bytes_accessed=len(steps) * 2 * wide * share, transcendentals=0
            ),
            name=name,
        )(attended, partner, out_weight, *after)

    steps = sorted(range(1, tps), key=lambda d: -d.bit_count())
    sent = list(project(steps[:1], jnp.bfloat16, "project_far"))
    sent += project(steps[1:], jnp.bfloat16, "project_near", sent)
    arrived = [lax.ppermute(part, "tp", [(i, i ^ d) for i in range(tps)]) for d, part in zip(steps, sent)]
    own = project([0], jnp.float32, "project_own")[0]
    total = functools.reduce(jnp.add, [part.astype(jnp.float32) for part in arrived], own)
    return total.astype(jnp.bfloat16)[None]


def solution(mesh):
    return jax.shard_map(
        per_device,
        mesh=mesh,
        in_specs=(
            P("role", "group", "tp", None, None, None),
            P(),
            P(),
            P("group", None),
            P("group", None, None),
            P("group", None, "tp"),
            P("group", None, "tp"),
            P("tp", "role"),
        ),
        out_specs=P("group", None, ("role", "tp")),
        check_vma=False,
    )
```

```python
import functools
import math

import jax
import jax.numpy as jnp
from jax import lax
from jax.experimental import pallas as pl
from jax.experimental.pallas import tpu as pltpu
from jax.sharding import PartitionSpec as P

KVH = 8
HD = 128
CAP = 4
CAPP = 2
PRE_DEV = 8
LANES = 128
PAGE = 128
NEG = -1e30
FLOOR = -1e29
SCALE = 1.0 / math.sqrt(HD)
PARTS = CAP + CAPP
CHUNK = 8
STATIC = (2, 3, 4, 5)
STATS = 16
MIB = 2**20


def dot(a, b, ca, cb):
    return lax.dot_general(a, b, (((ca,), (cb,)), ((), ())), preferred_element_type=jnp.float32)


def query_block(qa, held, per_held):
    q = qa[:, : held * per_held * HD].astype(jnp.float32)
    rows = q.shape[0]
    bands = []
    for j in range(held):
        heads = [q[:, (j * per_held + i) * HD : (j * per_held + i + 1) * HD] for i in range(per_held)]
        band = jnp.concatenate(heads, 0)
        blank = jnp.zeros_like(band)
        bands.append(jnp.concatenate([band if i == j else blank for i in range(held)], 1))
    return jnp.concatenate(bands, 0).astype(jnp.bfloat16)


def entry_rows(qa, held, per_held, maxp):
    rows = qa.shape[0]
    wide = held * per_held * HD
    aux = qa[:, wide : wide + LANES].astype(jnp.float32)
    lane = lax.broadcasted_iota(jnp.int32, (rows, LANES), 1) - maxp
    row = lax.broadcasted_iota(jnp.int32, (rows, LANES), 0)
    parts = jnp.where(lane == row, 8.0 * aux[:1], jnp.where(lane == row + rows, aux[:1], 0.0))
    length = jnp.sum(parts, 1, keepdims=True)
    turned = jnp.concatenate([jnp.where(lane == 0, length, aux)] * (held * per_held), 0).T
    first = lax.broadcasted_iota(jnp.int32, (maxp, 1), 0).astype(jnp.float32) * PAGE
    return turned[:maxp], jnp.clip(turned[maxp : maxp + 1] - first, 0.0, PAGE)


def lanes_of(page, first, held):
    return jnp.concatenate([page[:, (2 * j + first) * HD : (2 * j + first + 1) * HD] for j in range(held)], 1)


def pieces(x):
    high = x.astype(jnp.bfloat16).astype(jnp.float32)
    middle = (x - high).astype(jnp.bfloat16).astype(jnp.float32)
    return [high, middle, x - high - middle]


def write_part(out, acc, top, total, held, per_held):
    count = acc.shape[0]
    band = count // held
    out[:count, :] = jnp.concatenate(
        [acc[j * band : (j + 1) * band, j * HD : (j + 1) * HD] for j in range(held)], 0
    ).astype(out.dtype)
    rows = pieces(top) + pieces(total)
    block = jnp.concatenate(rows + [jnp.zeros((STATS - len(rows), count), jnp.float32)], 0)
    if count < LANES:
        block = jnp.concatenate([block, jnp.zeros((STATS, LANES - count), jnp.float32)], 1)
    out[count:, :] = block.astype(out.dtype)


def owner_part(qa, pages, entries, out, held, per_held, maxp):
    q = query_block(qa, held, per_held)
    tab, cnt = entry_rows(qa, held, per_held, maxp)
    count = q.shape[0]
    token = lax.broadcasted_iota(jnp.int32, (PAGE, count), 0).astype(jnp.float32)
    masks = []
    for c in range(PARTS):
        valid = jnp.sum(jnp.where(tab == entries[c : c + 1, :count], cnt, 0.0), 0, keepdims=True)
        masks.append(token < valid)
    mask = jnp.concatenate(masks, 0)
    keys = jnp.concatenate([lanes_of(pages.at[c], 0, held) for c in range(PARTS)], 0)
    values = jnp.concatenate([lanes_of(pages.at[c], 1, held) for c in range(PARTS)], 0)
    s = jnp.where(mask, dot(keys, q, 1, 1) * SCALE, NEG)
    top = jnp.max(s, 0, keepdims=True)
    p = jnp.where(mask, jnp.exp(s - top), 0.0)
    total = jnp.sum(p, 0, keepdims=True)
    acc = dot(p.astype(jnp.bfloat16), values, 0, 0)
    write_part(out, acc, top, total, held, per_held)


def fetch_pages(rows, lists_ready, send, tables, lengths, maxp, group, kv, pages, valid, flags, listed, sems):
    slots = kv.shape[0]
    lane_row = lax.rem(lax.broadcasted_iota(jnp.int32, (1, LANES), 1), rows)
    for i in range(slots):
        flags[i] = 0
    lists_ready()
    for o in range(send.shape[1]):
        for i in range(send.shape[2]):
            flags[jnp.where(send[1, o, i] == group, send[2, o, i], slots)] = 1

    def page_copy(slot, i):
        return pltpu.make_async_copy(kv.at[slot], pages.at[i], sems.at[i])

    found = jnp.int32(0)
    for r in range(rows):
        length = lengths[0, r]
        for e in range(maxp):
            slot = tables[r, e]
            tokens = jnp.minimum(length - e * PAGE, PAGE)
            here = jnp.logical_and(slot < slots, flags[jnp.minimum(slot, slots - 1)] == 0)
            needed = jnp.logical_and(tokens > 0, here)

            listed[0, found] = r
            listed[1, found] = tokens

            @pl.when(needed)
            def _(slot=slot, at=found):
                page_copy(slot, at).start()

            found = found + needed.astype(jnp.int32)
    chunks = jnp.maximum((found + CHUNK - 1) // CHUNK, STATIC[0])

    def fill(i, _):
        page_copy(0, i).start()
        listed[0, i] = 0
        listed[1, i] = 0
        return 0

    lax.fori_loop(found, chunks * CHUNK, fill, 0)
    last = valid.shape[0] - 1
    valid[last : last + 1, :] = jnp.full((1, LANES), chunks.astype(jnp.float32), jnp.float32)

    def describe(c, _):
        for i in range(CHUNK):
            at = c * CHUNK + i
            tokens = listed[1, at].astype(jnp.float32)
            valid[pl.ds(at, 1), :] = jnp.where(lane_row == listed[0, at], tokens, 0.0)
        return 0

    lax.fori_loop(0, chunks, describe, 0)

    def wait(c, _):
        for i in range(CHUNK):
            page_copy(0, c * CHUNK + i).wait()
        return 0

    lax.fori_loop(0, chunks, wait, 0)


def resident_part(qa, pages, valid, out, held, per_held):
    q = query_block(qa, held, per_held)
    count = q.shape[0]
    token = lax.broadcasted_iota(jnp.int32, (PAGE, count), 0).astype(jnp.float32)
    floor = jnp.full((1, count), FLOOR, jnp.float32)
    last = valid.shape[0] - 1
    chunks = jnp.max(valid[last : last + 1, :]).astype(jnp.int32)

    def score(c):
        first = c * CHUNK
        masks = [token < valid[pl.ds(first + i, 1), :][:, :count] for i in range(CHUNK)]
        keys = jnp.concatenate([lanes_of(pages.at[first + i], 0, held) for i in range(CHUNK)], 0)
        return jnp.where(jnp.concatenate(masks, 0), dot(keys, q, 1, 1) * SCALE, NEG)

    def weigh(c, s, top):
        p = jnp.exp(s - top)
        values = jnp.concatenate([lanes_of(pages.at[c * CHUNK + i], 1, held) for i in range(CHUNK)], 0)
        return jnp.sum(p, 0, keepdims=True), dot(p.astype(jnp.bfloat16), values, 0, 0)

    def straight(number):
        scores = [score(c) for c in range(number)]
        top = functools.reduce(jnp.maximum, [jnp.max(s, 0, keepdims=True) for s in scores], floor)
        terms = [weigh(c, s, top) for c, s in enumerate(scores)]
        total = functools.reduce(jnp.add, [t for t, _ in terms])
        acc = functools.reduce(jnp.add, [a for _, a in terms])
        write_part(out, acc, top, total, held, per_held)

    def step(c, carry):
        top, total, acc = carry
        s = score(c)
        new_top = jnp.maximum(top, jnp.max(s, 0, keepdims=True))
        fade = jnp.exp(top - new_top)
        more, part = weigh(c, s, new_top)
        return new_top, total * fade + more, acc * jnp.broadcast_to(fade, (8, count)).T[:, :1] + part

    for number in STATIC:

        @pl.when(chunks == number)
        def _(number=number):
            straight(number)

    @pl.when(chunks > STATIC[-1])
    def _():
        start = (floor, jnp.zeros((1, count), jnp.float32), jnp.zeros((count, held * HD), jnp.float32))
        top, total, acc = lax.fori_loop(0, chunks, step, start)
        write_part(out, acc, top, total, held, per_held)


def list_pages(send, wanted, owner, target, slots, page_list, slot_list, base):
    for c in range(PARTS):
        page_list[base + c] = 0
        slot_list[base + c] = -1
    at = jnp.int32(base)
    for i in range(send.shape[2]):
        hit = send[1, owner, i] == target
        page_list[at] = send[0, owner, i]
        slot_list[at] = jnp.where(hit, send[2, owner, i], -1)
        at = at + hit.astype(jnp.int32)
    at = jnp.int32(base + CAP)
    page_list[at] = 0
    slot_list[at] = -1
    for i in range(wanted.shape[1]):
        page = wanted[target, i] - owner * PRE_DEV
        hit = jnp.logical_and(page >= 0, page < PRE_DEV)
        page_list[at] = jnp.where(hit, page, 0)
        slot_list[at] = jnp.where(hit, slots + i, -1)
        at = at + hit.astype(jnp.int32)


def copy_lists(pairs, sems):
    copies = [pltpu.make_async_copy(a, b, sems.at[i]) for i, (a, b) in enumerate(pairs)]
    for copy in copies:
        copy.start()

    def ready():
        for copy in copies:
            copy.wait()

    return ready


def first_kernel(held, per_held, groups, maxp, qa, send_hbm, wanted_hbm, tables_hbm, lengths_hbm, kv, *refs):
    sent, chosen, entries, valid, send, wanted, tables, lengths = refs[:8]
    flags, listed, page_list, slot_list, list_sems, sems = refs[8:]
    group = lax.axis_index("group")
    prefill = lax.axis_index("role") == 0
    lists = ((send_hbm, send), (wanted_hbm, wanted), (tables_hbm, tables), (lengths_hbm, lengths))
    lists_ready = copy_lists(lists, list_sems)

    @pl.when(prefill)
    def _():
        lists_ready()

        def page_copy(at):
            return pltpu.make_async_copy(kv.at[page_list[at]], chosen.at[at], sems.at[at])

        def arrive(first, last):
            for at in range(first, last):

                @pl.when(slot_list[at] >= 0)
                def _(at=at):
                    page_copy(at).wait()

        for k in range(groups):
            target = lax.bitwise_xor(group, k)
            list_pages(send, wanted, group, target, kv.shape[0], page_list, slot_list, k * PARTS)
            for c in range(PARTS):
                at = k * PARTS + c
                entry = slot_list[at]
                entries[at : at + 1, :] = jnp.full((1, LANES), entry.astype(jnp.float32), jnp.float32)

                @pl.when(entry >= 0)
                def _(at=at):
                    page_copy(at).start()

                @pl.when(entry < 0)
                def _(at=at):
                    chosen[at] = jnp.zeros(chosen.shape[1:], chosen.dtype)

        arrive(0, PARTS)
        owner_part(qa, chosen.at[pl.ds(0, PARTS)], entries[:PARTS, :], sent, held, per_held, maxp)
        arrive(PARTS, groups * PARTS)

    @pl.when(jnp.logical_not(prefill))
    def _():
        fetch_pages(qa.shape[0], lists_ready, send, tables, lengths, maxp, group, kv, chosen, valid, flags, listed, sems)


def fresh_part(qa, new_kv, out, held, per_held):
    rows = qa.shape[0]
    q = query_block(qa, held, per_held)
    count = q.shape[0]
    lane_row = lax.rem(lax.broadcasted_iota(jnp.int32, (1, count), 1), rows)
    fresh = new_kv[...].astype(jnp.float32)
    fresh = jnp.concatenate([fresh, jnp.zeros_like(fresh)], 0).astype(jnp.bfloat16)
    mask = lax.broadcasted_iota(jnp.int32, (2 * rows, count), 0) == lane_row
    s = jnp.where(mask, dot(lanes_of(fresh, 0, held), q, 1, 1) * SCALE, NEG)
    top = jnp.max(s, 0, keepdims=True)
    p = jnp.exp(s - top)
    acc = dot(p.astype(jnp.bfloat16), lanes_of(fresh, 1, held), 0, 0)
    write_part(out, acc, top, jnp.sum(p, 0, keepdims=True), held, per_held)


def third_kernel(held, per_held, qa, new_kv, pages, valid, out, fresh):
    @pl.when(lax.axis_index("role") == 1)
    def _():
        fresh_part(qa, new_kv, fresh, held, per_held)
        resident_part(qa, pages, valid, out, held, per_held)


def second_kernel(held, per_held, maxp, first, count, chosen, entries, *refs):
    qas, outs = refs[:count][::-1], refs[len(refs) - count :]

    @pl.when(lax.axis_index("role") == 0)
    def _():
        for k in range(count):
            at = (first + k) * PARTS
            owner_part(
                qas[k], chosen.at[pl.ds(at, PARTS)], entries[at : at + PARTS, :], outs[k], held, per_held, maxp
            )


def merge_kernel(heads, rows, *refs):
    parts, out = refs[:-1], refs[-1]
    count = heads * rows
    pad = -len(parts) % 8
    stats = [part[count:, :].astype(jnp.float32)[:, :count] for part in parts]
    tops = jnp.concatenate([s[0:1] + (s[1:2] + s[2:3]) for s in stats], 0)
    totals = jnp.concatenate([s[3:4] + (s[4:5] + s[5:6]) for s in stats], 0)
    factors = jnp.exp(tops - jnp.max(tops, 0, keepdims=True))
    factors = factors / jnp.sum(factors * totals, 0, keepdims=True)
    factors = jnp.concatenate([factors, jnp.zeros((pad, count), jnp.float32)], 0).T
    terms = [factors[:, i : i + 1] * part[:count, :].astype(jnp.float32) for i, part in enumerate(parts)]
    merged = functools.reduce(jnp.add, terms)
    out[...] = jnp.concatenate([merged[h * rows : (h + 1) * rows] for h in range(heads)], 1).astype(out.dtype)


def project_kernel(steps, attended, partner, weight, *outs):
    share = outs[0].shape[1]
    here = jnp.where(lax.axis_index("role") == 0, partner[...].astype(jnp.float32), attended[...].astype(jnp.float32))
    here = here.astype(jnp.bfloat16)
    for d, out in zip(steps, outs):
        first = lax.bitwise_xor(lax.axis_index("tp"), d) * share
        columns = pl.ds(pl.multiple_of(first, LANES), share)
        out[...] = jnp.dot(here, weight[:, columns], preferred_element_type=jnp.float32).astype(out.dtype)


def per_device(kv_pages, send_list, wanted, lengths, tables, queries, new_kv, out_weight):
    stored = kv_pages[0, 0, 0]
    slots = stored.shape[0]
    groups, tps = lax.axis_size("group"), lax.axis_size("tp")
    held = max(1, KVH // tps)
    rows, wide = queries.shape[1], queries.shape[2]
    heads = wide // HD
    per_held = heads // held
    maxp = tables.shape[2]
    send = jnp.transpose(send_list, (2, 0, 1))
    def place(block, at):
        return jnp.pad(block, ((0, rows - block.shape[0]), (at, wide + LANES - at - block.shape[1])))

    high = lax.shift_right_logical(place(lengths, wide + maxp), 3)
    low = jnp.bitwise_and(place(lengths, wide + maxp + rows), 7)
    integers = place(tables[0], wide) + high + low
    qa = place(queries[0], 0) + integers.astype(jnp.bfloat16)
    def paired(value, k, to_decode):
        first, second = (0, groups) if to_decode else (groups, 0)
        pairs = [pair for i in range(groups) for pair in ((first + i, second + (i ^ k)), (second + i, first + i))]
        return lax.ppermute(value, ("role", "group"), pairs)

    asked = [paired(qa, k, False) for k in range(1, groups)]
    part_shape = jax.ShapeDtypeStruct((heads * rows + STATS, HD), jnp.float32)
    sent_shape = jax.ShapeDtypeStruct(part_shape.shape, jnp.bfloat16)
    vmem = pl.BlockSpec(memory_space=pltpu.VMEM)
    hbm = pl.BlockSpec(memory_space=pltpu.HBM)
    page_shape = stored.shape[1:]
    chosen_count = groups * PARTS
    read_count = -(-rows * maxp // CHUNK) * CHUNK
    page_count = max(read_count, chosen_count)
    lists = [send, wanted, tables[0], lengths]
    pinned = [pltpu.with_memory_space_constraint(x, pltpu.HBM) for x in lists + [stored]]
    mine_sent, chosen, entries, valid = pl.pallas_call(
        functools.partial(first_kernel, held, per_held, groups, maxp),
        out_shape=[
            sent_shape,
            jax.ShapeDtypeStruct((page_count,) + page_shape, jnp.bfloat16),
            jax.ShapeDtypeStruct((chosen_count, LANES), jnp.float32),
            jax.ShapeDtypeStruct((read_count + 8, LANES), jnp.float32),
        ],
        in_specs=[vmem] + [hbm] * 5,
        out_specs=[vmem] * 4,
        scratch_shapes=[
            *[pltpu.SMEM(x.shape, jnp.int32) for x in lists],
            pltpu.SMEM((slots + 1,), jnp.int32),
            pltpu.SMEM((2, read_count), jnp.int32),
            pltpu.SMEM((chosen_count + 1,), jnp.int32),
            pltpu.SMEM((chosen_count + 1,), jnp.int32),
            pltpu.SemaphoreType.DMA((len(lists),)),
            pltpu.SemaphoreType.DMA((page_count,)),
        ],
        compiler_params=pltpu.CompilerParams(vmem_limit_bytes=20 * MIB),
        name="resident",
    )(qa, *pinned)
    theirs = []
    for first, messages in ((1, asked[:-1]), (groups - 1, asked[-1:])):
        theirs += pl.pallas_call(
            functools.partial(second_kernel, held, per_held, maxp, first, len(messages)),
            out_shape=[sent_shape] * len(messages),
            in_specs=[vmem] * (2 + len(messages) + len(theirs)),
            out_specs=[vmem] * len(messages),
            compiler_params=pltpu.CompilerParams(vmem_limit_bytes=16 * MIB),
            cost_estimate=pl.CostEstimate(flops=2 * 10**10, bytes_accessed=8 * MIB, transcendentals=10**6),
            name="owned",
        )(chosen, entries, *reversed(messages), *theirs)
    qa, mine_sent, theirs = lax.optimization_barrier((qa, mine_sent, theirs))
    mine, fresh = pl.pallas_call(
        functools.partial(third_kernel, held, per_held),
        out_shape=[part_shape] * 2,
        in_specs=[vmem] * 4,
        out_specs=[vmem] * 2,
        compiler_params=pltpu.CompilerParams(vmem_limit_bytes=16 * MIB),
        name="attend",
    )(qa, new_kv[0], chosen, valid)
    parts = [mine, fresh] + [paired(part, k, True) for k, part in enumerate([mine_sent, *theirs])][::-1]
    attended = pl.pallas_call(
        functools.partial(merge_kernel, heads, rows),
        out_shape=jax.ShapeDtypeStruct((rows, wide), jnp.bfloat16),
        in_specs=[vmem] * len(parts),
        out_specs=vmem,
        compiler_params=pltpu.CompilerParams(vmem_limit_bytes=8 * MIB),
        name="merge",
    )(*parts)
    partner = lax.ppermute(attended, "role", [(0, 1), (1, 0)])
    share = out_weight.shape[1] // tps

    def project(steps, dtype, name):
        return pl.pallas_call(
            functools.partial(project_kernel, steps),
            out_shape=[jax.ShapeDtypeStruct((rows, share), dtype)] * len(steps),
            in_specs=[vmem] * 3,
            out_specs=[vmem] * len(steps),
            compiler_params=pltpu.CompilerParams(vmem_limit_bytes=24 * MIB),
            cost_estimate=pl.CostEstimate(
                flops=len(steps) * 32 * wide * share, bytes_accessed=len(steps) * 2 * wide * share, transcendentals=0
            ),
            name=name,
        )(attended, partner, out_weight)

    steps = sorted(range(1, tps), key=lambda d: -d.bit_count())
    sent = project(steps, jnp.bfloat16, "project")
    arrived = [lax.ppermute(part, "tp", [(i, i ^ d) for i in range(tps)]) for d, part in zip(steps, sent)]
    own = project([0], jnp.float32, "project_own")[0]
    total = functools.reduce(jnp.add, [part.astype(jnp.float32) for part in arrived], own)
    return total.astype(jnp.bfloat16)[None]


def solution(mesh):
    return jax.shard_map(
        per_device,
        mesh=mesh,
        in_specs=(
            P("role", "group", "tp", None, None, None),
            P(),
            P(),
            P("group", None),
            P("group", None, None),
            P("group", None, "tp"),
            P("group", None, "tp"),
            P("tp", "role"),
        ),
        out_specs=P("group", None, ("role", "tp")),
        check_vma=False,
    )
```

```python
import functools
import math

import jax
import jax.numpy as jnp
from jax import lax
from jax.experimental import pallas as pl
from jax.experimental.pallas import tpu as pltpu
from jax.sharding import PartitionSpec as P

KVH = 8
HD = 128
CAP = 4
CAPP = 2
PRE_DEV = 8
LANES = 128
PAGE = 128
NEG = -1e30
FLOOR = -1e29
SCALE = 1.0 / math.sqrt(HD)
PARTS = CAP + CAPP
CHUNK = 8
STATIC = (2, 3, 4, 5)
STATS = 16
MIB = 2**20


def dot(a, b, ca, cb):
    return lax.dot_general(a, b, (((ca,), (cb,)), ((), ())), preferred_element_type=jnp.float32)


def query_block(qa, held, per_held):
    q = qa[:, : held * per_held * HD].astype(jnp.float32)
    rows = q.shape[0]
    bands = []
    for j in range(held):
        heads = [q[:, (j * per_held + i) * HD : (j * per_held + i + 1) * HD] for i in range(per_held)]
        band = jnp.concatenate(heads, 0)
        blank = jnp.zeros_like(band)
        bands.append(jnp.concatenate([band if i == j else blank for i in range(held)], 1))
    return jnp.concatenate(bands, 0).astype(jnp.bfloat16)


def entry_rows(qa, held, per_held, maxp):
    rows = qa.shape[0]
    wide = held * per_held * HD
    aux = qa[:, wide : wide + LANES].astype(jnp.float32)
    lane = lax.broadcasted_iota(jnp.int32, (rows, LANES), 1) - maxp
    row = lax.broadcasted_iota(jnp.int32, (rows, LANES), 0)
    parts = jnp.where(lane == row, 8.0 * aux[:1], jnp.where(lane == row + rows, aux[:1], 0.0))
    length = jnp.sum(parts, 1, keepdims=True)
    turned = jnp.concatenate([jnp.where(lane == 0, length, aux)] * (held * per_held), 0).T
    first = lax.broadcasted_iota(jnp.int32, (maxp, 1), 0).astype(jnp.float32) * PAGE
    return turned[:maxp], jnp.clip(turned[maxp : maxp + 1] - first, 0.0, PAGE)


def lanes_of(page, first, held):
    return jnp.concatenate([page[:, (2 * j + first) * HD : (2 * j + first + 1) * HD] for j in range(held)], 1)


def pieces(x):
    high = x.astype(jnp.bfloat16).astype(jnp.float32)
    middle = (x - high).astype(jnp.bfloat16).astype(jnp.float32)
    return [high, middle, x - high - middle]


def write_part(out, acc, top, total, held, per_held):
    count = acc.shape[0]
    band = count // held
    out[:count, :] = jnp.concatenate(
        [acc[j * band : (j + 1) * band, j * HD : (j + 1) * HD] for j in range(held)], 0
    ).astype(out.dtype)
    rows = pieces(top) + pieces(total)
    block = jnp.concatenate(rows + [jnp.zeros((STATS - len(rows), count), jnp.float32)], 0)
    if count < LANES:
        block = jnp.concatenate([block, jnp.zeros((STATS, LANES - count), jnp.float32)], 1)
    out[count:, :] = block.astype(out.dtype)


def owner_part(qa, pages, entries, out, held, per_held, maxp):
    q = query_block(qa, held, per_held)
    tab, cnt = entry_rows(qa, held, per_held, maxp)
    count = q.shape[0]
    token = lax.broadcasted_iota(jnp.int32, (PAGE, count), 0).astype(jnp.float32)
    masks = []
    for c in range(PARTS):
        valid = jnp.sum(jnp.where(tab == entries[c : c + 1, :count], cnt, 0.0), 0, keepdims=True)
        masks.append(token < valid)
    mask = jnp.concatenate(masks, 0)
    keys = jnp.concatenate([lanes_of(pages.at[c], 0, held) for c in range(PARTS)], 0)
    values = jnp.concatenate([lanes_of(pages.at[c], 1, held) for c in range(PARTS)], 0)
    s = jnp.where(mask, dot(keys, q, 1, 1) * SCALE, NEG)
    top = jnp.max(s, 0, keepdims=True)
    p = jnp.where(mask, jnp.exp(s - top), 0.0)
    total = jnp.sum(p, 0, keepdims=True)
    acc = dot(p.astype(jnp.bfloat16), values, 0, 0)
    write_part(out, acc, top, total, held, per_held)


def fetch_pages(rows, lists_ready, send, tables, lengths, maxp, group, kv, pages, valid, flags, listed, sems):
    slots = kv.shape[0]
    lane_row = lax.rem(lax.broadcasted_iota(jnp.int32, (1, LANES), 1), rows)
    for i in range(slots):
        flags[i] = 0
    lists_ready()
    for o in range(send.shape[1]):
        for i in range(send.shape[2]):
            flags[jnp.where(send[1, o, i] == group, send[2, o, i], slots)] = 1

    def page_copy(slot, i):
        return pltpu.make_async_copy(kv.at[slot], pages.at[i], sems.at[i])

    found = jnp.int32(0)
    for r in range(rows):
        length = lengths[0, r]
        for e in range(maxp):
            slot = tables[r, e]
            tokens = jnp.minimum(length - e * PAGE, PAGE)
            here = jnp.logical_and(slot < slots, flags[jnp.minimum(slot, slots - 1)] == 0)
            needed = jnp.logical_and(tokens > 0, here)

            listed[0, found] = r
            listed[1, found] = tokens

            @pl.when(needed)
            def _(slot=slot, at=found):
                page_copy(slot, at).start()

            found = found + needed.astype(jnp.int32)
    chunks = jnp.maximum((found + CHUNK - 1) // CHUNK, STATIC[0])

    def fill(i, _):
        pages[i] = jnp.zeros(pages.shape[1:], pages.dtype)
        listed[0, i] = 0
        listed[1, i] = 0
        return 0

    lax.fori_loop(found, chunks * CHUNK, fill, 0)
    last = valid.shape[0] - 1
    valid[last : last + 1, :] = jnp.full((1, LANES), chunks.astype(jnp.float32), jnp.float32)

    def describe(c, _):
        for i in range(CHUNK):
            at = c * CHUNK + i
            tokens = listed[1, at].astype(jnp.float32)
            valid[pl.ds(at, 1), :] = jnp.where(lane_row == listed[0, at], tokens, 0.0)
        return 0

    lax.fori_loop(0, chunks, describe, 0)

    def wait(i, _):
        page_copy(0, i).wait()
        return 0

    lax.fori_loop(0, found, wait, 0)


def resident_part(qa, pages, valid, out, held, per_held):
    q = query_block(qa, held, per_held)
    count = q.shape[0]
    token = lax.broadcasted_iota(jnp.int32, (PAGE, count), 0).astype(jnp.float32)
    floor = jnp.full((1, count), FLOOR, jnp.float32)
    last = valid.shape[0] - 1
    chunks = jnp.max(valid[last : last + 1, :]).astype(jnp.int32)

    def score(c):
        first = c * CHUNK
        masks = [token < valid[pl.ds(first + i, 1), :][:, :count] for i in range(CHUNK)]
        keys = jnp.concatenate([lanes_of(pages.at[first + i], 0, held) for i in range(CHUNK)], 0)
        return jnp.where(jnp.concatenate(masks, 0), dot(keys, q, 1, 1) * SCALE, NEG)

    def weigh(c, s, top):
        p = jnp.exp(s - top)
        values = jnp.concatenate([lanes_of(pages.at[c * CHUNK + i], 1, held) for i in range(CHUNK)], 0)
        return jnp.sum(p, 0, keepdims=True), dot(p.astype(jnp.bfloat16), values, 0, 0)

    def straight(number):
        scores = [score(c) for c in range(number)]
        top = functools.reduce(jnp.maximum, [jnp.max(s, 0, keepdims=True) for s in scores], floor)
        terms = [weigh(c, s, top) for c, s in enumerate(scores)]
        total = functools.reduce(jnp.add, [t for t, _ in terms])
        acc = functools.reduce(jnp.add, [a for _, a in terms])
        write_part(out, acc, top, total, held, per_held)

    def step(c, carry):
        top, total, acc = carry
        s = score(c)
        new_top = jnp.maximum(top, jnp.max(s, 0, keepdims=True))
        fade = jnp.exp(top - new_top)
        more, part = weigh(c, s, new_top)
        return new_top, total * fade + more, acc * jnp.broadcast_to(fade, (8, count)).T[:, :1] + part

    for number in STATIC:

        @pl.when(chunks == number)
        def _(number=number):
            straight(number)

    @pl.when(chunks > STATIC[-1])
    def _():
        start = (floor, jnp.zeros((1, count), jnp.float32), jnp.zeros((count, held * HD), jnp.float32))
        top, total, acc = lax.fori_loop(0, chunks, step, start)
        write_part(out, acc, top, total, held, per_held)


def list_pages(send, wanted, owner, target, slots, page_list, slot_list, base):
    for c in range(PARTS):
        page_list[base + c] = 0
        slot_list[base + c] = -1
    at = jnp.int32(base)
    for i in range(send.shape[2]):
        hit = send[1, owner, i] == target
        page_list[at] = send[0, owner, i]
        slot_list[at] = jnp.where(hit, send[2, owner, i], -1)
        at = at + hit.astype(jnp.int32)
    at = jnp.int32(base + CAP)
    page_list[at] = 0
    slot_list[at] = -1
    for i in range(wanted.shape[1]):
        page = wanted[target, i] - owner * PRE_DEV
        hit = jnp.logical_and(page >= 0, page < PRE_DEV)
        page_list[at] = jnp.where(hit, page, 0)
        slot_list[at] = jnp.where(hit, slots + i, -1)
        at = at + hit.astype(jnp.int32)


def copy_lists(pairs, sems):
    copies = [pltpu.make_async_copy(a, b, sems.at[i]) for i, (a, b) in enumerate(pairs)]
    for copy in copies:
        copy.start()

    def ready():
        for copy in copies:
            copy.wait()

    return ready


def first_kernel(held, per_held, groups, maxp, qa, send_hbm, wanted_hbm, tables_hbm, lengths_hbm, kv, *refs):
    sent, chosen, entries, valid, send, wanted, tables, lengths = refs[:8]
    flags, listed, page_list, slot_list, list_sems, sems = refs[8:]
    group = lax.axis_index("group")
    prefill = lax.axis_index("role") == 0
    lists = ((send_hbm, send), (wanted_hbm, wanted), (tables_hbm, tables), (lengths_hbm, lengths))
    lists_ready = copy_lists(lists, list_sems)

    @pl.when(prefill)
    def _():
        lists_ready()
        copies = []
        for k in range(groups):
            target = lax.bitwise_xor(group, k)
            list_pages(send, wanted, group, target, kv.shape[0], page_list, slot_list, k * PARTS)
            for c in range(PARTS):
                at = k * PARTS + c
                copy = pltpu.make_async_copy(kv.at[page_list[at]], chosen.at[at], sems.at[at])
                copy.start()
                copies.append(copy)
                entry = slot_list[at].astype(jnp.float32)
                entries[at : at + 1, :] = jnp.full((1, LANES), entry, jnp.float32)
        for copy in copies[:PARTS]:
            copy.wait()
        owner_part(qa, chosen.at[pl.ds(0, PARTS)], entries[:PARTS, :], sent, held, per_held, maxp)
        for copy in copies[PARTS:]:
            copy.wait()

    @pl.when(jnp.logical_not(prefill))
    def _():
        fetch_pages(qa.shape[0], lists_ready, send, tables, lengths, maxp, group, kv, chosen, valid, flags, listed, sems)


def fresh_part(qa, new_kv, out, held, per_held):
    rows = qa.shape[0]
    q = query_block(qa, held, per_held)
    count = q.shape[0]
    lane_row = lax.rem(lax.broadcasted_iota(jnp.int32, (1, count), 1), rows)
    fresh = new_kv[...].astype(jnp.float32)
    fresh = jnp.concatenate([fresh, jnp.zeros_like(fresh)], 0).astype(jnp.bfloat16)
    mask = lax.broadcasted_iota(jnp.int32, (2 * rows, count), 0) == lane_row
    s = jnp.where(mask, dot(lanes_of(fresh, 0, held), q, 1, 1) * SCALE, NEG)
    top = jnp.max(s, 0, keepdims=True)
    p = jnp.exp(s - top)
    acc = dot(p.astype(jnp.bfloat16), lanes_of(fresh, 1, held), 0, 0)
    write_part(out, acc, top, jnp.sum(p, 0, keepdims=True), held, per_held)


def third_kernel(held, per_held, qa, new_kv, pages, valid, out, fresh):
    @pl.when(lax.axis_index("role") == 1)
    def _():
        fresh_part(qa, new_kv, fresh, held, per_held)
        resident_part(qa, pages, valid, out, held, per_held)


def second_kernel(held, per_held, maxp, first, count, chosen, entries, *refs):
    qas, outs = refs[:count][::-1], refs[len(refs) - count :]

    @pl.when(lax.axis_index("role") == 0)
    def _():
        for k in range(count):
            at = (first + k) * PARTS
            owner_part(
                qas[k], chosen.at[pl.ds(at, PARTS)], entries[at : at + PARTS, :], outs[k], held, per_held, maxp
            )


def merge_kernel(heads, rows, *refs):
    parts, out = refs[:-1], refs[-1]
    count = heads * rows
    pad = -len(parts) % 8
    stats = [part[count:, :].astype(jnp.float32)[:, :count] for part in parts]
    tops = jnp.concatenate([s[0:1] + (s[1:2] + s[2:3]) for s in stats], 0)
    totals = jnp.concatenate([s[3:4] + (s[4:5] + s[5:6]) for s in stats], 0)
    factors = jnp.exp(tops - jnp.max(tops, 0, keepdims=True))
    factors = factors / jnp.sum(factors * totals, 0, keepdims=True)
    factors = jnp.concatenate([factors, jnp.zeros((pad, count), jnp.float32)], 0).T
    terms = [factors[:, i : i + 1] * part[:count, :].astype(jnp.float32) for i, part in enumerate(parts)]
    merged = functools.reduce(jnp.add, terms)
    out[...] = jnp.concatenate([merged[h * rows : (h + 1) * rows] for h in range(heads)], 1).astype(out.dtype)


def project_kernel(steps, attended, partner, weight, *outs):
    share = outs[0].shape[1]
    here = jnp.where(lax.axis_index("role") == 0, partner[...].astype(jnp.float32), attended[...].astype(jnp.float32))
    here = here.astype(jnp.bfloat16)
    for d, out in zip(steps, outs):
        first = lax.bitwise_xor(lax.axis_index("tp"), d) * share
        columns = pl.ds(pl.multiple_of(first, LANES), share)
        out[...] = jnp.dot(here, weight[:, columns], preferred_element_type=jnp.float32).astype(out.dtype)


def per_device(kv_pages, send_list, wanted, lengths, tables, queries, new_kv, out_weight):
    stored = kv_pages[0, 0, 0]
    slots = stored.shape[0]
    groups, tps = lax.axis_size("group"), lax.axis_size("tp")
    held = max(1, KVH // tps)
    rows, wide = queries.shape[1], queries.shape[2]
    heads = wide // HD
    per_held = heads // held
    maxp = tables.shape[2]
    send = jnp.transpose(send_list, (2, 0, 1))
    def place(block, at):
        return jnp.pad(block, ((0, rows - block.shape[0]), (at, wide + LANES - at - block.shape[1])))

    high = lax.shift_right_logical(place(lengths, wide + maxp), 3)
    low = jnp.bitwise_and(place(lengths, wide + maxp + rows), 7)
    integers = place(tables[0], wide) + high + low
    qa = place(queries[0], 0) + integers.astype(jnp.bfloat16)
    def paired(value, k, to_decode):
        first, second = (0, groups) if to_decode else (groups, 0)
        pairs = [pair for i in range(groups) for pair in ((first + i, second + (i ^ k)), (second + i, first + i))]
        return lax.ppermute(value, ("role", "group"), pairs)

    asked = [paired(qa, k, False) for k in range(1, groups)]
    part_shape = jax.ShapeDtypeStruct((heads * rows + STATS, HD), jnp.float32)
    sent_shape = jax.ShapeDtypeStruct(part_shape.shape, jnp.bfloat16)
    vmem = pl.BlockSpec(memory_space=pltpu.VMEM)
    hbm = pl.BlockSpec(memory_space=pltpu.HBM)
    page_shape = stored.shape[1:]
    chosen_count = groups * PARTS
    read_count = -(-rows * maxp // CHUNK) * CHUNK
    page_count = max(read_count, chosen_count)
    lists = [send, wanted, tables[0], lengths]
    pinned = [pltpu.with_memory_space_constraint(x, pltpu.HBM) for x in lists + [stored]]
    mine_sent, chosen, entries, valid = pl.pallas_call(
        functools.partial(first_kernel, held, per_held, groups, maxp),
        out_shape=[
            sent_shape,
            jax.ShapeDtypeStruct((page_count,) + page_shape, jnp.bfloat16),
            jax.ShapeDtypeStruct((chosen_count, LANES), jnp.float32),
            jax.ShapeDtypeStruct((read_count + 8, LANES), jnp.float32),
        ],
        in_specs=[vmem] + [hbm] * 5,
        out_specs=[vmem] * 4,
        scratch_shapes=[
            *[pltpu.SMEM(x.shape, jnp.int32) for x in lists],
            pltpu.SMEM((slots + 1,), jnp.int32),
            pltpu.SMEM((2, read_count), jnp.int32),
            pltpu.SMEM((chosen_count + 1,), jnp.int32),
            pltpu.SMEM((chosen_count + 1,), jnp.int32),
            pltpu.SemaphoreType.DMA((len(lists),)),
            pltpu.SemaphoreType.DMA((page_count,)),
        ],
        compiler_params=pltpu.CompilerParams(vmem_limit_bytes=20 * MIB),
        name="resident",
    )(qa, *pinned)
    theirs = []
    for first, messages in ((1, asked[:-1]), (groups - 1, asked[-1:])):
        theirs += pl.pallas_call(
            functools.partial(second_kernel, held, per_held, maxp, first, len(messages)),
            out_shape=[sent_shape] * len(messages),
            in_specs=[vmem] * (2 + len(messages) + len(theirs)),
            out_specs=[vmem] * len(messages),
            compiler_params=pltpu.CompilerParams(vmem_limit_bytes=16 * MIB),
            cost_estimate=pl.CostEstimate(flops=2 * 10**10, bytes_accessed=8 * MIB, transcendentals=10**6),
            name="owned",
        )(chosen, entries, *reversed(messages), *theirs)
    qa, mine_sent, theirs = lax.optimization_barrier((qa, mine_sent, theirs))
    mine, fresh = pl.pallas_call(
        functools.partial(third_kernel, held, per_held),
        out_shape=[part_shape] * 2,
        in_specs=[vmem] * 4,
        out_specs=[vmem] * 2,
        compiler_params=pltpu.CompilerParams(vmem_limit_bytes=16 * MIB),
        name="attend",
    )(qa, new_kv[0], chosen, valid)
    parts = [mine, fresh] + [paired(part, k, True) for k, part in enumerate([mine_sent, *theirs])][::-1]
    attended = pl.pallas_call(
        functools.partial(merge_kernel, heads, rows),
        out_shape=jax.ShapeDtypeStruct((rows, wide), jnp.bfloat16),
        in_specs=[vmem] * len(parts),
        out_specs=vmem,
        compiler_params=pltpu.CompilerParams(vmem_limit_bytes=8 * MIB),
        name="merge",
    )(*parts)
    partner = lax.ppermute(attended, "role", [(0, 1), (1, 0)])
    share = out_weight.shape[1] // tps

    def project(steps, dtype, name):
        return pl.pallas_call(
            functools.partial(project_kernel, steps),
            out_shape=[jax.ShapeDtypeStruct((rows, share), dtype)] * len(steps),
            in_specs=[vmem] * 3,
            out_specs=[vmem] * len(steps),
            compiler_params=pltpu.CompilerParams(vmem_limit_bytes=24 * MIB),
            cost_estimate=pl.CostEstimate(
                flops=len(steps) * 32 * wide * share, bytes_accessed=len(steps) * 2 * wide * share, transcendentals=0
            ),
            name=name,
        )(attended, partner, out_weight)

    steps = sorted(range(1, tps), key=lambda d: -d.bit_count())
    sent = project(steps, jnp.bfloat16, "project")
    arrived = [lax.ppermute(part, "tp", [(i, i ^ d) for i in range(tps)]) for d, part in zip(steps, sent)]
    own = project([0], jnp.float32, "project_own")[0]
    total = functools.reduce(jnp.add, [part.astype(jnp.float32) for part in arrived], own)
    return total.astype(jnp.bfloat16)[None]


def solution(mesh):
    return jax.shard_map(
        per_device,
        mesh=mesh,
        in_specs=(
            P("role", "group", "tp", None, None, None),
            P(),
            P(),
            P("group", None),
            P("group", None, None),
            P("group", None, "tp"),
            P("group", None, "tp"),
            P("tp", "role"),
        ),
        out_specs=P("group", None, ("role", "tp")),
        check_vma=False,
    )
```

```python
import functools
import math

import jax
import jax.numpy as jnp
from jax import lax
from jax.experimental import pallas as pl
from jax.experimental.pallas import tpu as pltpu
from jax.sharding import PartitionSpec as P

KVH = 8
HD = 128
CAP = 4
CAPP = 2
PRE_DEV = 8
LANES = 128
PAGE = 128
NEG = -1e30
FLOOR = -1e29
SCALE = 1.0 / math.sqrt(HD)
PARTS = CAP + CAPP
CHUNK = 8
STATIC = (2, 3, 4, 5)
STATS = 16
MIB = 2**20


def dot(a, b, ca, cb):
    return lax.dot_general(a, b, (((ca,), (cb,)), ((), ())), preferred_element_type=jnp.float32)


def query_block(qa, held, per_held):
    q = qa[:, : held * per_held * HD].astype(jnp.float32)
    rows = q.shape[0]
    bands = []
    for j in range(held):
        heads = [q[:, (j * per_held + i) * HD : (j * per_held + i + 1) * HD] for i in range(per_held)]
        band = jnp.concatenate(heads, 0)
        blank = jnp.zeros_like(band)
        bands.append(jnp.concatenate([band if i == j else blank for i in range(held)], 1))
    return jnp.concatenate(bands, 0).astype(jnp.bfloat16)


def entry_rows(qa, held, per_held, maxp):
    rows = qa.shape[0]
    wide = held * per_held * HD
    aux = qa[:, wide : wide + LANES].astype(jnp.float32)
    lane = lax.broadcasted_iota(jnp.int32, (rows, LANES), 1) - maxp
    row = lax.broadcasted_iota(jnp.int32, (rows, LANES), 0)
    parts = jnp.where(lane == row, 8.0 * aux[:1], jnp.where(lane == row + rows, aux[:1], 0.0))
    length = jnp.sum(parts, 1, keepdims=True)
    turned = jnp.concatenate([jnp.where(lane == 0, length, aux)] * (held * per_held), 0).T
    first = lax.broadcasted_iota(jnp.int32, (maxp, 1), 0).astype(jnp.float32) * PAGE
    return turned[:maxp], jnp.clip(turned[maxp : maxp + 1] - first, 0.0, PAGE)


def lanes_of(page, first, held):
    return jnp.concatenate([page[:, (2 * j + first) * HD : (2 * j + first + 1) * HD] for j in range(held)], 1)


def pieces(x):
    high = x.astype(jnp.bfloat16).astype(jnp.float32)
    middle = (x - high).astype(jnp.bfloat16).astype(jnp.float32)
    return [high, middle, x - high - middle]


def write_part(out, acc, top, total, held, per_held):
    count = acc.shape[0]
    band = count // held
    out[:count, :] = jnp.concatenate(
        [acc[j * band : (j + 1) * band, j * HD : (j + 1) * HD] for j in range(held)], 0
    ).astype(out.dtype)
    rows = pieces(top) + pieces(total)
    block = jnp.concatenate(rows + [jnp.zeros((STATS - len(rows), count), jnp.float32)], 0)
    if count < LANES:
        block = jnp.concatenate([block, jnp.zeros((STATS, LANES - count), jnp.float32)], 1)
    out[count:, :] = block.astype(out.dtype)


def owner_part(qa, pages, entries, out, held, per_held, maxp):
    q = query_block(qa, held, per_held)
    tab, cnt = entry_rows(qa, held, per_held, maxp)
    count = q.shape[0]
    token = lax.broadcasted_iota(jnp.int32, (PAGE, count), 0).astype(jnp.float32)
    masks = []
    for c in range(PARTS):
        valid = jnp.sum(jnp.where(tab == entries[c : c + 1, :count], cnt, 0.0), 0, keepdims=True)
        masks.append(token < valid)
    mask = jnp.concatenate(masks, 0)
    keys = jnp.concatenate([lanes_of(pages.at[c], 0, held) for c in range(PARTS)], 0)
    values = jnp.concatenate([lanes_of(pages.at[c], 1, held) for c in range(PARTS)], 0)
    s = jnp.where(mask, dot(keys, q, 1, 1) * SCALE, NEG)
    top = jnp.max(s, 0, keepdims=True)
    p = jnp.where(mask, jnp.exp(s - top), 0.0)
    total = jnp.sum(p, 0, keepdims=True)
    acc = dot(p.astype(jnp.bfloat16), values, 0, 0)
    write_part(out, acc, top, total, held, per_held)


def fetch_pages(rows, lists_ready, send, tables, lengths, maxp, group, kv, pages, valid, flags, listed, sems):
    slots = kv.shape[0]
    lane_row = lax.rem(lax.broadcasted_iota(jnp.int32, (1, LANES), 1), rows)
    for i in range(slots):
        flags[i] = 0
    lists_ready()
    for o in range(send.shape[1]):
        for i in range(send.shape[2]):
            flags[jnp.where(send[1, o, i] == group, send[2, o, i], slots)] = 1

    def page_copy(slot, i):
        return pltpu.make_async_copy(kv.at[slot], pages.at[i], sems.at[i])

    found = jnp.int32(0)
    for r in range(rows):
        length = lengths[0, r]
        for e in range(maxp):
            slot = tables[r, e]
            tokens = jnp.minimum(length - e * PAGE, PAGE)
            here = jnp.logical_and(slot < slots, flags[jnp.minimum(slot, slots - 1)] == 0)
            needed = jnp.logical_and(tokens > 0, here)

            listed[0, found] = r
            listed[1, found] = tokens

            @pl.when(needed)
            def _(slot=slot, at=found):
                page_copy(slot, at).start()

            found = found + needed.astype(jnp.int32)
    chunks = jnp.maximum((found + CHUNK - 1) // CHUNK, STATIC[0])

    def fill(i, _):
        page_copy(0, i).start()
        listed[0, i] = 0
        listed[1, i] = 0
        return 0

    lax.fori_loop(found, chunks * CHUNK, fill, 0)
    last = valid.shape[0] - 1
    valid[last : last + 1, :] = jnp.full((1, LANES), chunks.astype(jnp.float32), jnp.float32)

    def describe(c, _):
        for i in range(CHUNK):
            at = c * CHUNK + i
            tokens = listed[1, at].astype(jnp.float32)
            valid[pl.ds(at, 1), :] = jnp.where(lane_row == listed[0, at], tokens, 0.0)
        return 0

    lax.fori_loop(0, chunks, describe, 0)

    def wait(c, _):
        for i in range(CHUNK):
            page_copy(0, c * CHUNK + i).wait()
        return 0

    lax.fori_loop(0, chunks, wait, 0)


def resident_part(qa, pages, valid, out, held, per_held):
    q = query_block(qa, held, per_held)
    count = q.shape[0]
    token = lax.broadcasted_iota(jnp.int32, (PAGE, count), 0).astype(jnp.float32)
    floor = jnp.full((1, count), FLOOR, jnp.float32)
    last = valid.shape[0] - 1
    chunks = jnp.max(valid[last : last + 1, :]).astype(jnp.int32)

    def score(c):
        first = c * CHUNK
        masks = [token < valid[pl.ds(first + i, 1), :][:, :count] for i in range(CHUNK)]
        keys = jnp.concatenate([lanes_of(pages.at[first + i], 0, held) for i in range(CHUNK)], 0)
        return jnp.where(jnp.concatenate(masks, 0), dot(keys, q, 1, 1) * SCALE, NEG)

    def weigh(c, s, top):
        p = jnp.exp(s - top)
        values = jnp.concatenate([lanes_of(pages.at[c * CHUNK + i], 1, held) for i in range(CHUNK)], 0)
        return jnp.sum(p, 0, keepdims=True), dot(p.astype(jnp.bfloat16), values, 0, 0)

    def straight(number):
        scores = [score(c) for c in range(number)]
        top = functools.reduce(jnp.maximum, [jnp.max(s, 0, keepdims=True) for s in scores], floor)
        terms = [weigh(c, s, top) for c, s in enumerate(scores)]
        total = functools.reduce(jnp.add, [t for t, _ in terms])
        acc = functools.reduce(jnp.add, [a for _, a in terms])
        write_part(out, acc, top, total, held, per_held)

    def step(c, carry):
        top, total, acc = carry
        s = score(c)
        new_top = jnp.maximum(top, jnp.max(s, 0, keepdims=True))
        fade = jnp.exp(top - new_top)
        more, part = weigh(c, s, new_top)
        return new_top, total * fade + more, acc * jnp.broadcast_to(fade, (8, count)).T[:, :1] + part

    for number in STATIC:

        @pl.when(chunks == number)
        def _(number=number):
            straight(number)

    @pl.when(chunks > STATIC[-1])
    def _():
        start = (floor, jnp.zeros((1, count), jnp.float32), jnp.zeros((count, held * HD), jnp.float32))
        top, total, acc = lax.fori_loop(0, chunks, step, start)
        write_part(out, acc, top, total, held, per_held)


def list_pages(send, wanted, owner, target, slots, page_list, slot_list, base):
    for c in range(PARTS):
        page_list[base + c] = 0
        slot_list[base + c] = -1
    at = jnp.int32(base)
    for i in range(send.shape[2]):
        hit = send[1, owner, i] == target
        page_list[at] = send[0, owner, i]
        slot_list[at] = jnp.where(hit, send[2, owner, i], -1)
        at = at + hit.astype(jnp.int32)
    at = jnp.int32(base + CAP)
    page_list[at] = 0
    slot_list[at] = -1
    for i in range(wanted.shape[1]):
        page = wanted[target, i] - owner * PRE_DEV
        hit = jnp.logical_and(page >= 0, page < PRE_DEV)
        page_list[at] = jnp.where(hit, page, 0)
        slot_list[at] = jnp.where(hit, slots + i, -1)
        at = at + hit.astype(jnp.int32)


def copy_lists(pairs, sems):
    copies = [pltpu.make_async_copy(a, b, sems.at[i]) for i, (a, b) in enumerate(pairs)]
    for copy in copies:
        copy.start()

    def ready():
        for copy in copies:
            copy.wait()

    return ready


def first_kernel(held, per_held, groups, maxp, qa, send_hbm, wanted_hbm, tables_hbm, lengths_hbm, kv, *refs):
    sent, chosen, entries, valid, send, wanted, tables, lengths = refs[:8]
    flags, listed, page_list, slot_list, list_sems, sems = refs[8:]
    group = lax.axis_index("group")
    prefill = lax.axis_index("role") == 0
    lists = ((send_hbm, send), (wanted_hbm, wanted), (tables_hbm, tables), (lengths_hbm, lengths))
    lists_ready = copy_lists(lists, list_sems)

    @pl.when(prefill)
    def _():
        lists_ready()
        copies = []
        for k in range(groups):
            target = lax.bitwise_xor(group, k)
            list_pages(send, wanted, group, target, kv.shape[0], page_list, slot_list, k * PARTS)
            for c in range(PARTS):
                at = k * PARTS + c
                copy = pltpu.make_async_copy(kv.at[page_list[at]], chosen.at[at], sems.at[at])
                copy.start()
                copies.append(copy)
                entry = slot_list[at].astype(jnp.float32)
                entries[at : at + 1, :] = jnp.full((1, LANES), entry, jnp.float32)
        for copy in copies[:PARTS]:
            copy.wait()
        owner_part(qa, chosen.at[pl.ds(0, PARTS)], entries[:PARTS, :], sent, held, per_held, maxp)
        for copy in copies[PARTS:]:
            copy.wait()

    @pl.when(jnp.logical_not(prefill))
    def _():
        fetch_pages(qa.shape[0], lists_ready, send, tables, lengths, maxp, group, kv, chosen, valid, flags, listed, sems)


def fresh_part(qa, new_kv, out, held, per_held):
    rows = qa.shape[0]
    q = query_block(qa, held, per_held)
    count = q.shape[0]
    lane_row = lax.rem(lax.broadcasted_iota(jnp.int32, (1, count), 1), rows)
    fresh = new_kv[...].astype(jnp.float32)
    fresh = jnp.concatenate([fresh, jnp.zeros_like(fresh)], 0).astype(jnp.bfloat16)
    mask = lax.broadcasted_iota(jnp.int32, (2 * rows, count), 0) == lane_row
    s = jnp.where(mask, dot(lanes_of(fresh, 0, held), q, 1, 1) * SCALE, NEG)
    top = jnp.max(s, 0, keepdims=True)
    p = jnp.exp(s - top)
    acc = dot(p.astype(jnp.bfloat16), lanes_of(fresh, 1, held), 0, 0)
    write_part(out, acc, top, jnp.sum(p, 0, keepdims=True), held, per_held)


def third_kernel(held, per_held, qa, new_kv, pages, valid, out, fresh):
    @pl.when(lax.axis_index("role") == 1)
    def _():
        fresh_part(qa, new_kv, fresh, held, per_held)
        resident_part(qa, pages, valid, out, held, per_held)


def second_kernel(held, per_held, maxp, first, count, chosen, entries, *refs):
    qas, outs = refs[:count][::-1], refs[len(refs) - count :]

    @pl.when(lax.axis_index("role") == 0)
    def _():
        for k in range(count):
            at = (first + k) * PARTS
            owner_part(
                qas[k], chosen.at[pl.ds(at, PARTS)], entries[at : at + PARTS, :], outs[k], held, per_held, maxp
            )


def merge_kernel(heads, rows, *refs):
    parts, out = refs[:-1], refs[-1]
    count = heads * rows
    pad = -len(parts) % 8
    stats = [part[count:, :].astype(jnp.float32)[:, :count] for part in parts]
    tops = jnp.concatenate([s[0:1] + (s[1:2] + s[2:3]) for s in stats], 0)
    totals = jnp.concatenate([s[3:4] + (s[4:5] + s[5:6]) for s in stats], 0)
    factors = jnp.exp(tops - jnp.max(tops, 0, keepdims=True))
    factors = factors / jnp.sum(factors * totals, 0, keepdims=True)
    factors = jnp.concatenate([factors, jnp.zeros((pad, count), jnp.float32)], 0).T
    terms = [factors[:, i : i + 1] * part[:count, :].astype(jnp.float32) for i, part in enumerate(parts)]
    merged = functools.reduce(jnp.add, terms)
    out[...] = jnp.concatenate([merged[h * rows : (h + 1) * rows] for h in range(heads)], 1).astype(out.dtype)


def project_kernel(steps, attended, partner, weight, *outs):
    share = outs[0].shape[1]
    here = jnp.where(lax.axis_index("role") == 0, partner[...].astype(jnp.float32), attended[...].astype(jnp.float32))
    here = here.astype(jnp.bfloat16)
    for d, out in zip(steps, outs):
        first = lax.bitwise_xor(lax.axis_index("tp"), d) * share
        columns = pl.ds(pl.multiple_of(first, LANES), share)
        out[...] = jnp.dot(here, weight[:, columns], preferred_element_type=jnp.float32).astype(out.dtype)


def per_device(kv_pages, send_list, wanted, lengths, tables, queries, new_kv, out_weight):
    stored = kv_pages[0, 0, 0]
    slots = stored.shape[0]
    groups, tps = lax.axis_size("group"), lax.axis_size("tp")
    held = max(1, KVH // tps)
    rows, wide = queries.shape[1], queries.shape[2]
    heads = wide // HD
    per_held = heads // held
    maxp = tables.shape[2]
    send = jnp.transpose(send_list, (2, 0, 1))
    def place(block, at):
        return jnp.pad(block, ((0, rows - block.shape[0]), (at, wide + LANES - at - block.shape[1])))

    high = lax.shift_right_logical(place(lengths, wide + maxp), 3)
    low = jnp.bitwise_and(place(lengths, wide + maxp + rows), 7)
    integers = place(tables[0], wide) + high + low
    qa = place(queries[0], 0) + integers.astype(jnp.bfloat16)
    def paired(value, k, to_decode):
        first, second = (0, groups) if to_decode else (groups, 0)
        pairs = [pair for i in range(groups) for pair in ((first + i, second + (i ^ k)), (second + i, first + i))]
        return lax.ppermute(value, ("role", "group"), pairs)

    asked = [paired(qa, k, False) for k in range(1, groups)]
    part_shape = jax.ShapeDtypeStruct((heads * rows + STATS, HD), jnp.float32)
    sent_shape = jax.ShapeDtypeStruct(part_shape.shape, jnp.bfloat16)
    vmem = pl.BlockSpec(memory_space=pltpu.VMEM)
    hbm = pl.BlockSpec(memory_space=pltpu.HBM)
    page_shape = stored.shape[1:]
    chosen_count = groups * PARTS
    read_count = -(-rows * maxp // CHUNK) * CHUNK
    page_count = max(read_count, chosen_count)
    lists = [send, wanted, tables[0], lengths]
    pinned = [pltpu.with_memory_space_constraint(x, pltpu.HBM) for x in lists + [stored]]
    mine_sent, chosen, entries, valid = pl.pallas_call(
        functools.partial(first_kernel, held, per_held, groups, maxp),
        out_shape=[
            sent_shape,
            jax.ShapeDtypeStruct((page_count,) + page_shape, jnp.bfloat16),
            jax.ShapeDtypeStruct((chosen_count, LANES), jnp.float32),
            jax.ShapeDtypeStruct((read_count + 8, LANES), jnp.float32),
        ],
        in_specs=[vmem] + [hbm] * 5,
        out_specs=[vmem] * 4,
        scratch_shapes=[
            *[pltpu.SMEM(x.shape, jnp.int32) for x in lists],
            pltpu.SMEM((slots + 1,), jnp.int32),
            pltpu.SMEM((2, read_count), jnp.int32),
            pltpu.SMEM((chosen_count + 1,), jnp.int32),
            pltpu.SMEM((chosen_count + 1,), jnp.int32),
            pltpu.SemaphoreType.DMA((len(lists),)),
            pltpu.SemaphoreType.DMA((page_count,)),
        ],
        compiler_params=pltpu.CompilerParams(vmem_limit_bytes=20 * MIB),
        name="resident",
    )(qa, *pinned)
    theirs = []
    for first, messages in ((1, asked[:-1]), (groups - 1, asked[-1:])):
        theirs += pl.pallas_call(
            functools.partial(second_kernel, held, per_held, maxp, first, len(messages)),
            out_shape=[sent_shape] * len(messages),
            in_specs=[vmem] * (2 + len(messages) + len(theirs)),
            out_specs=[vmem] * len(messages),
            compiler_params=pltpu.CompilerParams(vmem_limit_bytes=16 * MIB),
            cost_estimate=pl.CostEstimate(flops=2 * 10**10, bytes_accessed=8 * MIB, transcendentals=10**6),
            name="owned",
        )(chosen, entries, *reversed(messages), *theirs)
    qa, mine_sent, theirs = lax.optimization_barrier((qa, mine_sent, theirs))
    mine, fresh = pl.pallas_call(
        functools.partial(third_kernel, held, per_held),
        out_shape=[part_shape] * 2,
        in_specs=[vmem] * 4,
        out_specs=[vmem] * 2,
        compiler_params=pltpu.CompilerParams(vmem_limit_bytes=16 * MIB),
        name="attend",
    )(qa, new_kv[0], chosen, valid)
    parts = [mine, fresh] + [paired(part, k, True) for k, part in enumerate([mine_sent, *theirs])][::-1]
    attended = pl.pallas_call(
        functools.partial(merge_kernel, heads, rows),
        out_shape=jax.ShapeDtypeStruct((rows, wide), jnp.bfloat16),
        in_specs=[vmem] * len(parts),
        out_specs=vmem,
        compiler_params=pltpu.CompilerParams(vmem_limit_bytes=8 * MIB),
        name="merge",
    )(*parts)
    partner = lax.ppermute(attended, "role", [(0, 1), (1, 0)])
    share = out_weight.shape[1] // tps

    def project(steps, dtype, name):
        return pl.pallas_call(
            functools.partial(project_kernel, steps),
            out_shape=[jax.ShapeDtypeStruct((rows, share), dtype)] * len(steps),
            in_specs=[vmem] * 3,
            out_specs=[vmem] * len(steps),
            compiler_params=pltpu.CompilerParams(vmem_limit_bytes=24 * MIB),
            cost_estimate=pl.CostEstimate(
                flops=len(steps) * 32 * wide * share, bytes_accessed=len(steps) * 2 * wide * share, transcendentals=0
            ),
            name=name,
        )(attended, partner, out_weight)

    steps = sorted(range(1, tps), key=lambda d: d.bit_count())
    sent = project(steps, jnp.bfloat16, "project")
    arrived = [lax.ppermute(part, "tp", [(i, i ^ d) for i in range(tps)]) for d, part in zip(steps, sent)]
    own = project([0], jnp.float32, "project_own")[0]
    total = functools.reduce(jnp.add, [part.astype(jnp.float32) for part in arrived], own)
    return total.astype(jnp.bfloat16)[None]


def solution(mesh):
    return jax.shard_map(
        per_device,
        mesh=mesh,
        in_specs=(
            P("role", "group", "tp", None, None, None),
            P(),
            P(),
            P("group", None),
            P("group", None, None),
            P("group", None, "tp"),
            P("group", None, "tp"),
            P("tp", "role"),
        ),
        out_specs=P("group", None, ("role", "tp")),
        check_vma=False,
    )
```
